32 devices in a mesh: row: 4 (over z), col: 8 (over y, x, core).
Axes of the slice: x: 2, y: 2, z: 4, core: 2. Of those that a mesh axis runs over, the one named last changes fastest.
Arguments:
- inputs: bfloat16 [4096, 2048], P('row', 'col'), may hold values from -6 to 6
- query_weight: bfloat16 [2048, 2048], P('row', 'col'), may hold values from -0.125 to 0.125
- key_weight: bfloat16 [2048, 2048], P('row', 'col'), may hold values from -0.125 to 0.125
- value_weight: bfloat16 [2048, 2048], P('row', 'col'), may hold values from -0.125 to 0.125
- out_weight: bfloat16 [2048, 2048], P('row', 'col'), may hold values from -2 to 2
- gate_weight: bfloat16 [2048, 8192], P('row', 'col'), may hold values from -0.125 to 0.125
- up_weight: bfloat16 [2048, 8192], P('row', 'col'), may hold values from -0.125 to 0.125
- down_weight: bfloat16 [2048, 8192], P('row', 'col'), may hold values from -0.0625 to 0.0625
- first_gain: bfloat16 [2048], P('row'), may hold values from 0.5 to 1.5
- second_gain: bfloat16 [2048], P('row'), may hold values from 0.5 to 1.5
- segment_ids: int32 [4096], P('row'), may hold values from 0 to 7, as said below
- positions: int32 [4096], P('row'), may hold values from 0 to 767, as said below
- out_grad: bfloat16 [4096, 2048], P('row', 'col'), may hold values from -6 to 6
Outputs:
- block_out: bfloat16 [4096, 2048], P('row', 'col')
- input_grad: bfloat16 [4096, 2048], P('row', 'col')
- query_weight_grad: float32 [2048, 2048], P('row', 'col')
- key_weight_grad: float32 [2048, 2048], P('row', 'col')
- value_weight_grad: float32 [2048, 2048], P('row', 'col')
- out_weight_grad: float32 [2048, 2048], P('row', 'col')
- gate_weight_grad: float32 [2048, 8192], P('row', 'col')
- up_weight_grad: float32 [2048, 8192], P('row', 'col')
- down_weight_grad: float32 [2048, 8192], P('row', 'col')
- first_gain_grad: float32 [2048], P('row')
- second_gain_grad: float32 [2048], P('row')
The draws below stay inside these ranges and needn't reach their ends.
Inputs may be any that keep to these rules, and one draw needn't show every extreme that they name: `segment_ids`: ids never fall along the rows. Each aligned block of 1024 rows holds two documents, numbered 2 b and 2 b + 1 in block b; the second starts at a row from 256 to 768 of its block. `positions`: each row's offset from the first row of its document.
All inputs are finite; a program needn't handle non-finite values.
Results may differ from the reference program's by a relative error of at most 0.019.
Values may be sent and summed in bfloat16 or wider, within the bound.
No kernel may reach another device: no remote copies, remote signals or barrier semaphores. Data moves between devices by JAX's collectives and lax.ppermute only.
A program may use at most 192 MiB of HBM per device.

```python
import math
import jax
import jax.numpy as jnp
from jax import lax

D = 2048
HEADS = 32
HEAD_DIM = 64
FF = 8192
SEQ = 1024
TOKENS = 4096


def split_points(key):
    block_count = TOKENS // SEQ
    drawn = jax.random.randint(jax.random.fold_in(key, 17), (block_count,), SEQ // 4, 3 * SEQ // 4 + 1)
    first_block = jnp.arange(block_count, dtype=jnp.int32) == 0
    return jnp.where(first_block, SEQ // 4, drawn).astype(jnp.int32)


def draw_segment_ids(key, part):
    cut_rows = split_points(key)
    offset = jnp.arange(SEQ, dtype=jnp.int32)
    later = (offset[None, :] >= cut_rows[:, None]).astype(jnp.int32)
    numbers = 2 * jnp.arange(TOKENS // SEQ, dtype=jnp.int32)[:, None] + later
    return numbers.reshape(TOKENS).astype(jnp.int32)


def draw_positions(key, part):
    cut_rows = split_points(key)
    offset = jnp.arange(SEQ, dtype=jnp.int32)[None, :]
    placed = jnp.where(offset >= cut_rows[:, None], offset - cut_rows[:, None], offset)
    return placed.reshape(TOKENS).astype(jnp.int32)


def block_scale(own_key, dims, split, smallest, largest):
    def one(position, blocks):
        heights = jax.random.uniform(jax.random.fold_in(jax.random.fold_in(own_key, 6), position), (blocks,), jnp.float32, smallest / len(split), largest / len(split))
        return jnp.repeat(jnp.exp(heights), dims[position] // blocks).reshape((-1,) + (1,) * (len(dims) - position - 1))

    level = one(*split[0])
    for cut in split[1:]:
        level = level * one(*cut)
    return level


def bell_draw(own_key, dims, scale, reach, cuts=(), kind=jnp.bfloat16):
    values = jax.random.normal(own_key, dims, jnp.float32) * scale
    if len(cuts) > 0:
        values = block_scale(own_key, dims, cuts, -0.22, 0.18) * values
    return jnp.clip(values, min=-reach, max=reach).astype(kind)


def setup_inputs(seed: int = 0) -> dict:
    key_of = jax.random.split(jax.random.key(seed), 14)
    return {
        "inputs": bell_draw(key_of[0], (TOKENS, D), 1.0, 6.0, ((0, 4), (1, 8))),
        "query_weight": bell_draw(key_of[1], (D, D), D ** -0.5, 0.125, ((0, 4), (1, 8))),
        "key_weight": bell_draw(key_of[2], (D, D), D ** -0.5, 0.125, ((0, 4), (1, 8))),
        "value_weight": bell_draw(key_of[3], (D, D), D ** -0.5, 0.125, ((0, 4), (1, 8))),
        "out_weight": bell_draw(key_of[4], (D, D), (4 * D // SEQ) ** -0.5, 2.0, ((0, 4), (1, 8))),
        "gate_weight": bell_draw(key_of[5], (D, FF), D ** -0.5, 0.125, ((0, 4), (1, 8))),
        "up_weight": bell_draw(key_of[6], (D, FF), D ** -0.5, 0.125, ((0, 4), (1, 8))),
        "down_weight": bell_draw(key_of[7], (D, FF), FF ** -0.5, 0.0625, ((0, 4), (1, 8))),
        "first_gain": jnp.clip(1.0 + 0.1 * jax.random.normal(key_of[8], (D,), jnp.float32), 0.5, 1.5).astype(jnp.bfloat16),
        "second_gain": jnp.clip(1.0 + 0.1 * jax.random.normal(key_of[9], (D,), jnp.float32), 0.5, 1.5).astype(jnp.bfloat16),
        "segment_ids": draw_segment_ids(jax.random.fold_in(key_of[13], 71), 0),
        "positions": draw_positions(jax.random.fold_in(key_of[13], 71), 0),
        "out_grad": bell_draw(key_of[12], (TOKENS, D), 1.0, 6.0, ((0, 4), (1, 8))),
    }


@jax.custom_vjp
def low(v):
    return lax.optimization_barrier(v.astype(jnp.bfloat16)).astype(jnp.float32)

@jax.custom_vjp
def low_back(v):
    return v

def low_keep(v):
    return (low(v), None)

def low_pass(kept, grad):
    return (grad,)

def back_keep(v):
    return (v, None)

def back_low(kept, grad):
    return (low(grad),)
low.defvjp(low_keep, low_pass)
low_back.defvjp(back_keep, back_low)
eps = 1e-05
rope_base = 130000.0
highest = lax.Precision.HIGHEST

def product(left, right):
    return jnp.dot(left, right, precision=highest, preferred_element_type=jnp.float32)

def product_rows(left, right):
    return lax.dot_general(left, right, (((1,), (1,)), ((), ())), precision=highest, preferred_element_type=jnp.float32)

def rms_scaled(values, gain):
    return values * lax.rsqrt(lax.optimization_barrier(jnp.mean(values * values, axis=-1, keepdims=True)) + eps) * gain

def rope_tables(positions, head_size):
    half_size = head_size // 2
    freqs = jnp.exp(jnp.arange(half_size, dtype=jnp.float32) * (-2.0 * math.log(rope_base) / head_size))
    angles = positions.astype(jnp.float32)[:, None] * freqs[None, :]
    return (jnp.cos(angles), jnp.sin(angles))

def rotate(values, cosine, sine):
    half_size = values.shape[-1] // 2
    front_half = values[..., :half_size]
    back_half = values[..., half_size:]
    cosine_wide = cosine[:, None, :]
    sine_wide = sine[:, None, :]
    return jnp.concatenate([front_half * cosine_wide - back_half * sine_wide, back_half * cosine_wide + front_half * sine_wide], axis=-1)

def head_attention(query_head, key_head, value_head, allowed):
    scores = low_back(product_rows(query_head, key_head) * HEAD_DIM ** (-0.5))
    scores = jnp.where(allowed, scores, -1e+30)
    weights = jax.nn.softmax(scores, axis=-1)
    return product(low(weights), value_head)

def layer_block(inputs, query_weight, key_weight, value_weight, out_weight, gate_weight, up_weight, down_weight, first_gain, second_gain, segment_ids, positions):
    row_count = inputs.shape[0]
    normed = low(rms_scaled(inputs, first_gain))
    cosine, sine = rope_tables(positions, HEAD_DIM)
    query_rows = low_back(product(normed, query_weight)).reshape(row_count, HEADS, HEAD_DIM)
    query_rows = low(rotate(query_rows, cosine, sine))
    key_rows = low_back(product(normed, key_weight)).reshape(row_count, HEADS, HEAD_DIM)
    key_rows = low(rotate(key_rows, cosine, sine))
    value_rows = low(low_back(product(normed, value_weight))).reshape(row_count, HEADS, HEAD_DIM)
    index_rows = jnp.arange(row_count)
    allowed = (segment_ids[:, None] == segment_ids[None, :]) & (index_rows[:, None] >= index_rows[None, :])
    per_head = jax.checkpoint(lambda pieces: head_attention(pieces[0], pieces[1], pieces[2], allowed))
    attended = lax.map(per_head, (query_rows.transpose(1, 0, 2), key_rows.transpose(1, 0, 2), value_rows.transpose(1, 0, 2)))
    attended = attended.transpose(1, 0, 2).reshape(row_count, HEADS * HEAD_DIM)
    mixed = low(low_back(attended))
    attention = low_back(product_rows(mixed, out_weight))
    middle = inputs + attention
    normed_mid = low(rms_scaled(middle, second_gain))
    gate_rows = low_back(product(normed_mid, gate_weight))
    up_rows = low_back(product(normed_mid, up_weight))
    hidden = low(jax.nn.silu(gate_rows) * up_rows)
    return middle + product_rows(hidden, down_weight)

def reference(inputs, query_weight, key_weight, value_weight, out_weight, gate_weight, up_weight, down_weight, first_gain, second_gain, segment_ids, positions, out_grad):
    weights = tuple((item.astype(jnp.float32) for item in (query_weight, key_weight, value_weight, out_weight, gate_weight, up_weight, down_weight, first_gain, second_gain)))
    blocks = TOKENS // SEQ

    def one_block(carry, pieces):
        input_piece, ids_piece, position_piece, grad_piece = pieces

        def forward(input_values, *weight_values):
            return layer_block(input_values, *weight_values, ids_piece, position_piece)
        result, pull = jax.vjp(forward, input_piece.astype(jnp.float32), *weights)
        grads = pull(grad_piece.astype(jnp.float32))
        carry = tuple((left + right for left, right in zip(carry, grads[1:])))
        return (carry, (result.astype(jnp.bfloat16), grads[0].astype(jnp.bfloat16)))
    start = tuple((jnp.zeros(item.shape, jnp.float32) for item in weights))
    totals, (outputs, input_grads) = lax.scan(one_block, start, (inputs.reshape(blocks, SEQ, D), segment_ids.reshape(blocks, SEQ), positions.reshape(blocks, SEQ), out_grad.reshape(blocks, SEQ, D)))
    return (outputs.reshape(TOKENS, D), input_grads.reshape(TOKENS, D), totals[0], totals[1], totals[2], totals[3], totals[4], totals[5], totals[6], totals[7], totals[8])
```

```python
import functools
import math

import jax
import jax.numpy as jnp
from jax import lax
from jax.experimental import pallas as pl
from jax.experimental.pallas import tpu as pltpu
from jax.sharding import PartitionSpec as P

HEAD_DIM = 64
LANES = 128
EPS = 1e-05
ROPE_BASE = 130000.0
LOG2E = math.log2(math.e)
SCORE_SCALE = HEAD_DIM**-0.5
BF16 = jnp.bfloat16
F32 = jnp.float32
VMEM_BYTES = 56 * 1024 * 1024


def nn(left, right):
    return lax.dot_general(left, right, (((1,), (0,)), ((), ())), preferred_element_type=F32)


def nt(left, right):
    return lax.dot_general(left, right, (((1,), (1,)), ((), ())), preferred_element_type=F32)


def tn(left, right):
    return lax.dot_general(left, right, (((0,), (0,)), ((), ())), preferred_element_type=F32)


def spin(values, cosine, sine_front, sine_back):
    half = HEAD_DIM // 2
    lanes = values.shape[-1]
    return (
        values * cosine
        + pltpu.roll(values, lanes - half, 1) * sine_front
        + pltpu.roll(values, half, 1) * sine_back
    )


def weave(own, other, feat):
    pieces = []
    for at in range(0, own.shape[1], feat):
        pieces += [own[:, at : at + feat], other[:, at : at + feat]]
    return jnp.concatenate(pieces, axis=1)


def norm_scale(values):
    wide = values.astype(F32)
    return lax.rsqrt(jnp.sum(wide * wide, axis=1, keepdims=True) / values.shape[1] + EPS)


def whole_spec(a):
    return pl.BlockSpec(a.shape, lambda i: (0,) * a.ndim, pipeline_mode=pl.Buffered(1))


def row_spec(block, a):
    return pl.BlockSpec((block, a.shape[1]), lambda i: (i, 0))


def project_kernel(feat, own_ref, other_ref, weight_ref, cos_ref, front_ref, back_ref, q_ref, k_ref, v_ref, scale_ref):
    values = weave(own_ref[...], other_ref[...], feat)
    scale = norm_scale(values)
    scale_ref[...] = scale
    heads = q_ref.shape[1]
    cosine, front, back = cos_ref[...], front_ref[...], back_ref[...]
    for at, ref in enumerate((q_ref, k_ref, v_ref)):
        result = nn(values, weight_ref[:, at * heads : (at + 1) * heads]) * scale
        if at < 2:
            result = spin(result, cosine, front, back)
        ref[...] = result.astype(BF16)


def project(feat, own, other, weight, cosine, front, back):
    tokens = own.shape[0]
    heads = weight.shape[1] // 3
    block = 256
    result = jax.ShapeDtypeStruct((tokens, heads), BF16)
    scale = jax.ShapeDtypeStruct((tokens, 1), F32)
    return pl.pallas_call(
        functools.partial(project_kernel, feat),
        grid=(tokens // block,),
        in_specs=[row_spec(block, own), row_spec(block, other), whole_spec(weight)]
        + [row_spec(block, cosine)] * 3,
        out_specs=[row_spec(block, result)] * 3 + [row_spec(block, scale)],
        out_shape=[result] * 3 + [scale],
        compiler_params=pltpu.CompilerParams(vmem_limit_bytes=VMEM_BYTES),
        name="project",
    )(own, other, weight, cosine, front, back)


def unfold_kernel(feat, groups, *refs):
    count = sum(groups)
    lefts, weights = refs[: len(groups)], refs[len(groups) : len(groups) + count]
    own_ref, other_ref = refs[-2:]
    for at in range(0, own_ref.shape[1], feat):
        rows = slice(2 * at, 2 * (at + feat))
        total = None
        ids = iter(weights)
        for left, number in zip(lefts, groups):
            part = left.shape[1] // number
            for i in range(number):
                term = nt(left[:, i * part : (i + 1) * part], next(ids)[rows, :])
                total = term if total is None else total + term
        own_ref[:, at : at + feat] = total[:, :feat].astype(own_ref.dtype)
        other_ref[:, at : at + feat] = total[:, feat:].astype(BF16)


def unfold(feat, name, *pairs):
    lefts = [left for left, _ in pairs]
    weights = [w for _, ws in pairs for w in ws]
    tokens, half = lefts[0].shape[0], weights[0].shape[0] // 2
    block = 256
    own = jax.ShapeDtypeStruct((tokens, half), F32)
    other = jax.ShapeDtypeStruct((tokens, half), BF16)
    return pl.pallas_call(
        functools.partial(unfold_kernel, feat, tuple(len(ws) for _, ws in pairs)),
        grid=(tokens // block,),
        in_specs=[row_spec(block, a) for a in lefts] + [whole_spec(w) for w in weights],
        out_specs=[row_spec(block, own), row_spec(block, other)],
        out_shape=[own, other],
        compiler_params=pltpu.CompilerParams(vmem_limit_bytes=VMEM_BYTES),
        name=name,
    )(*lefts, *weights)


def hidden_kernel(feat, count, *refs):
    m_own, m_other, g_own, g_other = refs[:4]
    gates, ups, downs = (refs[4 + i * count : 4 + (i + 1) * count] for i in range(3))
    hidden_ref, gate_ref, up_ref, gate_scaled_ref, up_scaled_ref = refs[4 + 3 * count :]
    middle = weave(m_own[...], m_other[...], feat)
    grad = weave(g_own[...], g_other[...], feat)
    scale = norm_scale(middle)
    part = hidden_ref.shape[1] // count
    for i in range(count):
        columns = slice(i * part, (i + 1) * part)
        gate = nn(middle, gates[i][...]) * scale
        up = nn(middle, ups[i][...]) * scale
        hidden_grad = nn(grad, downs[i][...])
        sigmoid = 1.0 / (1.0 + jnp.exp(-gate))
        silu = gate * sigmoid
        hidden_ref[:, columns] = (silu * up).astype(BF16)
        gate_grad = hidden_grad * up * (sigmoid + silu * (1.0 - sigmoid))
        up_grad = hidden_grad * silu
        gate_ref[:, columns] = gate_grad.astype(BF16)
        up_ref[:, columns] = up_grad.astype(BF16)
        gate_scaled_ref[:, columns] = (gate_grad * scale).astype(BF16)
        up_scaled_ref[:, columns] = (up_grad * scale).astype(BF16)


def hidden_units(feat, halves, gates, ups, downs):
    tokens = halves[0].shape[0]
    count, part = len(gates), gates[0].shape[1]
    block = 256
    result = jax.ShapeDtypeStruct((tokens, count * part), BF16)
    weights = gates + ups + downs
    return pl.pallas_call(
        functools.partial(hidden_kernel, feat, count),
        grid=(tokens // block,),
        in_specs=[row_spec(block, a) for a in halves] + [whole_spec(w) for w in weights],
        out_specs=[row_spec(block, result)] * 5,
        out_shape=[result] * 5,
        compiler_params=pltpu.CompilerParams(vmem_limit_bytes=VMEM_BYTES),
        name="hidden_units",
    )(*halves, *weights)


def allowed_block(start_row, key_base, query_base, keys, queries):
    key_index = key_base + lax.broadcasted_iota(jnp.int32, (keys, queries), 0)
    query_index = query_base + lax.broadcasted_iota(jnp.int32, (keys, queries), 1)
    return (key_index >= start_row) & (key_index <= query_index)


def attend_kernel(q_ref, k_ref, v_ref, start_ref, out_ref, log_ref):
    tokens = q_ref.shape[0]
    block = 256
    keys_all = k_ref[...]
    values_turned = v_ref[...].T
    lane = lax.broadcasted_iota(jnp.int32, (1, LANES), 1)
    sub = lax.broadcasted_iota(jnp.int32, (LANES, 1), 0)
    for place in range(tokens // block):
        rows = slice(place * block, (place + 1) * block)
        reach = (place + 1) * block
        query = q_ref[rows, :]
        start_row = start_ref[:, rows]
        allowed = allowed_block(start_row, 0, place * block, reach, block)
        parts = []
        for head in range(LANES // HEAD_DIM):
            mine = lane // HEAD_DIM == head
            query_head = query * mine.astype(BF16)
            scores = nt(keys_all[:reach], query_head) * (SCORE_SCALE * LOG2E)
            scores = jnp.where(allowed, scores, -1e30)
            peak = jnp.max(scores, axis=0, keepdims=True)
            raised = jnp.exp2(scores - peak)
            total = jnp.sum(raised, axis=0, keepdims=True)
            mixed = nn(values_turned[:, :reach], raised.astype(BF16)) / total
            parts.append(mixed)
            log_ref[0, head : head + 1, rows] = peak + jnp.log2(total)
        joined = jnp.where(sub // HEAD_DIM == 0, parts[0], parts[1])
        out_ref[rows, :] = joined.T.astype(BF16)


def attend(query, key, value, start_row):
    tokens, width = query.shape
    pairs = width // LANES
    column = pl.BlockSpec((tokens, LANES), lambda i: (0, i))
    return pl.pallas_call(
        attend_kernel,
        grid=(pairs,),
        in_specs=[column, column, column, pl.BlockSpec((1, tokens), lambda i: (0, 0))],
        out_specs=[column, pl.BlockSpec((1, 2, tokens), lambda i: (i, 0, 0))],
        out_shape=[
            jax.ShapeDtypeStruct((tokens, width), BF16),
            jax.ShapeDtypeStruct((pairs, 2, tokens), F32),
        ],
        compiler_params=pltpu.CompilerParams(vmem_limit_bytes=VMEM_BYTES),
        name="attend",
    )(query, key, value, start_row)


def attend_back_kernel(
    q_ref, k_ref, v_ref, o_ref, do_ref, start_ref, log_ref, cos_ref, front_ref, back_ref,
    dq_ref, dk_ref, dv_ref, dq_acc,
):
    tokens = q_ref.shape[0]
    block = 256
    lane = lax.broadcasted_iota(jnp.int32, (1, LANES), 1)
    sub = lax.broadcasted_iota(jnp.int32, (LANES, 1), 0)
    query_all = q_ref[...]
    grad_all = do_ref[...]
    product = (o_ref[...].astype(F32) * grad_all.astype(F32)).T
    dots = [
        jnp.sum(product[head * HEAD_DIM : (head + 1) * HEAD_DIM], axis=0, keepdims=True)
        for head in range(LANES // HEAD_DIM)
    ]
    dq_acc[...] = jnp.zeros_like(dq_acc)
    for place in range(tokens // block):
        rows = slice(place * block, (place + 1) * block)
        tail = slice(place * block, tokens)
        keys = k_ref[rows, :]
        values = v_ref[rows, :]
        keys_turned = keys.T
        query = query_all[place * block :]
        grad = grad_all[place * block :]
        start_row = start_ref[:, tail]
        allowed = allowed_block(
            start_row, place * block, place * block, block, tokens - place * block
        )
        key_grad = jnp.zeros((block, LANES), F32)
        value_grad = jnp.zeros((block, LANES), F32)
        for head in range(LANES // HEAD_DIM):
            mine = lane // HEAD_DIM == head
            scores = nt(keys * mine.astype(BF16), query) * (SCORE_SCALE * LOG2E)
            weights = jnp.where(allowed, jnp.exp2(scores - log_ref[0, head : head + 1, tail]), 0.0)
            weight_grad = nt(values * mine.astype(BF16), grad)
            score_grad = (weights * (weight_grad - dots[head][:, place * block :])).astype(BF16)
            value_grad = jnp.where(mine, nn(weights.astype(BF16), grad), value_grad)
            key_grad = jnp.where(mine, nn(score_grad, query), key_grad)
            dq_acc[:, tail] += nn(
                keys_turned * (sub // HEAD_DIM == head).astype(BF16), score_grad
            )
        dv_ref[rows, :] = value_grad.astype(BF16)
        dk_ref[rows, :] = spin(
            key_grad * SCORE_SCALE, cos_ref[rows, :], -front_ref[rows, :], -back_ref[rows, :]
        ).astype(BF16)
    dq_ref[...] = spin(
        dq_acc[...].T * SCORE_SCALE, cos_ref[...], -front_ref[...], -back_ref[...]
    ).astype(BF16)


def attend_back(query, key, value, mixed, mixed_grad, start_row, logs, cosine, front, back):
    tokens, width = query.shape
    pairs = width // LANES
    column = pl.BlockSpec((tokens, LANES), lambda i: (0, i))
    table = pl.BlockSpec((tokens, LANES), lambda i: (0, 0))
    return pl.pallas_call(
        attend_back_kernel,
        grid=(pairs,),
        in_specs=[
            column, column, column, column, column,
            pl.BlockSpec((1, tokens), lambda i: (0, 0)),
            pl.BlockSpec((1, 2, tokens), lambda i: (i, 0, 0)),
            table, table, table,
        ],
        out_specs=[column, column, column],
        out_shape=[jax.ShapeDtypeStruct((tokens, width), BF16)] * 3,
        scratch_shapes=[pltpu.VMEM((LANES, tokens), F32)],
        compiler_params=pltpu.CompilerParams(vmem_limit_bytes=VMEM_BYTES),
        name="attend_back",
    )(query, key, value, mixed, mixed_grad, start_row, logs, cosine, front, back)


def rope_tables(positions, width):
    half = HEAD_DIM // 2
    freqs = jnp.exp(jnp.arange(half, dtype=F32) * (-2.0 * math.log(ROPE_BASE) / HEAD_DIM))
    angles = positions.astype(F32)[:, None] * freqs[None, :]
    cosine, sine = jnp.cos(angles), jnp.sin(angles)
    zero = jnp.zeros_like(sine)
    heads = width // HEAD_DIM
    return (
        jnp.tile(cosine, (1, 2 * heads)),
        jnp.tile(jnp.concatenate([-sine, zero], axis=1), (1, heads)),
        jnp.tile(jnp.concatenate([zero, sine], axis=1), (1, heads)),
    )


def local(
    inputs,
    query_weight,
    key_weight,
    value_weight,
    out_weight,
    gate_weight,
    up_weight,
    down_weight,
    first_gain,
    second_gain,
    segment_ids,
    positions,
    out_grad,
):
    rows = lax.axis_size("row")
    cols = lax.axis_size("col")
    places = cols // 2
    row = lax.axis_index("row")
    col = lax.axis_index("col")
    core = col % 2
    place = col // 2
    tokens, feat = inputs.shape
    width = feat * cols
    half = width // 2
    quarter = tokens // places

    def core_swap(a):
        return lax.ppermute(a, "col", [(i, i ^ 1) for i in range(cols)])

    def plane_swap(a, step):
        return lax.ppermute(a, "col", [(i, i ^ (2 * step)) for i in range(cols)])

    def token_part(a, step):
        return lax.dynamic_slice_in_dim(a, (place ^ step) * quarter, quarter, 0)

    def feat_part(a, step):
        return lax.dynamic_slice_in_dim(a, (place ^ step) * feat, feat, 1)

    def own_first(w):
        return jnp.concatenate(
            [jnp.where(core == 0, w[:feat], w[feat:]), jnp.where(core == 0, w[feat:], w[:feat])], axis=0
        )

    def shift(a, step):
        return lax.ppermute(a, "row", [(i, (i + step) % rows) for i in range(rows)])

    def put_rows(pieces):
        whole = jnp.zeros((tokens,) + pieces[0].shape[1:], pieces[0].dtype)
        for step, piece in enumerate(pieces):
            whole = lax.dynamic_update_slice_in_dim(whole, piece, (place ^ step) * quarter, 0)
        return whole

    def put_feats(pieces):
        whole = jnp.zeros((pieces[0].shape[0], half), pieces[0].dtype)
        for step, piece in enumerate(pieces):
            whole = lax.dynamic_update_slice_in_dim(whole, piece, (place ^ step) * feat, 1)
        return whole

    def spread(a):
        return [a] + [plane_swap(a, step) for step in range(1, places)]

    def to_parts(a):
        return put_feats(
            [token_part(a, 0)] + [plane_swap(token_part(a, s), s) for s in range(1, places)]
        )

    def to_home(a):
        return put_rows([feat_part(a, 0)] + [plane_swap(feat_part(a, s), s) for s in range(1, places)])

    def sum_cols(a):
        step = 1
        while step < cols:
            a = a + lax.ppermute(a, "col", [(i, i ^ step) for i in range(cols)])
            step *= 2
        return a

    gain_one = first_gain.astype(F32)[:, None]
    gain_two = second_gain.astype(F32)[:, None]

    def scaled(w, gain):
        return own_first((w.astype(F32) * gain).astype(BF16))

    def exchange(w):
        part = w.shape[1] // rows
        whole = jnp.zeros((width, part), BF16)
        for s in range(rows):
            piece = lax.dynamic_slice_in_dim(w, (row + s) % rows * part, part, 1)
            piece = shift(piece, s) if s else piece
            whole = lax.dynamic_update_slice_in_dim(whole, piece, (row - s) % rows * 2 * feat, 0)
        if places != 4:
            return spread(whole)
        first, second = plane_swap(whole, 1), plane_swap(whole, 2)
        return [
            whole,
            first,
            second,
            jnp.concatenate([plane_swap(second[:half], 1), plane_swap(first[half:], 2)], axis=0),
        ]

    def give_back(pieces):
        if places != 4:
            total = pieces[0].astype(F32)
            for s in range(1, places):
                total = total + plane_swap(pieces[s], s).astype(F32)
        else:
            to_second = pieces[2].astype(F32) + jnp.concatenate(
                [plane_swap(pieces[3][:half], 1), jnp.zeros_like(pieces[3][half:])], axis=0
            ).astype(F32)
            to_first = pieces[1].astype(F32) + jnp.concatenate(
                [jnp.zeros_like(pieces[3][:half]), plane_swap(pieces[3][half:], 2)], axis=0
            ).astype(F32)
            total = (
                pieces[0].astype(F32)
                + plane_swap(to_first.astype(BF16), 1).astype(F32)
                + plane_swap(to_second.astype(BF16), 2).astype(F32)
            )
        total = total.astype(BF16)
        part = total.shape[1]
        whole = jnp.zeros((2 * feat, rows * part), F32)
        for s in range(rows):
            piece = lax.dynamic_slice_in_dim(total, (row + s) % rows * 2 * feat, 2 * feat, 0)
            piece = own_first(shift(piece, s) if s else piece).astype(F32)
            whole = lax.dynamic_update_slice_in_dim(whole, piece, (row - s) % rows * part, 1)
        return whole

    def give_rows(w):
        return own_first(lax.psum_scatter(w, "row", scatter_dimension=0, tiled=True)).astype(F32)

    def outer(own, other, right):
        return tn(weave(own, other, feat), right).astype(BF16)

    qkv = jnp.concatenate(
        [scaled(w, gain_one) for w in (query_weight, key_weight, value_weight)], axis=1
    )
    qkv_full = lax.all_gather(qkv, "row", axis=0, tiled=True)
    out_full = lax.all_gather(own_first(out_weight), "row", axis=0, tiled=True)
    gates = exchange(scaled(gate_weight, gain_two))
    ups = exchange(scaled(up_weight, gain_two))
    downs = exchange(own_first(down_weight))

    x_own = put_feats(spread(inputs))
    x_other = core_swap(x_own)
    heads_width = query_weight.shape[1]
    cosine, front, back = rope_tables(positions, heads_width)
    start_row = jnp.sum(
        (segment_ids[None, :] < segment_ids[:, None]).astype(jnp.int32), axis=1
    )[None, :]
    query, key, value, scale_one = project(feat, x_own, x_other, qkv_full, cosine, front, back)
    mixed, logs = attend(query, key, value, start_row)

    def scatter_parts(own, other):
        own = own + core_swap(other).astype(F32)
        low = own.astype(BF16)
        total = token_part(own, 0)
        for s in range(1, places):
            total = total + plane_swap(token_part(low, s), s).astype(F32)
        return total

    middle = token_part(x_own, 0).astype(F32) + scatter_parts(*unfold(feat, "mix", (mixed, [out_full])))
    square = jnp.sum(middle * middle, axis=1, keepdims=True)
    square = square + core_swap(square)
    scale_mid = lax.rsqrt(square / width + EPS)

    m_own = lax.all_gather(middle.astype(BF16), "row", axis=0, tiled=True)
    m_other = core_swap(m_own)
    g_part = to_parts(out_grad)
    g_own = lax.all_gather(g_part, "row", axis=0, tiled=True)
    g_other = core_swap(g_own)
    hidden, gate_low, up_low, gate_scaled, up_scaled = hidden_units(
        feat, (m_own, m_other, g_own, g_other), gates, ups, downs
    )

    def gather_sum(own, other):
        own = own + core_swap(other).astype(F32)
        return lax.psum_scatter(own.astype(BF16), "row", scatter_dimension=0, tiled=True).astype(F32)

    unit_grad = gather_sum(*unfold(feat, "unit_grad", (gate_low, gates), (up_low, ups)))
    feed = gather_sum(*unfold(feat, "feed", (hidden, downs)))
    block_out = to_home((middle + feed).astype(BF16))

    unit_mid = middle * scale_mid
    dot_two = jnp.sum(unit_grad * unit_mid, axis=1, keepdims=True)
    dot_two = dot_two + core_swap(dot_two)
    middle_grad = g_part.astype(F32) + scale_mid * (unit_grad - unit_mid * (dot_two / width))

    d_own = put_rows(spread(middle_grad.astype(BF16)))
    d_other = core_swap(d_own)
    d_all = weave(d_own, d_other, feat)
    mixed_grad = nn(d_all, out_full).astype(BF16)
    query_grad, key_grad, value_grad = attend_back(
        query, key, value, mixed, mixed_grad, start_row, logs, cosine, front, back
    )
    grads = jnp.concatenate([query_grad, key_grad, value_grad], axis=1)
    grads_scaled = (grads.astype(F32) * scale_one).astype(BF16)
    qkv_part = tn(weave(x_own, x_other, feat), grads_scaled)
    qkv_grad = give_rows(qkv_part.astype(BF16))
    gain_dots = jnp.sum(qkv_part * qkv_full.astype(F32), axis=1).reshape(rows, 2, feat)
    gain_dots = sum_cols(jnp.where(core == 0, gain_dots, gain_dots[:, ::-1]).reshape(width))
    gain_row = sum(
        shift(lax.dynamic_slice_in_dim(gain_dots, (row + s) % rows * 2 * feat, 2 * feat, 0), s)
        for s in range(1, rows)
    ) + lax.dynamic_slice_in_dim(gain_dots, row * 2 * feat, 2 * feat, 0)
    first_gain_grad = gain_row / gain_one[:, 0]
    first_unit_grad = scatter_parts(*unfold(feat, "first_grad", (grads, [qkv_full])))
    scale_first = token_part(scale_one, 0)
    unit_first = token_part(x_own, 0).astype(F32) * scale_first
    dot_one = jnp.sum(first_unit_grad * unit_first, axis=1, keepdims=True)
    dot_one = dot_one + core_swap(dot_one)
    input_grad = to_home(
        (middle_grad + scale_first * (first_unit_grad - unit_first * (dot_one / width))).astype(BF16)
    )

    out_weight_grad = give_rows(tn(d_all, mixed).astype(BF16))

    def by_place(w):
        part = w.shape[1] // places
        return [w[:, s * part : (s + 1) * part] for s in range(places)]

    down_weight_grad = give_back(by_place(outer(g_own, g_other, hidden)))
    gate_unit = give_back(by_place(outer(m_own, m_other, gate_scaled)))
    up_unit = give_back(by_place(outer(m_own, m_other, up_scaled)))
    q_unit = qkv_grad[:, :heads_width]
    k_unit = qkv_grad[:, heads_width : 2 * heads_width]
    v_unit = qkv_grad[:, 2 * heads_width :]

    def row_dots(*pairs):
        return sum(jnp.sum(w.astype(F32) * d, axis=1) for w, d in pairs)

    second_gain_grad = sum_cols(row_dots((gate_weight, gate_unit), (up_weight, up_unit)))
    return (
        block_out,
        input_grad,
        q_unit * gain_one,
        k_unit * gain_one,
        v_unit * gain_one,
        out_weight_grad,
        gate_unit * gain_two,
        up_unit * gain_two,
        down_weight_grad,
        first_gain_grad,
        second_gain_grad,
    )


def solution(mesh):
    grid, line = P("row", "col"), P("row")
    return jax.shard_map(
        local,
        mesh=mesh,
        in_specs=(grid,) * 8 + (line,) * 4 + (grid,),
        out_specs=(grid,) * 9 + (line,) * 2,
        check_vma=False,
    )
```

```python
import functools
import math

import jax
import jax.numpy as jnp
from jax import lax
from jax.experimental import pallas as pl
from jax.experimental.pallas import tpu as pltpu
from jax.sharding import PartitionSpec as P

HEAD_DIM = 64
LANES = 128
EPS = 1e-05
ROPE_BASE = 130000.0
LOG2E = math.log2(math.e)
SCORE_SCALE = HEAD_DIM**-0.5
BF16 = jnp.bfloat16
F32 = jnp.float32
VMEM_BYTES = 56 * 1024 * 1024


def nn(left, right):
    return lax.dot_general(left, right, (((1,), (0,)), ((), ())), preferred_element_type=F32)


def nt(left, right):
    return lax.dot_general(left, right, (((1,), (1,)), ((), ())), preferred_element_type=F32)


def tn(left, right):
    return lax.dot_general(left, right, (((0,), (0,)), ((), ())), preferred_element_type=F32)


def spin(values, cosine, sine_front, sine_back):
    half = HEAD_DIM // 2
    lanes = values.shape[-1]
    return (
        values * cosine
        + pltpu.roll(values, lanes - half, 1) * sine_front
        + pltpu.roll(values, half, 1) * sine_back
    )


def weave(own, other, feat):
    pieces = []
    for at in range(0, own.shape[1], feat):
        pieces += [own[:, at : at + feat], other[:, at : at + feat]]
    return jnp.concatenate(pieces, axis=1)


def norm_scale(values):
    wide = values.astype(F32)
    return lax.rsqrt(jnp.sum(wide * wide, axis=1, keepdims=True) / values.shape[1] + EPS)


def whole_spec(a):
    return pl.BlockSpec(a.shape, lambda i: (0,) * a.ndim, pipeline_mode=pl.Buffered(1))


def row_spec(block, a):
    return pl.BlockSpec((block, a.shape[1]), lambda i: (i, 0))


def project_kernel(feat, own_ref, other_ref, weight_ref, cos_ref, front_ref, back_ref, q_ref, k_ref, v_ref, scale_ref):
    values = weave(own_ref[...], other_ref[...], feat)
    scale = norm_scale(values)
    scale_ref[...] = scale
    heads = q_ref.shape[1]
    cosine, front, back = cos_ref[...], front_ref[...], back_ref[...]
    for at, ref in enumerate((q_ref, k_ref, v_ref)):
        result = nn(values, weight_ref[:, at * heads : (at + 1) * heads]) * scale
        if at < 2:
            result = spin(result, cosine, front, back)
        ref[...] = result.astype(BF16)


def project(feat, own, other, weight, cosine, front, back):
    tokens = own.shape[0]
    heads = weight.shape[1] // 3
    block = 256
    result = jax.ShapeDtypeStruct((tokens, heads), BF16)
    scale = jax.ShapeDtypeStruct((tokens, 1), F32)
    return pl.pallas_call(
        functools.partial(project_kernel, feat),
        grid=(tokens // block,),
        in_specs=[row_spec(block, own), row_spec(block, other), whole_spec(weight)]
        + [row_spec(block, cosine)] * 3,
        out_specs=[row_spec(block, result)] * 3 + [row_spec(block, scale)],
        out_shape=[result] * 3 + [scale],
        compiler_params=pltpu.CompilerParams(vmem_limit_bytes=VMEM_BYTES),
        name="project",
    )(own, other, weight, cosine, front, back)


def unfold_kernel(feat, groups, *refs):
    count = sum(groups)
    lefts, weights = refs[: len(groups)], refs[len(groups) : len(groups) + count]
    own_ref, other_ref = refs[-2:]
    for at in range(0, own_ref.shape[1], feat):
        rows = slice(2 * at, 2 * (at + feat))
        total = None
        ids = iter(weights)
        for left, number in zip(lefts, groups):
            part = left.shape[1] // number
            for i in range(number):
                term = nt(left[:, i * part : (i + 1) * part], next(ids)[rows, :])
                total = term if total is None else total + term
        own_ref[:, at : at + feat] = total[:, :feat].astype(own_ref.dtype)
        other_ref[:, at : at + feat] = total[:, feat:].astype(BF16)


def unfold(feat, name, *pairs):
    lefts = [left for left, _ in pairs]
    weights = [w for _, ws in pairs for w in ws]
    tokens, half = lefts[0].shape[0], weights[0].shape[0] // 2
    block = 256
    own = jax.ShapeDtypeStruct((tokens, half), F32)
    other = jax.ShapeDtypeStruct((tokens, half), BF16)
    return pl.pallas_call(
        functools.partial(unfold_kernel, feat, tuple(len(ws) for _, ws in pairs)),
        grid=(tokens // block,),
        in_specs=[row_spec(block, a) for a in lefts] + [whole_spec(w) for w in weights],
        out_specs=[row_spec(block, own), row_spec(block, other)],
        out_shape=[own, other],
        compiler_params=pltpu.CompilerParams(vmem_limit_bytes=VMEM_BYTES),
        name=name,
    )(*lefts, *weights)


def units_kernel(feat, count, m_own, m_other, g_own, g_other, *refs):
    sources = refs[: 3 * count]
    hidden_ref, gate_ref, up_ref, own_ref, other_ref, held, arrived = refs[3 * count :]
    copies = [
        pltpu.make_async_copy(source, held.at[at], arrived.at[at]) for at, source in enumerate(sources)
    ]
    for copy in copies:
        copy.start()
    middle = weave(m_own[...], m_other[...], feat)
    grad = weave(g_own[...], g_other[...], feat)
    scale = norm_scale(middle)
    part = hidden_ref.shape[1] // count
    pairs = []
    for i in range(count):
        columns = slice(i * part, (i + 1) * part)
        for copy in copies[3 * i : 3 * i + 3]:
            copy.wait()
        gate = nn(middle, held[3 * i]) * scale
        up = nn(middle, held[3 * i + 1]) * scale
        hidden_grad = nn(grad, held[3 * i + 2])
        sigmoid = 1.0 / (1.0 + jnp.exp(-gate))
        silu = gate * sigmoid
        hidden_ref[:, columns] = (silu * up).astype(BF16)
        gate_grad = hidden_grad * up * (sigmoid + silu * (1.0 - sigmoid))
        up_grad = hidden_grad * silu
        pairs.append((gate_grad.astype(BF16), held.at[3 * i]))
        pairs.append((up_grad.astype(BF16), held.at[3 * i + 1]))
        gate_ref[:, columns] = (gate_grad * scale).astype(BF16)
        up_ref[:, columns] = (up_grad * scale).astype(BF16)
    for at in range(0, own_ref.shape[1], feat):
        rows = slice(2 * at, 2 * (at + feat))
        total = None
        for left, weight in pairs:
            term = nt(left, weight[rows, :])
            total = term if total is None else total + term
        own_ref[:, at : at + feat] = total[:, :feat]
        other_ref[:, at : at + feat] = total[:, feat:].astype(BF16)


def units(feat, m_own, m_other, g_own, g_other, gates, ups, downs):
    tokens, half = m_own.shape
    count, part = len(gates), gates[0].shape[1]
    hidden = jax.ShapeDtypeStruct((tokens, count * part), BF16)
    weights = [w for three in zip(gates, ups, downs) for w in three]
    return pl.pallas_call(
        functools.partial(units_kernel, feat, count),
        in_specs=[pl.BlockSpec(memory_space=pltpu.VMEM)] * 4
        + [pl.BlockSpec(memory_space=pl.ANY)] * len(weights),
        out_specs=[pl.BlockSpec(memory_space=pltpu.VMEM)] * 5,
        out_shape=[hidden] * 3
        + [jax.ShapeDtypeStruct((tokens, half), F32), jax.ShapeDtypeStruct((tokens, half), BF16)],
        scratch_shapes=[
            pltpu.VMEM((len(weights),) + weights[0].shape, BF16),
            pltpu.SemaphoreType.DMA((len(weights),)),
        ],
        compiler_params=pltpu.CompilerParams(vmem_limit_bytes=40 * 1024 * 1024),
        name="units",
    )(m_own, m_other, g_own, g_other, *weights)


def outer_kernel(groups, count, *refs):
    owns, others, rights = refs[:groups], refs[groups : 2 * groups], refs[2 * groups : 3 * groups]
    outs = refs[3 * groups : 3 * groups + count]
    left = jnp.concatenate(
        [jnp.concatenate([own[...], other[...]], axis=1) for own, other in zip(owns, others)], axis=0
    )
    part = outs[0].shape[1]
    for i, out in enumerate(outs):
        columns = slice(i * part, (i + 1) * part)
        right = jnp.concatenate([ref[:, columns] for ref in rights], axis=0)
        result = tn(left, right)
        out[...] = result.astype(BF16)


def outer(feat, name, owns, others, rights, count=1):
    half, columns = owns[0].shape[1], rights[0].shape[1]
    part = columns // count
    side = pl.BlockSpec((owns[0].shape[0], feat), lambda i: (0, i))
    return pl.pallas_call(
        functools.partial(outer_kernel, len(owns), count),
        grid=(half // feat,),
        in_specs=[side] * (2 * len(owns)) + [whole_spec(a) for a in rights],
        out_specs=[pl.BlockSpec((2 * feat, part), lambda i: (i, 0))] * count,
        out_shape=[jax.ShapeDtypeStruct((2 * half, part), BF16)] * count,
        compiler_params=pltpu.CompilerParams(vmem_limit_bytes=40 * 1024 * 1024),
        name=name,
    )(*owns, *others, *rights)


def fold_kernel(feat, own_ref, other_ref, weight_ref, out_ref):
    out_ref[...] = nn(weave(own_ref[...], other_ref[...], feat), weight_ref[...]).astype(BF16)


def fold(feat, own, other, weight):
    tokens = own.shape[0]
    block = 256
    result = jax.ShapeDtypeStruct((tokens, weight.shape[1]), BF16)
    return pl.pallas_call(
        functools.partial(fold_kernel, feat),
        grid=(tokens // block,),
        in_specs=[row_spec(block, own), row_spec(block, other), whole_spec(weight)],
        out_specs=row_spec(block, result),
        out_shape=result,
        compiler_params=pltpu.CompilerParams(vmem_limit_bytes=40 * 1024 * 1024),
        name="fold",
    )(own, other, weight)


def allowed_block(start_row, key_base, query_base, keys, queries):
    key_index = key_base + lax.broadcasted_iota(jnp.int32, (keys, queries), 0)
    query_index = query_base + lax.broadcasted_iota(jnp.int32, (keys, queries), 1)
    return (key_index >= start_row) & (key_index <= query_index)


def attend_kernel(q_ref, k_ref, v_ref, start_ref, out_ref, log_ref):
    tokens = q_ref.shape[0]
    block = 256
    keys_all = k_ref[...]
    values_turned = v_ref[...].T
    lane = lax.broadcasted_iota(jnp.int32, (1, LANES), 1)
    sub = lax.broadcasted_iota(jnp.int32, (LANES, 1), 0)
    for place in range(tokens // block):
        rows = slice(place * block, (place + 1) * block)
        reach = (place + 1) * block
        query = q_ref[rows, :]
        start_row = start_ref[:, rows]
        allowed = allowed_block(start_row, 0, place * block, reach, block)
        parts = []
        for head in range(LANES // HEAD_DIM):
            mine = lane // HEAD_DIM == head
            query_head = query * mine.astype(BF16)
            scores = nt(keys_all[:reach], query_head) * (SCORE_SCALE * LOG2E)
            scores = jnp.where(allowed, scores, -1e30)
            peak = jnp.max(scores, axis=0, keepdims=True)
            raised = jnp.exp2(scores - peak)
            total = jnp.sum(raised, axis=0, keepdims=True)
            mixed = nn(values_turned[:, :reach], raised.astype(BF16)) / total
            parts.append(mixed)
            log_ref[0, head : head + 1, rows] = peak + jnp.log2(total)
        joined = jnp.where(sub // HEAD_DIM == 0, parts[0], parts[1])
        out_ref[rows, :] = joined.T.astype(BF16)


def attend(query, key, value, start_row):
    tokens, width = query.shape
    pairs = width // LANES
    column = pl.BlockSpec((tokens, LANES), lambda i: (0, i))
    return pl.pallas_call(
        attend_kernel,
        grid=(pairs,),
        in_specs=[column, column, column, pl.BlockSpec((1, tokens), lambda i: (0, 0))],
        out_specs=[column, pl.BlockSpec((1, 2, tokens), lambda i: (i, 0, 0))],
        out_shape=[
            jax.ShapeDtypeStruct((tokens, width), BF16),
            jax.ShapeDtypeStruct((pairs, 2, tokens), F32),
        ],
        compiler_params=pltpu.CompilerParams(vmem_limit_bytes=VMEM_BYTES),
        name="attend",
    )(query, key, value, start_row)


def attend_back_kernel(
    q_ref, k_ref, v_ref, o_ref, do_ref, start_ref, log_ref, cos_ref, front_ref, back_ref,
    dq_ref, dk_ref, dv_ref, dq_acc,
):
    tokens = q_ref.shape[0]
    block = 256
    lane = lax.broadcasted_iota(jnp.int32, (1, LANES), 1)
    sub = lax.broadcasted_iota(jnp.int32, (LANES, 1), 0)
    query_all = q_ref[...]
    grad_all = do_ref[...]
    product = (o_ref[...].astype(F32) * grad_all.astype(F32)).T
    dots = [
        jnp.sum(product[head * HEAD_DIM : (head + 1) * HEAD_DIM], axis=0, keepdims=True)
        for head in range(LANES // HEAD_DIM)
    ]
    dq_acc[...] = jnp.zeros_like(dq_acc)
    for place in range(tokens // block):
        rows = slice(place * block, (place + 1) * block)
        tail = slice(place * block, tokens)
        keys = k_ref[rows, :]
        values = v_ref[rows, :]
        keys_turned = keys.T
        query = query_all[place * block :]
        grad = grad_all[place * block :]
        start_row = start_ref[:, tail]
        allowed = allowed_block(
            start_row, place * block, place * block, block, tokens - place * block
        )
        key_grad = jnp.zeros((block, LANES), F32)
        value_grad = jnp.zeros((block, LANES), F32)
        for head in range(LANES // HEAD_DIM):
            mine = lane // HEAD_DIM == head
            scores = nt(keys * mine.astype(BF16), query) * (SCORE_SCALE * LOG2E)
            weights = jnp.where(allowed, jnp.exp2(scores - log_ref[0, head : head + 1, tail]), 0.0)
            weight_grad = nt(values * mine.astype(BF16), grad)
            score_grad = (weights * (weight_grad - dots[head][:, place * block :])).astype(BF16)
            value_grad = jnp.where(mine, nn(weights.astype(BF16), grad), value_grad)
            key_grad = jnp.where(mine, nn(score_grad, query), key_grad)
            dq_acc[:, tail] += nn(
                keys_turned * (sub // HEAD_DIM == head).astype(BF16), score_grad
            )
        dv_ref[rows, :] = value_grad.astype(BF16)
        dk_ref[rows, :] = spin(
            key_grad * SCORE_SCALE, cos_ref[rows, :], -front_ref[rows, :], -back_ref[rows, :]
        ).astype(BF16)
    dq_ref[...] = spin(
        dq_acc[...].T * SCORE_SCALE, cos_ref[...], -front_ref[...], -back_ref[...]
    ).astype(BF16)


def attend_back(query, key, value, mixed, mixed_grad, start_row, logs, cosine, front, back):
    tokens, width = query.shape
    pairs = width // LANES
    column = pl.BlockSpec((tokens, LANES), lambda i: (0, i))
    table = pl.BlockSpec((tokens, LANES), lambda i: (0, 0))
    return pl.pallas_call(
        attend_back_kernel,
        grid=(pairs,),
        in_specs=[
            column, column, column, column, column,
            pl.BlockSpec((1, tokens), lambda i: (0, 0)),
            pl.BlockSpec((1, 2, tokens), lambda i: (i, 0, 0)),
            table, table, table,
        ],
        out_specs=[column, column, column],
        out_shape=[jax.ShapeDtypeStruct((tokens, width), BF16)] * 3,
        scratch_shapes=[pltpu.VMEM((LANES, tokens), F32)],
        compiler_params=pltpu.CompilerParams(vmem_limit_bytes=VMEM_BYTES),
        name="attend_back",
    )(query, key, value, mixed, mixed_grad, start_row, logs, cosine, front, back)


def rope_tables(positions, width):
    half = HEAD_DIM // 2
    freqs = jnp.exp(jnp.arange(half, dtype=F32) * (-2.0 * math.log(ROPE_BASE) / HEAD_DIM))
    angles = positions.astype(F32)[:, None] * freqs[None, :]
    cosine, sine = jnp.cos(angles), jnp.sin(angles)
    zero = jnp.zeros_like(sine)
    heads = width // HEAD_DIM
    return (
        jnp.tile(cosine, (1, 2 * heads)),
        jnp.tile(jnp.concatenate([-sine, zero], axis=1), (1, heads)),
        jnp.tile(jnp.concatenate([zero, sine], axis=1), (1, heads)),
    )


def local(
    inputs,
    query_weight,
    key_weight,
    value_weight,
    out_weight,
    gate_weight,
    up_weight,
    down_weight,
    first_gain,
    second_gain,
    segment_ids,
    positions,
    out_grad,
):
    rows = lax.axis_size("row")
    cols = lax.axis_size("col")
    places = cols // 2
    row = lax.axis_index("row")
    col = lax.axis_index("col")
    core = col % 2
    place = col // 2
    tokens, feat = inputs.shape
    width = feat * cols
    half = width // 2
    quarter = tokens // places

    def core_swap(a):
        return lax.ppermute(a, "col", [(i, i ^ 1) for i in range(cols)])

    def plane_swap(a, step):
        return lax.ppermute(a, "col", [(i, i ^ (2 * step)) for i in range(cols)])

    def token_part(a, step):
        return lax.dynamic_slice_in_dim(a, (place ^ step) * quarter, quarter, 0)

    def feat_part(a, step):
        return lax.dynamic_slice_in_dim(a, (place ^ step) * feat, feat, 1)

    def own_first(w):
        return jnp.concatenate(
            [jnp.where(core == 0, w[:feat], w[feat:]), jnp.where(core == 0, w[feat:], w[:feat])], axis=0
        )

    def row_swap(a, step):
        return lax.ppermute(a, "row", [(i, i ^ step) for i in range(rows)])

    def gather_row(a):
        got, bit = {0: a}, rows // 2
        while bit:
            for step in list(got):
                got[step ^ bit] = row_swap(got[step], bit)
            bit //= 2
        return [got[step] for step in range(rows)]

    def reduce_row(parts):
        parts, bit = list(parts), 1
        while bit < rows:
            for at in range(0, rows, 2 * bit):
                sent = row_swap(parts[at + bit].astype(BF16), bit)
                parts[at] = parts[at].astype(F32) + sent.astype(F32)
            bit *= 2
        return parts[0]

    def row_part(a, step):
        size = a.shape[0] // rows
        return lax.dynamic_slice_in_dim(a, (row ^ step) * size, size, 0)

    def join_rows(pieces, axis=0, dtype=BF16):
        size = pieces[0].shape[axis]
        shape = list(pieces[0].shape)
        shape[axis] *= rows
        whole = jnp.zeros(shape, dtype)
        for step, piece in enumerate(pieces):
            whole = lax.dynamic_update_slice_in_dim(whole, piece, (row ^ step) * size, axis)
        return whole

    def after(value, *others):
        return lax.optimization_barrier((value,) + others)[0]

    def put_rows(pieces):
        whole = jnp.zeros((tokens,) + pieces[0].shape[1:], pieces[0].dtype)
        for step, piece in enumerate(pieces):
            whole = lax.dynamic_update_slice_in_dim(whole, piece, (place ^ step) * quarter, 0)
        return whole

    def put_feats(pieces):
        whole = jnp.zeros((pieces[0].shape[0], half), pieces[0].dtype)
        for step, piece in enumerate(pieces):
            whole = lax.dynamic_update_slice_in_dim(whole, piece, (place ^ step) * feat, 1)
        return whole

    def spread(a):
        return [a] + [plane_swap(a, step) for step in range(1, places)]

    def to_parts(a):
        return put_feats(
            [token_part(a, 0)] + [plane_swap(token_part(a, s), s) for s in range(1, places)]
        )

    def to_home(a):
        return put_rows([feat_part(a, 0)] + [plane_swap(feat_part(a, s), s) for s in range(1, places)])

    def sum_cols(a):
        step = 1
        while step < cols:
            a = a + lax.ppermute(a, "col", [(i, i ^ step) for i in range(cols)])
            step *= 2
        return a

    gain_one = first_gain.astype(F32)[:, None]
    gain_two = second_gain.astype(F32)[:, None]

    def scaled(w, gain):
        return own_first((w.astype(F32) * gain).astype(BF16))

    def exchange(w):
        part = w.shape[1] // rows
        pieces = [lax.dynamic_slice_in_dim(w, (row ^ s) * part, part, 1) for s in range(rows)]
        return join_rows([row_swap(piece, s) if s else piece for s, piece in enumerate(pieces)])

    def spread_weights(whole):
        if places != 4:
            return spread(whole)
        first, second = plane_swap(whole, 1), plane_swap(whole, 2)
        return [
            whole,
            first,
            second,
            jnp.concatenate([plane_swap(second[:half], 1), plane_swap(first[half:], 2)], axis=0),
        ]

    def give_back(pieces):
        if places != 4:
            total = pieces[0].astype(F32)
            for s in range(1, places):
                total = total + plane_swap(pieces[s], s).astype(F32)
        else:
            to_second = pieces[2].astype(F32) + jnp.concatenate(
                [plane_swap(pieces[3][:half], 1), jnp.zeros_like(pieces[3][half:])], axis=0
            ).astype(F32)
            to_first = pieces[1].astype(F32) + jnp.concatenate(
                [jnp.zeros_like(pieces[3][:half]), plane_swap(pieces[3][half:], 2)], axis=0
            ).astype(F32)
            total = (
                pieces[0].astype(F32)
                + plane_swap(to_first.astype(BF16), 1).astype(F32)
                + plane_swap(to_second.astype(BF16), 2).astype(F32)
            )
        total = total.astype(BF16)
        pieces = [row_part(total, s) for s in range(rows)]
        pieces = [own_first(row_swap(piece, s) if s else piece).astype(F32) for s, piece in enumerate(pieces)]
        return join_rows(pieces, 1, F32)

    def give_rows(w):
        return own_first(reduce_row([row_part(w, s) for s in range(rows)]))

    qkv_list = gather_row(
        jnp.concatenate(
            [scaled(w, gain_one) for w in (query_weight, key_weight, value_weight)], axis=1
        )
    )
    gate_whole = exchange(scaled(gate_weight, gain_two))
    up_whole = exchange(after(scaled(up_weight, gain_two), gate_whole, *qkv_list[1:3]))
    out_list = gather_row(after(own_first(out_weight), *qkv_list))
    down_whole = exchange(after(own_first(down_weight), up_whole, *qkv_list))
    g_part = to_parts(out_grad)
    g_list = gather_row(after(g_part, down_whole))
    gates, ups, downs = (spread_weights(w) for w in (gate_whole, up_whole, down_whole))
    qkv_full = join_rows(qkv_list)
    out_full = join_rows(out_list)

    x_own = put_feats(spread(inputs))
    x_other = core_swap(x_own)
    heads_width = query_weight.shape[1]
    cosine, front, back = rope_tables(positions, heads_width)
    start_row = jnp.sum(
        (segment_ids[None, :] < segment_ids[:, None]).astype(jnp.int32), axis=1
    )[None, :]
    x_ready = after(x_own, gates[1], gates[2], g_part)
    query, key, value, scale_one = project(feat, x_ready, x_other, qkv_full, cosine, front, back)
    mixed, logs = attend(query, key, value, start_row)
    mixed = after(mixed, up_whole, gates[3])

    def scatter_parts(own, other):
        own = own + core_swap(other).astype(F32)
        low = own.astype(BF16)
        total = token_part(own, 0)
        for s in range(1, places):
            total = total + plane_swap(token_part(low, s), s).astype(F32)
        return total

    middle = token_part(x_own, 0).astype(F32) + scatter_parts(*unfold(feat, "mix", (mixed, [out_full])))
    square = jnp.sum(middle * middle, axis=1, keepdims=True)
    square = square + core_swap(square)
    scale_mid = lax.rsqrt(square / width + EPS)

    m_list = gather_row(middle.astype(BF16))
    m_others = [core_swap(m) for m in m_list]
    g_others = [core_swap(g) for g in g_list]
    found = [
        units(feat, m, m_other, g, g_other, gates, ups, downs)
        for m, m_other, g, g_other in zip(m_list, m_others, g_list, g_others)
    ]
    hidden = jnp.concatenate([f[0] for f in found], axis=0)
    unit_grad = reduce_row([f[3] + core_swap(f[4]).astype(F32) for f in found])
    feed_own, feed_other = unfold(feat, "feed", (after(hidden, found[-1][4]), downs))
    feed_own = feed_own + core_swap(feed_other).astype(F32)
    feed = reduce_row([feed_own[s * quarter : (s + 1) * quarter] for s in range(rows)])
    block_out = to_home((middle + feed).astype(BF16))

    unit_mid = middle * scale_mid
    dot_two = jnp.sum(unit_grad * unit_mid, axis=1, keepdims=True)
    dot_two = dot_two + core_swap(dot_two)
    middle_grad = g_part.astype(F32) + scale_mid * (unit_grad - unit_mid * (dot_two / width))

    d_own = put_rows(spread(middle_grad.astype(BF16)))
    d_other = core_swap(d_own)
    mixed_grad = fold(feat, d_own, d_other, out_full)
    query_grad, key_grad, value_grad = attend_back(
        query, key, value, mixed, mixed_grad, start_row, logs, cosine, front, back
    )
    grads = jnp.concatenate([query_grad, key_grad, value_grad], axis=1)
    grads_scaled = (grads.astype(F32) * scale_one).astype(BF16)
    qkv_part = outer(feat, "qkv_outer", [x_own], [x_other], [grads_scaled])[0]
    qkv_grad = give_rows(qkv_part)
    gain_dots = jnp.sum(qkv_part.astype(F32) * qkv_full.astype(F32), axis=1).reshape(rows, 2, feat)
    gain_dots = sum_cols(jnp.where(core == 0, gain_dots, gain_dots[:, ::-1]).reshape(width))
    gain_row = row_part(gain_dots, 0) + sum(row_swap(row_part(gain_dots, s), s) for s in range(1, rows))
    first_gain_grad = gain_row / gain_one[:, 0]
    first_unit_grad = scatter_parts(*unfold(feat, "first_grad", (grads, [qkv_full])))
    scale_first = token_part(scale_one, 0)
    unit_first = token_part(x_own, 0).astype(F32) * scale_first
    dot_one = jnp.sum(first_unit_grad * unit_first, axis=1, keepdims=True)
    dot_one = dot_one + core_swap(dot_one)
    input_grad = to_home(
        (middle_grad + scale_first * (first_unit_grad - unit_first * (dot_one / width))).astype(BF16)
    )

    out_weight_grad = give_rows(outer(feat, "out_outer", [d_own], [d_other], [mixed])[0])
    down_weight_grad = give_back(
        outer(feat, "down_outer", g_list, g_others, [f[0] for f in found], places)
    )
    gate_unit = give_back(outer(feat, "gate_outer", m_list, m_others, [f[1] for f in found], places))
    up_unit = give_back(outer(feat, "up_outer", m_list, m_others, [f[2] for f in found], places))
    q_unit = qkv_grad[:, :heads_width]
    k_unit = qkv_grad[:, heads_width : 2 * heads_width]
    v_unit = qkv_grad[:, 2 * heads_width :]

    def row_dots(*pairs):
        return sum(jnp.sum(w.astype(F32) * d, axis=1) for w, d in pairs)

    second_gain_grad = sum_cols(row_dots((gate_weight, gate_unit), (up_weight, up_unit)))
    return (
        block_out,
        input_grad,
        q_unit * gain_one,
        k_unit * gain_one,
        v_unit * gain_one,
        out_weight_grad,
        gate_unit * gain_two,
        up_unit * gain_two,
        down_weight_grad,
        first_gain_grad,
        second_gain_grad,
    )


def solution(mesh):
    grid, line = P("row", "col"), P("row")
    return jax.shard_map(
        local,
        mesh=mesh,
        in_specs=(grid,) * 8 + (line,) * 4 + (grid,),
        out_specs=(grid,) * 9 + (line,) * 2,
        check_vma=False,
    )
```

```python
import functools
import math

import jax
import jax.numpy as jnp
from jax import lax
from jax.experimental import pallas as pl
from jax.experimental.pallas import tpu as pltpu
from jax.sharding import PartitionSpec as P

HEAD_DIM = 64
LANES = 128
EPS = 1e-05
ROPE_BASE = 130000.0
LOG2E = math.log2(math.e)
SCORE_SCALE = HEAD_DIM**-0.5
BF16 = jnp.bfloat16
F32 = jnp.float32
VMEM_BYTES = 56 * 1024 * 1024


def nn(left, right):
    return lax.dot_general(left, right, (((1,), (0,)), ((), ())), preferred_element_type=F32)


def nt(left, right):
    return lax.dot_general(left, right, (((1,), (1,)), ((), ())), preferred_element_type=F32)


def tn(left, right):
    return lax.dot_general(left, right, (((0,), (0,)), ((), ())), preferred_element_type=F32)


def spin(values, cosine, sine_front, sine_back):
    half = HEAD_DIM // 2
    lanes = values.shape[-1]
    return (
        values * cosine
        + pltpu.roll(values, lanes - half, 1) * sine_front
        + pltpu.roll(values, half, 1) * sine_back
    )


def weave(own, other, feat):
    pieces = []
    for at in range(0, own.shape[1], feat):
        pieces += [own[:, at : at + feat], other[:, at : at + feat]]
    return jnp.concatenate(pieces, axis=1)


def norm_scale(values):
    wide = values.astype(F32)
    return lax.rsqrt(jnp.sum(wide * wide, axis=1, keepdims=True) / values.shape[1] + EPS)


def whole_spec(a):
    return pl.BlockSpec(a.shape, lambda i: (0,) * a.ndim, pipeline_mode=pl.Buffered(1))


def row_spec(block, a):
    return pl.BlockSpec((block, a.shape[1]), lambda i: (i, 0))


def project_kernel(feat, own_ref, other_ref, weight_ref, cos_ref, front_ref, back_ref, q_ref, k_ref, v_ref, scale_ref):
    values = weave(own_ref[...], other_ref[...], feat)
    scale = norm_scale(values)
    scale_ref[...] = scale
    heads = q_ref.shape[1]
    cosine, front, back = cos_ref[...], front_ref[...], back_ref[...]
    for at, ref in enumerate((q_ref, k_ref, v_ref)):
        result = nn(values, weight_ref[:, at * heads : (at + 1) * heads]) * scale
        if at < 2:
            result = spin(result, cosine, front, back)
        ref[...] = result.astype(BF16)


def project(feat, own, other, weight, cosine, front, back):
    tokens = own.shape[0]
    heads = weight.shape[1] // 3
    block = 256
    result = jax.ShapeDtypeStruct((tokens, heads), BF16)
    scale = jax.ShapeDtypeStruct((tokens, 1), F32)
    return pl.pallas_call(
        functools.partial(project_kernel, feat),
        grid=(tokens // block,),
        in_specs=[row_spec(block, own), row_spec(block, other), whole_spec(weight)]
        + [row_spec(block, cosine)] * 3,
        out_specs=[row_spec(block, result)] * 3 + [row_spec(block, scale)],
        out_shape=[result] * 3 + [scale],
        compiler_params=pltpu.CompilerParams(vmem_limit_bytes=VMEM_BYTES),
        name="project",
    )(own, other, weight, cosine, front, back)


def unfold_kernel(feat, groups, *refs):
    count = sum(groups)
    lefts, weights = refs[: len(groups)], refs[len(groups) : len(groups) + count]
    own_ref, other_ref = refs[-2:]
    for at in range(0, own_ref.shape[1], feat):
        rows = slice(2 * at, 2 * (at + feat))
        total = None
        ids = iter(weights)
        for left, number in zip(lefts, groups):
            part = left.shape[1] // number
            for i in range(number):
                term = nt(left[:, i * part : (i + 1) * part], next(ids)[rows, :])
                total = term if total is None else total + term
        own_ref[:, at : at + feat] = total[:, :feat].astype(own_ref.dtype)
        other_ref[:, at : at + feat] = total[:, feat:].astype(BF16)


def unfold(feat, name, *pairs):
    lefts = [left for left, _ in pairs]
    weights = [w for _, ws in pairs for w in ws]
    tokens, half = lefts[0].shape[0], weights[0].shape[0] // 2
    block = 256
    own = jax.ShapeDtypeStruct((tokens, half), F32)
    other = jax.ShapeDtypeStruct((tokens, half), BF16)
    return pl.pallas_call(
        functools.partial(unfold_kernel, feat, tuple(len(ws) for _, ws in pairs)),
        grid=(tokens // block,),
        in_specs=[row_spec(block, a) for a in lefts] + [whole_spec(w) for w in weights],
        out_specs=[row_spec(block, own), row_spec(block, other)],
        out_shape=[own, other],
        compiler_params=pltpu.CompilerParams(vmem_limit_bytes=VMEM_BYTES),
        name=name,
    )(*lefts, *weights)


def units_kernel(feat, parts, count, *refs):
    m_owns, m_others, g_owns, g_others = (refs[i * parts : (i + 1) * parts] for i in range(4))
    refs = refs[4 * parts :]
    sources = refs[: 3 * count]
    refs = refs[3 * count :]
    hidden_ref, gate_ref, up_ref = refs[:3]
    own_refs, other_refs = refs[3 : 3 + parts], refs[3 + parts : 3 + 2 * parts]
    held, arrived = refs[3 + 2 * parts :]
    copies = [
        pltpu.make_async_copy(source, held.at[at], arrived.at[at]) for at, source in enumerate(sources)
    ]
    for copy in copies:
        copy.start()

    def together(owns, others):
        return jnp.concatenate([weave(a[...], b[...], feat) for a, b in zip(owns, others)], axis=0)

    middle = together(m_owns, m_others)
    grad = together(g_owns, g_others)
    scale = norm_scale(middle)
    part = hidden_ref.shape[1] // count
    pairs = []
    for i in range(count):
        columns = slice(i * part, (i + 1) * part)
        for copy in copies[3 * i : 3 * i + 3]:
            copy.wait()
        gate = nn(middle, held[3 * i]) * scale
        up = nn(middle, held[3 * i + 1]) * scale
        hidden_grad = nn(grad, held[3 * i + 2])
        sigmoid = 1.0 / (1.0 + jnp.exp(-gate))
        silu = gate * sigmoid
        hidden_ref[:, columns] = (silu * up).astype(BF16)
        gate_grad = hidden_grad * up * (sigmoid + silu * (1.0 - sigmoid))
        up_grad = hidden_grad * silu
        pairs.append((gate_grad.astype(BF16), held.at[3 * i]))
        pairs.append((up_grad.astype(BF16), held.at[3 * i + 1]))
        gate_ref[:, columns] = (gate_grad * scale).astype(BF16)
        up_ref[:, columns] = (up_grad * scale).astype(BF16)
    tokens = own_refs[0].shape[0]
    for at in range(0, own_refs[0].shape[1], feat):
        rows = slice(2 * at, 2 * (at + feat))
        total = None
        for left, weight in pairs:
            term = nt(left, weight[rows, :])
            total = term if total is None else total + term
        for i, (own_ref, other_ref) in enumerate(zip(own_refs, other_refs)):
            mine = total[i * tokens : (i + 1) * tokens]
            own_ref[:, at : at + feat] = mine[:, :feat]
            other_ref[:, at : at + feat] = mine[:, feat:].astype(BF16)


def units(feat, m_owns, m_others, g_owns, g_others, gates, ups, downs):
    parts = len(m_owns)
    tokens, half = m_owns[0].shape
    count, part = len(gates), gates[0].shape[1]
    hidden = jax.ShapeDtypeStruct((parts * tokens, count * part), BF16)
    weights = [w for three in zip(gates, ups, downs) for w in three]
    result = pl.pallas_call(
        functools.partial(units_kernel, feat, parts, count),
        in_specs=[pl.BlockSpec(memory_space=pltpu.VMEM)] * (4 * parts)
        + [pl.BlockSpec(memory_space=pl.ANY)] * len(weights),
        out_specs=[pl.BlockSpec(memory_space=pltpu.VMEM)] * (3 + 2 * parts),
        out_shape=[hidden] * 3
        + [jax.ShapeDtypeStruct((tokens, half), F32)] * parts
        + [jax.ShapeDtypeStruct((tokens, half), BF16)] * parts,
        scratch_shapes=[
            pltpu.VMEM((len(weights),) + weights[0].shape, BF16),
            pltpu.SemaphoreType.DMA((len(weights),)),
        ],
        compiler_params=pltpu.CompilerParams(vmem_limit_bytes=48 * 1024 * 1024),
        name="units",
    )(*m_owns, *m_others, *g_owns, *g_others, *weights)
    return result[0], result[1], result[2], result[3 : 3 + parts], result[3 + parts :]


def outer_kernel(groups, count, *refs):
    owns, others, rights = refs[:groups], refs[groups : 2 * groups], refs[2 * groups : len(refs) - count]
    outs = refs[len(refs) - count :]
    left = jnp.concatenate(
        [jnp.concatenate([own[...], other[...]], axis=1) for own, other in zip(owns, others)], axis=0
    )
    part = outs[0].shape[1]
    for i, out in enumerate(outs):
        columns = slice(i * part, (i + 1) * part)
        right = jnp.concatenate([ref[:, columns] for ref in rights], axis=0)
        result = tn(left, right)
        out[...] = result.astype(BF16)


def outer(feat, name, owns, others, rights, count=1):
    half, columns = owns[0].shape[1], rights[0].shape[1]
    part = columns // count
    side = pl.BlockSpec((owns[0].shape[0], feat), lambda i: (0, i))
    return pl.pallas_call(
        functools.partial(outer_kernel, len(owns), count),
        grid=(half // feat,),
        in_specs=[side] * (2 * len(owns)) + [whole_spec(a) for a in rights],
        out_specs=[pl.BlockSpec((2 * feat, part), lambda i: (i, 0))] * count,
        out_shape=[jax.ShapeDtypeStruct((2 * half, part), BF16)] * count,
        compiler_params=pltpu.CompilerParams(vmem_limit_bytes=40 * 1024 * 1024),
        name=name,
    )(*owns, *others, *rights)


def fold_kernel(feat, own_ref, other_ref, weight_ref, out_ref):
    out_ref[...] = nn(weave(own_ref[...], other_ref[...], feat), weight_ref[...]).astype(BF16)


def fold(feat, own, other, weight):
    tokens = own.shape[0]
    block = 256
    result = jax.ShapeDtypeStruct((tokens, weight.shape[1]), BF16)
    return pl.pallas_call(
        functools.partial(fold_kernel, feat),
        grid=(tokens // block,),
        in_specs=[row_spec(block, own), row_spec(block, other), whole_spec(weight)],
        out_specs=row_spec(block, result),
        out_shape=result,
        compiler_params=pltpu.CompilerParams(vmem_limit_bytes=40 * 1024 * 1024),
        name="fold",
    )(own, other, weight)


def allowed_block(start_row, key_base, query_base, keys, queries):
    key_index = key_base + lax.broadcasted_iota(jnp.int32, (keys, queries), 0)
    query_index = query_base + lax.broadcasted_iota(jnp.int32, (keys, queries), 1)
    return (key_index >= start_row) & (key_index <= query_index)


def attend_kernel(q_ref, k_ref, v_ref, start_ref, out_ref, log_ref):
    tokens = q_ref.shape[0]
    block = 256
    keys_all = k_ref[...]
    values_turned = v_ref[...].T
    lane = lax.broadcasted_iota(jnp.int32, (1, LANES), 1)
    sub = lax.broadcasted_iota(jnp.int32, (LANES, 1), 0)
    for place in range(tokens // block):
        rows = slice(place * block, (place + 1) * block)
        reach = (place + 1) * block
        query = q_ref[rows, :]
        start_row = start_ref[:, rows]
        allowed = allowed_block(start_row, 0, place * block, reach, block)
        parts = []
        for head in range(LANES // HEAD_DIM):
            mine = lane // HEAD_DIM == head
            query_head = query * mine.astype(BF16)
            scores = nt(keys_all[:reach], query_head) * (SCORE_SCALE * LOG2E)
            scores = jnp.where(allowed, scores, -1e30)
            peak = jnp.max(scores, axis=0, keepdims=True)
            raised = jnp.exp2(scores - peak)
            total = jnp.sum(raised, axis=0, keepdims=True)
            mixed = nn(values_turned[:, :reach], raised.astype(BF16)) / total
            parts.append(mixed)
            log_ref[0, head : head + 1, rows] = peak + jnp.log2(total)
        joined = jnp.where(sub // HEAD_DIM == 0, parts[0], parts[1])
        out_ref[rows, :] = joined.T.astype(BF16)


def attend(query, key, value, start_row):
    tokens, width = query.shape
    pairs = width // LANES
    column = pl.BlockSpec((tokens, LANES), lambda i: (0, i))
    return pl.pallas_call(
        attend_kernel,
        grid=(pairs,),
        in_specs=[column, column, column, pl.BlockSpec((1, tokens), lambda i: (0, 0))],
        out_specs=[column, pl.BlockSpec((1, 2, tokens), lambda i: (i, 0, 0))],
        out_shape=[
            jax.ShapeDtypeStruct((tokens, width), BF16),
            jax.ShapeDtypeStruct((pairs, 2, tokens), F32),
        ],
        compiler_params=pltpu.CompilerParams(vmem_limit_bytes=VMEM_BYTES),
        name="attend",
    )(query, key, value, start_row)


def attend_back_kernel(
    q_ref, k_ref, v_ref, o_ref, do_ref, start_ref, log_ref, cos_ref, front_ref, back_ref,
    dq_ref, dk_ref, dv_ref, dq_acc,
):
    tokens = q_ref.shape[0]
    block = 256
    lane = lax.broadcasted_iota(jnp.int32, (1, LANES), 1)
    sub = lax.broadcasted_iota(jnp.int32, (LANES, 1), 0)
    query_all = q_ref[...]
    grad_all = do_ref[...]
    product = (o_ref[...].astype(F32) * grad_all.astype(F32)).T
    dots = [
        jnp.sum(product[head * HEAD_DIM : (head + 1) * HEAD_DIM], axis=0, keepdims=True)
        for head in range(LANES // HEAD_DIM)
    ]
    dq_acc[...] = jnp.zeros_like(dq_acc)
    for place in range(tokens // block):
        rows = slice(place * block, (place + 1) * block)
        tail = slice(place * block, tokens)
        keys = k_ref[rows, :]
        values = v_ref[rows, :]
        keys_turned = keys.T
        query = query_all[place * block :]
        grad = grad_all[place * block :]
        start_row = start_ref[:, tail]
        allowed = allowed_block(
            start_row, place * block, place * block, block, tokens - place * block
        )
        key_grad = jnp.zeros((block, LANES), F32)
        value_grad = jnp.zeros((block, LANES), F32)
        for head in range(LANES // HEAD_DIM):
            mine = lane // HEAD_DIM == head
            scores = nt(keys * mine.astype(BF16), query) * (SCORE_SCALE * LOG2E)
            weights = jnp.where(allowed, jnp.exp2(scores - log_ref[0, head : head + 1, tail]), 0.0)
            weight_grad = nt(values * mine.astype(BF16), grad)
            score_grad = (weights * (weight_grad - dots[head][:, place * block :])).astype(BF16)
            value_grad = jnp.where(mine, nn(weights.astype(BF16), grad), value_grad)
            key_grad = jnp.where(mine, nn(score_grad, query), key_grad)
            dq_acc[:, tail] += nn(
                keys_turned * (sub // HEAD_DIM == head).astype(BF16), score_grad
            )
        dv_ref[rows, :] = value_grad.astype(BF16)
        dk_ref[rows, :] = spin(
            key_grad * SCORE_SCALE, cos_ref[rows, :], -front_ref[rows, :], -back_ref[rows, :]
        ).astype(BF16)
    dq_ref[...] = spin(
        dq_acc[...].T * SCORE_SCALE, cos_ref[...], -front_ref[...], -back_ref[...]
    ).astype(BF16)


def attend_back(query, key, value, mixed, mixed_grad, start_row, logs, cosine, front, back):
    tokens, width = query.shape
    pairs = width // LANES
    column = pl.BlockSpec((tokens, LANES), lambda i: (0, i))
    table = pl.BlockSpec((tokens, LANES), lambda i: (0, 0))
    return pl.pallas_call(
        attend_back_kernel,
        grid=(pairs,),
        in_specs=[
            column, column, column, column, column,
            pl.BlockSpec((1, tokens), lambda i: (0, 0)),
            pl.BlockSpec((1, 2, tokens), lambda i: (i, 0, 0)),
            table, table, table,
        ],
        out_specs=[column, column, column],
        out_shape=[jax.ShapeDtypeStruct((tokens, width), BF16)] * 3,
        scratch_shapes=[pltpu.VMEM((LANES, tokens), F32)],
        compiler_params=pltpu.CompilerParams(vmem_limit_bytes=VMEM_BYTES),
        name="attend_back",
    )(query, key, value, mixed, mixed_grad, start_row, logs, cosine, front, back)


def rope_tables(positions, width):
    half = HEAD_DIM // 2
    freqs = jnp.exp(jnp.arange(half, dtype=F32) * (-2.0 * math.log(ROPE_BASE) / HEAD_DIM))
    angles = positions.astype(F32)[:, None] * freqs[None, :]
    cosine, sine = jnp.cos(angles), jnp.sin(angles)
    zero = jnp.zeros_like(sine)
    heads = width // HEAD_DIM
    return (
        jnp.tile(cosine, (1, 2 * heads)),
        jnp.tile(jnp.concatenate([-sine, zero], axis=1), (1, heads)),
        jnp.tile(jnp.concatenate([zero, sine], axis=1), (1, heads)),
    )


def local(
    inputs,
    query_weight,
    key_weight,
    value_weight,
    out_weight,
    gate_weight,
    up_weight,
    down_weight,
    first_gain,
    second_gain,
    segment_ids,
    positions,
    out_grad,
):
    rows = lax.axis_size("row")
    cols = lax.axis_size("col")
    places = cols // 2
    row = lax.axis_index("row")
    col = lax.axis_index("col")
    core = col % 2
    place = col // 2
    tokens, feat = inputs.shape
    width = feat * cols
    half = width // 2
    quarter = tokens // places

    def core_swap(a):
        return lax.ppermute(a, "col", [(i, i ^ 1) for i in range(cols)])

    def plane_swap(a, step):
        return lax.ppermute(a, "col", [(i, i ^ (2 * step)) for i in range(cols)])

    def token_part(a, step):
        return lax.dynamic_slice_in_dim(a, (place ^ step) * quarter, quarter, 0)

    def feat_part(a, step):
        return lax.dynamic_slice_in_dim(a, (place ^ step) * feat, feat, 1)

    def own_first(w):
        return jnp.concatenate(
            [jnp.where(core == 0, w[:feat], w[feat:]), jnp.where(core == 0, w[feat:], w[:feat])], axis=0
        )

    def row_swap(a, step):
        return lax.ppermute(a, "row", [(i, i ^ step) for i in range(rows)])

    def gather_row(a):
        got, bit = {0: a}, rows // 2
        while bit:
            for step in list(got):
                got[step ^ bit] = row_swap(got[step], bit)
            bit //= 2
        return [got[step] for step in range(rows)]

    def reduce_row(parts):
        parts, bit = list(parts), 1
        while bit < rows:
            for at in range(0, rows, 2 * bit):
                sent = row_swap(parts[at + bit].astype(BF16), bit)
                parts[at] = parts[at].astype(F32) + sent.astype(F32)
            bit *= 2
        return parts[0]

    def row_part(a, step):
        size = a.shape[0] // rows
        return lax.dynamic_slice_in_dim(a, (row ^ step) * size, size, 0)

    def join_rows(pieces, axis=0, dtype=BF16):
        size = pieces[0].shape[axis]
        shape = list(pieces[0].shape)
        shape[axis] *= rows
        whole = jnp.zeros(shape, dtype)
        for step, piece in enumerate(pieces):
            whole = lax.dynamic_update_slice_in_dim(whole, piece, (row ^ step) * size, axis)
        return whole

    def after(value, *others):
        return lax.optimization_barrier((value,) + others)[0]

    def put_rows(pieces):
        whole = jnp.zeros((tokens,) + pieces[0].shape[1:], pieces[0].dtype)
        for step, piece in enumerate(pieces):
            whole = lax.dynamic_update_slice_in_dim(whole, piece, (place ^ step) * quarter, 0)
        return whole

    def put_feats(pieces):
        whole = jnp.zeros((pieces[0].shape[0], half), pieces[0].dtype)
        for step, piece in enumerate(pieces):
            whole = lax.dynamic_update_slice_in_dim(whole, piece, (place ^ step) * feat, 1)
        return whole

    def spread(a):
        return [a] + [plane_swap(a, step) for step in range(1, places)]

    groups = [[2 * i + k for i in range(places)] for k in range(2)]

    def plane_exchange(a):
        return lax.all_to_all(
            a, "col", split_axis=0, concat_axis=0, axis_index_groups=groups, tiled=True
        )

    def to_parts(a):
        a = plane_exchange(a.reshape(places, quarter, feat))
        return jnp.concatenate([a[s] for s in range(places)], axis=1)

    def to_home(a):
        a = jnp.stack([a[:, s * feat : (s + 1) * feat] for s in range(places)])
        return plane_exchange(a).reshape(tokens, feat)

    def sum_cols(a):
        step = 1
        while step < cols:
            a = a + lax.ppermute(a, "col", [(i, i ^ step) for i in range(cols)])
            step *= 2
        return a

    gain_one = first_gain.astype(F32)[:, None]
    gain_two = second_gain.astype(F32)[:, None]

    def scaled(w, gain):
        return own_first((w.astype(F32) * gain).astype(BF16))

    def exchange(w):
        part = w.shape[1] // rows
        pieces = jnp.stack([w[:, s * part : (s + 1) * part] for s in range(rows)])
        return lax.all_to_all(pieces, "row", split_axis=0, concat_axis=0, tiled=True).reshape(width, part)

    def spread_weights(whole):
        if places != 4:
            return spread(whole)
        first, second = plane_swap(whole, 1), plane_swap(whole, 2)
        return [
            whole,
            first,
            second,
            jnp.concatenate([plane_swap(second[:half], 1), plane_swap(first[half:], 2)], axis=0),
        ]

    def give_back(pieces):
        if places != 4:
            total = pieces[0].astype(F32)
            for s in range(1, places):
                total = total + plane_swap(pieces[s], s).astype(F32)
        else:
            to_second = pieces[2].astype(F32) + jnp.concatenate(
                [plane_swap(pieces[3][:half], 1), jnp.zeros_like(pieces[3][half:])], axis=0
            ).astype(F32)
            to_first = pieces[1].astype(F32) + jnp.concatenate(
                [jnp.zeros_like(pieces[3][:half]), plane_swap(pieces[3][half:], 2)], axis=0
            ).astype(F32)
            total = (
                pieces[0].astype(F32)
                + plane_swap(to_first.astype(BF16), 1).astype(F32)
                + plane_swap(to_second.astype(BF16), 2).astype(F32)
            )
        total = total.astype(BF16).reshape(rows, 2 * feat, pieces[0].shape[1])
        total = lax.all_to_all(total, "row", split_axis=0, concat_axis=0, tiled=True).astype(F32)
        return jnp.concatenate([own_first(total[s]) for s in range(rows)], axis=1)

    def give_rows(w):
        return own_first(lax.psum_scatter(w, "row", scatter_dimension=0, tiled=True)).astype(F32)

    with jax.named_scope("gather_qkv"):
        qkv_full = lax.all_gather(
            jnp.concatenate(
                [scaled(w, gain_one) for w in (query_weight, key_weight, value_weight)], axis=1
            ),
            "row",
            axis=0,
            tiled=True,
        )
        out_full = lax.all_gather(own_first(out_weight), "row", axis=0, tiled=True)
    with jax.named_scope("gate_row"):
        gate_whole = exchange(scaled(gate_weight, gain_two))
    with jax.named_scope("up_row"):
        up_whole = exchange(after(scaled(up_weight, gain_two), gate_whole))
    with jax.named_scope("down_row"):
        down_whole = exchange(after(own_first(down_weight), up_whole))
    with jax.named_scope("grad_plane"):
        g_part = to_parts(after(out_grad, down_whole))
    with jax.named_scope("grad_row"):
        g_list = gather_row(g_part)
    with jax.named_scope("gate_plane"):
        gates = spread_weights(gate_whole)
    with jax.named_scope("up_plane"):
        ups = spread_weights(up_whole)

    with jax.named_scope("inputs"):
        x_own = put_feats(spread(inputs))
        x_other = core_swap(x_own)
    heads_width = query_weight.shape[1]
    cosine, front, back = rope_tables(positions, heads_width)
    start_row = jnp.sum(
        (segment_ids[None, :] < segment_ids[:, None]).astype(jnp.int32), axis=1
    )[None, :]
    x_ready = after(x_own, gates[1], gates[2])
    query, key, value, scale_one = project(feat, x_ready, x_other, qkv_full, cosine, front, back)
    mixed, logs = attend(query, key, value, start_row)
    mixed = after(mixed, up_whole, gates[3])

    def scatter_parts(own, other):
        own = own + core_swap(other).astype(F32)
        low = own.astype(BF16)
        total = token_part(own, 0)
        for s in range(1, places):
            total = total + plane_swap(token_part(low, s), s).astype(F32)
        return total

    with jax.named_scope("mix_plane"):
        middle = token_part(x_own, 0).astype(F32) + scatter_parts(*unfold(feat, "mix", (mixed, [out_full])))
    square = jnp.sum(middle * middle, axis=1, keepdims=True)
    square = square + core_swap(square)
    scale_mid = lax.rsqrt(square / width + EPS)

    with jax.named_scope("down_plane"):
        downs = spread_weights(after(down_whole, middle))
    with jax.named_scope("middle_row"):
        m_list = gather_row(after(middle.astype(BF16), ups[1], ups[2]))
        m_others = [core_swap(m) for m in m_list]
    with jax.named_scope("grad_core"):
        g_others = [core_swap(g) for g in g_list]
    found, own_shares, other_shares = [], [], []
    for at in range(0, rows, 2):
        pick = slice(at, at + 2)
        *three, owns, others = units(
            feat, m_list[pick], m_others[pick], g_list[pick], g_others[pick], gates, ups, downs
        )
        found.append(three)
        own_shares += owns
        other_shares += others
    with jax.named_scope("unit_grad"):
        shares = [own + core_swap(other).astype(F32) for own, other in zip(own_shares, other_shares)]
        last = shares[-1]
        unit_grad = reduce_row(shares)
    with jax.named_scope("feed"):
        shares = []
        for hidden, _, _ in found:
            own, other = unfold(feat, "feed", (after(hidden, last), downs))
            own = own + core_swap(other).astype(F32)
            shares += [own[:quarter], own[quarter:]]
        feed = reduce_row([after(a, unit_grad) for a in shares])
    with jax.named_scope("block_out"):
        block_out = to_home((middle + feed).astype(BF16))

    unit_mid = middle * scale_mid
    dot_two = jnp.sum(unit_grad * unit_mid, axis=1, keepdims=True)
    dot_two = dot_two + core_swap(dot_two)
    middle_grad = g_part.astype(F32) + scale_mid * (unit_grad - unit_mid * (dot_two / width))

    with jax.named_scope("middle_grad"):
        d_own = put_rows(spread(middle_grad.astype(BF16)))
        d_other = core_swap(d_own)
    mixed_grad = fold(feat, d_own, d_other, out_full)
    query_grad, key_grad, value_grad = attend_back(
        query, key, value, mixed, mixed_grad, start_row, logs, cosine, front, back
    )
    grads = jnp.concatenate([query_grad, key_grad, value_grad], axis=1)
    grads_scaled = (grads.astype(F32) * scale_one).astype(BF16)
    qkv_part = outer(feat, "qkv_outer", [x_own], [x_other], [grads_scaled])[0]
    with jax.named_scope("qkv_grad"):
        qkv_grad = give_rows(qkv_part)
    with jax.named_scope("first_gain"):
        gain_dots = jnp.sum(qkv_part.astype(F32) * qkv_full.astype(F32), axis=1).reshape(rows, 2, feat)
        gain_dots = sum_cols(jnp.where(core == 0, gain_dots, gain_dots[:, ::-1]).reshape(width))
        gain_row = row_part(gain_dots, 0) + sum(
            row_swap(row_part(gain_dots, s), s) for s in range(1, rows)
        )
        first_gain_grad = gain_row / gain_one[:, 0]
    with jax.named_scope("first_plane"):
        first_unit_grad = scatter_parts(*unfold(feat, "first_grad", (after(grads, qkv_part), [qkv_full])))
    scale_first = token_part(scale_one, 0)
    unit_first = token_part(x_own, 0).astype(F32) * scale_first
    dot_one = jnp.sum(first_unit_grad * unit_first, axis=1, keepdims=True)
    dot_one = dot_one + core_swap(dot_one)
    with jax.named_scope("input_grad"):
        input_grad = to_home(
            (middle_grad + scale_first * (first_unit_grad - unit_first * (dot_one / width))).astype(BF16)
        )

    with jax.named_scope("out_grad"):
        out_weight_grad = give_rows(outer(feat, "out_outer", [d_own], [d_other], [mixed])[0])
    with jax.named_scope("down_grad"):
        down_weight_grad = give_back(
            outer(feat, "down_outer", g_list, g_others, [after(f[0], last) for f in found], places)
        )
    with jax.named_scope("gate_grad"):
        gate_parts = outer(feat, "gate_outer", m_list, m_others, [after(f[1], last) for f in found], places)
        gate_unit = give_back([after(a, d_own) for a in gate_parts])
    with jax.named_scope("up_grad"):
        up_parts = outer(feat, "up_outer", m_list, m_others, [after(f[2], last) for f in found], places)
        up_unit = give_back([after(a, d_own, mixed_grad) for a in up_parts])
    q_unit = qkv_grad[:, :heads_width]
    k_unit = qkv_grad[:, heads_width : 2 * heads_width]
    v_unit = qkv_grad[:, 2 * heads_width :]

    def row_dots(*pairs):
        return sum(jnp.sum(w.astype(F32) * d, axis=1) for w, d in pairs)

    second_gain_grad = sum_cols(row_dots((gate_weight, gate_unit), (up_weight, up_unit)))
    return (
        block_out,
        input_grad,
        q_unit * gain_one,
        k_unit * gain_one,
        v_unit * gain_one,
        out_weight_grad,
        gate_unit * gain_two,
        up_unit * gain_two,
        down_weight_grad,
        first_gain_grad,
        second_gain_grad,
    )


def solution(mesh):
    grid, line = P("row", "col"), P("row")
    return jax.shard_map(
        local,
        mesh=mesh,
        in_specs=(grid,) * 8 + (line,) * 4 + (grid,),
        out_specs=(grid,) * 9 + (line,) * 2,
        check_vma=False,
    )
```

```python
import functools
import math

import jax
import jax.numpy as jnp
from jax import lax
from jax.experimental import pallas as pl
from jax.experimental.pallas import tpu as pltpu
from jax.sharding import PartitionSpec as P

HEAD_DIM = 64
LANES = 128
EPS = 1e-05
ROPE_BASE = 130000.0
LOG2E = math.log2(math.e)
SCORE_SCALE = HEAD_DIM**-0.5
BF16 = jnp.bfloat16
F32 = jnp.float32
VMEM_BYTES = 56 * 1024 * 1024


def nn(left, right):
    return lax.dot_general(left, right, (((1,), (0,)), ((), ())), preferred_element_type=F32)


def nt(left, right):
    return lax.dot_general(left, right, (((1,), (1,)), ((), ())), preferred_element_type=F32)


def tn(left, right):
    return lax.dot_general(left, right, (((0,), (0,)), ((), ())), preferred_element_type=F32)


def spin(values, cosine, sine_front, sine_back):
    half = HEAD_DIM // 2
    lanes = values.shape[-1]
    return (
        values * cosine
        + pltpu.roll(values, lanes - half, 1) * sine_front
        + pltpu.roll(values, half, 1) * sine_back
    )


def weave(own, other, feat):
    pieces = []
    for at in range(0, own.shape[1], feat):
        pieces += [own[:, at : at + feat], other[:, at : at + feat]]
    return jnp.concatenate(pieces, axis=1)


def norm_scale(values):
    wide = values.astype(F32)
    return lax.rsqrt(jnp.sum(wide * wide, axis=1, keepdims=True) / values.shape[1] + EPS)


def whole_spec(a):
    return pl.BlockSpec(a.shape, lambda i: (0,) * a.ndim, pipeline_mode=pl.Buffered(1))


def row_spec(block, a):
    return pl.BlockSpec((block, a.shape[1]), lambda i: (i, 0))


def project_kernel(feat, own_ref, other_ref, weight_ref, cos_ref, front_ref, back_ref, q_ref, k_ref, v_ref, scale_ref):
    values = weave(own_ref[...], other_ref[...], feat)
    scale = norm_scale(values)
    scale_ref[...] = scale
    heads = q_ref.shape[1]
    cosine, front, back = cos_ref[...], front_ref[...], back_ref[...]
    for at, ref in enumerate((q_ref, k_ref, v_ref)):
        result = nn(values, weight_ref[:, at * heads : (at + 1) * heads]) * scale
        if at < 2:
            result = spin(result, cosine, front, back)
        ref[...] = result.astype(BF16)


def project(feat, own, other, weight, cosine, front, back):
    tokens = own.shape[0]
    heads = weight.shape[1] // 3
    block = 256
    result = jax.ShapeDtypeStruct((tokens, heads), BF16)
    scale = jax.ShapeDtypeStruct((tokens, 1), F32)
    return pl.pallas_call(
        functools.partial(project_kernel, feat),
        grid=(tokens // block,),
        in_specs=[row_spec(block, own), row_spec(block, other), whole_spec(weight)]
        + [row_spec(block, cosine)] * 3,
        out_specs=[row_spec(block, result)] * 3 + [row_spec(block, scale)],
        out_shape=[result] * 3 + [scale],
        compiler_params=pltpu.CompilerParams(vmem_limit_bytes=VMEM_BYTES),
        name="project",
    )(own, other, weight, cosine, front, back)


def unfold_kernel(feat, joined, *refs):
    own_ref, other_ref = refs[-2:]
    lefts, weights = refs[:joined], refs[joined:-2]
    left = jnp.concatenate([ref[...] for ref in lefts], axis=1)
    part = weights[0].shape[1]
    for at in range(0, own_ref.shape[1], feat):
        rows = slice(2 * at, 2 * (at + feat))
        total = None
        for i, weight in enumerate(weights):
            term = nt(left[:, i * part : (i + 1) * part], weight[rows, :])
            total = term if total is None else total + term
        own_ref[:, at : at + feat] = total[:, :feat].astype(BF16)
        other_ref[:, at : at + feat] = total[:, feat:].astype(BF16)


def unfold(feat, name, lefts, weights):
    tokens, half = lefts[0].shape[0], weights[0].shape[0] // 2
    block = 256
    result = jax.ShapeDtypeStruct((tokens, half), BF16)
    return pl.pallas_call(
        functools.partial(unfold_kernel, feat, len(lefts)),
        grid=(tokens // block,),
        in_specs=[row_spec(block, a) for a in lefts] + [whole_spec(w) for w in weights],
        out_specs=[row_spec(block, result)] * 2,
        out_shape=[result] * 2,
        compiler_params=pltpu.CompilerParams(vmem_limit_bytes=VMEM_BYTES),
        name=name,
    )(*lefts, *weights)


def units_kernel(feat, parts, count, starts, *refs):
    m_owns, m_others = refs[:parts], refs[parts : 2 * parts]
    g_sources = refs[2 * parts : 2 * parts + 2]
    refs = refs[2 * parts + 2 :]
    sources, refs = refs[: 3 * count], refs[3 * count :]
    hidden_ref, gate_ref, up_ref = refs[:3]
    own_refs, other_refs = refs[3 : 3 + parts], refs[3 + parts : 3 + 2 * parts]
    held, arrived, g_held, g_arrived = refs[3 + 2 * parts :]
    tokens = own_refs[0].shape[0]
    copies = [
        pltpu.make_async_copy(source, held.at[at], arrived.at[at]) for at, source in enumerate(sources)
    ]
    g_copies = [
        pltpu.make_async_copy(
            source.at[pl.ds(pl.multiple_of(starts[i] * tokens, tokens), tokens)],
            g_held.at[side, i],
            g_arrived.at[side, i],
        )
        for side, source in enumerate(g_sources)
        for i in range(parts)
    ]
    for copy in copies[:2] + g_copies + copies[2:]:
        copy.start()
    middle = jnp.concatenate(
        [weave(a[...], b[...], feat) for a, b in zip(m_owns, m_others)], axis=0
    )
    scale = norm_scale(middle)
    part = hidden_ref.shape[1] // count
    pairs = []
    grad = None
    for i in range(count):
        columns = slice(i * part, (i + 1) * part)
        copies[3 * i].wait()
        gate = nn(middle, held[3 * i]) * scale
        copies[3 * i + 1].wait()
        up = nn(middle, held[3 * i + 1]) * scale
        copies[3 * i + 2].wait()
        if grad is None:
            for copy in g_copies:
                copy.wait()
            grad = jnp.concatenate(
                [weave(g_held[0, j], g_held[1, j], feat) for j in range(parts)], axis=0
            )
        hidden_grad = nn(grad, held[3 * i + 2])
        sigmoid = 1.0 / (1.0 + jnp.exp(-gate))
        silu = gate * sigmoid
        hidden_ref[:, columns] = (silu * up).astype(BF16)
        gate_grad = hidden_grad * up * (sigmoid + silu * (1.0 - sigmoid))
        up_grad = hidden_grad * silu
        pairs.append((gate_grad.astype(BF16), held.at[3 * i]))
        pairs.append((up_grad.astype(BF16), held.at[3 * i + 1]))
        gate_ref[:, columns] = (gate_grad * scale).astype(BF16)
        up_ref[:, columns] = (up_grad * scale).astype(BF16)
    for at in range(0, own_refs[0].shape[1], feat):
        rows = slice(2 * at, 2 * (at + feat))
        total = None
        for left, weight in pairs:
            term = nt(left, weight[rows, :])
            total = term if total is None else total + term
        for i, (own_ref, other_ref) in enumerate(zip(own_refs, other_refs)):
            mine = total[i * tokens : (i + 1) * tokens]
            own_ref[:, at : at + feat] = mine[:, :feat].astype(BF16)
            other_ref[:, at : at + feat] = mine[:, feat:].astype(BF16)


def units(feat, starts, m_owns, m_others, g_own, g_other, gates, ups, downs):
    parts = len(m_owns)
    tokens, half = m_owns[0].shape
    count, part = len(gates), gates[0].shape[1]
    hidden = jax.ShapeDtypeStruct((parts * tokens, count * part), BF16)
    share = jax.ShapeDtypeStruct((tokens, half), BF16)
    weights = [w for three in zip(gates, ups, downs) for w in three]
    vmem, anywhere = pl.BlockSpec(memory_space=pltpu.VMEM), pl.BlockSpec(memory_space=pl.ANY)
    result = pl.pallas_call(
        functools.partial(units_kernel, feat, parts, count),
        in_specs=[pl.BlockSpec(memory_space=pltpu.SMEM)]
        + [vmem] * (2 * parts)
        + [anywhere] * (2 + len(weights)),
        out_specs=[vmem] * (3 + 2 * parts),
        out_shape=[hidden] * 3 + [share] * (2 * parts),
        scratch_shapes=[
            pltpu.VMEM((len(weights),) + weights[0].shape, BF16),
            pltpu.SemaphoreType.DMA((len(weights),)),
            pltpu.VMEM((2, parts, tokens, half), BF16),
            pltpu.SemaphoreType.DMA((2, parts)),
        ],
        compiler_params=pltpu.CompilerParams(vmem_limit_bytes=VMEM_BYTES),
        name="units",
    )(starts, *m_owns, *m_others, g_own, g_other, *weights)
    return result[0], result[1], result[2], result[3 : 3 + parts], result[3 + parts :]


def outer_kernel(groups, count, starts, *refs):
    owns, others, rights = refs[:groups], refs[groups : 2 * groups], refs[2 * groups : len(refs) - count]
    outs = refs[len(refs) - count :]
    if groups == 1:
        tokens = owns[0].shape[0] // starts.shape[0]
        picks = [
            pl.ds(pl.multiple_of(starts[i] * tokens, tokens), tokens) for i in range(starts.shape[0])
        ]
        sides = [(owns[0][pick, :], others[0][pick, :]) for pick in picks]
    else:
        sides = [(own[...], other[...]) for own, other in zip(owns, others)]
    left = jnp.concatenate([jnp.concatenate(pair, axis=1) for pair in sides], axis=0)
    part = outs[0].shape[1]
    for i, out in enumerate(outs):
        columns = slice(i * part, (i + 1) * part)
        right = jnp.concatenate([ref[:, columns] for ref in rights], axis=0)
        out[...] = tn(left, right).astype(BF16)


def outer(feat, name, starts, owns, others, rights, count):
    half, columns = owns[0].shape[1], rights[0].shape[1]
    part = columns // count
    side = pl.BlockSpec((owns[0].shape[0], feat), lambda i: (0, i))
    return pl.pallas_call(
        functools.partial(outer_kernel, len(owns), count),
        grid=(half // feat,),
        in_specs=[pl.BlockSpec(memory_space=pltpu.SMEM)]
        + [side] * (2 * len(owns))
        + [whole_spec(a) for a in rights],
        out_specs=[pl.BlockSpec((2 * feat, part), lambda i: (i, 0))] * count,
        out_shape=[jax.ShapeDtypeStruct((2 * half, part), BF16)] * count,
        compiler_params=pltpu.CompilerParams(vmem_limit_bytes=VMEM_BYTES),
        name=name,
    )(starts, *owns, *others, *rights)


def heads_outer_kernel(x_own, x_other, d_own, d_other, dq_ref, dk_ref, dv_ref, mixed_ref, scale_ref, weight_ref, out_ref, dot_ref):
    part = mixed_ref.shape[1]
    left = jnp.concatenate([x_own[...], x_other[...]], axis=1)
    dots = None
    for i, ref in enumerate((dq_ref, dk_ref, dv_ref)):
        columns = slice(i * part, (i + 1) * part)
        result = tn(left, (ref[...].astype(F32) * scale_ref[...]).astype(BF16))
        out_ref[:, columns] = result.astype(BF16)
        term = jnp.sum(result * weight_ref[:, columns].astype(F32), axis=1, keepdims=True)
        dots = term if dots is None else dots + term
    dot_ref[...] = dots
    left = jnp.concatenate([d_own[...], d_other[...]], axis=1)
    out_ref[:, 3 * part :] = tn(left, mixed_ref[...]).astype(BF16)


def heads_outer(feat, x_own, x_other, d_own, d_other, dq, dk, dv, mixed, scale, weight):
    tokens, half = x_own.shape
    part = mixed.shape[1]
    side = pl.BlockSpec((tokens, feat), lambda i: (0, i))
    return pl.pallas_call(
        heads_outer_kernel,
        grid=(half // feat,),
        in_specs=[side] * 4
        + [whole_spec(a) for a in (dq, dk, dv, mixed, scale)]
        + [row_spec(2 * feat, weight)],
        out_specs=[pl.BlockSpec((2 * feat, 4 * part), lambda i: (i, 0)), pl.BlockSpec((2 * feat, 1), lambda i: (i, 0))],
        out_shape=[
            jax.ShapeDtypeStruct((2 * half, 4 * part), BF16),
            jax.ShapeDtypeStruct((2 * half, 1), F32),
        ],
        compiler_params=pltpu.CompilerParams(vmem_limit_bytes=VMEM_BYTES),
        name="heads_outer",
    )(x_own, x_other, d_own, d_other, dq, dk, dv, mixed, scale, weight)


def finish_kernel(core_ref, part_ref, gain_ref, *outs):
    feat = gain_ref.shape[0] // 2
    blocks, columns = part_ref.shape[0], part_ref.shape[2]
    width = blocks * columns // len(outs)
    for block in range(blocks):
        at = block * columns
        for side in range(2):
            rows = slice(side * feat, (side + 1) * feat)
            start = pl.multiple_of(lax.rem(core_ref[0] + side, 2) * feat, feat)
            value = part_ref[block, pl.ds(start, feat), :].astype(F32) * gain_ref[rows, :]
            outs[at // width][rows, at % width : at % width + columns] = value


def finish(core, part, gain, count=1):
    blocks, rows, columns = part.shape
    vmem = pl.BlockSpec(memory_space=pltpu.VMEM)
    result = jax.ShapeDtypeStruct((rows, blocks * columns // count), F32)
    return pl.pallas_call(
        finish_kernel,
        in_specs=[pl.BlockSpec(memory_space=pltpu.SMEM), vmem, vmem],
        out_specs=[vmem] * count,
        out_shape=[result] * count,
        compiler_params=pltpu.CompilerParams(vmem_limit_bytes=VMEM_BYTES),
        name="finish",
    )(core, part, gain)


def fold_kernel(feat, own_ref, other_ref, weight_ref, out_ref):
    out_ref[...] = nn(weave(own_ref[...], other_ref[...], feat), weight_ref[...]).astype(BF16)


def fold(feat, own, other, weight):
    tokens = own.shape[0]
    block = 256
    result = jax.ShapeDtypeStruct((tokens, weight.shape[1]), BF16)
    return pl.pallas_call(
        functools.partial(fold_kernel, feat),
        grid=(tokens // block,),
        in_specs=[row_spec(block, own), row_spec(block, other), whole_spec(weight)],
        out_specs=row_spec(block, result),
        out_shape=result,
        compiler_params=pltpu.CompilerParams(vmem_limit_bytes=VMEM_BYTES),
        name="fold",
    )(own, other, weight)


def allowed_block(start_row, key_base, query_base, keys, queries):
    key_index = key_base + lax.broadcasted_iota(jnp.int32, (keys, queries), 0)
    query_index = query_base + lax.broadcasted_iota(jnp.int32, (keys, queries), 1)
    return (key_index >= start_row) & (key_index <= query_index)


def attend_kernel(q_ref, k_ref, v_ref, start_ref, out_ref, log_ref):
    tokens = q_ref.shape[0]
    block = 256
    keys_all = k_ref[...]
    values_turned = v_ref[...].T
    lane = lax.broadcasted_iota(jnp.int32, (1, LANES), 1)
    sub = lax.broadcasted_iota(jnp.int32, (LANES, 1), 0)
    for place in range(tokens // block):
        rows = slice(place * block, (place + 1) * block)
        reach = (place + 1) * block
        query = q_ref[rows, :]
        start_row = start_ref[:, rows]
        allowed = allowed_block(start_row, 0, place * block, reach, block)
        parts = []
        for head in range(LANES // HEAD_DIM):
            mine = lane // HEAD_DIM == head
            query_head = query * mine.astype(BF16)
            scores = nt(keys_all[:reach], query_head) * (SCORE_SCALE * LOG2E)
            scores = jnp.where(allowed, scores, -1e30)
            peak = jnp.max(scores, axis=0, keepdims=True)
            raised = jnp.exp2(scores - peak)
            total = jnp.sum(raised, axis=0, keepdims=True)
            mixed = nn(values_turned[:, :reach], raised.astype(BF16)) / total
            parts.append(mixed)
            log_ref[0, head : head + 1, rows] = peak + jnp.log2(total)
        joined = jnp.where(sub // HEAD_DIM == 0, parts[0], parts[1])
        out_ref[rows, :] = joined.T.astype(BF16)


def attend(query, key, value, start_row):
    tokens, width = query.shape
    pairs = width // LANES
    column = pl.BlockSpec((tokens, LANES), lambda i: (0, i))
    return pl.pallas_call(
        attend_kernel,
        grid=(pairs,),
        in_specs=[column, column, column, pl.BlockSpec((1, tokens), lambda i: (0, 0))],
        out_specs=[column, pl.BlockSpec((1, 2, tokens), lambda i: (i, 0, 0))],
        out_shape=[
            jax.ShapeDtypeStruct((tokens, width), BF16),
            jax.ShapeDtypeStruct((pairs, 2, tokens), F32),
        ],
        compiler_params=pltpu.CompilerParams(vmem_limit_bytes=VMEM_BYTES),
        name="attend",
    )(query, key, value, start_row)


def attend_back_kernel(
    q_ref, k_ref, v_ref, o_ref, do_ref, start_ref, log_ref, cos_ref, front_ref, back_ref,
    dq_ref, dk_ref, dv_ref, dq_acc,
):
    tokens = q_ref.shape[0]
    block = 256
    lane = lax.broadcasted_iota(jnp.int32, (1, LANES), 1)
    sub = lax.broadcasted_iota(jnp.int32, (LANES, 1), 0)
    query_all = q_ref[...]
    grad_all = do_ref[...]
    product = (o_ref[...].astype(F32) * grad_all.astype(F32)).T
    dots = [
        jnp.sum(product[head * HEAD_DIM : (head + 1) * HEAD_DIM], axis=0, keepdims=True)
        for head in range(LANES // HEAD_DIM)
    ]
    dq_acc[...] = jnp.zeros_like(dq_acc)
    for place in range(tokens // block):
        rows = slice(place * block, (place + 1) * block)
        tail = slice(place * block, tokens)
        keys = k_ref[rows, :]
        values = v_ref[rows, :]
        keys_turned = keys.T
        query = query_all[place * block :]
        grad = grad_all[place * block :]
        start_row = start_ref[:, tail]
        allowed = allowed_block(
            start_row, place * block, place * block, block, tokens - place * block
        )
        key_grad = jnp.zeros((block, LANES), F32)
        value_grad = jnp.zeros((block, LANES), F32)
        for head in range(LANES // HEAD_DIM):
            mine = lane // HEAD_DIM == head
            scores = nt(keys * mine.astype(BF16), query) * (SCORE_SCALE * LOG2E)
            weights = jnp.where(allowed, jnp.exp2(scores - log_ref[0, head : head + 1, tail]), 0.0)
            weight_grad = nt(values * mine.astype(BF16), grad)
            score_grad = (weights * (weight_grad - dots[head][:, place * block :])).astype(BF16)
            value_grad = jnp.where(mine, nn(weights.astype(BF16), grad), value_grad)
            key_grad = jnp.where(mine, nn(score_grad, query), key_grad)
            dq_acc[:, tail] += nn(
                keys_turned * (sub // HEAD_DIM == head).astype(BF16), score_grad
            )
        dv_ref[rows, :] = value_grad.astype(BF16)
        dk_ref[rows, :] = spin(
            key_grad * SCORE_SCALE, cos_ref[rows, :], -front_ref[rows, :], -back_ref[rows, :]
        ).astype(BF16)
    dq_ref[...] = spin(
        dq_acc[...].T * SCORE_SCALE, cos_ref[...], -front_ref[...], -back_ref[...]
    ).astype(BF16)


def attend_back(query, key, value, mixed, mixed_grad, start_row, logs, cosine, front, back):
    tokens, width = query.shape
    pairs = width // LANES
    column = pl.BlockSpec((tokens, LANES), lambda i: (0, i))
    table = pl.BlockSpec((tokens, LANES), lambda i: (0, 0))
    return pl.pallas_call(
        attend_back_kernel,
        grid=(pairs,),
        in_specs=[
            column, column, column, column, column,
            pl.BlockSpec((1, tokens), lambda i: (0, 0)),
            pl.BlockSpec((1, 2, tokens), lambda i: (i, 0, 0)),
            table, table, table,
        ],
        out_specs=[column, column, column],
        out_shape=[jax.ShapeDtypeStruct((tokens, width), BF16)] * 3,
        scratch_shapes=[pltpu.VMEM((LANES, tokens), F32)],
        compiler_params=pltpu.CompilerParams(vmem_limit_bytes=VMEM_BYTES),
        name="attend_back",
    )(query, key, value, mixed, mixed_grad, start_row, logs, cosine, front, back)


def rope_tables(positions, width):
    half = HEAD_DIM // 2
    freqs = jnp.exp(jnp.arange(half, dtype=F32) * (-2.0 * math.log(ROPE_BASE) / HEAD_DIM))
    angles = positions.astype(F32)[:, None] * freqs[None, :]
    cosine, sine = jnp.cos(angles), jnp.sin(angles)
    zero = jnp.zeros_like(sine)
    heads = width // HEAD_DIM
    return (
        jnp.tile(cosine, (1, 2 * heads)),
        jnp.tile(jnp.concatenate([-sine, zero], axis=1), (1, heads)),
        jnp.tile(jnp.concatenate([zero, sine], axis=1), (1, heads)),
    )


def local(
    inputs,
    query_weight,
    key_weight,
    value_weight,
    out_weight,
    gate_weight,
    up_weight,
    down_weight,
    first_gain,
    second_gain,
    segment_ids,
    positions,
    out_grad,
):
    rows = lax.axis_size("row")
    cols = lax.axis_size("col")
    places = cols // 2
    row = lax.axis_index("row")
    col = lax.axis_index("col")
    core = col % 2
    place = col // 2
    tokens, feat = inputs.shape
    width = feat * cols
    half = width // 2
    quarter = tokens // places

    def core_swap(a):
        return lax.ppermute(a, "col", [(i, i ^ 1) for i in range(cols)])

    def plane_swap(a, step):
        return lax.ppermute(a, "col", [(i, i ^ (2 * step)) for i in range(cols)])

    def token_part(a, step):
        return lax.dynamic_slice_in_dim(a, (place ^ step) * quarter, quarter, 0)

    def feat_part(a, step):
        return lax.dynamic_slice_in_dim(a, (place ^ step) * feat, feat, 1)

    def own_first(w):
        return jnp.concatenate(
            [jnp.where(core == 0, w[:feat], w[feat:]), jnp.where(core == 0, w[feat:], w[:feat])], axis=0
        )

    def row_swap(a, step):
        return lax.ppermute(a, "row", [(i, i ^ step) for i in range(rows)])

    def gather_row(a):
        got, bit = {0: a}, rows // 2
        while bit:
            for step in list(got):
                got[step ^ bit] = row_swap(got[step], bit)
            bit //= 2
        return [got[step] for step in range(rows)]

    def reduce_row_traced(parts):
        parts, sends, bit = list(parts), [], 1
        while bit < rows:
            for at in range(rows - 2 * bit, -1, -2 * bit):
                low = parts[at + bit].astype(BF16)
                sends.append(low)
                parts[at] = parts[at].astype(F32) + row_swap(low, bit).astype(F32)
            bit *= 2
        return parts[0], sends

    def row_part(a, step):
        size = a.shape[0] // rows
        return lax.dynamic_slice_in_dim(a, (row ^ step) * size, size, 0)

    def after(value, *others):
        return lax.optimization_barrier((value,) + others)[0]

    def put_rows(pieces):
        whole = jnp.zeros((tokens,) + pieces[0].shape[1:], pieces[0].dtype)
        for step, piece in enumerate(pieces):
            whole = lax.dynamic_update_slice_in_dim(whole, piece, (place ^ step) * quarter, 0)
        return whole

    def put_feats(pieces):
        whole = jnp.zeros((pieces[0].shape[0], half), pieces[0].dtype)
        for step, piece in enumerate(pieces):
            whole = lax.dynamic_update_slice_in_dim(whole, piece, (place ^ step) * feat, 1)
        return whole

    def spread(a):
        return [a] + [plane_swap(a, step) for step in range(1, places)]

    groups = [[2 * i + k for i in range(places)] for k in range(2)]

    def plane_exchange(a):
        return lax.all_to_all(
            a, "col", split_axis=0, concat_axis=0, axis_index_groups=groups, tiled=True
        )

    def to_parts(a):
        a = plane_exchange(a.reshape(places, quarter, feat))
        return jnp.concatenate([a[s] for s in range(places)], axis=1)

    def to_home(a):
        a = jnp.stack([a[:, s * feat : (s + 1) * feat] for s in range(places)])
        return plane_exchange(a).reshape(tokens, feat)

    def sum_cols(a):
        step = 1
        while step < cols:
            a = a + lax.ppermute(a, "col", [(i, i ^ step) for i in range(cols)])
            step *= 2
        return a

    gain_one = first_gain.astype(F32)[:, None]
    gain_two = second_gain.astype(F32)[:, None]

    def scaled(w, gain):
        return own_first((w.astype(F32) * gain).astype(BF16))

    def exchange(w):
        part = w.shape[1] // rows
        pieces = jnp.stack([w[:, s * part : (s + 1) * part] for s in range(rows)])
        return lax.all_to_all(pieces, "row", split_axis=0, concat_axis=0, tiled=True).reshape(width, part)

    def spread_weights(whole):
        if places != 4:
            return spread(whole)
        first, second = plane_swap(whole, 1), plane_swap(whole, 2)
        return [
            whole,
            first,
            second,
            jnp.concatenate([plane_swap(second[:half], 1), plane_swap(first[half:], 2)], axis=0),
        ]

    def plane_sum(pieces, *hold):
        if places != 4:
            total = pieces[0].astype(F32)
            for s in range(1, places):
                total = total + plane_swap(pieces[s], s).astype(F32)
            return total.astype(BF16)
        top, bottom = plane_swap(pieces[3][:half], 1), plane_swap(pieces[3][half:], 2)
        top, bottom = after(top, *hold), after(bottom, *hold)
        to_second = jnp.concatenate(
            [(pieces[2][:half].astype(F32) + top.astype(F32)).astype(BF16), pieces[2][half:]], axis=0
        )
        to_first = jnp.concatenate(
            [pieces[1][:half], (pieces[1][half:].astype(F32) + bottom.astype(F32)).astype(BF16)], axis=0
        )
        total = (
            pieces[0].astype(F32)
            + plane_swap(to_first, 1).astype(F32)
            + plane_swap(to_second, 2).astype(F32)
        )
        return total.astype(BF16)

    def give_back(total):
        total = total.reshape(rows, 2 * feat, total.shape[1])
        return lax.all_to_all(total, "row", split_axis=0, concat_axis=0, tiled=True)

    starts = jnp.stack([row ^ s for s in range(rows)])
    cores = core.reshape(1)
    ones = jnp.ones((2 * feat, 1), F32)

    with jax.named_scope("gather_qkv"):
        qkv_full = lax.all_gather(
            jnp.concatenate(
                [scaled(w, gain_one) for w in (query_weight, key_weight, value_weight)], axis=1
            ),
            "row",
            axis=0,
            tiled=True,
        )
        out_full = lax.all_gather(own_first(out_weight), "row", axis=0, tiled=True)
    with jax.named_scope("grad_plane"):
        g_part = to_parts(out_grad)
    with jax.named_scope("gate_row"):
        gate_whole = exchange(after(scaled(gate_weight, gain_two), g_part))
    with jax.named_scope("up_row"):
        up_whole = exchange(after(scaled(up_weight, gain_two), gate_whole))
    with jax.named_scope("down_row"):
        down_whole = exchange(after(own_first(down_weight), up_whole))
    with jax.named_scope("grad_row"):
        g_own = lax.all_gather(after(g_part, out_full), "row", axis=0, tiled=True)
        g_other = core_swap(g_own)
    with jax.named_scope("gate_plane"):
        gates = spread_weights(gate_whole)
    with jax.named_scope("up_plane"):
        ups = spread_weights(up_whole)

    with jax.named_scope("inputs"):
        x_own = put_feats(spread(inputs))
        x_other = core_swap(x_own)
    heads_width = query_weight.shape[1]
    cosine, front, back = rope_tables(positions, heads_width)
    start_row = jnp.sum(
        (segment_ids[None, :] < segment_ids[:, None]).astype(jnp.int32), axis=1
    )[None, :]
    x_ready = after(x_own, gates[1], gates[2], up_whole)
    query, key, value, scale_one = project(feat, x_ready, x_other, qkv_full, cosine, front, back)
    mixed, logs = attend(query, key, value, start_row)
    mixed = after(mixed, gates[3], ups[1], ups[2], down_whole)

    def scatter_parts(own, other):
        low = (own.astype(F32) + core_swap(other).astype(F32)).astype(BF16)
        total = token_part(low, 0).astype(F32)
        for s in range(1, places):
            total = total + plane_swap(token_part(low, s), s).astype(F32)
        return total

    with jax.named_scope("mix_plane"):
        middle = token_part(x_own, 0).astype(F32) + scatter_parts(*unfold(feat, "mix", [mixed], [out_full]))
    square = jnp.sum(middle * middle, axis=1, keepdims=True)
    square = square + core_swap(square)
    scale_mid = lax.rsqrt(square / width + EPS)

    with jax.named_scope("down_plane"):
        downs = spread_weights(after(down_whole, middle))
    with jax.named_scope("middle_row"):
        m_list = gather_row(after(middle.astype(BF16), ups[3]))
        m_others = [core_swap(m) for m in m_list]
    found, own_shares, other_shares = [], [], []
    for at in range(0, rows, 2):
        pick = slice(at, at + 2)
        *three, owns, others = units(
            feat, starts[pick], m_list[pick], m_others[pick], g_own, g_other, gates, ups, downs
        )
        found.append(three)
        own_shares += owns
        other_shares += others
    with jax.named_scope("unit_grad"):
        unit_grad, sums = reduce_row_traced(
            [own.astype(F32) + core_swap(other).astype(F32) for own, other in zip(own_shares, other_shares)]
        )
    with jax.named_scope("down_grad"):
        down_total = plane_sum(
            outer(feat, "down_outer", starts, [g_own], [g_other], [after(f[0], *sums[:2]) for f in found], places)
        )
        down_blocks = give_back(down_total)

    unit_mid = middle * scale_mid
    dot_two = jnp.sum(unit_grad * unit_mid, axis=1, keepdims=True)
    dot_two = dot_two + core_swap(dot_two)
    middle_grad = g_part.astype(F32) + scale_mid * (unit_grad - unit_mid * (dot_two / width))

    with jax.named_scope("middle_grad"):
        d_low = middle_grad.astype(BF16)
        d_own = put_rows(spread(d_low))
        d_other = core_swap(d_own)
    with jax.named_scope("feed"):
        shares = []
        for hidden, _, _ in found:
            own, other = unfold(feat, "feed", [after(hidden, d_low)], downs)
            low = own.astype(F32) + core_swap(other).astype(F32)
            shares += [low[:quarter], low[quarter:]]
        feed, _ = reduce_row_traced(shares)
    gate_parts = outer(feat, "gate_outer", starts, m_list, m_others, [after(f[1], d_low) for f in found], places)
    up_parts = outer(feat, "up_outer", starts, m_list, m_others, [after(f[2], d_low) for f in found], places)
    mixed_grad = fold(feat, after(d_own, gate_parts[0], up_parts[0]), d_other, out_full)
    with jax.named_scope("gate_grad"):
        gate_total = plane_sum([after(a, d_own) for a in gate_parts], mixed_grad)
        gate_blocks = give_back(gate_total)
    query_grad, key_grad, value_grad = attend_back(
        query, key, value, mixed, mixed_grad, start_row, logs, cosine, front, back
    )
    heads_part, gain_dots = heads_outer(
        feat, x_own, x_other, d_own, d_other, query_grad, key_grad, value_grad, mixed, scale_one, qkv_full
    )
    with jax.named_scope("heads_grad"):
        heads_blocks = lax.psum_scatter(heads_part, "row", scatter_dimension=0, tiled=True)
    with jax.named_scope("up_grad"):
        up_total = plane_sum([after(a, gate_total) for a in up_parts], heads_part)
        up_blocks = give_back(up_total)
    with jax.named_scope("block_out"):
        block_out = to_home(after((middle + feed).astype(BF16), heads_part))
    with jax.named_scope("first_plane"):
        first_unit_grad = scatter_parts(
            *unfold(feat, "first_grad", [after(query_grad, heads_part), key_grad, value_grad], [qkv_full])
        )
    scale_first = token_part(scale_one, 0)
    unit_first = token_part(x_own, 0).astype(F32) * scale_first
    dot_one = jnp.sum(first_unit_grad * unit_first, axis=1, keepdims=True)
    dot_one = dot_one + core_swap(dot_one)
    with jax.named_scope("input_grad"):
        input_grad = to_home(
            (middle_grad + scale_first * (first_unit_grad - unit_first * (dot_one / width))).astype(BF16)
        )

    def row_dots(w, d):
        return jnp.sum(w.astype(F32) * d.astype(F32), axis=1)

    with jax.named_scope("gains"):
        dots = jnp.stack(
            [gain_dots[:, 0], row_dots(gates[0], gate_total) + row_dots(ups[0], up_total)]
        ).reshape(2, rows, 2, feat)
        dots = sum_cols(jnp.where(core == 0, dots, dots[:, :, ::-1])).transpose(1, 0, 2, 3)
        dots = dots.reshape(rows, 2, 2 * feat)
        mine = lax.dynamic_index_in_dim(dots, row, 0, False)
        for s in range(1, rows):
            mine = mine + row_swap(lax.dynamic_index_in_dim(dots, row ^ s, 0, False), s)
        first_gain_grad = mine[0] / gain_one[:, 0]
        second_gain_grad = mine[1] / gain_two[:, 0]
    (down_weight_grad,) = finish(cores, down_blocks, ones)
    (gate_weight_grad,) = finish(cores, gate_blocks, gain_two)
    (up_weight_grad,) = finish(cores, up_blocks, gain_two)
    part = query_weight.shape[1]
    (qkv_grad,) = finish(cores, heads_blocks[None, :, : 3 * part], gain_one)
    (out_weight_grad,) = finish(cores, heads_blocks[None, :, 3 * part :], ones)
    return (
        block_out,
        input_grad,
        qkv_grad[:, :part],
        qkv_grad[:, part : 2 * part],
        qkv_grad[:, 2 * part :],
        out_weight_grad,
        gate_weight_grad,
        up_weight_grad,
        down_weight_grad,
        first_gain_grad,
        second_gain_grad,
    )


def solution(mesh):
    grid, line = P("row", "col"), P("row")
    return jax.shard_map(
        local,
        mesh=mesh,
        in_specs=(grid,) * 8 + (line,) * 4 + (grid,),
        out_specs=(grid,) * 9 + (line,) * 2,
        check_vma=False,
    )
```

```python
import functools
import math

import jax
import jax.numpy as jnp
from jax import lax
from jax.experimental import pallas as pl
from jax.experimental.pallas import tpu as pltpu
from jax.sharding import PartitionSpec as P

HEAD_DIM = 64
LANES = 128
EPS = 1e-05
ROPE_BASE = 130000.0
LOG2E = math.log2(math.e)
SCORE_SCALE = HEAD_DIM**-0.5
BF16 = jnp.bfloat16
F32 = jnp.float32
VMEM_BYTES = 56 * 1024 * 1024


def nn(left, right):
    return lax.dot_general(left, right, (((1,), (0,)), ((), ())), preferred_element_type=F32)


def nt(left, right):
    return lax.dot_general(left, right, (((1,), (1,)), ((), ())), preferred_element_type=F32)


def tn(left, right):
    return lax.dot_general(left, right, (((0,), (0,)), ((), ())), preferred_element_type=F32)


def spin(values, cosine, sine_front, sine_back):
    half = HEAD_DIM // 2
    lanes = values.shape[-1]
    return (
        values * cosine
        + pltpu.roll(values, lanes - half, 1) * sine_front
        + pltpu.roll(values, half, 1) * sine_back
    )


def weave(own, other, feat):
    pieces = []
    for at in range(0, own.shape[1], feat):
        pieces += [own[:, at : at + feat], other[:, at : at + feat]]
    return jnp.concatenate(pieces, axis=1)


def norm_scale(values):
    wide = values.astype(F32)
    return lax.rsqrt(jnp.sum(wide * wide, axis=1, keepdims=True) / values.shape[1] + EPS)


def whole_spec(a):
    return pl.BlockSpec(a.shape, lambda i: (0,) * a.ndim, pipeline_mode=pl.Buffered(1))


def row_spec(block, a):
    return pl.BlockSpec((block, a.shape[1]), lambda i: (i, 0))


def project_kernel(feat, own_ref, other_ref, weight_ref, cos_ref, front_ref, back_ref, q_ref, k_ref, v_ref, scale_ref):
    values = weave(own_ref[...], other_ref[...], feat)
    scale = norm_scale(values)
    scale_ref[...] = scale
    heads = q_ref.shape[1]
    cosine, front, back = cos_ref[...], front_ref[...], back_ref[...]
    for at, ref in enumerate((q_ref, k_ref, v_ref)):
        result = nn(values, weight_ref[:, at * heads : (at + 1) * heads]) * scale
        if at < 2:
            result = spin(result, cosine, front, back)
        ref[...] = result.astype(BF16)


def project(feat, own, other, weight, cosine, front, back):
    tokens = own.shape[0]
    heads = weight.shape[1] // 3
    block = 256
    result = jax.ShapeDtypeStruct((tokens, heads), BF16)
    scale = jax.ShapeDtypeStruct((tokens, 1), F32)
    return pl.pallas_call(
        functools.partial(project_kernel, feat),
        grid=(tokens // block,),
        in_specs=[row_spec(block, own), row_spec(block, other), whole_spec(weight)]
        + [row_spec(block, cosine)] * 3,
        out_specs=[row_spec(block, result)] * 3 + [row_spec(block, scale)],
        out_shape=[result] * 3 + [scale],
        compiler_params=pltpu.CompilerParams(vmem_limit_bytes=VMEM_BYTES),
        name="project",
    )(own, other, weight, cosine, front, back)


def unfold_kernel(feat, joined, *refs):
    own_ref, other_ref = refs[-2:]
    lefts, weights = refs[:joined], refs[joined:-2]
    left = jnp.concatenate([ref[...] for ref in lefts], axis=1)
    part = weights[0].shape[1]
    for at in range(0, own_ref.shape[1], feat):
        rows = slice(2 * at, 2 * (at + feat))
        total = None
        for i, weight in enumerate(weights):
            term = nt(left[:, i * part : (i + 1) * part], weight[rows, :])
            total = term if total is None else total + term
        own_ref[:, at : at + feat] = total[:, :feat].astype(BF16)
        other_ref[:, at : at + feat] = total[:, feat:].astype(BF16)


def unfold(feat, name, lefts, weights):
    tokens, half = lefts[0].shape[0], weights[0].shape[0] // 2
    block = 256
    result = jax.ShapeDtypeStruct((tokens, half), BF16)
    return pl.pallas_call(
        functools.partial(unfold_kernel, feat, len(lefts)),
        grid=(tokens // block,),
        in_specs=[row_spec(block, a) for a in lefts] + [whole_spec(w) for w in weights],
        out_specs=[row_spec(block, result)] * 2,
        out_shape=[result] * 2,
        compiler_params=pltpu.CompilerParams(vmem_limit_bytes=VMEM_BYTES),
        name=name,
    )(*lefts, *weights)


def units_kernel(feat, parts, count, starts, *refs):
    m_owns, m_others = refs[:parts], refs[parts : 2 * parts]
    g_sources = refs[2 * parts : 2 * parts + 2]
    refs = refs[2 * parts + 2 :]
    sources, refs = refs[: 3 * count], refs[3 * count :]
    hidden_ref, gate_ref, up_ref = refs[:3]
    own_refs, other_refs = refs[3 : 3 + parts], refs[3 + parts : 3 + 2 * parts]
    held, arrived, g_held, g_arrived = refs[3 + 2 * parts :]
    tokens = own_refs[0].shape[0]
    copies = [
        pltpu.make_async_copy(source, held.at[at], arrived.at[at]) for at, source in enumerate(sources)
    ]
    g_copies = [
        pltpu.make_async_copy(
            source.at[pl.ds(pl.multiple_of(starts[i] * tokens, tokens), tokens)],
            g_held.at[side, i],
            g_arrived.at[side, i],
        )
        for side, source in enumerate(g_sources)
        for i in range(parts)
    ]
    for copy in copies[:2] + g_copies + copies[2:]:
        copy.start()
    middle = jnp.concatenate(
        [weave(a[...], b[...], feat) for a, b in zip(m_owns, m_others)], axis=0
    )
    scale = norm_scale(middle)
    part = hidden_ref.shape[1] // count
    pairs = []
    grad = None
    for i in range(count):
        columns = slice(i * part, (i + 1) * part)
        copies[3 * i].wait()
        gate = nn(middle, held[3 * i]) * scale
        copies[3 * i + 1].wait()
        up = nn(middle, held[3 * i + 1]) * scale
        copies[3 * i + 2].wait()
        if grad is None:
            for copy in g_copies:
                copy.wait()
            grad = jnp.concatenate(
                [weave(g_held[0, j], g_held[1, j], feat) for j in range(parts)], axis=0
            )
        hidden_grad = nn(grad, held[3 * i + 2])
        sigmoid = 1.0 / (1.0 + jnp.exp(-gate))
        silu = gate * sigmoid
        hidden_ref[:, columns] = (silu * up).astype(BF16)
        gate_grad = hidden_grad * up * (sigmoid + silu * (1.0 - sigmoid))
        up_grad = hidden_grad * silu
        pairs.append((gate_grad.astype(BF16), held.at[3 * i]))
        pairs.append((up_grad.astype(BF16), held.at[3 * i + 1]))
        gate_ref[:, columns] = (gate_grad * scale).astype(BF16)
        up_ref[:, columns] = (up_grad * scale).astype(BF16)
    for at in range(0, own_refs[0].shape[1], feat):
        rows = slice(2 * at, 2 * (at + feat))
        total = None
        for left, weight in pairs:
            term = nt(left, weight[rows, :])
            total = term if total is None else total + term
        for i, (own_ref, other_ref) in enumerate(zip(own_refs, other_refs)):
            mine = total[i * tokens : (i + 1) * tokens]
            own_ref[:, at : at + feat] = mine[:, :feat].astype(BF16)
            other_ref[:, at : at + feat] = mine[:, feat:].astype(BF16)


def units(feat, starts, m_owns, m_others, g_own, g_other, gates, ups, downs):
    parts = len(m_owns)
    tokens, half = m_owns[0].shape
    count, part = len(gates), gates[0].shape[1]
    hidden = jax.ShapeDtypeStruct((parts * tokens, count * part), BF16)
    share = jax.ShapeDtypeStruct((tokens, half), BF16)
    weights = [w for three in zip(gates, ups, downs) for w in three]
    vmem, anywhere = pl.BlockSpec(memory_space=pltpu.VMEM), pl.BlockSpec(memory_space=pl.ANY)
    result = pl.pallas_call(
        functools.partial(units_kernel, feat, parts, count),
        in_specs=[pl.BlockSpec(memory_space=pltpu.SMEM)]
        + [vmem] * (2 * parts)
        + [anywhere] * (2 + len(weights)),
        out_specs=[vmem] * (3 + 2 * parts),
        out_shape=[hidden] * 3 + [share] * (2 * parts),
        scratch_shapes=[
            pltpu.VMEM((len(weights),) + weights[0].shape, BF16),
            pltpu.SemaphoreType.DMA((len(weights),)),
            pltpu.VMEM((2, parts, tokens, half), BF16),
            pltpu.SemaphoreType.DMA((2, parts)),
        ],
        compiler_params=pltpu.CompilerParams(vmem_limit_bytes=48 * 1024 * 1024),
        name="units",
    )(starts, *m_owns, *m_others, g_own, g_other, *weights)
    return result[0], result[1], result[2], result[3 : 3 + parts], result[3 + parts :]


def outer_kernel(groups, count, starts, *refs):
    owns, others, rights = refs[:groups], refs[groups : 2 * groups], refs[2 * groups : len(refs) - count]
    outs = refs[len(refs) - count :]
    if groups == 1:
        tokens = owns[0].shape[0] // starts.shape[0]
        picks = [
            pl.ds(pl.multiple_of(starts[i] * tokens, tokens), tokens) for i in range(starts.shape[0])
        ]
        sides = [(owns[0][pick, :], others[0][pick, :]) for pick in picks]
    else:
        sides = [(own[...], other[...]) for own, other in zip(owns, others)]
    left = jnp.concatenate([jnp.concatenate(pair, axis=1) for pair in sides], axis=0)
    part = outs[0].shape[1]
    for i, out in enumerate(outs):
        columns = slice(i * part, (i + 1) * part)
        right = jnp.concatenate([ref[:, columns] for ref in rights], axis=0)
        out[...] = tn(left, right).astype(BF16)


def outer(feat, name, starts, owns, others, rights, count):
    half, columns = owns[0].shape[1], rights[0].shape[1]
    part = columns // count
    side = pl.BlockSpec((owns[0].shape[0], feat), lambda i: (0, i))
    return pl.pallas_call(
        functools.partial(outer_kernel, len(owns), count),
        grid=(half // feat,),
        in_specs=[pl.BlockSpec(memory_space=pltpu.SMEM)]
        + [side] * (2 * len(owns))
        + [whole_spec(a) for a in rights],
        out_specs=[pl.BlockSpec((2 * feat, part), lambda i: (i, 0))] * count,
        out_shape=[jax.ShapeDtypeStruct((2 * half, part), BF16)] * count,
        compiler_params=pltpu.CompilerParams(vmem_limit_bytes=40 * 1024 * 1024),
        name=name,
    )(starts, *owns, *others, *rights)


def heads_outer_kernel(x_own, x_other, d_own, d_other, dq_ref, dk_ref, dv_ref, mixed_ref, scale_ref, weight_ref, out_ref, dot_ref):
    part = mixed_ref.shape[1]
    left = jnp.concatenate([x_own[...], x_other[...]], axis=1)
    dots = None
    for i, ref in enumerate((dq_ref, dk_ref, dv_ref)):
        columns = slice(i * part, (i + 1) * part)
        result = tn(left, (ref[...].astype(F32) * scale_ref[...]).astype(BF16))
        out_ref[:, columns] = result.astype(BF16)
        term = jnp.sum(result * weight_ref[:, columns].astype(F32), axis=1, keepdims=True)
        dots = term if dots is None else dots + term
    dot_ref[...] = dots
    left = jnp.concatenate([d_own[...], d_other[...]], axis=1)
    out_ref[:, 3 * part :] = tn(left, mixed_ref[...]).astype(BF16)


def heads_outer(feat, x_own, x_other, d_own, d_other, dq, dk, dv, mixed, scale, weight):
    tokens, half = x_own.shape
    part = mixed.shape[1]
    side = pl.BlockSpec((tokens, feat), lambda i: (0, i))
    return pl.pallas_call(
        heads_outer_kernel,
        grid=(half // feat,),
        in_specs=[side] * 4
        + [whole_spec(a) for a in (dq, dk, dv, mixed, scale)]
        + [row_spec(2 * feat, weight)],
        out_specs=[pl.BlockSpec((2 * feat, 4 * part), lambda i: (i, 0)), pl.BlockSpec((2 * feat, 1), lambda i: (i, 0))],
        out_shape=[
            jax.ShapeDtypeStruct((2 * half, 4 * part), BF16),
            jax.ShapeDtypeStruct((2 * half, 1), F32),
        ],
        compiler_params=pltpu.CompilerParams(vmem_limit_bytes=40 * 1024 * 1024),
        name="heads_outer",
    )(x_own, x_other, d_own, d_other, dq, dk, dv, mixed, scale, weight)


def finish_kernel(scaled, core_ref, part_ref, gain_ref, *outs):
    feat = gain_ref.shape[0] // 2
    blocks, columns = part_ref.shape[0], part_ref.shape[2] // len(outs)
    for side in range(2):
        rows = slice(side * feat, (side + 1) * feat)
        start = pl.multiple_of(lax.rem(core_ref[0] + side, 2) * feat, feat)
        gain = gain_ref[rows, :]
        for block in range(blocks):
            for i, out in enumerate(outs):
                value = part_ref[block, pl.ds(start, feat), i * columns : (i + 1) * columns].astype(F32)
                at = block * columns
                out[rows, at : at + columns] = value * gain if i < scaled else value


def finish(core, part, gain, scaled, count=1):
    blocks, rows, columns = part.shape
    vmem = pl.BlockSpec(memory_space=pltpu.VMEM)
    result = jax.ShapeDtypeStruct((rows, blocks * columns // count), F32)
    return pl.pallas_call(
        functools.partial(finish_kernel, scaled),
        in_specs=[pl.BlockSpec(memory_space=pltpu.SMEM), vmem, vmem],
        out_specs=[vmem] * count,
        out_shape=[result] * count,
        compiler_params=pltpu.CompilerParams(vmem_limit_bytes=VMEM_BYTES),
        name="finish",
    )(core, part, gain)


def fold_kernel(feat, own_ref, other_ref, weight_ref, out_ref):
    out_ref[...] = nn(weave(own_ref[...], other_ref[...], feat), weight_ref[...]).astype(BF16)


def fold(feat, own, other, weight):
    tokens = own.shape[0]
    block = 256
    result = jax.ShapeDtypeStruct((tokens, weight.shape[1]), BF16)
    return pl.pallas_call(
        functools.partial(fold_kernel, feat),
        grid=(tokens // block,),
        in_specs=[row_spec(block, own), row_spec(block, other), whole_spec(weight)],
        out_specs=row_spec(block, result),
        out_shape=result,
        compiler_params=pltpu.CompilerParams(vmem_limit_bytes=40 * 1024 * 1024),
        name="fold",
    )(own, other, weight)


def allowed_block(start_row, key_base, query_base, keys, queries):
    key_index = key_base + lax.broadcasted_iota(jnp.int32, (keys, queries), 0)
    query_index = query_base + lax.broadcasted_iota(jnp.int32, (keys, queries), 1)
    return (key_index >= start_row) & (key_index <= query_index)


def attend_kernel(q_ref, k_ref, v_ref, start_ref, out_ref, log_ref):
    tokens = q_ref.shape[0]
    block = 256
    keys_all = k_ref[...]
    values_turned = v_ref[...].T
    lane = lax.broadcasted_iota(jnp.int32, (1, LANES), 1)
    sub = lax.broadcasted_iota(jnp.int32, (LANES, 1), 0)
    for place in range(tokens // block):
        rows = slice(place * block, (place + 1) * block)
        reach = (place + 1) * block
        query = q_ref[rows, :]
        start_row = start_ref[:, rows]
        allowed = allowed_block(start_row, 0, place * block, reach, block)
        parts = []
        for head in range(LANES // HEAD_DIM):
            mine = lane // HEAD_DIM == head
            query_head = query * mine.astype(BF16)
            scores = nt(keys_all[:reach], query_head) * (SCORE_SCALE * LOG2E)
            scores = jnp.where(allowed, scores, -1e30)
            peak = jnp.max(scores, axis=0, keepdims=True)
            raised = jnp.exp2(scores - peak)
            total = jnp.sum(raised, axis=0, keepdims=True)
            mixed = nn(values_turned[:, :reach], raised.astype(BF16)) / total
            parts.append(mixed)
            log_ref[0, head : head + 1, rows] = peak + jnp.log2(total)
        joined = jnp.where(sub // HEAD_DIM == 0, parts[0], parts[1])
        out_ref[rows, :] = joined.T.astype(BF16)


def attend(query, key, value, start_row):
    tokens, width = query.shape
    pairs = width // LANES
    column = pl.BlockSpec((tokens, LANES), lambda i: (0, i))
    return pl.pallas_call(
        attend_kernel,
        grid=(pairs,),
        in_specs=[column, column, column, pl.BlockSpec((1, tokens), lambda i: (0, 0))],
        out_specs=[column, pl.BlockSpec((1, 2, tokens), lambda i: (i, 0, 0))],
        out_shape=[
            jax.ShapeDtypeStruct((tokens, width), BF16),
            jax.ShapeDtypeStruct((pairs, 2, tokens), F32),
        ],
        compiler_params=pltpu.CompilerParams(vmem_limit_bytes=VMEM_BYTES),
        name="attend",
    )(query, key, value, start_row)


def attend_back_kernel(
    q_ref, k_ref, v_ref, o_ref, do_ref, start_ref, log_ref, cos_ref, front_ref, back_ref,
    dq_ref, dk_ref, dv_ref, dq_acc,
):
    tokens = q_ref.shape[0]
    block = 256
    lane = lax.broadcasted_iota(jnp.int32, (1, LANES), 1)
    sub = lax.broadcasted_iota(jnp.int32, (LANES, 1), 0)
    query_all = q_ref[...]
    grad_all = do_ref[...]
    product = (o_ref[...].astype(F32) * grad_all.astype(F32)).T
    dots = [
        jnp.sum(product[head * HEAD_DIM : (head + 1) * HEAD_DIM], axis=0, keepdims=True)
        for head in range(LANES // HEAD_DIM)
    ]
    dq_acc[...] = jnp.zeros_like(dq_acc)
    for place in range(tokens // block):
        rows = slice(place * block, (place + 1) * block)
        tail = slice(place * block, tokens)
        keys = k_ref[rows, :]
        values = v_ref[rows, :]
        keys_turned = keys.T
        query = query_all[place * block :]
        grad = grad_all[place * block :]
        start_row = start_ref[:, tail]
        allowed = allowed_block(
            start_row, place * block, place * block, block, tokens - place * block
        )
        key_grad = jnp.zeros((block, LANES), F32)
        value_grad = jnp.zeros((block, LANES), F32)
        for head in range(LANES // HEAD_DIM):
            mine = lane // HEAD_DIM == head
            scores = nt(keys * mine.astype(BF16), query) * (SCORE_SCALE * LOG2E)
            weights = jnp.where(allowed, jnp.exp2(scores - log_ref[0, head : head + 1, tail]), 0.0)
            weight_grad = nt(values * mine.astype(BF16), grad)
            score_grad = (weights * (weight_grad - dots[head][:, place * block :])).astype(BF16)
            value_grad = jnp.where(mine, nn(weights.astype(BF16), grad), value_grad)
            key_grad = jnp.where(mine, nn(score_grad, query), key_grad)
            dq_acc[:, tail] += nn(
                keys_turned * (sub // HEAD_DIM == head).astype(BF16), score_grad
            )
        dv_ref[rows, :] = value_grad.astype(BF16)
        dk_ref[rows, :] = spin(
            key_grad * SCORE_SCALE, cos_ref[rows, :], -front_ref[rows, :], -back_ref[rows, :]
        ).astype(BF16)
    dq_ref[...] = spin(
        dq_acc[...].T * SCORE_SCALE, cos_ref[...], -front_ref[...], -back_ref[...]
    ).astype(BF16)


def attend_back(query, key, value, mixed, mixed_grad, start_row, logs, cosine, front, back):
    tokens, width = query.shape
    pairs = width // LANES
    column = pl.BlockSpec((tokens, LANES), lambda i: (0, i))
    table = pl.BlockSpec((tokens, LANES), lambda i: (0, 0))
    return pl.pallas_call(
        attend_back_kernel,
        grid=(pairs,),
        in_specs=[
            column, column, column, column, column,
            pl.BlockSpec((1, tokens), lambda i: (0, 0)),
            pl.BlockSpec((1, 2, tokens), lambda i: (i, 0, 0)),
            table, table, table,
        ],
        out_specs=[column, column, column],
        out_shape=[jax.ShapeDtypeStruct((tokens, width), BF16)] * 3,
        scratch_shapes=[pltpu.VMEM((LANES, tokens), F32)],
        compiler_params=pltpu.CompilerParams(vmem_limit_bytes=VMEM_BYTES),
        name="attend_back",
    )(query, key, value, mixed, mixed_grad, start_row, logs, cosine, front, back)


def rope_tables(positions, width):
    half = HEAD_DIM // 2
    freqs = jnp.exp(jnp.arange(half, dtype=F32) * (-2.0 * math.log(ROPE_BASE) / HEAD_DIM))
    angles = positions.astype(F32)[:, None] * freqs[None, :]
    cosine, sine = jnp.cos(angles), jnp.sin(angles)
    zero = jnp.zeros_like(sine)
    heads = width // HEAD_DIM
    return (
        jnp.tile(cosine, (1, 2 * heads)),
        jnp.tile(jnp.concatenate([-sine, zero], axis=1), (1, heads)),
        jnp.tile(jnp.concatenate([zero, sine], axis=1), (1, heads)),
    )


def local(
    inputs,
    query_weight,
    key_weight,
    value_weight,
    out_weight,
    gate_weight,
    up_weight,
    down_weight,
    first_gain,
    second_gain,
    segment_ids,
    positions,
    out_grad,
):
    rows = lax.axis_size("row")
    cols = lax.axis_size("col")
    places = cols // 2
    row = lax.axis_index("row")
    col = lax.axis_index("col")
    core = col % 2
    place = col // 2
    tokens, feat = inputs.shape
    width = feat * cols
    half = width // 2
    quarter = tokens // places

    def core_swap(a):
        return lax.ppermute(a, "col", [(i, i ^ 1) for i in range(cols)])

    def plane_swap(a, step):
        return lax.ppermute(a, "col", [(i, i ^ (2 * step)) for i in range(cols)])

    def token_part(a, step):
        return lax.dynamic_slice_in_dim(a, (place ^ step) * quarter, quarter, 0)

    def feat_part(a, step):
        return lax.dynamic_slice_in_dim(a, (place ^ step) * feat, feat, 1)

    def own_first(w):
        return jnp.concatenate(
            [jnp.where(core == 0, w[:feat], w[feat:]), jnp.where(core == 0, w[feat:], w[:feat])], axis=0
        )

    def row_swap(a, step):
        return lax.ppermute(a, "row", [(i, i ^ step) for i in range(rows)])

    def gather_row(a):
        got, bit = {0: a}, rows // 2
        while bit:
            for step in list(got):
                got[step ^ bit] = row_swap(got[step], bit)
            bit //= 2
        return [got[step] for step in range(rows)]

    def reduce_row(parts, *works):
        parts, bit, step = list(parts), 1, 0
        while bit < rows:
            lows = {at: parts[at + bit].astype(BF16) for at in range(rows - 2 * bit, -1, -2 * bit)}
            held = works[step](*lows.values()) if step < len(works) else ()
            for at, low in lows.items():
                parts[at] = parts[at].astype(F32) + after(row_swap(low, bit), *held).astype(F32)
            bit, step = 2 * bit, step + 1
        return parts[0]

    def row_part(a, step):
        size = a.shape[0] // rows
        return lax.dynamic_slice_in_dim(a, (row ^ step) * size, size, 0)

    def after(value, *others):
        return lax.optimization_barrier((value,) + others)[0]

    def put_rows(pieces):
        whole = jnp.zeros((tokens,) + pieces[0].shape[1:], pieces[0].dtype)
        for step, piece in enumerate(pieces):
            whole = lax.dynamic_update_slice_in_dim(whole, piece, (place ^ step) * quarter, 0)
        return whole

    def put_feats(pieces):
        whole = jnp.zeros((pieces[0].shape[0], half), pieces[0].dtype)
        for step, piece in enumerate(pieces):
            whole = lax.dynamic_update_slice_in_dim(whole, piece, (place ^ step) * feat, 1)
        return whole

    def spread(a):
        return [a] + [plane_swap(a, step) for step in range(1, places)]

    groups = [[2 * i + k for i in range(places)] for k in range(2)]

    def plane_exchange(a):
        return lax.all_to_all(
            a, "col", split_axis=0, concat_axis=0, axis_index_groups=groups, tiled=True
        )

    def to_parts(a):
        a = plane_exchange(a.reshape(places, quarter, feat))
        return jnp.concatenate([a[s] for s in range(places)], axis=1)

    def to_home(a):
        a = jnp.stack([a[:, s * feat : (s + 1) * feat] for s in range(places)])
        return plane_exchange(a).reshape(tokens, feat)

    def sum_cols(a):
        step = 1
        while step < cols:
            a = a + lax.ppermute(a, "col", [(i, i ^ step) for i in range(cols)])
            step *= 2
        return a

    gain_one = first_gain.astype(F32)[:, None]
    gain_two = second_gain.astype(F32)[:, None]

    def scaled(w, gain):
        return own_first((w.astype(F32) * gain).astype(BF16))

    def exchange(w):
        part = w.shape[1] // rows
        pieces = jnp.stack([w[:, s * part : (s + 1) * part] for s in range(rows)])
        return lax.all_to_all(pieces, "row", split_axis=0, concat_axis=0, tiled=True).reshape(width, part)

    def spread_weights(whole):
        if places != 4:
            return spread(whole)
        first, second = plane_swap(whole, 1), plane_swap(whole, 2)
        return [
            whole,
            first,
            second,
            jnp.concatenate([plane_swap(second[:half], 1), plane_swap(first[half:], 2)], axis=0),
        ]

    def plane_first(pieces):
        if places != 4:
            return pieces
        top, bottom = plane_swap(pieces[3][:half], 1), plane_swap(pieces[3][half:], 2)
        to_second = jnp.concatenate(
            [(pieces[2][:half].astype(F32) + top.astype(F32)).astype(BF16), pieces[2][half:]], axis=0
        )
        to_first = jnp.concatenate(
            [pieces[1][:half], (pieces[1][half:].astype(F32) + bottom.astype(F32)).astype(BF16)], axis=0
        )
        return [pieces[0], to_first, to_second]

    def plane_second(pieces):
        total = pieces[0].astype(F32)
        for s, piece in enumerate(pieces[1:], 1):
            total = total + plane_swap(piece, s).astype(F32)
        return total.astype(BF16)

    def give_back(total):
        total = total.reshape(rows, 2 * feat, total.shape[1])
        return lax.all_to_all(total, "row", split_axis=0, concat_axis=0, tiled=True)

    starts = jnp.stack([row ^ s for s in range(rows)])
    cores = core.reshape(1)

    with jax.named_scope("gather_qkv"):
        qkv_full = lax.all_gather(
            jnp.concatenate(
                [scaled(w, gain_one) for w in (query_weight, key_weight, value_weight)], axis=1
            ),
            "row",
            axis=0,
            tiled=True,
        )
        out_full = lax.all_gather(own_first(out_weight), "row", axis=0, tiled=True)
    with jax.named_scope("inputs"):
        x_own = put_feats(spread(inputs))
        x_other = core_swap(x_own)
    with jax.named_scope("gate_row"):
        gate_whole = exchange(scaled(gate_weight, gain_two))
    with jax.named_scope("grad_plane"):
        g_part = to_parts(after(out_grad, gate_whole))
    with jax.named_scope("up_row"):
        up_whole = exchange(after(scaled(up_weight, gain_two), g_part, x_other, qkv_full))
    with jax.named_scope("down_row"):
        down_whole = exchange(after(own_first(down_weight), up_whole))
    with jax.named_scope("grad_row"):
        g_own = lax.all_gather(after(g_part, out_full), "row", axis=0, tiled=True)
        g_other = core_swap(g_own)
    with jax.named_scope("gate_plane"):
        gates = spread_weights(gate_whole)
    with jax.named_scope("up_plane"):
        ups = spread_weights(up_whole)

    heads_width = query_weight.shape[1]
    cosine, front, back = rope_tables(positions, heads_width)
    start_row = jnp.sum(
        (segment_ids[None, :] < segment_ids[:, None]).astype(jnp.int32), axis=1
    )[None, :]
    x_ready = after(x_own, gates[1], gates[2])
    query, key, value, scale_one = project(feat, x_ready, x_other, qkv_full, cosine, front, back)
    mixed, logs = attend(query, key, value, start_row)
    mixed = after(mixed, gates[3])

    def scatter_parts(own, other):
        low = (own.astype(F32) + core_swap(other).astype(F32)).astype(BF16)
        total = token_part(low, 0).astype(F32)
        for s in range(1, places):
            total = total + plane_swap(token_part(low, s), s).astype(F32)
        return total

    with jax.named_scope("mix_plane"):
        middle = token_part(x_own, 0).astype(F32) + scatter_parts(*unfold(feat, "mix", [mixed], [out_full]))
    square = jnp.sum(middle * middle, axis=1, keepdims=True)
    square = square + core_swap(square)
    scale_mid = lax.rsqrt(square / width + EPS)

    with jax.named_scope("down_plane"):
        downs = spread_weights(after(down_whole, middle))
    with jax.named_scope("middle_row"):
        m_list = gather_row(after(middle.astype(BF16), ups[1], ups[2], down_whole))
        m_others = [core_swap(m) for m in m_list]
    found, own_shares, other_shares = [], [], []
    for at in range(0, rows, 2):
        pick = slice(at, at + 2)
        *three, owns, others = units(
            feat, starts[pick], m_list[pick], m_others[pick], g_own, g_other, gates, ups, downs
        )
        found.append(three)
        own_shares += owns
        other_shares += others
    kept = {}

    def down_work(*lows):
        with jax.named_scope("down_grad"):
            kept["down"] = outer(
                feat, "down_outer", starts, [g_own], [g_other], [after(f[0], *lows) for f in found], places
            )
        return kept["down"][:1]

    def feed_work(*lows):
        with jax.named_scope("feed"):
            kept["feed"] = [unfold(feat, "feed", [after(f[0], *lows)], downs) for f in found]
        return [own for own, _ in kept["feed"]]

    with jax.named_scope("unit_grad"):
        unit_grad = reduce_row(
            [own.astype(F32) + core_swap(other).astype(F32) for own, other in zip(own_shares, other_shares)],
            down_work,
            feed_work,
        )
    with jax.named_scope("down_grad"):
        down_total = plane_second(plane_first(kept["down"]))
        down_blocks = give_back(down_total)

    unit_mid = middle * scale_mid
    dot_two = jnp.sum(unit_grad * unit_mid, axis=1, keepdims=True)
    dot_two = dot_two + core_swap(dot_two)
    middle_grad = g_part.astype(F32) + scale_mid * (unit_grad - unit_mid * (dot_two / width))

    d_low = after(middle_grad.astype(BF16), down_total)
    with jax.named_scope("feed"):
        shares = []
        for own, other in kept["feed"]:
            low = own.astype(F32) + core_swap(other).astype(F32)
            low = after(low.astype(BF16), d_low)
            shares += [low[:quarter], low[quarter:]]
    gate_parts = outer(feat, "gate_outer", starts, m_list, m_others, [after(f[1], d_low) for f in found], places)
    up_parts = outer(feat, "up_outer", starts, m_list, m_others, [after(f[2], d_low) for f in found], places)
    with jax.named_scope("feed"):
        feed_sent = []

        def note(*lows):
            feed_sent.extend(lows)
            return ()

        feed = reduce_row(shares, note, note)
        feed_low = (middle + feed).astype(BF16)
    with jax.named_scope("middle_grad"):
        pieces = spread(d_low)
        d_own = put_rows(
            [pieces[0]] + [after(a, gate_parts[0], up_parts[0], feed_sent[-1]) for a in pieces[1:]]
        )
        d_other = core_swap(d_own)
    mixed_grad = fold(feat, d_own, d_other, out_full)
    with jax.named_scope("gate_grad"):
        gate_middle = plane_first([after(a, d_own) for a in gate_parts])
        gate_total = plane_second(gate_middle)
        gate_blocks = give_back(gate_total)
    query_grad, key_grad, value_grad = attend_back(
        query, key, value, mixed, after(mixed_grad, *gate_middle), start_row, logs, cosine, front, back
    )
    query_grad = after(query_grad, feed_low, down_blocks)
    heads_part, gain_dots = heads_outer(
        feat, x_own, x_other, d_own, d_other, query_grad, key_grad, value_grad, mixed, scale_one, qkv_full
    )
    with jax.named_scope("heads_grad"):
        heads_blocks = lax.psum_scatter(heads_part, "row", scatter_dimension=0, tiled=True)
    with jax.named_scope("up_grad"):
        up_total = plane_second(plane_first([after(a, gate_total, heads_part) for a in up_parts]))
        up_blocks = give_back(up_total)
    with jax.named_scope("block_out"):
        block_out = to_home(after(feed_low, gate_blocks))
    with jax.named_scope("first_plane"):
        first_unit_grad = scatter_parts(
            *unfold(feat, "first_grad", [after(query_grad, heads_part), key_grad, value_grad], [qkv_full])
        )
    scale_first = token_part(scale_one, 0)
    unit_first = token_part(x_own, 0).astype(F32) * scale_first
    dot_one = jnp.sum(first_unit_grad * unit_first, axis=1, keepdims=True)
    dot_one = dot_one + core_swap(dot_one)
    with jax.named_scope("input_grad"):
        input_grad = to_home(
            (middle_grad + scale_first * (first_unit_grad - unit_first * (dot_one / width))).astype(BF16)
        )

    def row_dots(w, d):
        return jnp.sum(w.astype(F32) * d.astype(F32), axis=1)

    with jax.named_scope("gains"):
        dots = jnp.stack(
            [gain_dots[:, 0], row_dots(gates[0], gate_total) + row_dots(ups[0], up_total)]
        ).reshape(2, rows, 2, feat)
        dots = sum_cols(jnp.where(core == 0, dots, dots[:, :, ::-1])).transpose(1, 0, 2, 3)
        dots = dots.reshape(rows, 2, 2 * feat)
        mine = lax.dynamic_index_in_dim(dots, row, 0, False)
        for s in range(1, rows):
            mine = mine + row_swap(lax.dynamic_index_in_dim(dots, row ^ s, 0, False), s)
        first_gain_grad = mine[0] / gain_one[:, 0]
        second_gain_grad = mine[1] / gain_two[:, 0]
    (down_weight_grad,) = finish(cores, down_blocks, gain_two, 0)
    (gate_weight_grad,) = finish(cores, gate_blocks, gain_two, 1)
    (up_weight_grad,) = finish(cores, up_blocks, gain_two, 1)
    heads_blocks = after(
        heads_blocks, down_weight_grad, gate_weight_grad, up_weight_grad, second_gain_grad, input_grad
    )
    query_weight_grad, key_weight_grad, value_weight_grad, out_weight_grad = finish(
        cores, heads_blocks[None], gain_one, 3, 4
    )
    return (
        block_out,
        input_grad,
        query_weight_grad,
        key_weight_grad,
        value_weight_grad,
        out_weight_grad,
        gate_weight_grad,
        up_weight_grad,
        down_weight_grad,
        first_gain_grad,
        second_gain_grad,
    )


def solution(mesh):
    grid, line = P("row", "col"), P("row")
    return jax.shard_map(
        local,
        mesh=mesh,
        in_specs=(grid,) * 8 + (line,) * 4 + (grid,),
        out_specs=(grid,) * 9 + (line,) * 2,
        check_vma=False,
    )
```

```python
import functools
import math

import jax
import jax.numpy as jnp
from jax import lax
from jax.experimental import pallas as pl
from jax.experimental.pallas import tpu as pltpu
from jax.sharding import PartitionSpec as P

HEAD_DIM = 64
LANES = 128
EPS = 1e-05
ROPE_BASE = 130000.0
LOG2E = math.log2(math.e)
SCORE_SCALE = HEAD_DIM**-0.5
BF16 = jnp.bfloat16
F32 = jnp.float32
VMEM_BYTES = 56 * 1024 * 1024


def nn(left, right):
    return lax.dot_general(left, right, (((1,), (0,)), ((), ())), preferred_element_type=F32)


def nt(left, right):
    return lax.dot_general(left, right, (((1,), (1,)), ((), ())), preferred_element_type=F32)


def tn(left, right):
    return lax.dot_general(left, right, (((0,), (0,)), ((), ())), preferred_element_type=F32)


def spin(values, cosine, sine_front, sine_back):
    half = HEAD_DIM // 2
    lanes = values.shape[-1]
    return (
        values * cosine
        + pltpu.roll(values, lanes - half, 1) * sine_front
        + pltpu.roll(values, half, 1) * sine_back
    )


def weave(own, other, feat):
    pieces = []
    for at in range(0, own.shape[1], feat):
        pieces += [own[:, at : at + feat], other[:, at : at + feat]]
    return jnp.concatenate(pieces, axis=1)


def norm_scale(values):
    wide = values.astype(F32)
    return lax.rsqrt(jnp.sum(wide * wide, axis=1, keepdims=True) / values.shape[1] + EPS)


def whole_spec(a):
    return pl.BlockSpec(a.shape, lambda i: (0,) * a.ndim, pipeline_mode=pl.Buffered(1))


def row_spec(block, a):
    return pl.BlockSpec((block, a.shape[1]), lambda i: (i, 0))


def project_kernel(feat, starts, own_ref, other_ref, *refs):
    weights, (cos_ref, front_ref, back_ref), outs = refs[:-7], refs[-7:-4], refs[-4:]
    scale = norm_scale(jnp.concatenate([own_ref[...], other_ref[...]], axis=1))
    outs[3][...] = scale
    heads = outs[0].shape[1]
    picks = [pl.ds(pl.multiple_of(starts[i] * feat, feat), feat) for i in range(len(weights))]
    values = jnp.concatenate([ref[:, pick] for pick in picks for ref in (own_ref, other_ref)], axis=1)
    cosine, front, back = cos_ref[...], front_ref[...], back_ref[...]
    for at, ref in enumerate(outs[:3]):
        columns = slice(at * heads, (at + 1) * heads)
        result = nn(values, jnp.concatenate([w[:, columns] for w in weights], axis=0)) * scale
        if at < 2:
            result = spin(result, cosine, front, back)
        ref[...] = result.astype(BF16)


def project(feat, starts, own, other, weights, cosine, front, back):
    tokens = own.shape[0]
    heads = weights[0].shape[1] // 3
    block = 256
    result = jax.ShapeDtypeStruct((tokens, heads), BF16)
    scale = jax.ShapeDtypeStruct((tokens, 1), F32)
    return pl.pallas_call(
        functools.partial(project_kernel, feat),
        grid=(tokens // block,),
        in_specs=[pl.BlockSpec(memory_space=pltpu.SMEM), row_spec(block, own), row_spec(block, other)]
        + [whole_spec(w) for w in weights]
        + [row_spec(block, cosine)] * 3,
        out_specs=[row_spec(block, result)] * 3 + [row_spec(block, scale)],
        out_shape=[result] * 3 + [scale],
        compiler_params=pltpu.CompilerParams(vmem_limit_bytes=40 * 1024 * 1024),
        name="project",
    )(starts, own, other, *weights, cosine, front, back)


def unfold_kernel(feat, joined, *refs):
    own_ref, other_ref = refs[-2:]
    lefts, weights = refs[:joined], refs[joined:-2]
    left = jnp.concatenate([ref[...] for ref in lefts], axis=1)
    part = weights[0].shape[1]
    for at in range(0, own_ref.shape[1], feat):
        rows = slice(2 * at, 2 * (at + feat))
        total = None
        for i, weight in enumerate(weights):
            term = nt(left[:, i * part : (i + 1) * part], weight[rows, :])
            total = term if total is None else total + term
        own_ref[:, at : at + feat] = total[:, :feat].astype(BF16)
        other_ref[:, at : at + feat] = total[:, feat:].astype(BF16)


def unfold(feat, name, lefts, weights):
    tokens, half = lefts[0].shape[0], weights[0].shape[0] // 2
    block = 256
    result = jax.ShapeDtypeStruct((tokens, half), BF16)
    return pl.pallas_call(
        functools.partial(unfold_kernel, feat, len(lefts)),
        grid=(tokens // block,),
        in_specs=[row_spec(block, a) for a in lefts] + [whole_spec(w) for w in weights],
        out_specs=[row_spec(block, result)] * 2,
        out_shape=[result] * 2,
        compiler_params=pltpu.CompilerParams(vmem_limit_bytes=VMEM_BYTES),
        name=name,
    )(*lefts, *weights)


def activate_kernel(feat, parts, count, *refs):
    m_owns, m_others, refs = refs[:parts], refs[parts : 2 * parts], refs[2 * parts :]
    sources, refs = refs[: 2 * count], refs[2 * count :]
    hidden_ref, gate_ref, up_ref, scale_ref, held, arrived = refs
    copies = [
        pltpu.make_async_copy(source, held.at[at], arrived.at[at]) for at, source in enumerate(sources)
    ]
    for copy in copies:
        copy.start()
    middle = jnp.concatenate(
        [weave(a[...], b[...], feat) for a, b in zip(m_owns, m_others)], axis=0
    )
    scale = norm_scale(middle)
    scale_ref[...] = scale
    part = hidden_ref.shape[1] // count
    for i in range(count):
        if i % 2 == 0:
            for copy in copies[2 * i : 2 * i + 4]:
                copy.wait()
        columns = slice(i * part, (i + 1) * part)
        gate = nn(middle, held[2 * i]) * scale
        up = nn(middle, held[2 * i + 1]) * scale
        sigmoid = 1.0 / (1.0 + jnp.exp(-gate))
        silu = gate * sigmoid
        hidden_ref[:, columns] = (silu * up).astype(BF16)
        gate_ref[:, columns] = (up * (sigmoid + silu * (1.0 - sigmoid))).astype(BF16)
        up_ref[:, columns] = silu.astype(BF16)


def activate(feat, m_owns, m_others, gates, ups):
    parts = len(m_owns)
    tokens = m_owns[0].shape[0]
    count, part = len(gates), gates[0].shape[1]
    hidden = jax.ShapeDtypeStruct((parts * tokens, count * part), BF16)
    weights = [w for two in zip(gates, ups) for w in two]
    vmem, anywhere = pl.BlockSpec(memory_space=pltpu.VMEM), pl.BlockSpec(memory_space=pl.ANY)
    return pl.pallas_call(
        functools.partial(activate_kernel, feat, parts, count),
        in_specs=[vmem] * (2 * parts) + [anywhere] * len(weights),
        out_specs=[vmem] * 4,
        out_shape=[hidden] * 3 + [jax.ShapeDtypeStruct((parts * tokens, 1), F32)],
        scratch_shapes=[
            pltpu.VMEM((len(weights),) + weights[0].shape, BF16),
            pltpu.SemaphoreType.DMA((len(weights),)),
        ],
        compiler_params=pltpu.CompilerParams(vmem_limit_bytes=36 * 1024 * 1024),
        name="activate",
    )(*m_owns, *m_others, *weights)


def units_back_kernel(feat, parts, count, starts, *refs):
    g_sources, (gate_in, up_in, scale_in) = refs[:2], refs[2:5]
    sources, refs = refs[5 : 5 + 3 * count], refs[5 + 3 * count :]
    gate_ref, up_ref, own_ref, other_ref, held, arrived, g_held, g_arrived = refs
    tokens = own_ref.shape[0] // parts
    copies = [
        pltpu.make_async_copy(source, held.at[at], arrived.at[at]) for at, source in enumerate(sources)
    ]
    g_copies = [
        pltpu.make_async_copy(
            source.at[pl.ds(pl.multiple_of(starts[i] * tokens, tokens), tokens)],
            g_held.at[side, i],
            g_arrived.at[side, i],
        )
        for side, source in enumerate(g_sources)
        for i in range(parts)
    ]
    for copy in g_copies + copies:
        copy.start()
    for copy in g_copies + copies[:count]:
        copy.wait()
    grad = jnp.concatenate([weave(g_held[0, j], g_held[1, j], feat) for j in range(parts)], axis=0)
    scale = scale_in[...]
    part = gate_ref.shape[1] // count
    lefts = [], []
    for i in range(count):
        columns = slice(i * part, (i + 1) * part)
        hidden_grad = nn(grad, held[i])
        for side, (slope, out) in enumerate(((gate_in, gate_ref), (up_in, up_ref))):
            value = hidden_grad * slope[:, columns].astype(F32)
            out[:, columns] = (value * scale).astype(BF16)
            lefts[side].append(value.astype(BF16))
    left = jnp.concatenate(lefts[0] + lefts[1], axis=1)
    for copy in copies[count:]:
        copy.wait()
    for at in range(0, own_ref.shape[1], feat):
        rows = slice(2 * at, 2 * (at + feat))
        right = jnp.concatenate([held[i, rows, :] for i in range(count, 3 * count)], axis=1)
        total = nt(left, right)
        own_ref[:, at : at + feat] = total[:, :feat].astype(BF16)
        other_ref[:, at : at + feat] = total[:, feat:].astype(BF16)


def units_back(feat, starts, g_own, g_other, gate, up, scale, gates, ups, downs):
    tokens, half = gate.shape[0], g_own.shape[1]
    parts = starts.shape[0]
    count = len(gates)
    hidden = jax.ShapeDtypeStruct(gate.shape, BF16)
    share = jax.ShapeDtypeStruct((tokens, half), BF16)
    weights = downs + gates + ups
    vmem, anywhere = pl.BlockSpec(memory_space=pltpu.VMEM), pl.BlockSpec(memory_space=pl.ANY)
    return pl.pallas_call(
        functools.partial(units_back_kernel, feat, parts, count),
        in_specs=[pl.BlockSpec(memory_space=pltpu.SMEM)]
        + [anywhere] * 2
        + [vmem] * 3
        + [anywhere] * len(weights),
        out_specs=[vmem] * 4,
        out_shape=[hidden] * 2 + [share] * 2,
        scratch_shapes=[
            pltpu.VMEM((len(weights),) + weights[0].shape, BF16),
            pltpu.SemaphoreType.DMA((len(weights),)),
            pltpu.VMEM((2, parts, tokens // parts, half), BF16),
            pltpu.SemaphoreType.DMA((2, parts)),
        ],
        compiler_params=pltpu.CompilerParams(vmem_limit_bytes=40 * 1024 * 1024),
        name="units_back",
    )(starts, g_own, g_other, gate, up, scale, *weights)


def outer_kernel(groups, count, starts, *refs):
    owns, others, rights = refs[:groups], refs[groups : 2 * groups], refs[2 * groups : len(refs) - count]
    outs = refs[len(refs) - count :]
    if groups == 1:
        tokens = owns[0].shape[0] // starts.shape[0]
        picks = [
            pl.ds(pl.multiple_of(starts[i] * tokens, tokens), tokens) for i in range(starts.shape[0])
        ]
        sides = [(owns[0][pick, :], others[0][pick, :]) for pick in picks]
    else:
        sides = [(own[...], other[...]) for own, other in zip(owns, others)]
    left = jnp.concatenate([jnp.concatenate(pair, axis=1) for pair in sides], axis=0)
    part = outs[0].shape[1]
    for i, out in enumerate(outs):
        columns = slice(i * part, (i + 1) * part)
        right = jnp.concatenate([ref[:, columns] for ref in rights], axis=0)
        out[...] = tn(left, right).astype(BF16)


def outer(feat, name, starts, owns, others, rights, count):
    half, columns = owns[0].shape[1], rights[0].shape[1]
    part = columns // count
    side = pl.BlockSpec((owns[0].shape[0], feat), lambda i: (0, i))
    return pl.pallas_call(
        functools.partial(outer_kernel, len(owns), count),
        grid=(half // feat,),
        in_specs=[pl.BlockSpec(memory_space=pltpu.SMEM)]
        + [side] * (2 * len(owns))
        + [whole_spec(a) for a in rights],
        out_specs=[pl.BlockSpec((2 * feat, part), lambda i: (i, 0))] * count,
        out_shape=[jax.ShapeDtypeStruct((2 * half, part), BF16)] * count,
        compiler_params=pltpu.CompilerParams(vmem_limit_bytes=40 * 1024 * 1024),
        name=name,
    )(starts, *owns, *others, *rights)


def heads_outer_kernel(x_own, x_other, d_own, d_other, dq_ref, dk_ref, dv_ref, mixed_ref, scale_ref, weight_ref, out_ref, dot_ref):
    part = mixed_ref.shape[1]
    left = jnp.concatenate([x_own[...], x_other[...]], axis=1)
    dots = None
    for i, ref in enumerate((dq_ref, dk_ref, dv_ref)):
        columns = slice(i * part, (i + 1) * part)
        result = tn(left, (ref[...].astype(F32) * scale_ref[...]).astype(BF16))
        out_ref[:, columns] = result.astype(BF16)
        term = jnp.sum(result * weight_ref[:, columns].astype(F32), axis=1, keepdims=True)
        dots = term if dots is None else dots + term
    dot_ref[...] = dots
    left = jnp.concatenate([d_own[...], d_other[...]], axis=1)
    out_ref[:, 3 * part :] = tn(left, mixed_ref[...]).astype(BF16)


def heads_outer(feat, x_own, x_other, d_own, d_other, dq, dk, dv, mixed, scale, weight):
    tokens, half = x_own.shape
    part = mixed.shape[1]
    side = pl.BlockSpec((tokens, feat), lambda i: (0, i))
    return pl.pallas_call(
        heads_outer_kernel,
        grid=(half // feat,),
        in_specs=[side] * 4
        + [whole_spec(a) for a in (dq, dk, dv, mixed, scale)]
        + [row_spec(2 * feat, weight)],
        out_specs=[pl.BlockSpec((2 * feat, 4 * part), lambda i: (i, 0)), pl.BlockSpec((2 * feat, 1), lambda i: (i, 0))],
        out_shape=[
            jax.ShapeDtypeStruct((2 * half, 4 * part), BF16),
            jax.ShapeDtypeStruct((2 * half, 1), F32),
        ],
        compiler_params=pltpu.CompilerParams(vmem_limit_bytes=40 * 1024 * 1024),
        name="heads_outer",
    )(x_own, x_other, d_own, d_other, dq, dk, dv, mixed, scale, weight)


def finish_kernel(scaled, core_ref, part_ref, gain_ref, *outs):
    feat = gain_ref.shape[0] // 2
    blocks, columns = part_ref.shape[0], part_ref.shape[2] // len(outs)
    for side in range(2):
        rows = slice(side * feat, (side + 1) * feat)
        start = pl.multiple_of(lax.rem(core_ref[0] + side, 2) * feat, feat)
        gain = gain_ref[rows, :]
        for block in range(blocks):
            for i, out in enumerate(outs):
                value = part_ref[block, pl.ds(start, feat), i * columns : (i + 1) * columns].astype(F32)
                at = block * columns
                out[rows, at : at + columns] = value * gain if i < scaled else value


def finish(core, part, gain, scaled, count=1):
    blocks, rows, columns = part.shape
    vmem = pl.BlockSpec(memory_space=pltpu.VMEM)
    result = jax.ShapeDtypeStruct((rows, blocks * columns // count), F32)
    return pl.pallas_call(
        functools.partial(finish_kernel, scaled),
        in_specs=[pl.BlockSpec(memory_space=pltpu.SMEM), vmem, vmem],
        out_specs=[vmem] * count,
        out_shape=[result] * count,
        compiler_params=pltpu.CompilerParams(vmem_limit_bytes=VMEM_BYTES),
        name="finish",
    )(core, part, gain)


def fold_kernel(feat, own_ref, other_ref, weight_ref, out_ref):
    out_ref[...] = nn(weave(own_ref[...], other_ref[...], feat), weight_ref[...]).astype(BF16)


def fold(feat, own, other, weight):
    tokens = own.shape[0]
    block = 256
    result = jax.ShapeDtypeStruct((tokens, weight.shape[1]), BF16)
    return pl.pallas_call(
        functools.partial(fold_kernel, feat),
        grid=(tokens // block,),
        in_specs=[row_spec(block, own), row_spec(block, other), whole_spec(weight)],
        out_specs=row_spec(block, result),
        out_shape=result,
        compiler_params=pltpu.CompilerParams(vmem_limit_bytes=40 * 1024 * 1024),
        name="fold",
    )(own, other, weight)


def allowed_block(start_row, key_base, query_base, keys, queries):
    key_index = key_base + lax.broadcasted_iota(jnp.int32, (keys, queries), 0)
    query_index = query_base + lax.broadcasted_iota(jnp.int32, (keys, queries), 1)
    return (key_index >= start_row) & (key_index <= query_index)


def attend_kernel(q_ref, k_ref, v_ref, start_ref, out_ref, log_ref):
    tokens = q_ref.shape[0]
    block = 256
    keys_all = k_ref[...]
    values_turned = v_ref[...].T
    lane = lax.broadcasted_iota(jnp.int32, (1, LANES), 1)
    sub = lax.broadcasted_iota(jnp.int32, (LANES, 1), 0)
    for place in range(tokens // block):
        rows = slice(place * block, (place + 1) * block)
        reach = (place + 1) * block
        query = q_ref[rows, :]
        start_row = start_ref[:, rows]
        allowed = allowed_block(start_row, 0, place * block, reach, block)
        parts = []
        for head in range(LANES // HEAD_DIM):
            mine = lane // HEAD_DIM == head
            query_head = query * mine.astype(BF16)
            scores = nt(keys_all[:reach], query_head) * (SCORE_SCALE * LOG2E)
            scores = jnp.where(allowed, scores, -1e30)
            peak = jnp.max(scores, axis=0, keepdims=True)
            raised = jnp.exp2(scores - peak)
            total = jnp.sum(raised, axis=0, keepdims=True)
            mixed = nn(values_turned[:, :reach], raised.astype(BF16)) / total
            parts.append(mixed)
            log_ref[0, head : head + 1, rows] = peak + jnp.log2(total)
        joined = jnp.where(sub // HEAD_DIM == 0, parts[0], parts[1])
        out_ref[rows, :] = joined.T.astype(BF16)


def attend(query, key, value, start_row):
    tokens, width = query.shape
    pairs = width // LANES
    column = pl.BlockSpec((tokens, LANES), lambda i: (0, i))
    return pl.pallas_call(
        attend_kernel,
        grid=(pairs,),
        in_specs=[column, column, column, pl.BlockSpec((1, tokens), lambda i: (0, 0))],
        out_specs=[column, pl.BlockSpec((1, 2, tokens), lambda i: (i, 0, 0))],
        out_shape=[
            jax.ShapeDtypeStruct((tokens, width), BF16),
            jax.ShapeDtypeStruct((pairs, 2, tokens), F32),
        ],
        compiler_params=pltpu.CompilerParams(vmem_limit_bytes=VMEM_BYTES),
        name="attend",
    )(query, key, value, start_row)


def attend_back_kernel(
    q_ref, k_ref, v_ref, o_ref, do_ref, start_ref, log_ref, cos_ref, front_ref, back_ref,
    dq_ref, dk_ref, dv_ref, dq_acc,
):
    tokens = q_ref.shape[0]
    block = 256
    lane = lax.broadcasted_iota(jnp.int32, (1, LANES), 1)
    sub = lax.broadcasted_iota(jnp.int32, (LANES, 1), 0)
    query_all = q_ref[...]
    grad_all = do_ref[...]
    product = (o_ref[...].astype(F32) * grad_all.astype(F32)).T
    dots = [
        jnp.sum(product[head * HEAD_DIM : (head + 1) * HEAD_DIM], axis=0, keepdims=True)
        for head in range(LANES // HEAD_DIM)
    ]
    dq_acc[...] = jnp.zeros_like(dq_acc)
    for place in range(tokens // block):
        rows = slice(place * block, (place + 1) * block)
        tail = slice(place * block, tokens)
        keys = k_ref[rows, :]
        values = v_ref[rows, :]
        keys_turned = keys.T
        query = query_all[place * block :]
        grad = grad_all[place * block :]
        start_row = start_ref[:, tail]
        allowed = allowed_block(
            start_row, place * block, place * block, block, tokens - place * block
        )
        key_grad = jnp.zeros((block, LANES), F32)
        value_grad = jnp.zeros((block, LANES), F32)
        for head in range(LANES // HEAD_DIM):
            mine = lane // HEAD_DIM == head
            scores = nt(keys * mine.astype(BF16), query) * (SCORE_SCALE * LOG2E)
            weights = jnp.where(allowed, jnp.exp2(scores - log_ref[0, head : head + 1, tail]), 0.0)
            weight_grad = nt(values * mine.astype(BF16), grad)
            score_grad = (weights * (weight_grad - dots[head][:, place * block :])).astype(BF16)
            value_grad = jnp.where(mine, nn(weights.astype(BF16), grad), value_grad)
            key_grad = jnp.where(mine, nn(score_grad, query), key_grad)
            dq_acc[:, tail] += nn(
                keys_turned * (sub // HEAD_DIM == head).astype(BF16), score_grad
            )
        dv_ref[rows, :] = value_grad.astype(BF16)
        dk_ref[rows, :] = spin(
            key_grad * SCORE_SCALE, cos_ref[rows, :], -front_ref[rows, :], -back_ref[rows, :]
        ).astype(BF16)
    dq_ref[...] = spin(
        dq_acc[...].T * SCORE_SCALE, cos_ref[...], -front_ref[...], -back_ref[...]
    ).astype(BF16)


def attend_back(query, key, value, mixed, mixed_grad, start_row, logs, cosine, front, back):
    tokens, width = query.shape
    pairs = width // LANES
    column = pl.BlockSpec((tokens, LANES), lambda i: (0, i))
    table = pl.BlockSpec((tokens, LANES), lambda i: (0, 0))
    return pl.pallas_call(
        attend_back_kernel,
        grid=(pairs,),
        in_specs=[
            column, column, column, column, column,
            pl.BlockSpec((1, tokens), lambda i: (0, 0)),
            pl.BlockSpec((1, 2, tokens), lambda i: (i, 0, 0)),
            table, table, table,
        ],
        out_specs=[column, column, column],
        out_shape=[jax.ShapeDtypeStruct((tokens, width), BF16)] * 3,
        scratch_shapes=[pltpu.VMEM((LANES, tokens), F32)],
        compiler_params=pltpu.CompilerParams(vmem_limit_bytes=VMEM_BYTES),
        name="attend_back",
    )(query, key, value, mixed, mixed_grad, start_row, logs, cosine, front, back)


def rope_tables(positions, width):
    half = HEAD_DIM // 2
    freqs = jnp.exp(jnp.arange(half, dtype=F32) * (-2.0 * math.log(ROPE_BASE) / HEAD_DIM))
    angles = positions.astype(F32)[:, None] * freqs[None, :]
    cosine, sine = jnp.cos(angles), jnp.sin(angles)
    zero = jnp.zeros_like(sine)
    heads = width // HEAD_DIM
    return (
        jnp.tile(cosine, (1, 2 * heads)),
        jnp.tile(jnp.concatenate([-sine, zero], axis=1), (1, heads)),
        jnp.tile(jnp.concatenate([zero, sine], axis=1), (1, heads)),
    )


def local(
    inputs,
    query_weight,
    key_weight,
    value_weight,
    out_weight,
    gate_weight,
    up_weight,
    down_weight,
    first_gain,
    second_gain,
    segment_ids,
    positions,
    out_grad,
):
    rows = lax.axis_size("row")
    cols = lax.axis_size("col")
    places = cols // 2
    row = lax.axis_index("row")
    col = lax.axis_index("col")
    core = col % 2
    place = col // 2
    tokens, feat = inputs.shape
    width = feat * cols
    half = width // 2
    quarter = tokens // places

    def core_swap(a):
        return lax.ppermute(a, "col", [(i, i ^ 1) for i in range(cols)])

    def plane_swap(a, step):
        return lax.ppermute(a, "col", [(i, i ^ (2 * step)) for i in range(cols)])

    def token_part(a, step):
        return lax.dynamic_slice_in_dim(a, (place ^ step) * quarter, quarter, 0)

    def feat_part(a, step):
        return lax.dynamic_slice_in_dim(a, (place ^ step) * feat, feat, 1)

    def own_first(w):
        return jnp.concatenate(
            [jnp.where(core == 0, w[:feat], w[feat:]), jnp.where(core == 0, w[feat:], w[:feat])], axis=0
        )

    def row_swap(a, step):
        return lax.ppermute(a, "row", [(i, i ^ step) for i in range(rows)])

    def gather_row(a):
        got, bit = {0: a}, rows // 2
        while bit:
            for step in list(got):
                got[step ^ bit] = row_swap(got[step], bit)
            bit //= 2
        return [got[step] for step in range(rows)]

    def reduce_row(parts, *works, split=False):
        parts, bit, step = list(parts), 1, 0
        while bit < rows:
            lows = {at: parts[at + bit].astype(BF16) for at in range(rows - 2 * bit, -1, -2 * bit)}
            held = works[step](*lows.values()) if step < len(works) else ()
            for at, low in lows.items():
                came = after(row_swap(low, bit), *held)
                if split and 2 * bit == rows:
                    return parts[0], came
                parts[at] = parts[at].astype(F32) + came.astype(F32)
            bit, step = 2 * bit, step + 1
        return parts[0]

    def row_part(a, step):
        size = a.shape[0] // rows
        return lax.dynamic_slice_in_dim(a, (row ^ step) * size, size, 0)

    def after(value, *others):
        return lax.optimization_barrier((value,) + others)[0]

    def put_rows(pieces):
        whole = jnp.zeros((tokens,) + pieces[0].shape[1:], pieces[0].dtype)
        for step, piece in enumerate(pieces):
            whole = lax.dynamic_update_slice_in_dim(whole, piece, (place ^ step) * quarter, 0)
        return whole

    def put_feats(pieces):
        whole = jnp.zeros((pieces[0].shape[0], half), pieces[0].dtype)
        for step, piece in enumerate(pieces):
            whole = lax.dynamic_update_slice_in_dim(whole, piece, (place ^ step) * feat, 1)
        return whole

    def spread(a):
        return [a] + [plane_swap(a, step) for step in range(1, places)]

    groups = [[2 * i + k for i in range(places)] for k in range(2)]

    def plane_exchange(a):
        return lax.all_to_all(
            a, "col", split_axis=0, concat_axis=0, axis_index_groups=groups, tiled=True
        )

    def to_parts(a):
        a = plane_exchange(a.reshape(places, quarter, feat))
        return jnp.concatenate([a[s] for s in range(places)], axis=1)

    def to_home(a):
        a = jnp.stack([a[:, s * feat : (s + 1) * feat] for s in range(places)])
        return plane_exchange(a).reshape(tokens, feat)

    def to_home_swaps(a):
        return put_rows([feat_part(a, 0)] + [plane_swap(feat_part(a, s), s) for s in range(1, places)])

    def sum_cols(a):
        step = 1
        while step < cols:
            a = a + lax.ppermute(a, "col", [(i, i ^ step) for i in range(cols)])
            step *= 2
        return a

    gain_one = first_gain.astype(F32)[:, None]
    gain_two = second_gain.astype(F32)[:, None]

    def scaled(w, gain):
        return own_first((w.astype(F32) * gain).astype(BF16))

    def exchange(w):
        part = w.shape[1] // rows
        pieces = jnp.stack([w[:, s * part : (s + 1) * part] for s in range(rows)])
        return lax.all_to_all(pieces, "row", split_axis=0, concat_axis=0, tiled=True).reshape(width, part)

    def spread_weights(whole):
        if places != 4:
            return spread(whole)
        first, second = plane_swap(whole, 1), plane_swap(whole, 2)
        return [
            whole,
            first,
            second,
            jnp.concatenate([plane_swap(second[:half], 1), plane_swap(first[half:], 2)], axis=0),
        ]

    def plane_first(pieces):
        if places != 4:
            return pieces
        top, bottom = plane_swap(pieces[3][:half], 1), plane_swap(pieces[3][half:], 2)
        to_second = jnp.concatenate(
            [(pieces[2][:half].astype(F32) + top.astype(F32)).astype(BF16), pieces[2][half:]], axis=0
        )
        to_first = jnp.concatenate(
            [pieces[1][:half], (pieces[1][half:].astype(F32) + bottom.astype(F32)).astype(BF16)], axis=0
        )
        return [pieces[0], to_first, to_second]

    def plane_second(pieces):
        total = pieces[0].astype(F32)
        for s, piece in enumerate(pieces[1:], 1):
            total = total + plane_swap(piece, s).astype(F32)
        return total.astype(BF16)

    def give_back(total):
        total = total.reshape(rows, 2 * feat, total.shape[1])
        return lax.all_to_all(total, "row", split_axis=0, concat_axis=0, tiled=True)

    def join_rows(pieces):
        size = pieces[0].shape[0]
        whole = jnp.zeros((rows * size, pieces[0].shape[1]), BF16)
        for step, piece in enumerate(pieces):
            whole = lax.dynamic_update_slice_in_dim(whole, piece, (row ^ step) * size, 0)
        return whole

    starts = jnp.stack([row ^ s for s in range(rows)])
    cores = core.reshape(1)

    with jax.named_scope("qkv_row"):
        qkv_list = gather_row(
            jnp.concatenate(
                [scaled(w, gain_one) for w in (query_weight, key_weight, value_weight)], axis=1
            )
        )
    with jax.named_scope("inputs"):
        x_own = put_feats(spread(inputs))
        x_other = core_swap(x_own)
    with jax.named_scope("gate_row"):
        gate_whole = exchange(scaled(gate_weight, gain_two))
    with jax.named_scope("out_row"):
        out_full = lax.all_gather(
            after(own_first(out_weight), *qkv_list[1:3]), "row", axis=0, tiled=True
        )
    with jax.named_scope("grad_plane"):
        g_part = to_parts(after(out_grad, gate_whole))
    with jax.named_scope("up_row"):
        up_whole = exchange(after(scaled(up_weight, gain_two), g_part, x_other, *qkv_list))
    with jax.named_scope("down_row"):
        down_whole = exchange(after(own_first(down_weight), up_whole))
    with jax.named_scope("gate_plane"):
        gates = spread_weights(gate_whole)
    heads_width = query_weight.shape[1]
    cosine, front, back = rope_tables(positions, heads_width)
    start_row = jnp.sum(
        (segment_ids[None, :] < segment_ids[:, None]).astype(jnp.int32), axis=1
    )[None, :]
    query, key, value, scale_one = project(
        feat, starts, x_own, x_other, qkv_list, cosine, front, back
    )
    qkv_full = join_rows([after(a, query) for a in qkv_list])
    mixed, logs = attend(after(query, gates[1], gates[2]), key, value, start_row)
    mixed = after(mixed, gates[3])

    def scatter_parts(own, other):
        low = (own.astype(F32) + core_swap(other).astype(F32)).astype(BF16)
        total = token_part(low, 0).astype(F32)
        for s in range(1, places):
            total = total + plane_swap(token_part(low, s), s).astype(F32)
        return total

    with jax.named_scope("mix_plane"):
        own, other = unfold(feat, "mix", [mixed], [out_full])
        middle = token_part(x_own, 0).astype(F32) + scatter_parts(after(own, up_whole), other)
        middle = after(middle, down_whole)
    middle_low = middle.astype(BF16)
    with jax.named_scope("middle_row"):
        m_list = gather_row(middle_low)
        m_others = [core_swap(m) for m in m_list]
    with jax.named_scope("up_plane"):
        ups = spread_weights(after(up_whole, middle_low))
    with jax.named_scope("down_plane"):
        downs = spread_weights(after(down_whole, ups[1], ups[2]))
    with jax.named_scope("grad_row"):
        g_own = lax.all_gather(after(g_part, out_full, *m_list[1:3]), "row", axis=0, tiled=True)
        g_other = core_swap(g_own)
    square = jnp.sum(middle * middle, axis=1, keepdims=True)
    square = square + core_swap(square)
    scale_mid = lax.rsqrt(square / width + EPS)

    pairs = [slice(at, at + 2) for at in range(0, rows, 2)]
    found = [activate(feat, m_list[pair], m_others[pair], gates, ups) for pair in pairs]
    hiddens = [f[0] for f in found]
    parts, scaled_grads, held, down_parts = [None] * rows, [None] * len(pairs), (), None
    for at in reversed(range(len(pairs))):
        with jax.named_scope("unit_grad"):
            _, slope_gate, slope_up, scale = found[at]
            gate_grad, up_grad, own, other = units_back(
                feat, starts[pairs[at]], g_own, g_other, after(slope_gate, *held), slope_up, scale, gates, ups, downs
            )
            scaled_grads[at] = gate_grad, up_grad
            low = own.astype(F32) + core_swap(other).astype(F32)
            parts[2 * at], parts[2 * at + 1] = low[:quarter], low[quarter:].astype(BF16)
        if down_parts is None:
            with jax.named_scope("down_grad"):
                down_parts = outer(
                    feat, "down_outer", starts, [g_own], [g_other], [after(h, parts[-1]) for h in hiddens], places
                )
            held = down_parts[:1]
    kept = []

    def feed_work(*lows):
        with jax.named_scope("feed"):
            kept.extend(unfold(feat, "feed", [after(h, *lows)], downs) for h in hiddens)
        return [own for own, _ in kept]

    with jax.named_scope("unit_grad"):
        unit_grad = reduce_row(parts, lambda *lows: (), feed_work)
    with jax.named_scope("down_grad"):
        down_total = plane_second(plane_first(down_parts))
        down_blocks = give_back(down_total)

    unit_mid = middle * scale_mid
    dot_two = jnp.sum(unit_grad * unit_mid, axis=1, keepdims=True)
    dot_two = dot_two + core_swap(dot_two)
    middle_grad = g_part.astype(F32) + scale_mid * (unit_grad - unit_mid * (dot_two / width))

    d_low = after(middle_grad.astype(BF16), down_total)
    with jax.named_scope("feed"):
        shares = []
        for own, other in kept:
            low = own.astype(F32) + core_swap(other).astype(F32)
            low = after(low.astype(BF16), d_low)
            shares += [low[:quarter], low[quarter:]]
    gate_parts = outer(feat, "gate_outer", starts, m_list, m_others, [after(a, d_low) for a, _ in scaled_grads], places)
    up_parts = outer(feat, "up_outer", starts, m_list, m_others, [after(a, d_low) for _, a in scaled_grads], places)
    with jax.named_scope("feed"):
        feed_sent = []

        def note(*lows):
            feed_sent.extend(lows)
            return ()

        feed_first, feed_last = reduce_row(shares, note, split=True)
    with jax.named_scope("middle_grad"):
        pieces = spread(d_low)
        d_own = put_rows(
            [pieces[0]] + [after(a, gate_parts[0], up_parts[0], feed_sent[-1]) for a in pieces[1:]]
        )
        d_other = core_swap(d_own)
    mixed_grad = fold(feat, d_own, d_other, out_full)
    with jax.named_scope("gate_grad"):
        gate_middle = plane_first([after(a, d_own) for a in gate_parts])
        gate_total = plane_second(gate_middle)
        gate_blocks = give_back(gate_total)
    query_grad, key_grad, value_grad = attend_back(
        query, key, value, mixed, after(mixed_grad, *gate_middle), start_row, logs, cosine, front, back
    )
    with jax.named_scope("feed"):
        feed_low = (middle + feed_first.astype(F32) + after(feed_last, query_grad).astype(F32)).astype(BF16)
    query_grad = after(query_grad, down_blocks, gate_total)
    heads_part, gain_dots = heads_outer(
        feat, x_own, x_other, d_own, d_other, query_grad, key_grad, value_grad, mixed, scale_one, qkv_full
    )
    with jax.named_scope("heads_grad"):
        heads_blocks = lax.psum_scatter(heads_part, "row", scatter_dimension=0, tiled=True)
    with jax.named_scope("up_grad"):
        up_total = plane_second(plane_first([after(a, gate_total, heads_part) for a in up_parts]))
        up_blocks = give_back(up_total)
    with jax.named_scope("block_out"):
        block_out = to_home(after(feed_low, gate_blocks))
    with jax.named_scope("first_plane"):
        first_unit_grad = scatter_parts(
            *unfold(feat, "first_grad", [after(query_grad, heads_part), key_grad, value_grad], [qkv_full])
        )
    scale_first = token_part(scale_one, 0)
    unit_first = token_part(x_own, 0).astype(F32) * scale_first
    dot_one = jnp.sum(first_unit_grad * unit_first, axis=1, keepdims=True)
    dot_one = dot_one + core_swap(dot_one)
    with jax.named_scope("input_grad"):
        input_grad = to_home_swaps(
            (middle_grad + scale_first * (first_unit_grad - unit_first * (dot_one / width))).astype(BF16)
        )

    def row_dots(w, d):
        return jnp.sum(w.astype(F32) * d.astype(F32), axis=1)

    with jax.named_scope("gains"):
        dots = jnp.stack(
            [gain_dots[:, 0], row_dots(gates[0], gate_total) + row_dots(ups[0], up_total)]
        ).reshape(2, rows, 2, feat)
        dots = sum_cols(jnp.where(core == 0, dots, dots[:, :, ::-1])).transpose(1, 0, 2, 3)
        dots = dots.reshape(rows, 2, 2 * feat)
        mine = lax.dynamic_index_in_dim(dots, row, 0, False)
        for s in range(1, rows):
            mine = mine + row_swap(lax.dynamic_index_in_dim(dots, row ^ s, 0, False), s)
        first_gain_grad = mine[0] / gain_one[:, 0]
        second_gain_grad = mine[1] / gain_two[:, 0]
    (down_weight_grad,) = finish(cores, down_blocks, gain_two, 0)
    (gate_weight_grad,) = finish(cores, gate_blocks, gain_two, 1)
    (up_weight_grad,) = finish(cores, up_blocks, gain_two, 1)
    heads_blocks = after(
        heads_blocks, down_weight_grad, gate_weight_grad, up_weight_grad, second_gain_grad, input_grad
    )
    query_weight_grad, key_weight_grad, value_weight_grad, out_weight_grad = finish(
        cores, heads_blocks[None], gain_one, 3, 4
    )
    return (
        block_out,
        input_grad,
        query_weight_grad,
        key_weight_grad,
        value_weight_grad,
        out_weight_grad,
        gate_weight_grad,
        up_weight_grad,
        down_weight_grad,
        first_gain_grad,
        second_gain_grad,
    )


def solution(mesh):
    grid, line = P("row", "col"), P("row")
    return jax.shard_map(
        local,
        mesh=mesh,
        in_specs=(grid,) * 8 + (line,) * 4 + (grid,),
        out_specs=(grid,) * 9 + (line,) * 2,
        check_vma=False,
    )
```

```python
import functools
import math

import jax
import jax.numpy as jnp
from jax import lax
from jax.experimental import pallas as pl
from jax.experimental.pallas import tpu as pltpu
from jax.sharding import PartitionSpec as P

HEAD_DIM = 64
LANES = 128
EPS = 1e-05
ROPE_BASE = 130000.0
LOG2E = math.log2(math.e)
SCORE_SCALE = HEAD_DIM**-0.5
BF16 = jnp.bfloat16
F32 = jnp.float32
VMEM_BYTES = 56 * 1024 * 1024


def nn(left, right):
    return lax.dot_general(left, right, (((1,), (0,)), ((), ())), preferred_element_type=F32)


def nt(left, right):
    return lax.dot_general(left, right, (((1,), (1,)), ((), ())), preferred_element_type=F32)


def tn(left, right):
    return lax.dot_general(left, right, (((0,), (0,)), ((), ())), preferred_element_type=F32)


def spin(values, cosine, sine_front, sine_back):
    half = HEAD_DIM // 2
    lanes = values.shape[-1]
    return (
        values * cosine
        + pltpu.roll(values, lanes - half, 1) * sine_front
        + pltpu.roll(values, half, 1) * sine_back
    )


def weave(own, other, feat):
    pieces = []
    for at in range(0, own.shape[1], feat):
        pieces += [own[:, at : at + feat], other[:, at : at + feat]]
    return jnp.concatenate(pieces, axis=1)


def norm_scale(values):
    wide = values.astype(F32)
    return lax.rsqrt(jnp.sum(wide * wide, axis=1, keepdims=True) / values.shape[1] + EPS)


def whole_spec(a):
    return pl.BlockSpec(a.shape, lambda i: (0,) * a.ndim, pipeline_mode=pl.Buffered(1))


def row_spec(block, a):
    return pl.BlockSpec((block, a.shape[1]), lambda i: (i, 0))


def project_kernel(feat, starts, own_ref, other_ref, *refs):
    weights, (cos_ref, front_ref, back_ref), outs = refs[:-7], refs[-7:-4], refs[-4:]
    scale = norm_scale(jnp.concatenate([own_ref[...], other_ref[...]], axis=1))
    outs[3][...] = scale
    heads = outs[0].shape[1]
    picks = [pl.ds(pl.multiple_of(starts[i] * feat, feat), feat) for i in range(len(weights))]
    values = jnp.concatenate([ref[:, pick] for pick in picks for ref in (own_ref, other_ref)], axis=1)
    cosine, front, back = cos_ref[...], front_ref[...], back_ref[...]
    for at, ref in enumerate(outs[:3]):
        columns = slice(at * heads, (at + 1) * heads)
        result = nn(values, jnp.concatenate([w[:, columns] for w in weights], axis=0)) * scale
        if at < 2:
            result = spin(result, cosine, front, back)
        ref[...] = result.astype(BF16)


def project(feat, starts, own, other, weights, cosine, front, back):
    tokens = own.shape[0]
    heads = weights[0].shape[1] // 3
    block = 256
    result = jax.ShapeDtypeStruct((tokens, heads), BF16)
    scale = jax.ShapeDtypeStruct((tokens, 1), F32)
    return pl.pallas_call(
        functools.partial(project_kernel, feat),
        grid=(tokens // block,),
        in_specs=[pl.BlockSpec(memory_space=pltpu.SMEM), row_spec(block, own), row_spec(block, other)]
        + [whole_spec(w) for w in weights]
        + [row_spec(block, cosine)] * 3,
        out_specs=[row_spec(block, result)] * 3 + [row_spec(block, scale)],
        out_shape=[result] * 3 + [scale],
        compiler_params=pltpu.CompilerParams(vmem_limit_bytes=40 * 1024 * 1024),
        name="project",
    )(starts, own, other, *weights, cosine, front, back)


def unfold_kernel(feat, joined, *refs):
    own_ref, other_ref = refs[-2:]
    lefts, weights = refs[:joined], refs[joined:-2]
    left = jnp.concatenate([ref[...] for ref in lefts], axis=1)
    part = weights[0].shape[1]
    for at in range(0, own_ref.shape[1], feat):
        rows = slice(2 * at, 2 * (at + feat))
        total = None
        for i, weight in enumerate(weights):
            term = nt(left[:, i * part : (i + 1) * part], weight[rows, :])
            total = term if total is None else total + term
        own_ref[:, at : at + feat] = total[:, :feat].astype(BF16)
        other_ref[:, at : at + feat] = total[:, feat:].astype(BF16)


def unfold(feat, name, lefts, weights):
    tokens, half = lefts[0].shape[0], weights[0].shape[0] // 2
    block = 256
    result = jax.ShapeDtypeStruct((tokens, half), BF16)
    return pl.pallas_call(
        functools.partial(unfold_kernel, feat, len(lefts)),
        grid=(tokens // block,),
        in_specs=[row_spec(block, a) for a in lefts] + [whole_spec(w) for w in weights],
        out_specs=[row_spec(block, result)] * 2,
        out_shape=[result] * 2,
        compiler_params=pltpu.CompilerParams(vmem_limit_bytes=VMEM_BYTES),
        name=name,
    )(*lefts, *weights)


def activate_kernel(feat, parts, count, *refs):
    m_owns, m_others, refs = refs[:parts], refs[parts : 2 * parts], refs[2 * parts :]
    sources, refs = refs[: 2 * count], refs[2 * count :]
    hidden_ref, gate_ref, up_ref, scale_ref, held, arrived = refs
    copies = [
        pltpu.make_async_copy(source, held.at[at], arrived.at[at]) for at, source in enumerate(sources)
    ]
    for copy in copies:
        copy.start()
    middle = jnp.concatenate(
        [weave(a[...], b[...], feat) for a, b in zip(m_owns, m_others)], axis=0
    )
    scale = norm_scale(middle)
    scale_ref[...] = scale
    part = hidden_ref.shape[1] // count
    for i in range(count):
        if i % 2 == 0:
            for copy in copies[2 * i : 2 * i + 4]:
                copy.wait()
        columns = slice(i * part, (i + 1) * part)
        gate = nn(middle, held[2 * i]) * scale
        up = nn(middle, held[2 * i + 1]) * scale
        sigmoid = 1.0 / (1.0 + jnp.exp(-gate))
        silu = gate * sigmoid
        hidden_ref[:, columns] = (silu * up).astype(BF16)
        gate_ref[:, columns] = (up * (sigmoid + silu * (1.0 - sigmoid))).astype(BF16)
        up_ref[:, columns] = silu.astype(BF16)


def activate(feat, m_owns, m_others, gates, ups):
    parts = len(m_owns)
    tokens = m_owns[0].shape[0]
    count, part = len(gates), gates[0].shape[1]
    hidden = jax.ShapeDtypeStruct((parts * tokens, count * part), BF16)
    weights = [w for two in zip(gates, ups) for w in two]
    vmem, anywhere = pl.BlockSpec(memory_space=pltpu.VMEM), pl.BlockSpec(memory_space=pl.ANY)
    return pl.pallas_call(
        functools.partial(activate_kernel, feat, parts, count),
        in_specs=[vmem] * (2 * parts) + [anywhere] * len(weights),
        out_specs=[vmem] * 4,
        out_shape=[hidden] * 3 + [jax.ShapeDtypeStruct((parts * tokens, 1), F32)],
        scratch_shapes=[
            pltpu.VMEM((len(weights),) + weights[0].shape, BF16),
            pltpu.SemaphoreType.DMA((len(weights),)),
        ],
        compiler_params=pltpu.CompilerParams(vmem_limit_bytes=36 * 1024 * 1024),
        name="activate",
    )(*m_owns, *m_others, *weights)


def units_back_kernel(feat, parts, count, starts, *refs):
    g_sources, (gate_in, up_in, scale_in) = refs[:2], refs[2:5]
    sources, refs = refs[5 : 5 + 3 * count], refs[5 + 3 * count :]
    gate_ref, up_ref, own_ref, other_ref, held, arrived, g_held, g_arrived = refs
    tokens = own_ref.shape[0] // parts
    copies = [
        pltpu.make_async_copy(source, held.at[at], arrived.at[at]) for at, source in enumerate(sources)
    ]
    g_copies = [
        pltpu.make_async_copy(
            source.at[pl.ds(pl.multiple_of(starts[i] * tokens, tokens), tokens)],
            g_held.at[side, i],
            g_arrived.at[side, i],
        )
        for side, source in enumerate(g_sources)
        for i in range(parts)
    ]
    for copy in g_copies + copies:
        copy.start()
    for copy in g_copies + copies[:count]:
        copy.wait()
    grad = jnp.concatenate([weave(g_held[0, j], g_held[1, j], feat) for j in range(parts)], axis=0)
    scale = scale_in[...]
    part = gate_ref.shape[1] // count
    lefts = [], []
    for i in range(count):
        columns = slice(i * part, (i + 1) * part)
        hidden_grad = nn(grad, held[i])
        for side, (slope, out) in enumerate(((gate_in, gate_ref), (up_in, up_ref))):
            value = hidden_grad * slope[:, columns].astype(F32)
            out[:, columns] = (value * scale).astype(BF16)
            lefts[side].append(value.astype(BF16))
    left = jnp.concatenate(lefts[0] + lefts[1], axis=1)
    for copy in copies[count:]:
        copy.wait()
    for at in range(0, own_ref.shape[1], feat):
        rows = slice(2 * at, 2 * (at + feat))
        right = jnp.concatenate([held[i, rows, :] for i in range(count, 3 * count)], axis=1)
        total = nt(left, right)
        own_ref[:, at : at + feat] = total[:, :feat].astype(BF16)
        other_ref[:, at : at + feat] = total[:, feat:].astype(BF16)


def units_back(feat, starts, g_own, g_other, gate, up, scale, gates, ups, downs):
    tokens, half = gate.shape[0], g_own.shape[1]
    parts = starts.shape[0]
    count = len(gates)
    hidden = jax.ShapeDtypeStruct(gate.shape, BF16)
    share = jax.ShapeDtypeStruct((tokens, half), BF16)
    weights = downs + gates + ups
    vmem, anywhere = pl.BlockSpec(memory_space=pltpu.VMEM), pl.BlockSpec(memory_space=pl.ANY)
    return pl.pallas_call(
        functools.partial(units_back_kernel, feat, parts, count),
        in_specs=[pl.BlockSpec(memory_space=pltpu.SMEM)]
        + [anywhere] * 2
        + [vmem] * 3
        + [anywhere] * len(weights),
        out_specs=[vmem] * 4,
        out_shape=[hidden] * 2 + [share] * 2,
        scratch_shapes=[
            pltpu.VMEM((len(weights),) + weights[0].shape, BF16),
            pltpu.SemaphoreType.DMA((len(weights),)),
            pltpu.VMEM((2, parts, tokens // parts, half), BF16),
            pltpu.SemaphoreType.DMA((2, parts)),
        ],
        compiler_params=pltpu.CompilerParams(vmem_limit_bytes=40 * 1024 * 1024),
        name="units_back",
    )(starts, g_own, g_other, gate, up, scale, *weights)


def outer_kernel(groups, count, starts, *refs):
    owns, others, rights = refs[:groups], refs[groups : 2 * groups], refs[2 * groups : len(refs) - count]
    outs = refs[len(refs) - count :]
    if groups == 1:
        tokens = owns[0].shape[0] // starts.shape[0]
        picks = [
            pl.ds(pl.multiple_of(starts[i] * tokens, tokens), tokens) for i in range(starts.shape[0])
        ]
        sides = [(owns[0][pick, :], others[0][pick, :]) for pick in picks]
    else:
        sides = [(own[...], other[...]) for own, other in zip(owns, others)]
    left = jnp.concatenate([jnp.concatenate(pair, axis=1) for pair in sides], axis=0)
    part = outs[0].shape[1]
    for i, out in enumerate(outs):
        columns = slice(i * part, (i + 1) * part)
        right = jnp.concatenate([ref[:, columns] for ref in rights], axis=0)
        out[...] = tn(left, right).astype(BF16)


def outer(feat, name, starts, owns, others, rights, count):
    half, columns = owns[0].shape[1], rights[0].shape[1]
    part = columns // count
    side = pl.BlockSpec((owns[0].shape[0], feat), lambda i: (0, i))
    return pl.pallas_call(
        functools.partial(outer_kernel, len(owns), count),
        grid=(half // feat,),
        in_specs=[pl.BlockSpec(memory_space=pltpu.SMEM)]
        + [side] * (2 * len(owns))
        + [whole_spec(a) for a in rights],
        out_specs=[pl.BlockSpec((2 * feat, part), lambda i: (i, 0))] * count,
        out_shape=[jax.ShapeDtypeStruct((2 * half, part), BF16)] * count,
        compiler_params=pltpu.CompilerParams(vmem_limit_bytes=40 * 1024 * 1024),
        name=name,
    )(starts, *owns, *others, *rights)


def heads_outer_kernel(x_own, x_other, d_own, d_other, dq_ref, dk_ref, dv_ref, mixed_ref, scale_ref, weight_ref, out_ref, dot_ref):
    part = mixed_ref.shape[1]
    left = jnp.concatenate([x_own[...], x_other[...]], axis=1)
    dots = None
    for i, ref in enumerate((dq_ref, dk_ref, dv_ref)):
        columns = slice(i * part, (i + 1) * part)
        result = tn(left, (ref[...].astype(F32) * scale_ref[...]).astype(BF16))
        out_ref[:, columns] = result.astype(BF16)
        term = jnp.sum(result * weight_ref[:, columns].astype(F32), axis=1, keepdims=True)
        dots = term if dots is None else dots + term
    dot_ref[...] = dots
    left = jnp.concatenate([d_own[...], d_other[...]], axis=1)
    out_ref[:, 3 * part :] = tn(left, mixed_ref[...]).astype(BF16)


def heads_outer(feat, x_own, x_other, d_own, d_other, dq, dk, dv, mixed, scale, weight):
    tokens, half = x_own.shape
    part = mixed.shape[1]
    side = pl.BlockSpec((tokens, feat), lambda i: (0, i))
    return pl.pallas_call(
        heads_outer_kernel,
        grid=(half // feat,),
        in_specs=[side] * 4
        + [whole_spec(a) for a in (dq, dk, dv, mixed, scale)]
        + [row_spec(2 * feat, weight)],
        out_specs=[pl.BlockSpec((2 * feat, 4 * part), lambda i: (i, 0)), pl.BlockSpec((2 * feat, 1), lambda i: (i, 0))],
        out_shape=[
            jax.ShapeDtypeStruct((2 * half, 4 * part), BF16),
            jax.ShapeDtypeStruct((2 * half, 1), F32),
        ],
        compiler_params=pltpu.CompilerParams(vmem_limit_bytes=40 * 1024 * 1024),
        name="heads_outer",
    )(x_own, x_other, d_own, d_other, dq, dk, dv, mixed, scale, weight)


def finish_kernel(scaled, core_ref, part_ref, gain_ref, *outs):
    feat = gain_ref.shape[0] // 2
    blocks, columns = part_ref.shape[0], part_ref.shape[2] // len(outs)
    for side in range(2):
        rows = slice(side * feat, (side + 1) * feat)
        start = pl.multiple_of(lax.rem(core_ref[0] + side, 2) * feat, feat)
        gain = gain_ref[rows, :]
        for block in range(blocks):
            for i, out in enumerate(outs):
                value = part_ref[block, pl.ds(start, feat), i * columns : (i + 1) * columns].astype(F32)
                at = block * columns
                out[rows, at : at + columns] = value * gain if i < scaled else value


def finish(core, part, gain, scaled, count=1):
    blocks, rows, columns = part.shape
    vmem = pl.BlockSpec(memory_space=pltpu.VMEM)
    result = jax.ShapeDtypeStruct((rows, blocks * columns // count), F32)
    return pl.pallas_call(
        functools.partial(finish_kernel, scaled),
        in_specs=[pl.BlockSpec(memory_space=pltpu.SMEM), vmem, vmem],
        out_specs=[vmem] * count,
        out_shape=[result] * count,
        compiler_params=pltpu.CompilerParams(vmem_limit_bytes=VMEM_BYTES),
        name="finish",
    )(core, part, gain)


def fold_kernel(feat, own_ref, other_ref, weight_ref, out_ref):
    out_ref[...] = nn(weave(own_ref[...], other_ref[...], feat), weight_ref[...]).astype(BF16)


def fold(feat, own, other, weight):
    tokens = own.shape[0]
    block = 256
    result = jax.ShapeDtypeStruct((tokens, weight.shape[1]), BF16)
    return pl.pallas_call(
        functools.partial(fold_kernel, feat),
        grid=(tokens // block,),
        in_specs=[row_spec(block, own), row_spec(block, other), whole_spec(weight)],
        out_specs=row_spec(block, result),
        out_shape=result,
        compiler_params=pltpu.CompilerParams(vmem_limit_bytes=40 * 1024 * 1024),
        name="fold",
    )(own, other, weight)


def allowed_block(start_row, key_base, query_base, keys, queries):
    key_index = key_base + lax.broadcasted_iota(jnp.int32, (keys, queries), 0)
    query_index = query_base + lax.broadcasted_iota(jnp.int32, (keys, queries), 1)
    return (key_index >= start_row) & (key_index <= query_index)


def attend_kernel(q_ref, k_ref, v_ref, start_ref, out_ref, log_ref):
    tokens = q_ref.shape[0]
    block = 256
    keys_all = k_ref[...]
    values_turned = v_ref[...].T
    lane = lax.broadcasted_iota(jnp.int32, (1, LANES), 1)
    sub = lax.broadcasted_iota(jnp.int32, (LANES, 1), 0)
    for place in range(tokens // block):
        rows = slice(place * block, (place + 1) * block)
        reach = (place + 1) * block
        query = q_ref[rows, :]
        start_row = start_ref[:, rows]
        allowed = allowed_block(start_row, 0, place * block, reach, block)
        parts = []
        for head in range(LANES // HEAD_DIM):
            mine = lane // HEAD_DIM == head
            query_head = query * mine.astype(BF16)
            scores = nt(keys_all[:reach], query_head) * (SCORE_SCALE * LOG2E)
            scores = jnp.where(allowed, scores, -1e30)
            peak = jnp.max(scores, axis=0, keepdims=True)
            raised = jnp.exp2(scores - peak)
            total = jnp.sum(raised, axis=0, keepdims=True)
            mixed = nn(values_turned[:, :reach], raised.astype(BF16)) / total
            parts.append(mixed)
            log_ref[0, head : head + 1, rows] = peak + jnp.log2(total)
        joined = jnp.where(sub // HEAD_DIM == 0, parts[0], parts[1])
        out_ref[rows, :] = joined.T.astype(BF16)


def attend(query, key, value, start_row):
    tokens, width = query.shape
    pairs = width // LANES
    column = pl.BlockSpec((tokens, LANES), lambda i: (0, i))
    return pl.pallas_call(
        attend_kernel,
        grid=(pairs,),
        in_specs=[column, column, column, pl.BlockSpec((1, tokens), lambda i: (0, 0))],
        out_specs=[column, pl.BlockSpec((1, 2, tokens), lambda i: (i, 0, 0))],
        out_shape=[
            jax.ShapeDtypeStruct((tokens, width), BF16),
            jax.ShapeDtypeStruct((pairs, 2, tokens), F32),
        ],
        compiler_params=pltpu.CompilerParams(vmem_limit_bytes=VMEM_BYTES),
        name="attend",
    )(query, key, value, start_row)


def attend_back_kernel(
    q_ref, k_ref, v_ref, o_ref, do_ref, start_ref, log_ref, cos_ref, front_ref, back_ref,
    dq_ref, dk_ref, dv_ref, dq_acc,
):
    tokens = q_ref.shape[0]
    block = 256
    lane = lax.broadcasted_iota(jnp.int32, (1, LANES), 1)
    sub = lax.broadcasted_iota(jnp.int32, (LANES, 1), 0)
    query_all = q_ref[...]
    grad_all = do_ref[...]
    product = (o_ref[...].astype(F32) * grad_all.astype(F32)).T
    dots = [
        jnp.sum(product[head * HEAD_DIM : (head + 1) * HEAD_DIM], axis=0, keepdims=True)
        for head in range(LANES // HEAD_DIM)
    ]
    dq_acc[...] = jnp.zeros_like(dq_acc)
    for place in range(tokens // block):
        rows = slice(place * block, (place + 1) * block)
        tail = slice(place * block, tokens)
        keys = k_ref[rows, :]
        values = v_ref[rows, :]
        keys_turned = keys.T
        query = query_all[place * block :]
        grad = grad_all[place * block :]
        start_row = start_ref[:, tail]
        allowed = allowed_block(
            start_row, place * block, place * block, block, tokens - place * block
        )
        key_grad = jnp.zeros((block, LANES), F32)
        value_grad = jnp.zeros((block, LANES), F32)
        for head in range(LANES // HEAD_DIM):
            mine = lane // HEAD_DIM == head
            scores = nt(keys * mine.astype(BF16), query) * (SCORE_SCALE * LOG2E)
            weights = jnp.where(allowed, jnp.exp2(scores - log_ref[0, head : head + 1, tail]), 0.0)
            weight_grad = nt(values * mine.astype(BF16), grad)
            score_grad = (weights * (weight_grad - dots[head][:, place * block :])).astype(BF16)
            value_grad = jnp.where(mine, nn(weights.astype(BF16), grad), value_grad)
            key_grad = jnp.where(mine, nn(score_grad, query), key_grad)
            dq_acc[:, tail] += nn(
                keys_turned * (sub // HEAD_DIM == head).astype(BF16), score_grad
            )
        dv_ref[rows, :] = value_grad.astype(BF16)
        dk_ref[rows, :] = spin(
            key_grad * SCORE_SCALE, cos_ref[rows, :], -front_ref[rows, :], -back_ref[rows, :]
        ).astype(BF16)
    dq_ref[...] = spin(
        dq_acc[...].T * SCORE_SCALE, cos_ref[...], -front_ref[...], -back_ref[...]
    ).astype(BF16)


def attend_back(query, key, value, mixed, mixed_grad, start_row, logs, cosine, front, back):
    tokens, width = query.shape
    pairs = width // LANES
    column = pl.BlockSpec((tokens, LANES), lambda i: (0, i))
    table = pl.BlockSpec((tokens, LANES), lambda i: (0, 0))
    return pl.pallas_call(
        attend_back_kernel,
        grid=(pairs,),
        in_specs=[
            column, column, column, column, column,
            pl.BlockSpec((1, tokens), lambda i: (0, 0)),
            pl.BlockSpec((1, 2, tokens), lambda i: (i, 0, 0)),
            table, table, table,
        ],
        out_specs=[column, column, column],
        out_shape=[jax.ShapeDtypeStruct((tokens, width), BF16)] * 3,
        scratch_shapes=[pltpu.VMEM((LANES, tokens), F32)],
        compiler_params=pltpu.CompilerParams(vmem_limit_bytes=VMEM_BYTES),
        name="attend_back",
    )(query, key, value, mixed, mixed_grad, start_row, logs, cosine, front, back)


def rope_tables(positions, width):
    half = HEAD_DIM // 2
    freqs = jnp.exp(jnp.arange(half, dtype=F32) * (-2.0 * math.log(ROPE_BASE) / HEAD_DIM))
    angles = positions.astype(F32)[:, None] * freqs[None, :]
    cosine, sine = jnp.cos(angles), jnp.sin(angles)
    zero = jnp.zeros_like(sine)
    heads = width // HEAD_DIM
    return (
        jnp.tile(cosine, (1, 2 * heads)),
        jnp.tile(jnp.concatenate([-sine, zero], axis=1), (1, heads)),
        jnp.tile(jnp.concatenate([zero, sine], axis=1), (1, heads)),
    )


def local(
    inputs,
    query_weight,
    key_weight,
    value_weight,
    out_weight,
    gate_weight,
    up_weight,
    down_weight,
    first_gain,
    second_gain,
    segment_ids,
    positions,
    out_grad,
):
    rows = lax.axis_size("row")
    cols = lax.axis_size("col")
    places = cols // 2
    row = lax.axis_index("row")
    col = lax.axis_index("col")
    core = col % 2
    place = col // 2
    tokens, feat = inputs.shape
    width = feat * cols
    half = width // 2
    quarter = tokens // places

    def core_swap(a):
        return lax.ppermute(a, "col", [(i, i ^ 1) for i in range(cols)])

    def plane_swap(a, step):
        return lax.ppermute(a, "col", [(i, i ^ (2 * step)) for i in range(cols)])

    def token_part(a, step):
        return lax.dynamic_slice_in_dim(a, (place ^ step) * quarter, quarter, 0)

    def feat_part(a, step):
        return lax.dynamic_slice_in_dim(a, (place ^ step) * feat, feat, 1)

    def own_first(w):
        return jnp.concatenate(
            [jnp.where(core == 0, w[:feat], w[feat:]), jnp.where(core == 0, w[feat:], w[:feat])], axis=0
        )

    def row_swap(a, step):
        return lax.ppermute(a, "row", [(i, i ^ step) for i in range(rows)])

    def gather_row(a):
        got, bit = {0: a}, rows // 2
        while bit:
            for step in list(got):
                got[step ^ bit] = row_swap(got[step], bit)
            bit //= 2
        return [got[step] for step in range(rows)]

    def reduce_row(parts, *works, split=False):
        parts, bit, step = list(parts), 1, 0
        while bit < rows:
            lows = {at: parts[at + bit].astype(BF16) for at in range(rows - 2 * bit, -1, -2 * bit)}
            held = works[step](*lows.values()) if step < len(works) else ()
            for at, low in lows.items():
                came = after(row_swap(low, bit), *held)
                if split and 2 * bit == rows:
                    return parts[0], came
                parts[at] = parts[at].astype(F32) + came.astype(F32)
            bit, step = 2 * bit, step + 1
        return parts[0]

    def row_part(a, step):
        size = a.shape[0] // rows
        return lax.dynamic_slice_in_dim(a, (row ^ step) * size, size, 0)

    def after(value, *others):
        return lax.optimization_barrier((value,) + others)[0]

    def put_rows(pieces):
        whole = jnp.zeros((tokens,) + pieces[0].shape[1:], pieces[0].dtype)
        for step, piece in enumerate(pieces):
            whole = lax.dynamic_update_slice_in_dim(whole, piece, (place ^ step) * quarter, 0)
        return whole

    def put_feats(pieces):
        whole = jnp.zeros((pieces[0].shape[0], half), pieces[0].dtype)
        for step, piece in enumerate(pieces):
            whole = lax.dynamic_update_slice_in_dim(whole, piece, (place ^ step) * feat, 1)
        return whole

    def spread(a):
        return [a] + [plane_swap(a, step) for step in range(1, places)]

    groups = [[2 * i + k for i in range(places)] for k in range(2)]

    def plane_exchange(a):
        return lax.all_to_all(
            a, "col", split_axis=0, concat_axis=0, axis_index_groups=groups, tiled=True
        )

    def to_parts(a):
        a = plane_exchange(a.reshape(places, quarter, feat))
        return jnp.concatenate([a[s] for s in range(places)], axis=1)

    def to_home(a):
        a = jnp.stack([a[:, s * feat : (s + 1) * feat] for s in range(places)])
        return plane_exchange(a).reshape(tokens, feat)

    def to_home_swaps(a):
        return put_rows([feat_part(a, 0)] + [plane_swap(feat_part(a, s), s) for s in range(1, places)])

    def sum_cols(a):
        step = 1
        while step < cols:
            a = a + lax.ppermute(a, "col", [(i, i ^ step) for i in range(cols)])
            step *= 2
        return a

    gain_one = first_gain.astype(F32)[:, None]
    gain_two = second_gain.astype(F32)[:, None]

    def scaled(w, gain):
        return own_first((w.astype(F32) * gain).astype(BF16))

    def exchange(w):
        part = w.shape[1] // rows
        pieces = jnp.stack([w[:, s * part : (s + 1) * part] for s in range(rows)])
        return lax.all_to_all(pieces, "row", split_axis=0, concat_axis=0, tiled=True).reshape(width, part)

    def spread_weights(whole):
        if places != 4:
            return spread(whole)
        first, second = plane_swap(whole, 1), plane_swap(whole, 2)
        return [
            whole,
            first,
            second,
            jnp.concatenate([plane_swap(second[:half], 1), plane_swap(first[half:], 2)], axis=0),
        ]

    def plane_first(pieces):
        if places != 4:
            return pieces
        top, bottom = plane_swap(pieces[3][:half], 1), plane_swap(pieces[3][half:], 2)
        to_second = jnp.concatenate(
            [(pieces[2][:half].astype(F32) + top.astype(F32)).astype(BF16), pieces[2][half:]], axis=0
        )
        to_first = jnp.concatenate(
            [pieces[1][:half], (pieces[1][half:].astype(F32) + bottom.astype(F32)).astype(BF16)], axis=0
        )
        return [pieces[0], to_first, to_second]

    def plane_second(pieces, *hold):
        total = pieces[0].astype(F32)
        for s, piece in enumerate(pieces[1:], 1):
            total = total + after(plane_swap(piece, s), *hold).astype(F32)
        return total.astype(BF16)

    def give_back(total):
        total = total.reshape(rows, 2 * feat, total.shape[1])
        return lax.all_to_all(total, "row", split_axis=0, concat_axis=0, tiled=True)

    def join_rows(pieces):
        size = pieces[0].shape[0]
        whole = jnp.zeros((rows * size, pieces[0].shape[1]), BF16)
        for step, piece in enumerate(pieces):
            whole = lax.dynamic_update_slice_in_dim(whole, piece, (row ^ step) * size, 0)
        return whole

    starts = jnp.stack([row ^ s for s in range(rows)])
    cores = core.reshape(1)

    with jax.named_scope("qkv_row"):
        qkv_list = gather_row(
            jnp.concatenate(
                [scaled(w, gain_one) for w in (query_weight, key_weight, value_weight)], axis=1
            )
        )
    with jax.named_scope("inputs"):
        x_own = put_feats(spread(inputs))
        x_other = core_swap(x_own)
    with jax.named_scope("gate_row"):
        gate_whole = exchange(scaled(gate_weight, gain_two))
    with jax.named_scope("out_row"):
        out_full = lax.all_gather(
            after(own_first(out_weight), *qkv_list), "row", axis=0, tiled=True
        )
    with jax.named_scope("grad_plane"):
        g_part = to_parts(after(out_grad, gate_whole))
    with jax.named_scope("up_row"):
        up_whole = exchange(after(scaled(up_weight, gain_two), g_part, x_other, *qkv_list))
    with jax.named_scope("down_row"):
        down_whole = exchange(after(own_first(down_weight), up_whole))
    with jax.named_scope("gate_plane"):
        gates = spread_weights(gate_whole)
    heads_width = query_weight.shape[1]
    cosine, front, back = rope_tables(positions, heads_width)
    start_row = jnp.sum(
        (segment_ids[None, :] < segment_ids[:, None]).astype(jnp.int32), axis=1
    )[None, :]
    query, key, value, scale_one = project(
        feat, starts, x_own, x_other, qkv_list, cosine, front, back
    )
    qkv_full = join_rows([after(a, query) for a in qkv_list])
    mixed, logs = attend(after(query, gates[1], gates[2]), key, value, start_row)
    mixed = after(mixed, gates[3])
    with jax.named_scope("grad_row"):
        g_own = lax.all_gather(after(g_part, out_full), "row", axis=0, tiled=True)

    def scatter_parts(own, other):
        low = (own.astype(F32) + core_swap(other).astype(F32)).astype(BF16)
        total = token_part(low, 0).astype(F32)
        for s in range(1, places):
            total = total + plane_swap(token_part(low, s), s).astype(F32)
        return total

    with jax.named_scope("mix_plane"):
        own, other = unfold(feat, "mix", [mixed], [out_full])
        middle = token_part(x_own, 0).astype(F32) + scatter_parts(after(own, up_whole), other)
        middle = after(middle, down_whole)
    middle_low = middle.astype(BF16)
    with jax.named_scope("middle_row"):
        m_list = gather_row(middle_low)
        m_others = [core_swap(m) for m in m_list]
    with jax.named_scope("up_plane"):
        ups = spread_weights(after(up_whole, middle_low))
    with jax.named_scope("down_plane"):
        downs = spread_weights(after(down_whole, ups[1], ups[2]))
    square = jnp.sum(middle * middle, axis=1, keepdims=True)
    square = square + core_swap(square)
    scale_mid = lax.rsqrt(square / width + EPS)

    pairs = [slice(at, at + 2) for at in range(0, rows, 2)]
    found = [activate(feat, m_list[pair], m_others[pair], gates, ups) for pair in pairs]
    hiddens = [f[0] for f in found]
    with jax.named_scope("grad_row"):
        g_own = after(g_own, *m_others)
        g_other = core_swap(g_own)
    parts, scaled_grads, held, down_parts = [None] * rows, [None] * len(pairs), hiddens, None
    for at in reversed(range(len(pairs))):
        with jax.named_scope("unit_grad"):
            _, slope_gate, slope_up, scale = found[at]
            gate_grad, up_grad, own, other = units_back(
                feat, starts[pairs[at]], g_own, g_other, after(slope_gate, *held), slope_up, scale, gates, ups, downs
            )
            scaled_grads[at] = gate_grad, up_grad
            low = own.astype(F32) + core_swap(other).astype(F32)
            parts[2 * at], parts[2 * at + 1] = low[:quarter], low[quarter:].astype(BF16)
        if down_parts is None:
            with jax.named_scope("down_grad"):
                down_parts = outer(
                    feat, "down_outer", starts, [g_own], [g_other], [after(h, parts[-1]) for h in hiddens], places
                )
            held = down_parts[:1]
    kept = []

    def feed_work(*lows):
        with jax.named_scope("feed"):
            kept.extend(unfold(feat, "feed", [after(h, *lows)], downs) for h in hiddens)
        return [own for own, _ in kept]

    with jax.named_scope("unit_grad"):
        unit_grad = reduce_row(parts, lambda *lows: (), feed_work)
    with jax.named_scope("down_grad"):
        down_total = plane_second(plane_first(down_parts))
        down_blocks = give_back(down_total)

    unit_mid = middle * scale_mid
    dot_two = jnp.sum(unit_grad * unit_mid, axis=1, keepdims=True)
    dot_two = dot_two + core_swap(dot_two)
    middle_grad = g_part.astype(F32) + scale_mid * (unit_grad - unit_mid * (dot_two / width))

    d_low = after(middle_grad.astype(BF16), down_total)
    with jax.named_scope("feed"):
        shares = []
        for own, other in kept:
            low = own.astype(F32) + core_swap(other).astype(F32)
            low = after(low.astype(BF16), d_low)
            shares += [low[:quarter], low[quarter:]]
    gate_parts = outer(feat, "gate_outer", starts, m_list, m_others, [after(a, d_low) for a, _ in scaled_grads], places)
    up_parts = outer(feat, "up_outer", starts, m_list, m_others, [after(a, d_low) for _, a in scaled_grads], places)
    with jax.named_scope("feed"):
        feed_sent = []

        def note(*lows):
            feed_sent.extend(lows)
            return ()

        feed_first, feed_last = reduce_row(shares, note, note, split=True)
    with jax.named_scope("middle_grad"):
        pieces = spread(d_low)
        d_own = put_rows(
            [pieces[0]] + [after(a, gate_parts[0], up_parts[0], feed_sent[-1]) for a in pieces[1:]]
        )
        d_other = core_swap(d_own)
    mixed_grad = fold(feat, d_own, d_other, out_full)
    with jax.named_scope("gate_grad"):
        gate_middle = plane_first([after(a, d_own) for a in gate_parts])
    query_grad, key_grad, value_grad = attend_back(
        query, key, value, mixed, after(mixed_grad, *gate_middle), start_row, logs, cosine, front, back
    )
    with jax.named_scope("feed"):
        feed_low = (middle + feed_first.astype(F32) + after(feed_last, query_grad).astype(F32)).astype(BF16)
    with jax.named_scope("gate_grad"):
        gate_total = plane_second(gate_middle, query_grad)
        gate_blocks = give_back(gate_total)
    query_grad = after(query_grad, down_blocks, gate_total, feed_low)
    heads_part, gain_dots = heads_outer(
        feat, x_own, x_other, d_own, d_other, query_grad, key_grad, value_grad, mixed, scale_one, qkv_full
    )
    with jax.named_scope("heads_grad"):
        heads_blocks = lax.psum_scatter(heads_part, "row", scatter_dimension=0, tiled=True)
    with jax.named_scope("up_grad"):
        up_total = plane_second(plane_first([after(a, gate_total, heads_part) for a in up_parts]))
        up_blocks = give_back(up_total)
    with jax.named_scope("block_out"):
        block_out = to_home(after(feed_low, gate_blocks))
    with jax.named_scope("first_plane"):
        first_unit_grad = scatter_parts(
            *unfold(feat, "first_grad", [after(query_grad, heads_part), key_grad, value_grad], [qkv_full])
        )
    scale_first = token_part(scale_one, 0)
    unit_first = token_part(x_own, 0).astype(F32) * scale_first
    dot_one = jnp.sum(first_unit_grad * unit_first, axis=1, keepdims=True)
    dot_one = dot_one + core_swap(dot_one)
    with jax.named_scope("input_grad"):
        input_grad = to_home_swaps(
            (middle_grad + scale_first * (first_unit_grad - unit_first * (dot_one / width))).astype(BF16)
        )

    def row_dots(w, d):
        return jnp.sum(w.astype(F32) * d.astype(F32), axis=1)

    with jax.named_scope("gains"):
        dots = jnp.stack(
            [gain_dots[:, 0], row_dots(gates[0], gate_total) + row_dots(ups[0], up_total)]
        ).reshape(2, rows, 2, feat)
        dots = sum_cols(jnp.where(core == 0, dots, dots[:, :, ::-1])).transpose(1, 0, 2, 3)
        dots = dots.reshape(rows, 2, 2 * feat)
        mine = lax.dynamic_index_in_dim(dots, row, 0, False)
        for s in range(1, rows):
            mine = mine + row_swap(lax.dynamic_index_in_dim(dots, row ^ s, 0, False), s)
        first_gain_grad = mine[0] / gain_one[:, 0]
        second_gain_grad = mine[1] / gain_two[:, 0]
    (down_weight_grad,) = finish(cores, down_blocks, gain_two, 0)
    (gate_weight_grad,) = finish(cores, gate_blocks, gain_two, 1)
    (up_weight_grad,) = finish(cores, up_blocks, gain_two, 1)
    heads_blocks = after(
        heads_blocks, down_weight_grad, gate_weight_grad, up_weight_grad, second_gain_grad, input_grad
    )
    query_weight_grad, key_weight_grad, value_weight_grad, out_weight_grad = finish(
        cores, heads_blocks[None], gain_one, 3, 4
    )
    return (
        block_out,
        input_grad,
        query_weight_grad,
        key_weight_grad,
        value_weight_grad,
        out_weight_grad,
        gate_weight_grad,
        up_weight_grad,
        down_weight_grad,
        first_gain_grad,
        second_gain_grad,
    )


def solution(mesh):
    grid, line = P("row", "col"), P("row")
    return jax.shard_map(
        local,
        mesh=mesh,
        in_specs=(grid,) * 8 + (line,) * 4 + (grid,),
        out_specs=(grid,) * 9 + (line,) * 2,
        check_vma=False,
    )
```

```python
import functools
import math

import jax
import jax.numpy as jnp
from jax import lax
from jax.experimental import pallas as pl
from jax.experimental.pallas import tpu as pltpu
from jax.sharding import PartitionSpec as P

HEAD_DIM = 64
LANES = 128
EPS = 1e-05
ROPE_BASE = 130000.0
LOG2E = math.log2(math.e)
SCORE_SCALE = HEAD_DIM**-0.5
BF16 = jnp.bfloat16
F32 = jnp.float32
VMEM_BYTES = 56 * 1024 * 1024


def nn(left, right):
    return lax.dot_general(left, right, (((1,), (0,)), ((), ())), preferred_element_type=F32)


def nt(left, right):
    return lax.dot_general(left, right, (((1,), (1,)), ((), ())), preferred_element_type=F32)


def tn(left, right):
    return lax.dot_general(left, right, (((0,), (0,)), ((), ())), preferred_element_type=F32)


def spin(values, cosine, sine_front, sine_back):
    half = HEAD_DIM // 2
    lanes = values.shape[-1]
    return (
        values * cosine
        + pltpu.roll(values, lanes - half, 1) * sine_front
        + pltpu.roll(values, half, 1) * sine_back
    )


def weave(own, other, feat):
    pieces = []
    for at in range(0, own.shape[1], feat):
        pieces += [own[:, at : at + feat], other[:, at : at + feat]]
    return jnp.concatenate(pieces, axis=1)


def norm_scale(values):
    wide = values.astype(F32)
    return lax.rsqrt(jnp.sum(wide * wide, axis=1, keepdims=True) / values.shape[1] + EPS)


def whole_spec(a):
    return pl.BlockSpec(a.shape, lambda i: (0,) * a.ndim, pipeline_mode=pl.Buffered(1))


def row_spec(block, a):
    return pl.BlockSpec((block, a.shape[1]), lambda i: (i, 0))


def project_kernel(feat, starts, own_ref, other_ref, *refs):
    weights, (cos_ref, front_ref, back_ref), outs = refs[:-7], refs[-7:-4], refs[-4:]
    scale = norm_scale(jnp.concatenate([own_ref[...], other_ref[...]], axis=1))
    outs[3][...] = scale
    heads = outs[0].shape[1]
    picks = [pl.ds(pl.multiple_of(starts[i] * feat, feat), feat) for i in range(len(weights))]
    values = jnp.concatenate([ref[:, pick] for pick in picks for ref in (own_ref, other_ref)], axis=1)
    times = heads // cos_ref.shape[1]
    cosine, front, back = (
        jnp.concatenate([ref[...]] * times, axis=1) for ref in (cos_ref, front_ref, back_ref)
    )
    for at, ref in enumerate(outs[:3]):
        columns = slice(at * heads, (at + 1) * heads)
        result = nn(values, jnp.concatenate([w[:, columns] for w in weights], axis=0)) * scale
        if at < 2:
            result = spin(result, cosine, front, back)
        ref[...] = result.astype(BF16)


def project(feat, starts, own, other, weights, cosine, front, back):
    tokens = own.shape[0]
    heads = weights[0].shape[1] // 3
    block = 256
    result = jax.ShapeDtypeStruct((tokens, heads), BF16)
    scale = jax.ShapeDtypeStruct((tokens, 1), F32)
    return pl.pallas_call(
        functools.partial(project_kernel, feat),
        grid=(tokens // block,),
        in_specs=[pl.BlockSpec(memory_space=pltpu.SMEM), row_spec(block, own), row_spec(block, other)]
        + [whole_spec(w) for w in weights]
        + [row_spec(block, cosine)] * 3,
        out_specs=[row_spec(block, result)] * 3 + [row_spec(block, scale)],
        out_shape=[result] * 3 + [scale],
        compiler_params=pltpu.CompilerParams(vmem_limit_bytes=40 * 1024 * 1024),
        name="project",
    )(starts, own, other, *weights, cosine, front, back)


def unfold_kernel(feat, joined, *refs):
    own_ref, other_ref = refs[-2:]
    lefts, weights = refs[:joined], refs[joined:-2]
    left = jnp.concatenate([ref[...] for ref in lefts], axis=1)
    part = weights[0].shape[1]
    for at in range(0, own_ref.shape[1], feat):
        rows = slice(2 * at, 2 * (at + feat))
        total = None
        for i, weight in enumerate(weights):
            term = nt(left[:, i * part : (i + 1) * part], weight[rows, :])
            total = term if total is None else total + term
        own_ref[:, at : at + feat] = total[:, :feat].astype(BF16)
        other_ref[:, at : at + feat] = total[:, feat:].astype(BF16)


def unfold(feat, name, lefts, weights):
    tokens, half = lefts[0].shape[0], weights[0].shape[0] // 2
    block = 256
    result = jax.ShapeDtypeStruct((tokens, half), BF16)
    return pl.pallas_call(
        functools.partial(unfold_kernel, feat, len(lefts)),
        grid=(tokens // block,),
        in_specs=[row_spec(block, a) for a in lefts] + [whole_spec(w) for w in weights],
        out_specs=[row_spec(block, result)] * 2,
        out_shape=[result] * 2,
        compiler_params=pltpu.CompilerParams(vmem_limit_bytes=VMEM_BYTES),
        name=name,
    )(*lefts, *weights)


def activate_kernel(feat, parts, count, *refs):
    m_owns, m_others, refs = refs[:parts], refs[parts : 2 * parts], refs[2 * parts :]
    sources, refs = refs[: 2 * count], refs[2 * count :]
    hidden_ref, gate_ref, up_ref, scale_ref, held, arrived = refs
    copies = [
        pltpu.make_async_copy(source, held.at[at], arrived.at[at]) for at, source in enumerate(sources)
    ]
    for copy in copies:
        copy.start()
    middle = jnp.concatenate(
        [weave(a[...], b[...], feat) for a, b in zip(m_owns, m_others)], axis=0
    )
    scale = norm_scale(middle)
    scale_ref[...] = scale
    part = hidden_ref.shape[1] // count
    for i in range(count):
        if i % 2 == 0:
            for copy in copies[2 * i : 2 * i + 4]:
                copy.wait()
        columns = slice(i * part, (i + 1) * part)
        gate = nn(middle, held[2 * i]) * scale
        up = nn(middle, held[2 * i + 1]) * scale
        sigmoid = 1.0 / (1.0 + jnp.exp(-gate))
        silu = gate * sigmoid
        hidden_ref[:, columns] = (silu * up).astype(BF16)
        gate_ref[:, columns] = (up * (sigmoid + silu * (1.0 - sigmoid))).astype(BF16)
        up_ref[:, columns] = silu.astype(BF16)


def activate(feat, m_owns, m_others, gates, ups):
    parts = len(m_owns)
    tokens = m_owns[0].shape[0]
    count, part = len(gates), gates[0].shape[1]
    hidden = jax.ShapeDtypeStruct((parts * tokens, count * part), BF16)
    weights = [w for two in zip(gates, ups) for w in two]
    vmem, anywhere = pl.BlockSpec(memory_space=pltpu.VMEM), pl.BlockSpec(memory_space=pl.ANY)
    return pl.pallas_call(
        functools.partial(activate_kernel, feat, parts, count),
        in_specs=[vmem] * (2 * parts) + [anywhere] * len(weights),
        out_specs=[vmem] * 4,
        out_shape=[hidden] * 3 + [jax.ShapeDtypeStruct((parts * tokens, 1), F32)],
        scratch_shapes=[
            pltpu.VMEM((len(weights),) + weights[0].shape, BF16),
            pltpu.SemaphoreType.DMA((len(weights),)),
        ],
        compiler_params=pltpu.CompilerParams(vmem_limit_bytes=36 * 1024 * 1024),
        name="activate",
    )(*m_owns, *m_others, *weights)


def units_back_kernel(feat, parts, count, starts, *refs):
    g_sources, (gate_in, up_in, scale_in) = refs[:2], refs[2:5]
    sources, refs = refs[5 : 5 + 3 * count], refs[5 + 3 * count :]
    gate_ref, up_ref, own_ref, other_ref, held, arrived, g_held, g_arrived = refs
    tokens = own_ref.shape[0] // parts
    copies = [
        pltpu.make_async_copy(source, held.at[at], arrived.at[at]) for at, source in enumerate(sources)
    ]
    g_copies = [
        pltpu.make_async_copy(
            source.at[pl.ds(pl.multiple_of(starts[i] * tokens, tokens), tokens)],
            g_held.at[side, i],
            g_arrived.at[side, i],
        )
        for side, source in enumerate(g_sources)
        for i in range(parts)
    ]
    for copy in g_copies + copies:
        copy.start()
    for copy in g_copies + copies[:count]:
        copy.wait()
    grad = jnp.concatenate([weave(g_held[0, j], g_held[1, j], feat) for j in range(parts)], axis=0)
    scale = scale_in[...]
    part = gate_ref.shape[1] // count
    lefts = [], []
    for i in range(count):
        columns = slice(i * part, (i + 1) * part)
        hidden_grad = nn(grad, held[i])
        for side, (slope, out) in enumerate(((gate_in, gate_ref), (up_in, up_ref))):
            value = hidden_grad * slope[:, columns].astype(F32)
            out[:, columns] = (value * scale).astype(BF16)
            lefts[side].append(value.astype(BF16))
    left = jnp.concatenate(lefts[0] + lefts[1], axis=1)
    for copy in copies[count:]:
        copy.wait()
    for at in range(0, own_ref.shape[1], feat):
        rows = slice(2 * at, 2 * (at + feat))
        right = jnp.concatenate([held[i, rows, :] for i in range(count, 3 * count)], axis=1)
        total = nt(left, right)
        own_ref[:, at : at + feat] = total[:, :feat].astype(BF16)
        other_ref[:, at : at + feat] = total[:, feat:].astype(BF16)


def units_back(feat, starts, g_own, g_other, gate, up, scale, gates, ups, downs):
    tokens, half = gate.shape[0], g_own.shape[1]
    parts = starts.shape[0]
    count = len(gates)
    hidden = jax.ShapeDtypeStruct(gate.shape, BF16)
    share = jax.ShapeDtypeStruct((tokens, half), BF16)
    weights = downs + gates + ups
    vmem, anywhere = pl.BlockSpec(memory_space=pltpu.VMEM), pl.BlockSpec(memory_space=pl.ANY)
    return pl.pallas_call(
        functools.partial(units_back_kernel, feat, parts, count),
        in_specs=[pl.BlockSpec(memory_space=pltpu.SMEM)]
        + [anywhere] * 2
        + [vmem] * 3
        + [anywhere] * len(weights),
        out_specs=[vmem] * 4,
        out_shape=[hidden] * 2 + [share] * 2,
        scratch_shapes=[
            pltpu.VMEM((len(weights),) + weights[0].shape, BF16),
            pltpu.SemaphoreType.DMA((len(weights),)),
            pltpu.VMEM((2, parts, tokens // parts, half), BF16),
            pltpu.SemaphoreType.DMA((2, parts)),
        ],
        compiler_params=pltpu.CompilerParams(vmem_limit_bytes=40 * 1024 * 1024),
        name="units_back",
    )(starts, g_own, g_other, gate, up, scale, *weights)


def outer_kernel(groups, count, starts, *refs):
    owns, others, rights = refs[:groups], refs[groups : 2 * groups], refs[2 * groups : len(refs) - count]
    outs = refs[len(refs) - count :]
    if groups == 1:
        tokens = owns[0].shape[0] // starts.shape[0]
        picks = [
            pl.ds(pl.multiple_of(starts[i] * tokens, tokens), tokens) for i in range(starts.shape[0])
        ]
        sides = [(owns[0][pick, :], others[0][pick, :]) for pick in picks]
    else:
        sides = [(own[...], other[...]) for own, other in zip(owns, others)]
    left = jnp.concatenate([jnp.concatenate(pair, axis=1) for pair in sides], axis=0)
    part = outs[0].shape[1]
    for i, out in enumerate(outs):
        columns = slice(i * part, (i + 1) * part)
        right = jnp.concatenate([ref[:, columns] for ref in rights], axis=0)
        out[...] = tn(left, right).astype(BF16)


def outer(feat, name, starts, owns, others, rights, count):
    half, columns = owns[0].shape[1], rights[0].shape[1]
    part = columns // count
    side = pl.BlockSpec((owns[0].shape[0], feat), lambda i: (0, i))
    return pl.pallas_call(
        functools.partial(outer_kernel, len(owns), count),
        grid=(half // feat,),
        in_specs=[pl.BlockSpec(memory_space=pltpu.SMEM)]
        + [side] * (2 * len(owns))
        + [whole_spec(a) for a in rights],
        out_specs=[pl.BlockSpec((2 * feat, part), lambda i: (i, 0))] * count,
        out_shape=[jax.ShapeDtypeStruct((2 * half, part), BF16)] * count,
        compiler_params=pltpu.CompilerParams(vmem_limit_bytes=40 * 1024 * 1024),
        name=name,
    )(starts, *owns, *others, *rights)


def heads_outer_kernel(x_own, x_other, d_own, d_other, dq_ref, dk_ref, dv_ref, mixed_ref, scale_ref, weight_ref, out_ref, dot_ref):
    part = mixed_ref.shape[1]
    left = jnp.concatenate([x_own[...], x_other[...]], axis=1)
    dots = None
    for i, ref in enumerate((dq_ref, dk_ref, dv_ref)):
        columns = slice(i * part, (i + 1) * part)
        result = tn(left, (ref[...].astype(F32) * scale_ref[...]).astype(BF16))
        out_ref[:, columns] = result.astype(BF16)
        term = jnp.sum(result * weight_ref[:, columns].astype(F32), axis=1, keepdims=True)
        dots = term if dots is None else dots + term
    dot_ref[...] = dots
    left = jnp.concatenate([d_own[...], d_other[...]], axis=1)
    out_ref[:, 3 * part :] = tn(left, mixed_ref[...]).astype(BF16)


def heads_outer(feat, x_own, x_other, d_own, d_other, dq, dk, dv, mixed, scale, weight):
    tokens, half = x_own.shape
    part = mixed.shape[1]
    side = pl.BlockSpec((tokens, feat), lambda i: (0, i))
    return pl.pallas_call(
        heads_outer_kernel,
        grid=(half // feat,),
        in_specs=[side] * 4
        + [whole_spec(a) for a in (dq, dk, dv, mixed, scale)]
        + [row_spec(2 * feat, weight)],
        out_specs=[pl.BlockSpec((2 * feat, 4 * part), lambda i: (i, 0)), pl.BlockSpec((2 * feat, 1), lambda i: (i, 0))],
        out_shape=[
            jax.ShapeDtypeStruct((2 * half, 4 * part), BF16),
            jax.ShapeDtypeStruct((2 * half, 1), F32),
        ],
        compiler_params=pltpu.CompilerParams(vmem_limit_bytes=40 * 1024 * 1024),
        name="heads_outer",
    )(x_own, x_other, d_own, d_other, dq, dk, dv, mixed, scale, weight)


def finish_kernel(scaled, core_ref, part_ref, gain_ref, *outs):
    feat = gain_ref.shape[0] // 2
    blocks, columns = part_ref.shape[0], part_ref.shape[2] // len(outs)
    for side in range(2):
        rows = slice(side * feat, (side + 1) * feat)
        start = pl.multiple_of(lax.rem(core_ref[0] + side, 2) * feat, feat)
        gain = gain_ref[rows, :]
        for block in range(blocks):
            for i, out in enumerate(outs):
                value = part_ref[block, pl.ds(start, feat), i * columns : (i + 1) * columns].astype(F32)
                at = block * columns
                out[rows, at : at + columns] = value * gain if i < scaled else value


def finish(core, part, gain, scaled, count=1):
    blocks, rows, columns = part.shape
    vmem = pl.BlockSpec(memory_space=pltpu.VMEM)
    result = jax.ShapeDtypeStruct((rows, blocks * columns // count), F32)
    return pl.pallas_call(
        functools.partial(finish_kernel, scaled),
        in_specs=[pl.BlockSpec(memory_space=pltpu.SMEM), vmem, vmem],
        out_specs=[vmem] * count,
        out_shape=[result] * count,
        compiler_params=pltpu.CompilerParams(vmem_limit_bytes=VMEM_BYTES),
        name="finish",
    )(core, part, gain)


def fold_kernel(feat, own_ref, other_ref, weight_ref, out_ref):
    out_ref[...] = nn(weave(own_ref[...], other_ref[...], feat), weight_ref[...]).astype(BF16)


def fold(feat, own, other, weight):
    tokens = own.shape[0]
    block = 256
    result = jax.ShapeDtypeStruct((tokens, weight.shape[1]), BF16)
    return pl.pallas_call(
        functools.partial(fold_kernel, feat),
        grid=(tokens // block,),
        in_specs=[row_spec(block, own), row_spec(block, other), whole_spec(weight)],
        out_specs=row_spec(block, result),
        out_shape=result,
        compiler_params=pltpu.CompilerParams(vmem_limit_bytes=40 * 1024 * 1024),
        name="fold",
    )(own, other, weight)


def allowed_block(start_row, key_base, query_base, keys, queries):
    key_index = key_base + lax.broadcasted_iota(jnp.int32, (keys, queries), 0)
    query_index = query_base + lax.broadcasted_iota(jnp.int32, (keys, queries), 1)
    return (key_index >= start_row) & (key_index <= query_index)


def attend_kernel(q_ref, k_ref, v_ref, start_ref, out_ref, log_ref):
    tokens = q_ref.shape[0]
    block = 256
    keys_all = k_ref[...]
    values_turned = v_ref[...].T
    lane = lax.broadcasted_iota(jnp.int32, (1, LANES), 1)
    sub = lax.broadcasted_iota(jnp.int32, (LANES, 1), 0)
    for place in range(tokens // block):
        rows = slice(place * block, (place + 1) * block)
        reach = (place + 1) * block
        query = q_ref[rows, :]
        start_row = start_ref[:, rows]
        allowed = allowed_block(start_row, 0, place * block, reach, block)
        parts = []
        for head in range(LANES // HEAD_DIM):
            mine = lane // HEAD_DIM == head
            query_head = query * mine.astype(BF16)
            scores = nt(keys_all[:reach], query_head) * (SCORE_SCALE * LOG2E)
            scores = jnp.where(allowed, scores, -1e30)
            peak = jnp.max(scores, axis=0, keepdims=True)
            raised = jnp.exp2(scores - peak)
            total = jnp.sum(raised, axis=0, keepdims=True)
            mixed = nn(values_turned[:, :reach], raised.astype(BF16)) / total
            parts.append(mixed)
            log_ref[0, head : head + 1, rows] = peak + jnp.log2(total)
        joined = jnp.where(sub // HEAD_DIM == 0, parts[0], parts[1])
        out_ref[rows, :] = joined.T.astype(BF16)


def attend(query, key, value, start_row):
    tokens, width = query.shape
    pairs = width // LANES
    column = pl.BlockSpec((tokens, LANES), lambda i: (0, i))
    return pl.pallas_call(
        attend_kernel,
        grid=(pairs,),
        in_specs=[column, column, column, pl.BlockSpec((1, tokens), lambda i: (0, 0))],
        out_specs=[column, pl.BlockSpec((1, 2, tokens), lambda i: (i, 0, 0))],
        out_shape=[
            jax.ShapeDtypeStruct((tokens, width), BF16),
            jax.ShapeDtypeStruct((pairs, 2, tokens), F32),
        ],
        compiler_params=pltpu.CompilerParams(vmem_limit_bytes=VMEM_BYTES),
        name="attend",
    )(query, key, value, start_row)


def attend_back_kernel(
    q_ref, k_ref, v_ref, o_ref, do_ref, start_ref, log_ref, cos_ref, front_ref, back_ref,
    dq_ref, dk_ref, dv_ref, dq_acc,
):
    tokens = q_ref.shape[0]
    block = 256
    lane = lax.broadcasted_iota(jnp.int32, (1, LANES), 1)
    sub = lax.broadcasted_iota(jnp.int32, (LANES, 1), 0)
    query_all = q_ref[...]
    grad_all = do_ref[...]
    product = (o_ref[...].astype(F32) * grad_all.astype(F32)).T
    dots = [
        jnp.sum(product[head * HEAD_DIM : (head + 1) * HEAD_DIM], axis=0, keepdims=True)
        for head in range(LANES // HEAD_DIM)
    ]
    dq_acc[...] = jnp.zeros_like(dq_acc)
    for place in range(tokens // block):
        rows = slice(place * block, (place + 1) * block)
        tail = slice(place * block, tokens)
        keys = k_ref[rows, :]
        values = v_ref[rows, :]
        keys_turned = keys.T
        query = query_all[place * block :]
        grad = grad_all[place * block :]
        start_row = start_ref[:, tail]
        allowed = allowed_block(
            start_row, place * block, place * block, block, tokens - place * block
        )
        key_grad = jnp.zeros((block, LANES), F32)
        value_grad = jnp.zeros((block, LANES), F32)
        for head in range(LANES // HEAD_DIM):
            mine = lane // HEAD_DIM == head
            scores = nt(keys * mine.astype(BF16), query) * (SCORE_SCALE * LOG2E)
            weights = jnp.where(allowed, jnp.exp2(scores - log_ref[0, head : head + 1, tail]), 0.0)
            weight_grad = nt(values * mine.astype(BF16), grad)
            score_grad = (weights * (weight_grad - dots[head][:, place * block :])).astype(BF16)
            value_grad = jnp.where(mine, nn(weights.astype(BF16), grad), value_grad)
            key_grad = jnp.where(mine, nn(score_grad, query), key_grad)
            dq_acc[:, tail] += nn(
                keys_turned * (sub // HEAD_DIM == head).astype(BF16), score_grad
            )
        dv_ref[rows, :] = value_grad.astype(BF16)
        dk_ref[rows, :] = spin(
            key_grad * SCORE_SCALE, cos_ref[rows, :], -front_ref[rows, :], -back_ref[rows, :]
        ).astype(BF16)
    dq_ref[...] = spin(
        dq_acc[...].T * SCORE_SCALE, cos_ref[...], -front_ref[...], -back_ref[...]
    ).astype(BF16)


def attend_back(query, key, value, mixed, mixed_grad, start_row, logs, cosine, front, back):
    tokens, width = query.shape
    pairs = width // LANES
    column = pl.BlockSpec((tokens, LANES), lambda i: (0, i))
    table = pl.BlockSpec((tokens, LANES), lambda i: (0, 0))
    return pl.pallas_call(
        attend_back_kernel,
        grid=(pairs,),
        in_specs=[
            column, column, column, column, column,
            pl.BlockSpec((1, tokens), lambda i: (0, 0)),
            pl.BlockSpec((1, 2, tokens), lambda i: (i, 0, 0)),
            table, table, table,
        ],
        out_specs=[column, column, column],
        out_shape=[jax.ShapeDtypeStruct((tokens, width), BF16)] * 3,
        scratch_shapes=[pltpu.VMEM((LANES, tokens), F32)],
        compiler_params=pltpu.CompilerParams(vmem_limit_bytes=VMEM_BYTES),
        name="attend_back",
    )(query, key, value, mixed, mixed_grad, start_row, logs, cosine, front, back)


def rope_tables(positions, width):
    half = HEAD_DIM // 2
    freqs = jnp.exp(jnp.arange(half, dtype=F32) * (-2.0 * math.log(ROPE_BASE) / HEAD_DIM))
    angles = positions.astype(F32)[:, None] * freqs[None, :]
    cosine, sine = jnp.cos(angles), jnp.sin(angles)
    zero = jnp.zeros_like(sine)
    heads = width // HEAD_DIM
    return (
        jnp.concatenate([cosine] * (2 * heads), axis=1),
        jnp.concatenate([-sine, zero] * heads, axis=1),
        jnp.concatenate([zero, sine] * heads, axis=1),
    )


def local(
    inputs,
    query_weight,
    key_weight,
    value_weight,
    out_weight,
    gate_weight,
    up_weight,
    down_weight,
    first_gain,
    second_gain,
    segment_ids,
    positions,
    out_grad,
):
    rows = lax.axis_size("row")
    cols = lax.axis_size("col")
    places = cols // 2
    row = lax.axis_index("row")
    col = lax.axis_index("col")
    core = col % 2
    place = col // 2
    tokens, feat = inputs.shape
    width = feat * cols
    half = width // 2
    quarter = tokens // places

    def core_swap(a):
        return lax.ppermute(a, "col", [(i, i ^ 1) for i in range(cols)])

    def plane_swap(a, step):
        return lax.ppermute(a, "col", [(i, i ^ (2 * step)) for i in range(cols)])

    def token_part(a, step):
        return lax.dynamic_slice_in_dim(a, (place ^ step) * quarter, quarter, 0)

    def feat_part(a, step):
        return lax.dynamic_slice_in_dim(a, (place ^ step) * feat, feat, 1)

    def own_first(w):
        return jnp.concatenate(
            [jnp.where(core == 0, w[:feat], w[feat:]), jnp.where(core == 0, w[feat:], w[:feat])], axis=0
        )

    def row_swap(a, step):
        return lax.ppermute(a, "row", [(i, i ^ step) for i in range(rows)])

    def gather_row(a, held=()):
        got, bit = {0: a}, rows // 2
        while bit:
            for step in list(got):
                came = row_swap(got[step], bit)
                got[step ^ bit] = after(came, *held) if 2 * bit == rows else came
            bit //= 2
        return [got[step] for step in range(rows)]

    def reduce_row(parts, *works):
        parts, bit, step = list(parts), 1, 0
        while bit < rows:
            lows = {at: parts[at + bit].astype(BF16) for at in range(rows - 2 * bit, -1, -2 * bit)}
            held = works[step](*lows.values()) if step < len(works) else ()
            for at, low in lows.items():
                came = after(row_swap(low, bit), *held)
                parts[at] = parts[at].astype(F32) + came.astype(F32)
            bit, step = 2 * bit, step + 1
        return parts[0]

    def row_part(a, step):
        size = a.shape[0] // rows
        return lax.dynamic_slice_in_dim(a, (row ^ step) * size, size, 0)

    def after(value, *others):
        return lax.optimization_barrier((value,) + others)[0]

    def put_rows(pieces):
        whole = jnp.zeros((tokens,) + pieces[0].shape[1:], pieces[0].dtype)
        for step, piece in enumerate(pieces):
            whole = lax.dynamic_update_slice_in_dim(whole, piece, (place ^ step) * quarter, 0)
        return whole

    def put_feats(pieces):
        whole = jnp.zeros((pieces[0].shape[0], half), pieces[0].dtype)
        for step, piece in enumerate(pieces):
            whole = lax.dynamic_update_slice_in_dim(whole, piece, (place ^ step) * feat, 1)
        return whole

    def spread(a):
        return [a] + [plane_swap(a, step) for step in range(1, places)]

    groups = [[2 * i + k for i in range(places)] for k in range(2)]

    def plane_exchange(a):
        return lax.all_to_all(
            a, "col", split_axis=0, concat_axis=0, axis_index_groups=groups, tiled=True
        )

    def to_parts(a):
        return put_feats(
            [token_part(a, 0)] + [plane_swap(token_part(a, s), s) for s in range(1, places)]
        )

    def to_home(a):
        a = jnp.stack([a[:, s * feat : (s + 1) * feat] for s in range(places)])
        return plane_exchange(a).reshape(tokens, feat)

    def to_home_swaps(a):
        return put_rows([feat_part(a, 0)] + [plane_swap(feat_part(a, s), s) for s in range(1, places)])

    def sum_cols(a):
        step = 1
        while step < cols:
            a = a + lax.ppermute(a, "col", [(i, i ^ step) for i in range(cols)])
            step *= 2
        return a

    gain_one = first_gain.astype(F32)[:, None]
    gain_two = second_gain.astype(F32)[:, None]

    def scaled(w, gain):
        return own_first((w.astype(F32) * gain).astype(BF16))

    def cut(w):
        part = w.shape[1] // rows
        return jnp.stack([w[:, s * part : (s + 1) * part] for s in range(rows)])

    def exchange(pieces):
        got = lax.all_to_all(pieces, "row", split_axis=0, concat_axis=0, tiled=True)
        return got.reshape(width, pieces.shape[2])

    def spread_weights(whole):
        if places != 4:
            return spread(whole)
        first, second = plane_swap(whole, 1), plane_swap(whole, 2)
        return [
            whole,
            first,
            second,
            jnp.concatenate([plane_swap(second[:half], 1), plane_swap(first[half:], 2)], axis=0),
        ]

    def plane_first(pieces):
        if places != 4:
            return pieces
        top, bottom = plane_swap(pieces[3][:half], 1), plane_swap(pieces[3][half:], 2)
        to_second = jnp.concatenate(
            [(pieces[2][:half].astype(F32) + top.astype(F32)).astype(BF16), pieces[2][half:]], axis=0
        )
        to_first = jnp.concatenate(
            [pieces[1][:half], (pieces[1][half:].astype(F32) + bottom.astype(F32)).astype(BF16)], axis=0
        )
        return [pieces[0], to_first, to_second]

    def plane_second(pieces, *hold):
        total = pieces[0].astype(F32)
        for s, piece in enumerate(pieces[1:], 1):
            total = total + after(plane_swap(piece, s), *hold).astype(F32)
        return total.astype(BF16)

    def give_back(total):
        total = total.reshape(rows, 2 * feat, total.shape[1])
        return lax.all_to_all(total, "row", split_axis=0, concat_axis=0, tiled=True)

    def join_rows(pieces):
        size = pieces[0].shape[0]
        whole = jnp.zeros((rows * size, pieces[0].shape[1]), BF16)
        for step, piece in enumerate(pieces):
            whole = lax.dynamic_update_slice_in_dim(whole, piece, (row ^ step) * size, 0)
        return whole

    starts = jnp.stack([row ^ s for s in range(rows)])
    cores = core.reshape(1)

    with jax.named_scope("prepare"):
        cosine, front, back = rope_tables(positions, LANES)
        start_row = jnp.sum(
            (segment_ids[None, :] < segment_ids[:, None]).astype(jnp.int32), axis=1
        )[None, :]
        up_cut = cut(scaled(up_weight, gain_two))
        down_cut = cut(own_first(down_weight))
        out_block = own_first(out_weight)
    with jax.named_scope("inputs"):
        x_own = put_feats(spread(inputs))
        x_other = core_swap(x_own)
    with jax.named_scope("grad_plane"):
        g_part = to_parts(after(out_grad, x_own))
    with jax.named_scope("qkv_row"):
        qkv_list = gather_row(
            jnp.concatenate(
                [scaled(w, gain_one) for w in (query_weight, key_weight, value_weight)], axis=1
            ),
            (cosine, front, back, start_row, up_cut, down_cut, out_block, g_part),
        )
    with jax.named_scope("gate_row"):
        gate_whole = exchange(cut(scaled(gate_weight, gain_two)))
    with jax.named_scope("out_row"):
        out_full = lax.all_gather(after(out_block, *qkv_list[1:3]), "row", axis=0, tiled=True)
    with jax.named_scope("up_row"):
        up_whole = exchange(after(up_cut, gate_whole))
    with jax.named_scope("down_row"):
        down_whole = exchange(after(down_cut, up_whole))
    with jax.named_scope("gate_plane"):
        gates = spread_weights(gate_whole)
    query, key, value, scale_one = project(
        feat, starts, x_own, x_other, qkv_list, cosine, front, back
    )
    qkv_full = join_rows([after(a, query) for a in qkv_list])
    mixed, logs = attend(after(query, gates[1], gates[2]), key, value, start_row)
    mixed = after(mixed, gates[3])
    with jax.named_scope("grad_row"):
        g_own = lax.all_gather(after(g_part, out_full), "row", axis=0, tiled=True)

    def scatter_parts(own, other):
        low = (own.astype(F32) + core_swap(other).astype(F32)).astype(BF16)
        total = token_part(low, 0).astype(F32)
        for s in range(1, places):
            total = total + plane_swap(token_part(low, s), s).astype(F32)
        return total

    with jax.named_scope("mix_plane"):
        own, other = unfold(feat, "mix", [mixed], [out_full])
        middle = token_part(x_own, 0).astype(F32) + scatter_parts(after(own, up_whole), other)
        middle = after(middle, down_whole)
    with jax.named_scope("up_plane"):
        ups = spread_weights(up_whole)
    middle_low = after(middle.astype(BF16), ups[1], ups[2])
    with jax.named_scope("middle_row"):
        m_list = gather_row(middle_low)
        m_others = [core_swap(m) for m in m_list]
    with jax.named_scope("down_plane"):
        downs = spread_weights(down_whole)
    square = jnp.sum(middle * middle, axis=1, keepdims=True)
    square = square + core_swap(square)
    scale_mid = lax.rsqrt(square / width + EPS)

    pairs = [slice(at, at + 2) for at in range(0, rows, 2)]
    found = [activate(feat, m_list[pair], m_others[pair], gates, ups) for pair in pairs]
    hiddens = [f[0] for f in found]
    with jax.named_scope("grad_row"):
        g_own = after(g_own, hiddens[0])
        g_other = core_swap(g_own)
    parts, scaled_grads, held, down_parts = [None] * rows, [None] * len(pairs), hiddens, None
    for at in reversed(range(len(pairs))):
        with jax.named_scope("unit_grad"):
            _, slope_gate, slope_up, scale = found[at]
            gate_grad, up_grad, own, other = units_back(
                feat, starts[pairs[at]], g_own, g_other, after(slope_gate, *held), slope_up, scale, gates, ups, downs
            )
            scaled_grads[at] = gate_grad, up_grad
            low = own.astype(F32) + core_swap(other).astype(F32)
            parts[2 * at], parts[2 * at + 1] = low[:quarter], low[quarter:].astype(BF16)
        if down_parts is None:
            with jax.named_scope("down_grad"):
                down_parts = outer(
                    feat, "down_outer", starts, [g_own], [g_other], [after(h, parts[-1]) for h in hiddens], places
                )
            held = down_parts[:1]
    kept = []

    def feed_work(*lows):
        with jax.named_scope("feed"):
            kept.extend(unfold(feat, "feed", [after(h, *lows)], downs) for h in hiddens)
        return [own for own, _ in kept]

    with jax.named_scope("unit_grad"):
        unit_grad = reduce_row(parts, lambda *lows: (), feed_work)
    with jax.named_scope("down_grad"):
        down_total = plane_second(plane_first(down_parts))
        down_blocks = give_back(down_total)

    unit_mid = middle * scale_mid
    dot_two = jnp.sum(unit_grad * unit_mid, axis=1, keepdims=True)
    dot_two = dot_two + core_swap(dot_two)
    middle_grad = g_part.astype(F32) + scale_mid * (unit_grad - unit_mid * (dot_two / width))

    d_low = after(middle_grad.astype(BF16), down_total)
    with jax.named_scope("feed"):
        shares = jnp.zeros((rows * quarter, half), BF16)
        for pair, (own, other) in zip(pairs, kept):
            low = (own.astype(F32) + core_swap(other).astype(F32)).astype(BF16)
            for i in range(2):
                shares = lax.dynamic_update_slice_in_dim(
                    shares, low[i * quarter : (i + 1) * quarter], starts[pair.start + i] * quarter, 0
                )
        feed = lax.psum_scatter(after(shares, d_low), "row", scatter_dimension=0, tiled=True)
    gate_parts = outer(feat, "gate_outer", starts, m_list, m_others, [after(a, d_low) for a, _ in scaled_grads], places)
    up_parts = outer(feat, "up_outer", starts, m_list, m_others, [after(a, d_low) for _, a in scaled_grads], places)
    with jax.named_scope("middle_grad"):
        pieces = spread(d_low)
        d_own = put_rows(
            [pieces[0]] + [after(a, gate_parts[0], up_parts[0], shares) for a in pieces[1:]]
        )
        d_other = core_swap(d_own)
    mixed_grad = fold(feat, d_own, d_other, out_full)
    with jax.named_scope("gate_grad"):
        gate_middle = plane_first([after(a, d_own) for a in gate_parts])
    query_grad, key_grad, value_grad = attend_back(
        query, key, value, mixed, after(mixed_grad, *gate_middle), start_row, logs, cosine, front, back
    )
    with jax.named_scope("feed"):
        feed_low = (middle + after(feed, query_grad).astype(F32)).astype(BF16)
    with jax.named_scope("gate_grad"):
        gate_total = plane_second(gate_middle, query_grad)
        gate_blocks = give_back(gate_total)
    query_grad = after(query_grad, down_blocks, gate_total)
    heads_part, gain_dots = heads_outer(
        feat, x_own, x_other, d_own, d_other, query_grad, key_grad, value_grad, mixed, scale_one, qkv_full
    )
    with jax.named_scope("heads_grad"):
        heads_blocks = lax.psum_scatter(heads_part, "row", scatter_dimension=0, tiled=True)
    with jax.named_scope("up_grad"):
        up_total = plane_second(plane_first([after(a, gate_total, heads_part) for a in up_parts]))
        up_blocks = give_back(up_total)
    with jax.named_scope("block_out"):
        block_out = to_home(after(feed_low, gate_blocks, heads_part))
    with jax.named_scope("first_plane"):
        first_unit_grad = scatter_parts(
            *unfold(feat, "first_grad", [after(query_grad, heads_part), key_grad, value_grad], [qkv_full])
        )
    scale_first = token_part(scale_one, 0)
    unit_first = token_part(x_own, 0).astype(F32) * scale_first
    dot_one = jnp.sum(first_unit_grad * unit_first, axis=1, keepdims=True)
    dot_one = dot_one + core_swap(dot_one)
    with jax.named_scope("input_grad"):
        input_grad = to_home_swaps(
            (middle_grad + scale_first * (first_unit_grad - unit_first * (dot_one / width))).astype(BF16)
        )

    def row_dots(w, d):
        return jnp.sum(w.astype(F32) * d.astype(F32), axis=1)

    with jax.named_scope("gains"):
        dots = jnp.stack(
            [gain_dots[:, 0], row_dots(gates[0], gate_total) + row_dots(ups[0], up_total)]
        ).reshape(2, rows, 2, feat)
        dots = sum_cols(jnp.where(core == 0, dots, dots[:, :, ::-1])).transpose(1, 0, 2, 3)
        dots = dots.reshape(rows, 2, 2 * feat)
        mine = lax.dynamic_index_in_dim(dots, row, 0, False)
        for s in range(1, rows):
            mine = mine + row_swap(lax.dynamic_index_in_dim(dots, row ^ s, 0, False), s)
        first_gain_grad = mine[0] / gain_one[:, 0]
        second_gain_grad = mine[1] / gain_two[:, 0]
    (down_weight_grad,) = finish(cores, down_blocks, gain_two, 0)
    (gate_weight_grad,) = finish(cores, gate_blocks, gain_two, 1)
    (up_weight_grad,) = finish(cores, up_blocks, gain_two, 1)
    heads_blocks = after(
        heads_blocks, down_weight_grad, gate_weight_grad, up_weight_grad, second_gain_grad, input_grad
    )
    query_weight_grad, key_weight_grad, value_weight_grad, out_weight_grad = finish(
        cores, heads_blocks[None], gain_one, 3, 4
    )
    return (
        block_out,
        input_grad,
        query_weight_grad,
        key_weight_grad,
        value_weight_grad,
        out_weight_grad,
        gate_weight_grad,
        up_weight_grad,
        down_weight_grad,
        first_gain_grad,
        second_gain_grad,
    )


def solution(mesh):
    grid, line = P("row", "col"), P("row")
    return jax.shard_map(
        local,
        mesh=mesh,
        in_specs=(grid,) * 8 + (line,) * 4 + (grid,),
        out_specs=(grid,) * 9 + (line,) * 2,
        check_vma=False,
    )
```

```python
import functools
import math

import jax
import jax.numpy as jnp
from jax import lax
from jax.experimental import pallas as pl
from jax.experimental.pallas import tpu as pltpu
from jax.sharding import PartitionSpec as P

HEAD_DIM = 64
LANES = 128
EPS = 1e-05
ROPE_BASE = 130000.0
LOG2E = math.log2(math.e)
SCORE_SCALE = HEAD_DIM**-0.5
BF16 = jnp.bfloat16
F32 = jnp.float32
VMEM_BYTES = 56 * 1024 * 1024


def nn(left, right):
    return lax.dot_general(left, right, (((1,), (0,)), ((), ())), preferred_element_type=F32)


def nt(left, right):
    return lax.dot_general(left, right, (((1,), (1,)), ((), ())), preferred_element_type=F32)


def tn(left, right):
    return lax.dot_general(left, right, (((0,), (0,)), ((), ())), preferred_element_type=F32)


def spin(values, cosine, sine_front, sine_back):
    half = HEAD_DIM // 2
    lanes = values.shape[-1]
    return (
        values * cosine
        + pltpu.roll(values, lanes - half, 1) * sine_front
        + pltpu.roll(values, half, 1) * sine_back
    )


def weave(own, other, feat):
    pieces = []
    for at in range(0, own.shape[1], feat):
        pieces += [own[:, at : at + feat], other[:, at : at + feat]]
    return jnp.concatenate(pieces, axis=1)


def norm_scale(values):
    wide = values.astype(F32)
    return lax.rsqrt(jnp.sum(wide * wide, axis=1, keepdims=True) / values.shape[1] + EPS)


def whole_spec(a):
    return pl.BlockSpec(a.shape, lambda i: (0,) * a.ndim, pipeline_mode=pl.Buffered(1))


def row_spec(block, a):
    return pl.BlockSpec((block, a.shape[1]), lambda i: (i, 0))


def project_kernel(feat, starts, own_ref, other_ref, *refs):
    weights, (cos_ref, front_ref, back_ref), outs = refs[:-7], refs[-7:-4], refs[-4:]
    scale = norm_scale(jnp.concatenate([own_ref[...], other_ref[...]], axis=1))
    outs[3][...] = scale
    heads = outs[0].shape[1]
    picks = [pl.ds(pl.multiple_of(starts[i] * feat, feat), feat) for i in range(len(weights))]
    values = jnp.concatenate([ref[:, pick] for pick in picks for ref in (own_ref, other_ref)], axis=1)
    times = heads // cos_ref.shape[1]
    cosine, front, back = (
        jnp.concatenate([ref[...]] * times, axis=1) for ref in (cos_ref, front_ref, back_ref)
    )
    for at, ref in enumerate(outs[:3]):
        columns = slice(at * heads, (at + 1) * heads)
        result = nn(values, jnp.concatenate([w[:, columns] for w in weights], axis=0)) * scale
        if at < 2:
            result = spin(result, cosine, front, back)
        ref[...] = result.astype(BF16)


def project(feat, starts, own, other, weights, cosine, front, back):
    tokens = own.shape[0]
    heads = weights[0].shape[1] // 3
    block = 256
    result = jax.ShapeDtypeStruct((tokens, heads), BF16)
    scale = jax.ShapeDtypeStruct((tokens, 1), F32)
    return pl.pallas_call(
        functools.partial(project_kernel, feat),
        grid=(tokens // block,),
        in_specs=[pl.BlockSpec(memory_space=pltpu.SMEM), row_spec(block, own), row_spec(block, other)]
        + [whole_spec(w) for w in weights]
        + [row_spec(block, cosine)] * 3,
        out_specs=[row_spec(block, result)] * 3 + [row_spec(block, scale)],
        out_shape=[result] * 3 + [scale],
        compiler_params=pltpu.CompilerParams(vmem_limit_bytes=40 * 1024 * 1024),
        name="project",
    )(starts, own, other, *weights, cosine, front, back)


def unfold_kernel(feat, joined, *refs):
    own_ref, other_ref = refs[-2:]
    lefts, weights = refs[:joined], refs[joined:-2]
    left = jnp.concatenate([ref[...] for ref in lefts], axis=1)
    part = weights[0].shape[1]
    for at in range(0, own_ref.shape[1], feat):
        rows = slice(2 * at, 2 * (at + feat))
        total = None
        for i, weight in enumerate(weights):
            term = nt(left[:, i * part : (i + 1) * part], weight[rows, :])
            total = term if total is None else total + term
        own_ref[:, at : at + feat] = total[:, :feat].astype(BF16)
        other_ref[:, at : at + feat] = total[:, feat:].astype(BF16)


def unfold(feat, name, lefts, weights):
    tokens, half = lefts[0].shape[0], weights[0].shape[0] // 2
    block = 256
    result = jax.ShapeDtypeStruct((tokens, half), BF16)
    return pl.pallas_call(
        functools.partial(unfold_kernel, feat, len(lefts)),
        grid=(tokens // block,),
        in_specs=[row_spec(block, a) for a in lefts] + [whole_spec(w) for w in weights],
        out_specs=[row_spec(block, result)] * 2,
        out_shape=[result] * 2,
        compiler_params=pltpu.CompilerParams(vmem_limit_bytes=VMEM_BYTES),
        name=name,
    )(*lefts, *weights)


def activate_kernel(feat, parts, count, *refs):
    m_owns, m_others, refs = refs[:parts], refs[parts : 2 * parts], refs[2 * parts :]
    sources, refs = refs[: 2 * count], refs[2 * count :]
    hidden_ref, gate_ref, up_ref, scale_ref, held, arrived = refs
    copies = [
        pltpu.make_async_copy(source, held.at[at], arrived.at[at]) for at, source in enumerate(sources)
    ]
    for copy in copies:
        copy.start()
    middle = jnp.concatenate(
        [weave(a[...], b[...], feat) for a, b in zip(m_owns, m_others)], axis=0
    )
    scale = norm_scale(middle)
    scale_ref[...] = scale
    part = hidden_ref.shape[1] // count
    for i in range(count):
        if i % 2 == 0:
            for copy in copies[2 * i : 2 * i + 4]:
                copy.wait()
        columns = slice(i * part, (i + 1) * part)
        gate = nn(middle, held[2 * i]) * scale
        up = nn(middle, held[2 * i + 1]) * scale
        sigmoid = 1.0 / (1.0 + jnp.exp(-gate))
        silu = gate * sigmoid
        hidden_ref[:, columns] = (silu * up).astype(BF16)
        gate_ref[:, columns] = (up * (sigmoid + silu * (1.0 - sigmoid))).astype(BF16)
        up_ref[:, columns] = silu.astype(BF16)


def activate(feat, m_owns, m_others, gates, ups):
    parts = len(m_owns)
    tokens = m_owns[0].shape[0]
    count, part = len(gates), gates[0].shape[1]
    hidden = jax.ShapeDtypeStruct((parts * tokens, count * part), BF16)
    weights = [w for two in zip(gates, ups) for w in two]
    vmem, anywhere = pl.BlockSpec(memory_space=pltpu.VMEM), pl.BlockSpec(memory_space=pl.ANY)
    return pl.pallas_call(
        functools.partial(activate_kernel, feat, parts, count),
        in_specs=[vmem] * (2 * parts) + [anywhere] * len(weights),
        out_specs=[vmem] * 4,
        out_shape=[hidden] * 3 + [jax.ShapeDtypeStruct((parts * tokens, 1), F32)],
        scratch_shapes=[
            pltpu.VMEM((len(weights),) + weights[0].shape, BF16),
            pltpu.SemaphoreType.DMA((len(weights),)),
        ],
        compiler_params=pltpu.CompilerParams(vmem_limit_bytes=36 * 1024 * 1024),
        name="activate",
    )(*m_owns, *m_others, *weights)


def units_back_kernel(feat, parts, count, starts, *refs):
    g_sources, (gate_in, up_in, scale_in) = refs[:2], refs[2:5]
    sources, refs = refs[5 : 5 + 3 * count], refs[5 + 3 * count :]
    gate_ref, up_ref, own_ref, other_ref, held, arrived, g_held, g_arrived = refs
    tokens = own_ref.shape[0] // parts
    copies = [
        pltpu.make_async_copy(source, held.at[at], arrived.at[at]) for at, source in enumerate(sources)
    ]
    g_copies = [
        pltpu.make_async_copy(
            source.at[pl.ds(pl.multiple_of(starts[i] * tokens, tokens), tokens)],
            g_held.at[side, i],
            g_arrived.at[side, i],
        )
        for side, source in enumerate(g_sources)
        for i in range(parts)
    ]
    for copy in g_copies + copies:
        copy.start()
    for copy in g_copies + copies[:count]:
        copy.wait()
    grad = jnp.concatenate([weave(g_held[0, j], g_held[1, j], feat) for j in range(parts)], axis=0)
    scale = scale_in[...]
    part = gate_ref.shape[1] // count
    lefts = [], []
    for i in range(count):
        columns = slice(i * part, (i + 1) * part)
        hidden_grad = nn(grad, held[i])
        for side, (slope, out) in enumerate(((gate_in, gate_ref), (up_in, up_ref))):
            value = hidden_grad * slope[:, columns].astype(F32)
            out[:, columns] = (value * scale).astype(BF16)
            lefts[side].append(value.astype(BF16))
    left = jnp.concatenate(lefts[0] + lefts[1], axis=1)
    for copy in copies[count:]:
        copy.wait()
    for at in range(0, own_ref.shape[1], feat):
        rows = slice(2 * at, 2 * (at + feat))
        right = jnp.concatenate([held[i, rows, :] for i in range(count, 3 * count)], axis=1)
        total = nt(left, right)
        own_ref[:, at : at + feat] = total[:, :feat].astype(BF16)
        other_ref[:, at : at + feat] = total[:, feat:].astype(BF16)


def units_back(feat, starts, g_own, g_other, gate, up, scale, gates, ups, downs):
    tokens, half = gate.shape[0], g_own.shape[1]
    parts = starts.shape[0]
    count = len(gates)
    hidden = jax.ShapeDtypeStruct(gate.shape, BF16)
    share = jax.ShapeDtypeStruct((tokens, half), BF16)
    weights = downs + gates + ups
    vmem, anywhere = pl.BlockSpec(memory_space=pltpu.VMEM), pl.BlockSpec(memory_space=pl.ANY)
    return pl.pallas_call(
        functools.partial(units_back_kernel, feat, parts, count),
        in_specs=[pl.BlockSpec(memory_space=pltpu.SMEM)]
        + [anywhere] * 2
        + [vmem] * 3
        + [anywhere] * len(weights),
        out_specs=[vmem] * 4,
        out_shape=[hidden] * 2 + [share] * 2,
        scratch_shapes=[
            pltpu.VMEM((len(weights),) + weights[0].shape, BF16),
            pltpu.SemaphoreType.DMA((len(weights),)),
            pltpu.VMEM((2, parts, tokens // parts, half), BF16),
            pltpu.SemaphoreType.DMA((2, parts)),
        ],
        compiler_params=pltpu.CompilerParams(vmem_limit_bytes=40 * 1024 * 1024),
        name="units_back",
    )(starts, g_own, g_other, gate, up, scale, *weights)


def outer_kernel(groups, count, starts, *refs):
    owns, others, rights = refs[:groups], refs[groups : 2 * groups], refs[2 * groups : len(refs) - count]
    outs = refs[len(refs) - count :]
    if groups == 1:
        tokens = owns[0].shape[0] // starts.shape[0]
        picks = [
            pl.ds(pl.multiple_of(starts[i] * tokens, tokens), tokens) for i in range(starts.shape[0])
        ]
        sides = [(owns[0][pick, :], others[0][pick, :]) for pick in picks]
    else:
        sides = [(own[...], other[...]) for own, other in zip(owns, others)]
    left = jnp.concatenate([jnp.concatenate(pair, axis=1) for pair in sides], axis=0)
    part = outs[0].shape[1]
    for i, out in enumerate(outs):
        columns = slice(i * part, (i + 1) * part)
        right = jnp.concatenate([ref[:, columns] for ref in rights], axis=0)
        out[...] = tn(left, right).astype(BF16)


def outer(feat, name, starts, owns, others, rights, count):
    half, columns = owns[0].shape[1], rights[0].shape[1]
    part = columns // count
    side = pl.BlockSpec((owns[0].shape[0], feat), lambda i: (0, i))
    return pl.pallas_call(
        functools.partial(outer_kernel, len(owns), count),
        grid=(half // feat,),
        in_specs=[pl.BlockSpec(memory_space=pltpu.SMEM)]
        + [side] * (2 * len(owns))
        + [whole_spec(a) for a in rights],
        out_specs=[pl.BlockSpec((2 * feat, part), lambda i: (i, 0))] * count,
        out_shape=[jax.ShapeDtypeStruct((2 * half, part), BF16)] * count,
        compiler_params=pltpu.CompilerParams(vmem_limit_bytes=40 * 1024 * 1024),
        name=name,
    )(starts, *owns, *others, *rights)


def heads_outer_kernel(x_own, x_other, d_own, d_other, dq_ref, dk_ref, dv_ref, mixed_ref, scale_ref, weight_ref, out_ref, dot_ref):
    part = mixed_ref.shape[1]
    left = jnp.concatenate([x_own[...], x_other[...]], axis=1)
    dots = None
    for i, ref in enumerate((dq_ref, dk_ref, dv_ref)):
        columns = slice(i * part, (i + 1) * part)
        result = tn(left, (ref[...].astype(F32) * scale_ref[...]).astype(BF16))
        out_ref[:, columns] = result.astype(BF16)
        term = jnp.sum(result * weight_ref[:, columns].astype(F32), axis=1, keepdims=True)
        dots = term if dots is None else dots + term
    dot_ref[...] = dots
    left = jnp.concatenate([d_own[...], d_other[...]], axis=1)
    out_ref[:, 3 * part :] = tn(left, mixed_ref[...]).astype(BF16)


def heads_outer(feat, x_own, x_other, d_own, d_other, dq, dk, dv, mixed, scale, weight):
    tokens, half = x_own.shape
    part = mixed.shape[1]
    side = pl.BlockSpec((tokens, feat), lambda i: (0, i))
    return pl.pallas_call(
        heads_outer_kernel,
        grid=(half // feat,),
        in_specs=[side] * 4
        + [whole_spec(a) for a in (dq, dk, dv, mixed, scale)]
        + [row_spec(2 * feat, weight)],
        out_specs=[pl.BlockSpec((2 * feat, 4 * part), lambda i: (i, 0)), pl.BlockSpec((2 * feat, 1), lambda i: (i, 0))],
        out_shape=[
            jax.ShapeDtypeStruct((2 * half, 4 * part), BF16),
            jax.ShapeDtypeStruct((2 * half, 1), F32),
        ],
        compiler_params=pltpu.CompilerParams(vmem_limit_bytes=40 * 1024 * 1024),
        name="heads_outer",
    )(x_own, x_other, d_own, d_other, dq, dk, dv, mixed, scale, weight)


def finish_kernel(scaled, core_ref, part_ref, gain_ref, *outs):
    feat = gain_ref.shape[0] // 2
    blocks, columns = part_ref.shape[0], part_ref.shape[2] // len(outs)
    for side in range(2):
        rows = slice(side * feat, (side + 1) * feat)
        start = pl.multiple_of(lax.rem(core_ref[0] + side, 2) * feat, feat)
        gain = gain_ref[rows, :]
        for block in range(blocks):
            for i, out in enumerate(outs):
                value = part_ref[block, pl.ds(start, feat), i * columns : (i + 1) * columns].astype(F32)
                at = block * columns
                out[rows, at : at + columns] = value * gain if i < scaled else value


def finish(core, part, gain, scaled, count=1):
    blocks, rows, columns = part.shape
    vmem = pl.BlockSpec(memory_space=pltpu.VMEM)
    result = jax.ShapeDtypeStruct((rows, blocks * columns // count), F32)
    return pl.pallas_call(
        functools.partial(finish_kernel, scaled),
        in_specs=[pl.BlockSpec(memory_space=pltpu.SMEM), vmem, vmem],
        out_specs=[vmem] * count,
        out_shape=[result] * count,
        compiler_params=pltpu.CompilerParams(vmem_limit_bytes=VMEM_BYTES),
        name="finish",
    )(core, part, gain)


def fold_kernel(feat, own_ref, other_ref, weight_ref, out_ref):
    out_ref[...] = nn(weave(own_ref[...], other_ref[...], feat), weight_ref[...]).astype(BF16)


def fold(feat, own, other, weight):
    tokens = own.shape[0]
    block = 256
    result = jax.ShapeDtypeStruct((tokens, weight.shape[1]), BF16)
    return pl.pallas_call(
        functools.partial(fold_kernel, feat),
        grid=(tokens // block,),
        in_specs=[row_spec(block, own), row_spec(block, other), whole_spec(weight)],
        out_specs=row_spec(block, result),
        out_shape=result,
        compiler_params=pltpu.CompilerParams(vmem_limit_bytes=40 * 1024 * 1024),
        name="fold",
    )(own, other, weight)


def allowed_block(start_row, key_base, query_base, keys, queries):
    key_index = key_base + lax.broadcasted_iota(jnp.int32, (keys, queries), 0)
    query_index = query_base + lax.broadcasted_iota(jnp.int32, (keys, queries), 1)
    return (key_index >= start_row) & (key_index <= query_index)


def attend_kernel(q_ref, k_ref, v_ref, start_ref, out_ref, log_ref):
    tokens = q_ref.shape[0]
    block = 256
    keys_all = k_ref[...]
    values_turned = v_ref[...].T
    lane = lax.broadcasted_iota(jnp.int32, (1, LANES), 1)
    sub = lax.broadcasted_iota(jnp.int32, (LANES, 1), 0)
    for place in range(tokens // block):
        rows = slice(place * block, (place + 1) * block)
        reach = (place + 1) * block
        query = q_ref[rows, :]
        start_row = start_ref[:, rows]
        allowed = allowed_block(start_row, 0, place * block, reach, block)
        parts = []
        for head in range(LANES // HEAD_DIM):
            mine = lane // HEAD_DIM == head
            query_head = query * mine.astype(BF16)
            scores = nt(keys_all[:reach], query_head) * (SCORE_SCALE * LOG2E)
            scores = jnp.where(allowed, scores, -1e30)
            peak = jnp.max(scores, axis=0, keepdims=True)
            raised = jnp.exp2(scores - peak)
            total = jnp.sum(raised, axis=0, keepdims=True)
            mixed = nn(values_turned[:, :reach], raised.astype(BF16)) / total
            parts.append(mixed)
            log_ref[0, head : head + 1, rows] = peak + jnp.log2(total)
        joined = jnp.where(sub // HEAD_DIM == 0, parts[0], parts[1])
        out_ref[rows, :] = joined.T.astype(BF16)


def attend(query, key, value, start_row):
    tokens, width = query.shape
    pairs = width // LANES
    column = pl.BlockSpec((tokens, LANES), lambda i: (0, i))
    return pl.pallas_call(
        attend_kernel,
        grid=(pairs,),
        in_specs=[column, column, column, pl.BlockSpec((1, tokens), lambda i: (0, 0))],
        out_specs=[column, pl.BlockSpec((1, 2, tokens), lambda i: (i, 0, 0))],
        out_shape=[
            jax.ShapeDtypeStruct((tokens, width), BF16),
            jax.ShapeDtypeStruct((pairs, 2, tokens), F32),
        ],
        compiler_params=pltpu.CompilerParams(vmem_limit_bytes=VMEM_BYTES),
        name="attend",
    )(query, key, value, start_row)


def attend_back_kernel(
    q_ref, k_ref, v_ref, o_ref, do_ref, start_ref, log_ref, cos_ref, front_ref, back_ref,
    dq_ref, dk_ref, dv_ref, dq_acc,
):
    tokens = q_ref.shape[0]
    block = 256
    lane = lax.broadcasted_iota(jnp.int32, (1, LANES), 1)
    sub = lax.broadcasted_iota(jnp.int32, (LANES, 1), 0)
    query_all = q_ref[...]
    grad_all = do_ref[...]
    product = (o_ref[...].astype(F32) * grad_all.astype(F32)).T
    dots = [
        jnp.sum(product[head * HEAD_DIM : (head + 1) * HEAD_DIM], axis=0, keepdims=True)
        for head in range(LANES // HEAD_DIM)
    ]
    dq_acc[...] = jnp.zeros_like(dq_acc)
    for place in range(tokens // block):
        rows = slice(place * block, (place + 1) * block)
        tail = slice(place * block, tokens)
        keys = k_ref[rows, :]
        values = v_ref[rows, :]
        keys_turned = keys.T
        query = query_all[place * block :]
        grad = grad_all[place * block :]
        start_row = start_ref[:, tail]
        allowed = allowed_block(
            start_row, place * block, place * block, block, tokens - place * block
        )
        key_grad = jnp.zeros((block, LANES), F32)
        value_grad = jnp.zeros((block, LANES), F32)
        for head in range(LANES // HEAD_DIM):
            mine = lane // HEAD_DIM == head
            scores = nt(keys * mine.astype(BF16), query) * (SCORE_SCALE * LOG2E)
            weights = jnp.where(allowed, jnp.exp2(scores - log_ref[0, head : head + 1, tail]), 0.0)
            weight_grad = nt(values * mine.astype(BF16), grad)
            score_grad = (weights * (weight_grad - dots[head][:, place * block :])).astype(BF16)
            value_grad = jnp.where(mine, nn(weights.astype(BF16), grad), value_grad)
            key_grad = jnp.where(mine, nn(score_grad, query), key_grad)
            dq_acc[:, tail] += nn(
                keys_turned * (sub // HEAD_DIM == head).astype(BF16), score_grad
            )
        dv_ref[rows, :] = value_grad.astype(BF16)
        dk_ref[rows, :] = spin(
            key_grad * SCORE_SCALE, cos_ref[rows, :], -front_ref[rows, :], -back_ref[rows, :]
        ).astype(BF16)
    dq_ref[...] = spin(
        dq_acc[...].T * SCORE_SCALE, cos_ref[...], -front_ref[...], -back_ref[...]
    ).astype(BF16)


def attend_back(query, key, value, mixed, mixed_grad, start_row, logs, cosine, front, back):
    tokens, width = query.shape
    pairs = width // LANES
    column = pl.BlockSpec((tokens, LANES), lambda i: (0, i))
    table = pl.BlockSpec((tokens, LANES), lambda i: (0, 0))
    return pl.pallas_call(
        attend_back_kernel,
        grid=(pairs,),
        in_specs=[
            column, column, column, column, column,
            pl.BlockSpec((1, tokens), lambda i: (0, 0)),
            pl.BlockSpec((1, 2, tokens), lambda i: (i, 0, 0)),
            table, table, table,
        ],
        out_specs=[column, column, column],
        out_shape=[jax.ShapeDtypeStruct((tokens, width), BF16)] * 3,
        scratch_shapes=[pltpu.VMEM((LANES, tokens), F32)],
        compiler_params=pltpu.CompilerParams(vmem_limit_bytes=VMEM_BYTES),
        name="attend_back",
    )(query, key, value, mixed, mixed_grad, start_row, logs, cosine, front, back)


def rope_tables(positions, width):
    half = HEAD_DIM // 2
    freqs = jnp.exp(jnp.arange(half, dtype=F32) * (-2.0 * math.log(ROPE_BASE) / HEAD_DIM))
    angles = positions.astype(F32)[:, None] * freqs[None, :]
    cosine, sine = jnp.cos(angles), jnp.sin(angles)
    zero = jnp.zeros_like(sine)
    heads = width // HEAD_DIM
    return (
        jnp.concatenate([cosine] * (2 * heads), axis=1),
        jnp.concatenate([-sine, zero] * heads, axis=1),
        jnp.concatenate([zero, sine] * heads, axis=1),
    )


def local(
    inputs,
    query_weight,
    key_weight,
    value_weight,
    out_weight,
    gate_weight,
    up_weight,
    down_weight,
    first_gain,
    second_gain,
    segment_ids,
    positions,
    out_grad,
):
    rows = lax.axis_size("row")
    cols = lax.axis_size("col")
    places = cols // 2
    row = lax.axis_index("row")
    col = lax.axis_index("col")
    core = col % 2
    place = col // 2
    tokens, feat = inputs.shape
    width = feat * cols
    half = width // 2
    quarter = tokens // places

    def core_swap(a):
        return lax.ppermute(a, "col", [(i, i ^ 1) for i in range(cols)])

    def plane_swap(a, step):
        return lax.ppermute(a, "col", [(i, i ^ (2 * step)) for i in range(cols)])

    def token_part(a, step):
        return lax.dynamic_slice_in_dim(a, (place ^ step) * quarter, quarter, 0)

    def feat_part(a, step):
        return lax.dynamic_slice_in_dim(a, (place ^ step) * feat, feat, 1)

    def own_first(w):
        return jnp.concatenate(
            [jnp.where(core == 0, w[:feat], w[feat:]), jnp.where(core == 0, w[feat:], w[:feat])], axis=0
        )

    def row_swap(a, step):
        return lax.ppermute(a, "row", [(i, i ^ step) for i in range(rows)])

    def gather_row(a, held=()):
        got, bit = {0: a}, rows // 2
        while bit:
            for step in list(got):
                came = row_swap(got[step], bit)
                got[step ^ bit] = after(came, *held) if 2 * bit == rows else came
            bit //= 2
        return [got[step] for step in range(rows)]

    def reduce_row(parts, *works):
        parts, bit, step = list(parts), 1, 0
        while bit < rows:
            lows = {at: parts[at + bit].astype(BF16) for at in range(rows - 2 * bit, -1, -2 * bit)}
            held = works[step](*lows.values()) if step < len(works) else ()
            for at, low in lows.items():
                came = after(row_swap(low, bit), *held)
                parts[at] = parts[at].astype(F32) + came.astype(F32)
            bit, step = 2 * bit, step + 1
        return parts[0]

    def row_part(a, step):
        size = a.shape[0] // rows
        return lax.dynamic_slice_in_dim(a, (row ^ step) * size, size, 0)

    def after(value, *others):
        return lax.optimization_barrier((value,) + others)[0]

    def put_rows(pieces):
        whole = jnp.zeros((tokens,) + pieces[0].shape[1:], pieces[0].dtype)
        for step, piece in enumerate(pieces):
            whole = lax.dynamic_update_slice_in_dim(whole, piece, (place ^ step) * quarter, 0)
        return whole

    def put_feats(pieces):
        whole = jnp.zeros((pieces[0].shape[0], half), pieces[0].dtype)
        for step, piece in enumerate(pieces):
            whole = lax.dynamic_update_slice_in_dim(whole, piece, (place ^ step) * feat, 1)
        return whole

    def spread(a):
        return [a] + [plane_swap(a, step) for step in range(1, places)]

    def to_parts(a):
        return put_feats(
            [token_part(a, 0)] + [plane_swap(token_part(a, s), s) for s in range(1, places)]
        )

    def to_home(a):
        return put_rows([feat_part(a, 0)] + [plane_swap(feat_part(a, s), s) for s in range(1, places)])

    def sum_cols(a):
        step = 1
        while step < cols:
            a = a + lax.ppermute(a, "col", [(i, i ^ step) for i in range(cols)])
            step *= 2
        return a

    gain_one = first_gain.astype(F32)[:, None]
    gain_two = second_gain.astype(F32)[:, None]

    def scaled(w, gain):
        return own_first((w.astype(F32) * gain).astype(BF16))

    def cut(w):
        part = w.shape[1] // rows
        return jnp.stack([w[:, s * part : (s + 1) * part] for s in range(rows)])

    def exchange(pieces):
        got = lax.all_to_all(pieces, "row", split_axis=0, concat_axis=0, tiled=True)
        return got.reshape(width, pieces.shape[2])

    def spread_weights(whole):
        if places != 4:
            return spread(whole)
        first, second = plane_swap(whole, 1), plane_swap(whole, 2)
        return [
            whole,
            first,
            second,
            jnp.concatenate([plane_swap(second[:half], 1), plane_swap(first[half:], 2)], axis=0),
        ]

    def plane_first(pieces):
        if places != 4:
            return pieces
        top, bottom = plane_swap(pieces[3][:half], 1), plane_swap(pieces[3][half:], 2)
        to_second = jnp.concatenate(
            [(pieces[2][:half].astype(F32) + top.astype(F32)).astype(BF16), pieces[2][half:]], axis=0
        )
        to_first = jnp.concatenate(
            [pieces[1][:half], (pieces[1][half:].astype(F32) + bottom.astype(F32)).astype(BF16)], axis=0
        )
        return [pieces[0], to_first, to_second]

    def plane_second(pieces, *hold):
        total = pieces[0].astype(F32)
        for s, piece in enumerate(pieces[1:], 1):
            total = total + after(plane_swap(piece, s), *hold).astype(F32)
        return total.astype(BF16)

    def give_back(total):
        total = total.reshape(rows, 2 * feat, total.shape[1])
        return lax.all_to_all(total, "row", split_axis=0, concat_axis=0, tiled=True)

    def join_rows(pieces):
        size = pieces[0].shape[0]
        whole = jnp.zeros((rows * size, pieces[0].shape[1]), BF16)
        for step, piece in enumerate(pieces):
            whole = lax.dynamic_update_slice_in_dim(whole, piece, (row ^ step) * size, 0)
        return whole

    starts = jnp.stack([row ^ s for s in range(rows)])
    cores = core.reshape(1)

    with jax.named_scope("prepare"):
        cosine, front, back = rope_tables(positions, LANES)
        start_row = jnp.sum(
            (segment_ids[None, :] < segment_ids[:, None]).astype(jnp.int32), axis=1
        )[None, :]
        up_cut = cut(scaled(up_weight, gain_two))
        down_cut = cut(own_first(down_weight))
        out_block = own_first(out_weight)
    with jax.named_scope("inputs"):
        x_own = put_feats(spread(inputs))
        x_other = core_swap(x_own)
    with jax.named_scope("grad_plane"):
        g_part = to_parts(after(out_grad, x_own))
    with jax.named_scope("qkv_row"):
        qkv_list = gather_row(
            jnp.concatenate(
                [scaled(w, gain_one) for w in (query_weight, key_weight, value_weight)], axis=1
            ),
            (cosine, front, back, start_row, up_cut, down_cut, out_block, g_part),
        )
    with jax.named_scope("gate_row"):
        gate_whole = exchange(cut(scaled(gate_weight, gain_two)))
    with jax.named_scope("out_row"):
        out_full = lax.all_gather(after(out_block, *qkv_list[1:3]), "row", axis=0, tiled=True)
    with jax.named_scope("up_row"):
        up_whole = exchange(after(up_cut, gate_whole))
    with jax.named_scope("down_row"):
        down_whole = exchange(after(down_cut, up_whole))
    with jax.named_scope("gate_plane"):
        gates = spread_weights(gate_whole)
    query, key, value, scale_one = project(
        feat, starts, x_own, x_other, qkv_list, cosine, front, back
    )
    qkv_full = join_rows([after(a, query) for a in qkv_list])
    mixed, logs = attend(after(query, gates[1], gates[2], up_whole), key, value, start_row)
    mixed = after(mixed, gates[3])
    with jax.named_scope("grad_row"):
        g_own = lax.all_gather(after(g_part, out_full), "row", axis=0, tiled=True)

    def scatter_parts(own, other):
        low = (own.astype(F32) + core_swap(other).astype(F32)).astype(BF16)
        total = token_part(low, 0).astype(F32)
        for s in range(1, places):
            total = total + plane_swap(token_part(low, s), s).astype(F32)
        return total

    with jax.named_scope("mix_plane"):
        own, other = unfold(feat, "mix", [mixed], [out_full])
        middle = token_part(x_own, 0).astype(F32) + scatter_parts(after(own, down_whole), other)
    with jax.named_scope("up_plane"):
        ups = spread_weights(up_whole)
    middle_low = after(middle.astype(BF16), ups[1], ups[2])
    with jax.named_scope("middle_row"):
        m_list = gather_row(middle_low)
        m_others = [core_swap(m) for m in m_list]
    with jax.named_scope("down_plane"):
        downs = spread_weights(down_whole)
    square = jnp.sum(middle * middle, axis=1, keepdims=True)
    square = square + core_swap(square)
    scale_mid = lax.rsqrt(square / width + EPS)

    m_list = list(lax.optimization_barrier((*m_list, downs[1], downs[2])))[:rows]
    pairs = [slice(at, at + 2) for at in range(0, rows, 2)]
    found = [activate(feat, m_list[pair], m_others[pair], gates, ups) for pair in pairs]
    hiddens = [f[0] for f in found]
    with jax.named_scope("grad_row"):
        g_own = after(g_own, hiddens[0])
        g_other = core_swap(g_own)
    parts, scaled_grads, held, down_parts = [None] * rows, [None] * len(pairs), hiddens, None
    for at in reversed(range(len(pairs))):
        with jax.named_scope("unit_grad"):
            _, slope_gate, slope_up, scale = found[at]
            gate_grad, up_grad, own, other = units_back(
                feat, starts[pairs[at]], g_own, g_other, after(slope_gate, *held), slope_up, scale, gates, ups, downs
            )
            scaled_grads[at] = gate_grad, up_grad
            low = own.astype(F32) + core_swap(other).astype(F32)
            parts[2 * at], parts[2 * at + 1] = low[:quarter], low[quarter:].astype(BF16)
        if down_parts is None:
            with jax.named_scope("down_grad"):
                down_parts = outer(
                    feat, "down_outer", starts, [g_own], [g_other], [after(h, parts[-1]) for h in hiddens], places
                )
            held = down_parts[:1]
    with jax.named_scope("unit_grad"):
        unit_grad = reduce_row(parts)
    with jax.named_scope("down_grad"):
        down_total = plane_second(plane_first(down_parts))
        down_blocks = give_back(down_total)

    unit_mid = middle * scale_mid
    dot_two = jnp.sum(unit_grad * unit_mid, axis=1, keepdims=True)
    dot_two = dot_two + core_swap(dot_two)
    middle_grad = g_part.astype(F32) + scale_mid * (unit_grad - unit_mid * (dot_two / width))

    d_low = after(middle_grad.astype(BF16), down_total)
    with jax.named_scope("feed"):
        pieces = spread(d_low)
        kept = [unfold(feat, "feed", [after(h, pieces[1])], downs) for h in hiddens]
        shares = jnp.zeros((rows * quarter, half), BF16)
        for pair, (own, other) in zip(pairs, kept):
            low = (own.astype(F32) + core_swap(other).astype(F32)).astype(BF16)
            for i in range(2):
                shares = lax.dynamic_update_slice_in_dim(
                    shares, low[i * quarter : (i + 1) * quarter], starts[pair.start + i] * quarter, 0
                )
        feed = lax.psum_scatter(after(shares, d_low), "row", scatter_dimension=0, tiled=True)
    gate_parts = outer(feat, "gate_outer", starts, m_list, m_others, [after(a, d_low) for a, _ in scaled_grads], places)
    up_parts = outer(feat, "up_outer", starts, m_list, m_others, [after(a, d_low) for _, a in scaled_grads], places)
    with jax.named_scope("middle_grad"):
        d_own = put_rows(
            pieces[:2] + [after(a, gate_parts[0], up_parts[0], shares) for a in pieces[2:]]
        )
        d_other = core_swap(d_own)
    mixed_grad = fold(feat, d_own, d_other, out_full)
    with jax.named_scope("gate_grad"):
        gate_middle = plane_first([after(a, d_own) for a in gate_parts])
    query_grad, key_grad, value_grad = attend_back(
        query, key, value, mixed, after(mixed_grad, *gate_middle), start_row, logs, cosine, front, back
    )
    with jax.named_scope("feed"):
        feed_low = (middle + after(feed, query_grad).astype(F32)).astype(BF16)
    with jax.named_scope("gate_grad"):
        gate_total = plane_second(gate_middle, query_grad)
        gate_blocks = give_back(gate_total)
    query_grad = after(query_grad, down_blocks, gate_total)
    heads_part, gain_dots = heads_outer(
        feat, x_own, x_other, d_own, d_other, query_grad, key_grad, value_grad, mixed, scale_one, qkv_full
    )
    with jax.named_scope("heads_grad"):
        heads_blocks = lax.psum_scatter(heads_part, "row", scatter_dimension=0, tiled=True)
    with jax.named_scope("up_grad"):
        up_total = plane_second(plane_first([after(a, gate_total, heads_part) for a in up_parts]))
        up_blocks = give_back(up_total)
    with jax.named_scope("block_out"):
        block_out = to_home(after(feed_low, up_total))
    with jax.named_scope("first_plane"):
        first_unit_grad = scatter_parts(
            *unfold(feat, "first_grad", [after(query_grad, heads_part), key_grad, value_grad], [qkv_full])
        )
    scale_first = token_part(scale_one, 0)
    unit_first = token_part(x_own, 0).astype(F32) * scale_first
    dot_one = jnp.sum(first_unit_grad * unit_first, axis=1, keepdims=True)
    dot_one = dot_one + core_swap(dot_one)
    with jax.named_scope("input_grad"):
        input_grad = to_home(
            (middle_grad + scale_first * (first_unit_grad - unit_first * (dot_one / width))).astype(BF16)
        )

    def row_dots(w, d):
        return jnp.sum(w.astype(F32) * d.astype(F32), axis=1)

    with jax.named_scope("gains"):
        dots = jnp.stack(
            [gain_dots[:, 0], row_dots(gates[0], gate_total) + row_dots(ups[0], up_total)]
        ).reshape(2, rows, 2, feat)
        dots = sum_cols(jnp.where(core == 0, dots, dots[:, :, ::-1])).transpose(1, 0, 2, 3)
        dots = dots.reshape(rows, 2, 2 * feat)
        mine = lax.dynamic_index_in_dim(dots, row, 0, False)
        for s in range(1, rows):
            mine = mine + row_swap(lax.dynamic_index_in_dim(dots, row ^ s, 0, False), s)
        first_gain_grad = mine[0] / gain_one[:, 0]
        second_gain_grad = mine[1] / gain_two[:, 0]
    (down_weight_grad,) = finish(cores, down_blocks, gain_two, 0)
    (gate_weight_grad,) = finish(cores, gate_blocks, gain_two, 1)
    (up_weight_grad,) = finish(cores, up_blocks, gain_two, 1)
    heads_blocks = after(
        heads_blocks, down_weight_grad, gate_weight_grad, up_weight_grad, second_gain_grad, input_grad
    )
    query_weight_grad, key_weight_grad, value_weight_grad, out_weight_grad = finish(
        cores, heads_blocks[None], gain_one, 3, 4
    )
    return (
        block_out,
        input_grad,
        query_weight_grad,
        key_weight_grad,
        value_weight_grad,
        out_weight_grad,
        gate_weight_grad,
        up_weight_grad,
        down_weight_grad,
        first_gain_grad,
        second_gain_grad,
    )


def solution(mesh):
    grid, line = P("row", "col"), P("row")
    return jax.shard_map(
        local,
        mesh=mesh,
        in_specs=(grid,) * 8 + (line,) * 4 + (grid,),
        out_specs=(grid,) * 9 + (line,) * 2,
        check_vma=False,
    )
```

```python
import functools
import math

import jax
import jax.numpy as jnp
from jax import lax
from jax.experimental import pallas as pl
from jax.experimental.pallas import tpu as pltpu
from jax.sharding import PartitionSpec as P

HEAD_DIM = 64
LANES = 128
EPS = 1e-05
ROPE_BASE = 130000.0
LOG2E = math.log2(math.e)
SCORE_SCALE = HEAD_DIM**-0.5
BF16 = jnp.bfloat16
F32 = jnp.float32
VMEM_BYTES = 56 * 1024 * 1024


def lasts(microseconds):
    return pl.CostEstimate(flops=int(microseconds * 1.15e9), bytes_accessed=1, transcendentals=0)


def nn(left, right):
    return lax.dot_general(left, right, (((1,), (0,)), ((), ())), preferred_element_type=F32)


def nt(left, right):
    return lax.dot_general(left, right, (((1,), (1,)), ((), ())), preferred_element_type=F32)


def tn(left, right):
    return lax.dot_general(left, right, (((0,), (0,)), ((), ())), preferred_element_type=F32)


def spin(values, cosine, sine_front, sine_back):
    half = HEAD_DIM // 2
    lanes = values.shape[-1]
    return (
        values * cosine
        + pltpu.roll(values, lanes - half, 1) * sine_front
        + pltpu.roll(values, half, 1) * sine_back
    )


def weave(own, other, feat):
    pieces = []
    for at in range(0, own.shape[1], feat):
        pieces += [own[:, at : at + feat], other[:, at : at + feat]]
    return jnp.concatenate(pieces, axis=1)


def norm_scale(values):
    wide = values.astype(F32)
    return lax.rsqrt(jnp.sum(wide * wide, axis=1, keepdims=True) / values.shape[1] + EPS)


def whole_spec(a):
    return pl.BlockSpec(a.shape, lambda i: (0,) * a.ndim, pipeline_mode=pl.Buffered(1))


def row_spec(block, a):
    return pl.BlockSpec((block, a.shape[1]), lambda i: (i, 0))


def project_kernel(feat, starts, own_ref, other_ref, *refs):
    weights, (cos_ref, front_ref, back_ref), outs = refs[:-7], refs[-7:-4], refs[-4:]
    scale = norm_scale(jnp.concatenate([own_ref[...], other_ref[...]], axis=1))
    outs[3][...] = scale
    heads = outs[0].shape[1]
    picks = [pl.ds(pl.multiple_of(starts[i] * feat, feat), feat) for i in range(len(weights))]
    values = jnp.concatenate([ref[:, pick] for pick in picks for ref in (own_ref, other_ref)], axis=1)
    times = heads // cos_ref.shape[1]
    cosine, front, back = (
        jnp.concatenate([ref[...]] * times, axis=1) for ref in (cos_ref, front_ref, back_ref)
    )
    for at, ref in enumerate(outs[:3]):
        columns = slice(at * heads, (at + 1) * heads)
        result = nn(values, jnp.concatenate([w[:, columns] for w in weights], axis=0)) * scale
        if at < 2:
            result = spin(result, cosine, front, back)
        ref[...] = result.astype(BF16)


def project(feat, starts, own, other, weights, cosine, front, back):
    tokens = own.shape[0]
    heads = weights[0].shape[1] // 3
    block = 256
    result = jax.ShapeDtypeStruct((tokens, heads), BF16)
    scale = jax.ShapeDtypeStruct((tokens, 1), F32)
    return pl.pallas_call(
        functools.partial(project_kernel, feat),
        grid=(tokens // block,),
        in_specs=[pl.BlockSpec(memory_space=pltpu.SMEM), row_spec(block, own), row_spec(block, other)]
        + [whole_spec(w) for w in weights]
        + [row_spec(block, cosine)] * 3,
        out_specs=[row_spec(block, result)] * 3 + [row_spec(block, scale)],
        out_shape=[result] * 3 + [scale],
        compiler_params=pltpu.CompilerParams(vmem_limit_bytes=40 * 1024 * 1024),
        cost_estimate=lasts(7),
        name="project",
    )(starts, own, other, *weights, cosine, front, back)


def unfold_kernel(feat, joined, *refs):
    own_ref, other_ref = refs[-2:]
    lefts, weights = refs[:joined], refs[joined:-2]
    left = jnp.concatenate([ref[...] for ref in lefts], axis=1)
    part = weights[0].shape[1]
    for at in range(0, own_ref.shape[1], feat):
        rows = slice(2 * at, 2 * (at + feat))
        total = None
        for i, weight in enumerate(weights):
            term = nt(left[:, i * part : (i + 1) * part], weight[rows, :])
            total = term if total is None else total + term
        own_ref[:, at : at + feat] = total[:, :feat].astype(BF16)
        other_ref[:, at : at + feat] = total[:, feat:].astype(BF16)


def unfold(feat, name, lefts, weights):
    tokens, half = lefts[0].shape[0], weights[0].shape[0] // 2
    block = 256
    result = jax.ShapeDtypeStruct((tokens, half), BF16)
    return pl.pallas_call(
        functools.partial(unfold_kernel, feat, len(lefts)),
        grid=(tokens // block,),
        in_specs=[row_spec(block, a) for a in lefts] + [whole_spec(w) for w in weights],
        out_specs=[row_spec(block, result)] * 2,
        out_shape=[result] * 2,
        compiler_params=pltpu.CompilerParams(vmem_limit_bytes=VMEM_BYTES),
        cost_estimate=lasts(6),
        name=name,
    )(*lefts, *weights)


def activate_kernel(feat, parts, count, *refs):
    m_owns, m_others, refs = refs[:parts], refs[parts : 2 * parts], refs[2 * parts :]
    sources, refs = refs[: 2 * count], refs[2 * count :]
    hidden_ref, gate_ref, up_ref, scale_ref, held, arrived = refs
    copies = [
        pltpu.make_async_copy(source, held.at[at], arrived.at[at]) for at, source in enumerate(sources)
    ]
    for copy in copies:
        copy.start()
    middle = jnp.concatenate(
        [weave(a[...], b[...], feat) for a, b in zip(m_owns, m_others)], axis=0
    )
    scale = norm_scale(middle)
    scale_ref[...] = scale
    part = hidden_ref.shape[1] // count
    for i in range(count):
        if i % 2 == 0:
            for copy in copies[2 * i : 2 * i + 4]:
                copy.wait()
        columns = slice(i * part, (i + 1) * part)
        gate = nn(middle, held[2 * i]) * scale
        up = nn(middle, held[2 * i + 1]) * scale
        sigmoid = 1.0 / (1.0 + jnp.exp(-gate))
        silu = gate * sigmoid
        hidden_ref[:, columns] = (silu * up).astype(BF16)
        gate_ref[:, columns] = (up * (sigmoid + silu * (1.0 - sigmoid))).astype(BF16)
        up_ref[:, columns] = silu.astype(BF16)


def activate(feat, m_owns, m_others, gates, ups):
    parts = len(m_owns)
    tokens = m_owns[0].shape[0]
    count, part = len(gates), gates[0].shape[1]
    hidden = jax.ShapeDtypeStruct((parts * tokens, count * part), BF16)
    weights = [w for two in zip(gates, ups) for w in two]
    vmem, anywhere = pl.BlockSpec(memory_space=pltpu.VMEM), pl.BlockSpec(memory_space=pl.ANY)
    return pl.pallas_call(
        functools.partial(activate_kernel, feat, parts, count),
        in_specs=[vmem] * (2 * parts) + [anywhere] * len(weights),
        out_specs=[vmem] * 4,
        out_shape=[hidden] * 3 + [jax.ShapeDtypeStruct((parts * tokens, 1), F32)],
        scratch_shapes=[
            pltpu.VMEM((len(weights),) + weights[0].shape, BF16),
            pltpu.SemaphoreType.DMA((len(weights),)),
        ],
        compiler_params=pltpu.CompilerParams(vmem_limit_bytes=36 * 1024 * 1024),
        cost_estimate=lasts(7.5),
        name="activate",
    )(*m_owns, *m_others, *weights)


def units_back_kernel(feat, parts, count, starts, *refs):
    g_sources, (gate_in, up_in, scale_in) = refs[:2], refs[2:5]
    sources, refs = refs[5 : 5 + 3 * count], refs[5 + 3 * count :]
    gate_ref, up_ref, own_ref, other_ref, held, arrived, g_held, g_arrived = refs
    tokens = own_ref.shape[0] // parts
    copies = [
        pltpu.make_async_copy(source, held.at[at], arrived.at[at]) for at, source in enumerate(sources)
    ]
    g_copies = [
        pltpu.make_async_copy(
            source.at[pl.ds(pl.multiple_of(starts[i] * tokens, tokens), tokens)],
            g_held.at[side, i],
            g_arrived.at[side, i],
        )
        for side, source in enumerate(g_sources)
        for i in range(parts)
    ]
    for copy in g_copies + copies:
        copy.start()
    for copy in g_copies + copies[:count]:
        copy.wait()
    grad = jnp.concatenate([weave(g_held[0, j], g_held[1, j], feat) for j in range(parts)], axis=0)
    scale = scale_in[...]
    part = gate_ref.shape[1] // count
    lefts = [], []
    for i in range(count):
        columns = slice(i * part, (i + 1) * part)
        hidden_grad = nn(grad, held[i])
        for side, (slope, out) in enumerate(((gate_in, gate_ref), (up_in, up_ref))):
            value = hidden_grad * slope[:, columns].astype(F32)
            out[:, columns] = (value * scale).astype(BF16)
            lefts[side].append(value.astype(BF16))
    left = jnp.concatenate(lefts[0] + lefts[1], axis=1)
    for copy in copies[count:]:
        copy.wait()
    for at in range(0, own_ref.shape[1], feat):
        rows = slice(2 * at, 2 * (at + feat))
        right = jnp.concatenate([held[i, rows, :] for i in range(count, 3 * count)], axis=1)
        total = nt(left, right)
        own_ref[:, at : at + feat] = total[:, :feat].astype(BF16)
        other_ref[:, at : at + feat] = total[:, feat:].astype(BF16)


def units_back(feat, starts, g_own, g_other, gate, up, scale, gates, ups, downs):
    tokens, half = gate.shape[0], g_own.shape[1]
    parts = starts.shape[0]
    count = len(gates)
    hidden = jax.ShapeDtypeStruct(gate.shape, BF16)
    share = jax.ShapeDtypeStruct((tokens, half), BF16)
    weights = downs + gates + ups
    vmem, anywhere = pl.BlockSpec(memory_space=pltpu.VMEM), pl.BlockSpec(memory_space=pl.ANY)
    return pl.pallas_call(
        functools.partial(units_back_kernel, feat, parts, count),
        in_specs=[pl.BlockSpec(memory_space=pltpu.SMEM)]
        + [anywhere] * 2
        + [vmem] * 3
        + [anywhere] * len(weights),
        out_specs=[vmem] * 4,
        out_shape=[hidden] * 2 + [share] * 2,
        scratch_shapes=[
            pltpu.VMEM((len(weights),) + weights[0].shape, BF16),
            pltpu.SemaphoreType.DMA((len(weights),)),
            pltpu.VMEM((2, parts, tokens // parts, half), BF16),
            pltpu.SemaphoreType.DMA((2, parts)),
        ],
        compiler_params=pltpu.CompilerParams(vmem_limit_bytes=40 * 1024 * 1024),
        cost_estimate=lasts(9.3),
        name="units_back",
    )(starts, g_own, g_other, gate, up, scale, *weights)


def outer_kernel(groups, count, starts, *refs):
    owns, others, rights = refs[:groups], refs[groups : 2 * groups], refs[2 * groups : len(refs) - count]
    outs = refs[len(refs) - count :]
    if groups == 1:
        tokens = owns[0].shape[0] // starts.shape[0]
        picks = [
            pl.ds(pl.multiple_of(starts[i] * tokens, tokens), tokens) for i in range(starts.shape[0])
        ]
        sides = [(owns[0][pick, :], others[0][pick, :]) for pick in picks]
    else:
        sides = [(own[...], other[...]) for own, other in zip(owns, others)]
    left = jnp.concatenate([jnp.concatenate(pair, axis=1) for pair in sides], axis=0)
    part = outs[0].shape[1]
    for i, out in enumerate(outs):
        columns = slice(i * part, (i + 1) * part)
        right = jnp.concatenate([ref[:, columns] for ref in rights], axis=0)
        out[...] = tn(left, right).astype(BF16)


def outer(feat, name, starts, owns, others, rights, count):
    half, columns = owns[0].shape[1], rights[0].shape[1]
    part = columns // count
    side = pl.BlockSpec((owns[0].shape[0], feat), lambda i: (0, i))
    return pl.pallas_call(
        functools.partial(outer_kernel, len(owns), count),
        grid=(half // feat,),
        in_specs=[pl.BlockSpec(memory_space=pltpu.SMEM)]
        + [side] * (2 * len(owns))
        + [whole_spec(a) for a in rights],
        out_specs=[pl.BlockSpec((2 * feat, part), lambda i: (i, 0))] * count,
        out_shape=[jax.ShapeDtypeStruct((2 * half, part), BF16)] * count,
        compiler_params=pltpu.CompilerParams(vmem_limit_bytes=40 * 1024 * 1024),
        cost_estimate=lasts(6.3),
        name=name,
    )(starts, *owns, *others, *rights)


def heads_outer_kernel(x_own, x_other, d_own, d_other, dq_ref, dk_ref, dv_ref, mixed_ref, scale_ref, weight_ref, out_ref, dot_ref):
    part = mixed_ref.shape[1]
    left = jnp.concatenate([x_own[...], x_other[...]], axis=1)
    dots = None
    for i, ref in enumerate((dq_ref, dk_ref, dv_ref)):
        columns = slice(i * part, (i + 1) * part)
        result = tn(left, (ref[...].astype(F32) * scale_ref[...]).astype(BF16))
        out_ref[:, columns] = result.astype(BF16)
        term = jnp.sum(result * weight_ref[:, columns].astype(F32), axis=1, keepdims=True)
        dots = term if dots is None else dots + term
    dot_ref[...] = dots
    left = jnp.concatenate([d_own[...], d_other[...]], axis=1)
    out_ref[:, 3 * part :] = tn(left, mixed_ref[...]).astype(BF16)


def heads_outer(feat, x_own, x_other, d_own, d_other, dq, dk, dv, mixed, scale, weight):
    tokens, half = x_own.shape
    part = mixed.shape[1]
    side = pl.BlockSpec((tokens, feat), lambda i: (0, i))
    return pl.pallas_call(
        heads_outer_kernel,
        grid=(half // feat,),
        in_specs=[side] * 4
        + [whole_spec(a) for a in (dq, dk, dv, mixed, scale)]
        + [row_spec(2 * feat, weight)],
        out_specs=[pl.BlockSpec((2 * feat, 4 * part), lambda i: (i, 0)), pl.BlockSpec((2 * feat, 1), lambda i: (i, 0))],
        out_shape=[
            jax.ShapeDtypeStruct((2 * half, 4 * part), BF16),
            jax.ShapeDtypeStruct((2 * half, 1), F32),
        ],
        compiler_params=pltpu.CompilerParams(vmem_limit_bytes=40 * 1024 * 1024),
        cost_estimate=lasts(9.4),
        name="heads_outer",
    )(x_own, x_other, d_own, d_other, dq, dk, dv, mixed, scale, weight)


def finish_kernel(scaled, core_ref, part_ref, gain_ref, *outs):
    feat = gain_ref.shape[0] // 2
    blocks, columns = part_ref.shape[0], part_ref.shape[2] // len(outs)
    for side in range(2):
        rows = slice(side * feat, (side + 1) * feat)
        start = pl.multiple_of(lax.rem(core_ref[0] + side, 2) * feat, feat)
        gain = gain_ref[rows, :]
        for block in range(blocks):
            for i, out in enumerate(outs):
                value = part_ref[block, pl.ds(start, feat), i * columns : (i + 1) * columns].astype(F32)
                at = block * columns
                out[rows, at : at + columns] = value * gain if i < scaled else value


def finish(core, part, gain, scaled, count=1):
    blocks, rows, columns = part.shape
    vmem = pl.BlockSpec(memory_space=pltpu.VMEM)
    result = jax.ShapeDtypeStruct((rows, blocks * columns // count), F32)
    return pl.pallas_call(
        functools.partial(finish_kernel, scaled),
        in_specs=[pl.BlockSpec(memory_space=pltpu.SMEM), vmem, vmem],
        out_specs=[vmem] * count,
        out_shape=[result] * count,
        compiler_params=pltpu.CompilerParams(vmem_limit_bytes=VMEM_BYTES),
        cost_estimate=lasts(2.8),
        name="finish",
    )(core, part, gain)


def fold_kernel(feat, own_ref, other_ref, weight_ref, out_ref):
    out_ref[...] = nn(weave(own_ref[...], other_ref[...], feat), weight_ref[...]).astype(BF16)


def fold(feat, own, other, weight):
    tokens = own.shape[0]
    block = 256
    result = jax.ShapeDtypeStruct((tokens, weight.shape[1]), BF16)
    return pl.pallas_call(
        functools.partial(fold_kernel, feat),
        grid=(tokens // block,),
        in_specs=[row_spec(block, own), row_spec(block, other), whole_spec(weight)],
        out_specs=row_spec(block, result),
        out_shape=result,
        compiler_params=pltpu.CompilerParams(vmem_limit_bytes=40 * 1024 * 1024),
        cost_estimate=lasts(3.5),
        name="fold",
    )(own, other, weight)


def allowed_block(start_row, key_base, query_base, keys, queries):
    key_index = key_base + lax.broadcasted_iota(jnp.int32, (keys, queries), 0)
    query_index = query_base + lax.broadcasted_iota(jnp.int32, (keys, queries), 1)
    return (key_index >= start_row) & (key_index <= query_index)


def attend_kernel(q_ref, k_ref, v_ref, start_ref, out_ref, log_ref):
    tokens = q_ref.shape[0]
    block = 256
    keys_all = k_ref[...]
    values_turned = v_ref[...].T
    lane = lax.broadcasted_iota(jnp.int32, (1, LANES), 1)
    sub = lax.broadcasted_iota(jnp.int32, (LANES, 1), 0)
    for place in range(tokens // block):
        rows = slice(place * block, (place + 1) * block)
        reach = (place + 1) * block
        query = q_ref[rows, :]
        start_row = start_ref[:, rows]
        allowed = allowed_block(start_row, 0, place * block, reach, block)
        parts = []
        for head in range(LANES // HEAD_DIM):
            mine = lane // HEAD_DIM == head
            query_head = query * mine.astype(BF16)
            scores = nt(keys_all[:reach], query_head) * (SCORE_SCALE * LOG2E)
            scores = jnp.where(allowed, scores, -1e30)
            peak = jnp.max(scores, axis=0, keepdims=True)
            raised = jnp.exp2(scores - peak)
            total = jnp.sum(raised, axis=0, keepdims=True)
            mixed = nn(values_turned[:, :reach], raised.astype(BF16)) / total
            parts.append(mixed)
            log_ref[0, head : head + 1, rows] = peak + jnp.log2(total)
        joined = jnp.where(sub // HEAD_DIM == 0, parts[0], parts[1])
        out_ref[rows, :] = joined.T.astype(BF16)


def attend(query, key, value, start_row):
    tokens, width = query.shape
    pairs = width // LANES
    column = pl.BlockSpec((tokens, LANES), lambda i: (0, i))
    return pl.pallas_call(
        attend_kernel,
        grid=(pairs,),
        in_specs=[column, column, column, pl.BlockSpec((1, tokens), lambda i: (0, 0))],
        out_specs=[column, pl.BlockSpec((1, 2, tokens), lambda i: (i, 0, 0))],
        out_shape=[
            jax.ShapeDtypeStruct((tokens, width), BF16),
            jax.ShapeDtypeStruct((pairs, 2, tokens), F32),
        ],
        compiler_params=pltpu.CompilerParams(vmem_limit_bytes=VMEM_BYTES),
        cost_estimate=lasts(10),
        name="attend",
    )(query, key, value, start_row)


def attend_back_kernel(
    q_ref, k_ref, v_ref, o_ref, do_ref, start_ref, log_ref, cos_ref, front_ref, back_ref,
    dq_ref, dk_ref, dv_ref, dq_acc,
):
    tokens = q_ref.shape[0]
    block = 256
    lane = lax.broadcasted_iota(jnp.int32, (1, LANES), 1)
    sub = lax.broadcasted_iota(jnp.int32, (LANES, 1), 0)
    query_all = q_ref[...]
    grad_all = do_ref[...]
    product = (o_ref[...].astype(F32) * grad_all.astype(F32)).T
    dots = [
        jnp.sum(product[head * HEAD_DIM : (head + 1) * HEAD_DIM], axis=0, keepdims=True)
        for head in range(LANES // HEAD_DIM)
    ]
    dq_acc[...] = jnp.zeros_like(dq_acc)
    for place in range(tokens // block):
        rows = slice(place * block, (place + 1) * block)
        tail = slice(place * block, tokens)
        keys = k_ref[rows, :]
        values = v_ref[rows, :]
        keys_turned = keys.T
        query = query_all[place * block :]
        grad = grad_all[place * block :]
        start_row = start_ref[:, tail]
        allowed = allowed_block(
            start_row, place * block, place * block, block, tokens - place * block
        )
        key_grad = jnp.zeros((block, LANES), F32)
        value_grad = jnp.zeros((block, LANES), F32)
        for head in range(LANES // HEAD_DIM):
            mine = lane // HEAD_DIM == head
            scores = nt(keys * mine.astype(BF16), query) * (SCORE_SCALE * LOG2E)
            weights = jnp.where(allowed, jnp.exp2(scores - log_ref[0, head : head + 1, tail]), 0.0)
            weight_grad = nt(values * mine.astype(BF16), grad)
            score_grad = (weights * (weight_grad - dots[head][:, place * block :])).astype(BF16)
            value_grad = jnp.where(mine, nn(weights.astype(BF16), grad), value_grad)
            key_grad = jnp.where(mine, nn(score_grad, query), key_grad)
            dq_acc[:, tail] += nn(
                keys_turned * (sub // HEAD_DIM == head).astype(BF16), score_grad
            )
        dv_ref[rows, :] = value_grad.astype(BF16)
        dk_ref[rows, :] = spin(
            key_grad * SCORE_SCALE, cos_ref[rows, :], -front_ref[rows, :], -back_ref[rows, :]
        ).astype(BF16)
    dq_ref[...] = spin(
        dq_acc[...].T * SCORE_SCALE, cos_ref[...], -front_ref[...], -back_ref[...]
    ).astype(BF16)


def attend_back(query, key, value, mixed, mixed_grad, start_row, logs, cosine, front, back):
    tokens, width = query.shape
    pairs = width // LANES
    column = pl.BlockSpec((tokens, LANES), lambda i: (0, i))
    table = pl.BlockSpec((tokens, LANES), lambda i: (0, 0))
    return pl.pallas_call(
        attend_back_kernel,
        grid=(pairs,),
        in_specs=[
            column, column, column, column, column,
            pl.BlockSpec((1, tokens), lambda i: (0, 0)),
            pl.BlockSpec((1, 2, tokens), lambda i: (i, 0, 0)),
            table, table, table,
        ],
        out_specs=[column, column, column],
        out_shape=[jax.ShapeDtypeStruct((tokens, width), BF16)] * 3,
        scratch_shapes=[pltpu.VMEM((LANES, tokens), F32)],
        compiler_params=pltpu.CompilerParams(vmem_limit_bytes=VMEM_BYTES),
        cost_estimate=lasts(11),
        name="attend_back",
    )(query, key, value, mixed, mixed_grad, start_row, logs, cosine, front, back)


def rope_tables(positions, width):
    half = HEAD_DIM // 2
    freqs = jnp.exp(jnp.arange(half, dtype=F32) * (-2.0 * math.log(ROPE_BASE) / HEAD_DIM))
    angles = positions.astype(F32)[:, None] * freqs[None, :]
    cosine, sine = jnp.cos(angles), jnp.sin(angles)
    zero = jnp.zeros_like(sine)
    heads = width // HEAD_DIM
    return (
        jnp.concatenate([cosine] * (2 * heads), axis=1),
        jnp.concatenate([-sine, zero] * heads, axis=1),
        jnp.concatenate([zero, sine] * heads, axis=1),
    )


def local(
    inputs,
    query_weight,
    key_weight,
    value_weight,
    out_weight,
    gate_weight,
    up_weight,
    down_weight,
    first_gain,
    second_gain,
    segment_ids,
    positions,
    out_grad,
):
    rows = lax.axis_size("row")
    cols = lax.axis_size("col")
    places = cols // 2
    row = lax.axis_index("row")
    col = lax.axis_index("col")
    core = col % 2
    place = col // 2
    tokens, feat = inputs.shape
    width = feat * cols
    half = width // 2
    quarter = tokens // places

    def core_swap(a):
        return lax.ppermute(a, "col", [(i, i ^ 1) for i in range(cols)])

    def plane_swap(a, step):
        return lax.ppermute(a, "col", [(i, i ^ (2 * step)) for i in range(cols)])

    def token_part(a, step):
        return lax.dynamic_slice_in_dim(a, (place ^ step) * quarter, quarter, 0)

    def feat_part(a, step):
        return lax.dynamic_slice_in_dim(a, (place ^ step) * feat, feat, 1)

    def own_first(w):
        return jnp.concatenate(
            [jnp.where(core == 0, w[:feat], w[feat:]), jnp.where(core == 0, w[feat:], w[:feat])], axis=0
        )

    def row_swap(a, step):
        return lax.ppermute(a, "row", [(i, i ^ step) for i in range(rows)])

    def gather_row(a, held=()):
        got, bit = {0: a}, rows // 2
        while bit:
            for step in list(got):
                came = row_swap(got[step], bit)
                got[step ^ bit] = after(came, *held) if 2 * bit == rows else came
            bit //= 2
        return [got[step] for step in range(rows)]

    def reduce_row(parts, bit):
        parts = list(parts)
        while bit < rows:
            for at in range(rows - 2 * bit, -1, -2 * bit):
                sent = row_swap(parts[at + bit].astype(BF16), bit)
                parts[at] = parts[at].astype(F32) + sent.astype(F32)
            bit *= 2
        return parts[0]

    def row_part(a, step):
        size = a.shape[0] // rows
        return lax.dynamic_slice_in_dim(a, (row ^ step) * size, size, 0)

    def after(value, *others):
        return lax.optimization_barrier((value,) + others)[0]

    def put_rows(pieces):
        whole = jnp.zeros((tokens,) + pieces[0].shape[1:], pieces[0].dtype)
        for step, piece in enumerate(pieces):
            whole = lax.dynamic_update_slice_in_dim(whole, piece, (place ^ step) * quarter, 0)
        return whole

    def put_feats(pieces):
        whole = jnp.zeros((pieces[0].shape[0], half), pieces[0].dtype)
        for step, piece in enumerate(pieces):
            whole = lax.dynamic_update_slice_in_dim(whole, piece, (place ^ step) * feat, 1)
        return whole

    def spread(a):
        return [a] + [plane_swap(a, step) for step in range(1, places)]

    def to_parts(a):
        return put_feats(
            [token_part(a, 0)] + [plane_swap(token_part(a, s), s) for s in range(1, places)]
        )

    def to_home(a):
        return put_rows([feat_part(a, 0)] + [plane_swap(feat_part(a, s), s) for s in range(1, places)])

    def sum_cols(a):
        step = 1
        while step < cols:
            a = a + lax.ppermute(a, "col", [(i, i ^ step) for i in range(cols)])
            step *= 2
        return a

    gain_one = first_gain.astype(F32)[:, None]
    gain_two = second_gain.astype(F32)[:, None]

    def scaled(w, gain):
        return own_first((w.astype(F32) * gain).astype(BF16))

    def cut(w):
        part = w.shape[1] // rows
        return jnp.stack([w[:, s * part : (s + 1) * part] for s in range(rows)])

    def exchange(pieces):
        got = lax.all_to_all(pieces, "row", split_axis=0, concat_axis=0, tiled=True)
        return got.reshape(width, pieces.shape[2])

    def spread_weights(whole):
        if places != 4:
            return spread(whole)
        first, second = plane_swap(whole, 1), plane_swap(whole, 2)
        return [
            whole,
            first,
            second,
            jnp.concatenate([plane_swap(second[:half], 1), plane_swap(first[half:], 2)], axis=0),
        ]

    def plane_first(pieces):
        if places != 4:
            return pieces
        top, bottom = plane_swap(pieces[3][:half], 1), plane_swap(pieces[3][half:], 2)
        to_second = jnp.concatenate(
            [(pieces[2][:half].astype(F32) + top.astype(F32)).astype(BF16), pieces[2][half:]], axis=0
        )
        to_first = jnp.concatenate(
            [pieces[1][:half], (pieces[1][half:].astype(F32) + bottom.astype(F32)).astype(BF16)], axis=0
        )
        return [pieces[0], to_first, to_second]

    def plane_second(pieces, *hold):
        total = pieces[0].astype(F32)
        for s, piece in enumerate(pieces[1:], 1):
            total = total + after(plane_swap(piece, s), *hold).astype(F32)
        return total.astype(BF16)

    def give_back(total):
        total = total.reshape(rows, 2 * feat, total.shape[1])
        return lax.all_to_all(total, "row", split_axis=0, concat_axis=0, tiled=True)

    def join_rows(pieces):
        size = pieces[0].shape[0]
        whole = jnp.zeros((rows * size, pieces[0].shape[1]), BF16)
        for step, piece in enumerate(pieces):
            whole = lax.dynamic_update_slice_in_dim(whole, piece, (row ^ step) * size, 0)
        return whole

    starts = jnp.stack([row ^ s for s in range(rows)])
    cores = core.reshape(1)

    with jax.named_scope("prepare"):
        cosine, front, back = rope_tables(positions, LANES)
        start_row = jnp.sum(
            (segment_ids[None, :] < segment_ids[:, None]).astype(jnp.int32), axis=1
        )[None, :]
        up_cut = cut(scaled(up_weight, gain_two))
        down_cut = cut(own_first(down_weight))
        out_block = own_first(out_weight)
    with jax.named_scope("inputs"):
        x_own = put_feats(spread(inputs))
        x_other = core_swap(x_own)
    with jax.named_scope("qkv_row"):
        qkv_list = gather_row(
            jnp.concatenate(
                [scaled(w, gain_one) for w in (query_weight, key_weight, value_weight)], axis=1
            ),
            (cosine, front, back, start_row, up_cut, down_cut, out_block),
        )
    with jax.named_scope("grad_plane"):
        g_part = to_parts(after(out_grad, *qkv_list))
    with jax.named_scope("gate_row"):
        gate_whole = exchange(cut(scaled(gate_weight, gain_two)))
    with jax.named_scope("out_row"):
        out_full = lax.all_gather(after(out_block, *qkv_list), "row", axis=0, tiled=True)
    with jax.named_scope("up_row"):
        up_whole = exchange(after(up_cut, gate_whole))
    with jax.named_scope("down_row"):
        down_whole = exchange(after(down_cut, up_whole))
    with jax.named_scope("gate_plane"):
        gates = spread_weights(gate_whole)
    query, key, value, scale_one = project(
        feat, starts, x_own, x_other, qkv_list, cosine, front, back
    )
    qkv_full = join_rows([after(a, query) for a in qkv_list])
    mixed, logs = attend(after(query, gates[1], gates[2], up_whole), key, value, start_row)
    with jax.named_scope("grad_row"):
        g_own = lax.all_gather(after(g_part, mixed), "row", axis=0, tiled=True)
    with jax.named_scope("up_plane"):
        ups = spread_weights(up_whole)
    mixed = after(mixed, gates[3], ups[1], ups[2], down_whole)

    def join_cores(own, other):
        return (own.astype(F32) + core_swap(other).astype(F32)).astype(BF16)

    def scatter_parts(low):
        total = token_part(low, 0).astype(F32)
        for s in range(1, places):
            total = total + plane_swap(token_part(low, s), s).astype(F32)
        return total

    with jax.named_scope("mix_plane"):
        own, other = unfold(feat, "mix", [mixed], [out_full])
        middle = token_part(x_own, 0).astype(F32) + scatter_parts(join_cores(after(own, ups[3]), other))
    middle_low = middle.astype(BF16)
    with jax.named_scope("middle_row"):
        m_list = gather_row(middle_low)
        m_others = [core_swap(m) for m in m_list]
    with jax.named_scope("down_plane"):
        downs = spread_weights(down_whole)
    square = jnp.sum(middle * middle, axis=1, keepdims=True)
    square = square + core_swap(square)
    scale_mid = lax.rsqrt(square / width + EPS)

    m_list = list(lax.optimization_barrier(tuple(m_list)))
    pairs = [slice(at, at + 2) for at in range(0, rows, 2)]
    found = [
        activate(feat, [after(a, *(downs[1:3] if pair.start else ())) for a in m_list[pair]], m_others[pair], gates, ups)
        for pair in pairs
    ]
    hiddens = [f[0] for f in found]
    with jax.named_scope("grad_row"):
        g_own = after(g_own, hiddens[0])
        g_other = core_swap(g_own)
    parts, scaled_grads, held, down_parts = [None] * rows, [None] * len(pairs), hiddens, None
    for at in reversed(range(len(pairs))):
        with jax.named_scope("unit_grad"):
            _, slope_gate, slope_up, scale = found[at]
            gate_grad, up_grad, own, other = units_back(
                feat, starts[pairs[at]], g_own, g_other, after(slope_gate, *held), slope_up, scale, gates, ups, downs
            )
            scaled_grads[at] = gate_grad, up_grad
            low = own.astype(F32) + core_swap(other).astype(F32)
            sent = low[quarter:].astype(BF16)
            parts[2 * at] = low[:quarter] + row_swap(sent, 1).astype(F32)
        if down_parts is None:
            with jax.named_scope("down_grad"):
                down_parts = outer(
                    feat, "down_outer", starts, [g_own], [g_other], [after(h, sent) for h in hiddens], places
                )
            held = down_parts[:1]
        held = *held, parts[2 * at].astype(BF16)
    with jax.named_scope("unit_grad"):
        unit_grad = reduce_row(parts, 2)
    with jax.named_scope("down_grad"):
        down_total = plane_second(plane_first(down_parts))
        down_blocks = give_back(down_total)

    unit_mid = middle * scale_mid
    dot_two = jnp.sum(unit_grad * unit_mid, axis=1, keepdims=True)
    dot_two = dot_two + core_swap(dot_two)
    middle_grad = g_part.astype(F32) + scale_mid * (unit_grad - unit_mid * (dot_two / width))

    d_low = after(middle_grad.astype(BF16), down_total)
    with jax.named_scope("feed"):
        pieces = spread(d_low)
        kept = [unfold(feat, "feed", [after(h, pieces[1])], downs) for h in hiddens]
        shares = jnp.zeros((rows * quarter, half), BF16)
        for pair, (own, other) in zip(pairs, kept):
            low = (own.astype(F32) + core_swap(other).astype(F32)).astype(BF16)
            for i in range(2):
                shares = lax.dynamic_update_slice_in_dim(
                    shares, low[i * quarter : (i + 1) * quarter], starts[pair.start + i] * quarter, 0
                )
        feed = lax.psum_scatter(after(shares, d_low), "row", scatter_dimension=0, tiled=True)
    gate_parts = outer(feat, "gate_outer", starts, m_list, m_others, [after(a, d_low) for a, _ in scaled_grads], places)
    up_parts = outer(feat, "up_outer", starts, m_list, m_others, [after(a, d_low) for _, a in scaled_grads], places)
    with jax.named_scope("middle_grad"):
        d_own = put_rows(
            pieces[:2] + [after(a, gate_parts[0], up_parts[0], shares) for a in pieces[2:]]
        )
        d_other = core_swap(d_own)
    mixed_grad = fold(feat, d_own, d_other, out_full)
    with jax.named_scope("gate_grad"):
        gate_middle = plane_first([after(a, d_own) for a in gate_parts])
    query_grad, key_grad, value_grad = attend_back(
        query, key, value, mixed, after(mixed_grad, *gate_middle), start_row, logs, cosine, front, back
    )
    with jax.named_scope("feed"):
        feed_low = (middle + after(feed, query_grad).astype(F32)).astype(BF16)
    with jax.named_scope("gate_grad"):
        gate_total = plane_second(gate_middle, query_grad)
        gate_blocks = give_back(gate_total)
    query_grad = after(query_grad, down_blocks, gate_total)
    heads_part, gain_dots = heads_outer(
        feat, x_own, x_other, d_own, d_other, query_grad, key_grad, value_grad, mixed, scale_one, qkv_full
    )
    with jax.named_scope("heads_grad"):
        heads_blocks = lax.psum_scatter(heads_part, "row", scatter_dimension=0, tiled=True)
    with jax.named_scope("first_plane"):
        first_low = join_cores(
            *unfold(feat, "first_grad", [after(query_grad, heads_part), key_grad, value_grad], [qkv_full])
        )
        first_unit_grad = scatter_parts(first_low)
    with jax.named_scope("up_grad"):
        up_total = plane_second(plane_first([after(a, gate_total, first_low) for a in up_parts]))
        up_blocks = give_back(up_total)
    with jax.named_scope("block_out"):
        block_out = to_home(after(feed_low, up_total))
    scale_first = token_part(scale_one, 0)
    unit_first = token_part(x_own, 0).astype(F32) * scale_first
    dot_one = jnp.sum(first_unit_grad * unit_first, axis=1, keepdims=True)
    dot_one = dot_one + core_swap(dot_one)
    with jax.named_scope("input_grad"):
        input_grad = to_home(
            (after(middle_grad, up_total) + scale_first * (first_unit_grad - unit_first * (dot_one / width))).astype(BF16)
        )

    def row_dots(w, d):
        return jnp.sum(w.astype(F32) * d.astype(F32), axis=1)

    with jax.named_scope("gains"):
        dots = jnp.stack(
            [gain_dots[:, 0], row_dots(gates[0], gate_total) + row_dots(ups[0], up_total)]
        ).reshape(2, rows, 2, feat)
        dots = sum_cols(jnp.where(core == 0, dots, dots[:, :, ::-1])).transpose(1, 0, 2, 3)
        dots = dots.reshape(rows, 2, 2 * feat)
        mine = lax.dynamic_index_in_dim(dots, row, 0, False)
        for s in range(1, rows):
            mine = mine + row_swap(lax.dynamic_index_in_dim(dots, row ^ s, 0, False), s)
        first_gain_grad = mine[0] / gain_one[:, 0]
        second_gain_grad = mine[1] / gain_two[:, 0]
    (down_weight_grad,) = finish(cores, down_blocks, gain_two, 0)
    (gate_weight_grad,) = finish(cores, gate_blocks, gain_two, 1)
    (up_weight_grad,) = finish(cores, up_blocks, gain_two, 1)
    heads_blocks = after(
        heads_blocks, down_weight_grad, gate_weight_grad, up_weight_grad, second_gain_grad, input_grad
    )
    query_weight_grad, key_weight_grad, value_weight_grad, out_weight_grad = finish(
        cores, heads_blocks[None], gain_one, 3, 4
    )
    return (
        block_out,
        input_grad,
        query_weight_grad,
        key_weight_grad,
        value_weight_grad,
        out_weight_grad,
        gate_weight_grad,
        up_weight_grad,
        down_weight_grad,
        first_gain_grad,
        second_gain_grad,
    )


def solution(mesh):
    grid, line = P("row", "col"), P("row")
    return jax.shard_map(
        local,
        mesh=mesh,
        in_specs=(grid,) * 8 + (line,) * 4 + (grid,),
        out_specs=(grid,) * 9 + (line,) * 2,
        check_vma=False,
    )
```

```python
import functools
import math

import jax
import jax.numpy as jnp
from jax import lax
from jax.experimental import pallas as pl
from jax.experimental.pallas import tpu as pltpu
from jax.sharding import PartitionSpec as P

HEAD_DIM = 64
LANES = 128
EPS = 1e-05
ROPE_BASE = 130000.0
LOG2E = math.log2(math.e)
SCORE_SCALE = HEAD_DIM**-0.5
BF16 = jnp.bfloat16
F32 = jnp.float32
VMEM_BYTES = 56 * 1024 * 1024


COST_RATE = 1e10
ORDER = {
    "gate_row": (),
    "up_row": (0,),
    "grad_plane": (0,),
    "out_row": (0,),
    "down_row": (0,),
    "grad_row": (),
    "project": (),
    "attend": (0, 2),
    "mix": (1, 3, 5),
    "mix_plane": (1,),
    "middle_row": (3,),
    "down_plane": (2,),
    "activate": (),
    "activate_more": (1,),
    "grad_core": (0, 1),
    "units_back": (0,),
    "units_back_more": (0, 2),
    "down_outer": (0,),
    "d_low": (1,),
    "feed": (0, 1),
    "feed_row": (0,),
    "gate_outer": (1,),
    "up_outer": (),
    "gate_plane_back": (0,),
    "fold": (0, 1, 2),
    "attend_back": (0,),
    "feed_end": (0,),
    "gate_second": (0,),
    "heads_outer": (0, 1),
    "first_grad": (0,),
    "up_plane_back": (3,),
    "block_out": (0, 3),
    "input_grad": (0,),
    "gain_dots": (),
}


def lasts(microseconds):
    return pl.CostEstimate(flops=int(microseconds * COST_RATE), bytes_accessed=1, transcendentals=0)


def nn(left, right):
    return lax.dot_general(left, right, (((1,), (0,)), ((), ())), preferred_element_type=F32)


def nt(left, right):
    return lax.dot_general(left, right, (((1,), (1,)), ((), ())), preferred_element_type=F32)


def tn(left, right):
    return lax.dot_general(left, right, (((0,), (0,)), ((), ())), preferred_element_type=F32)


def spin(values, cosine, sine_front, sine_back):
    half = HEAD_DIM // 2
    lanes = values.shape[-1]
    return (
        values * cosine
        + pltpu.roll(values, lanes - half, 1) * sine_front
        + pltpu.roll(values, half, 1) * sine_back
    )


def weave(own, other, feat):
    pieces = []
    for at in range(0, own.shape[1], feat):
        pieces += [own[:, at : at + feat], other[:, at : at + feat]]
    return jnp.concatenate(pieces, axis=1)


def norm_scale(values):
    wide = values.astype(F32)
    return lax.rsqrt(jnp.sum(wide * wide, axis=1, keepdims=True) / values.shape[1] + EPS)


def whole_spec(a):
    return pl.BlockSpec(a.shape, lambda i: (0,) * a.ndim, pipeline_mode=pl.Buffered(1))


def row_spec(block, a):
    return pl.BlockSpec((block, a.shape[1]), lambda i: (i, 0))


def project_kernel(feat, own_ref, other_ref, weight_ref, cos_ref, front_ref, back_ref, *outs):
    values = weave(own_ref[...], other_ref[...], feat)
    scale = norm_scale(values)
    outs[3][...] = scale
    heads = outs[0].shape[1]
    times = heads // cos_ref.shape[1]
    cosine, front, back = (
        jnp.concatenate([ref[...]] * times, axis=1) for ref in (cos_ref, front_ref, back_ref)
    )
    for at, ref in enumerate(outs[:3]):
        result = nn(values, weight_ref[:, at * heads : (at + 1) * heads]) * scale
        if at < 2:
            result = spin(result, cosine, front, back)
        ref[...] = result.astype(BF16)


def project(feat, own, other, weight, cosine, front, back):
    tokens = own.shape[0]
    heads = weight.shape[1] // 3
    block = 256
    result = jax.ShapeDtypeStruct((tokens, heads), BF16)
    scale = jax.ShapeDtypeStruct((tokens, 1), F32)
    return pl.pallas_call(
        functools.partial(project_kernel, feat),
        grid=(tokens // block,),
        in_specs=[row_spec(block, own), row_spec(block, other), whole_spec(weight)]
        + [row_spec(block, cosine)] * 3,
        out_specs=[row_spec(block, result)] * 3 + [row_spec(block, scale)],
        out_shape=[result] * 3 + [scale],
        compiler_params=pltpu.CompilerParams(vmem_limit_bytes=40 * 1024 * 1024),
        cost_estimate=lasts(7),
        name="project",
    )(own, other, weight, cosine, front, back)


def unfold_kernel(feat, joined, *refs):
    own_ref, other_ref = refs[-2:]
    lefts, weights = refs[:joined], refs[joined:-2]
    left = jnp.concatenate([ref[...] for ref in lefts], axis=1)
    part = weights[0].shape[1]
    for at in range(0, own_ref.shape[1], feat):
        rows = slice(2 * at, 2 * (at + feat))
        total = None
        for i, weight in enumerate(weights):
            term = nt(left[:, i * part : (i + 1) * part], weight[rows, :])
            total = term if total is None else total + term
        own_ref[:, at : at + feat] = total[:, :feat].astype(BF16)
        other_ref[:, at : at + feat] = total[:, feat:].astype(BF16)


def unfold(feat, name, lefts, weights):
    tokens, half = lefts[0].shape[0], weights[0].shape[0] // 2
    block = 256
    result = jax.ShapeDtypeStruct((tokens, half), BF16)
    return pl.pallas_call(
        functools.partial(unfold_kernel, feat, len(lefts)),
        grid=(tokens // block,),
        in_specs=[row_spec(block, a) for a in lefts] + [whole_spec(w) for w in weights],
        out_specs=[row_spec(block, result)] * 2,
        out_shape=[result] * 2,
        compiler_params=pltpu.CompilerParams(vmem_limit_bytes=VMEM_BYTES),
        cost_estimate=lasts(6),
        name=name,
    )(*lefts, *weights)


def activate_kernel(feat, parts, count, *refs):
    m_owns, m_others, refs = refs[:parts], refs[parts : 2 * parts], refs[2 * parts :]
    sources, refs = refs[: 2 * count], refs[2 * count :]
    hidden_ref, gate_ref, up_ref, scale_ref, held, arrived = refs
    copies = [
        pltpu.make_async_copy(source, held.at[at], arrived.at[at]) for at, source in enumerate(sources)
    ]
    for copy in copies:
        copy.start()
    middle = jnp.concatenate(
        [weave(a[...], b[...], feat) for a, b in zip(m_owns, m_others)], axis=0
    )
    scale = norm_scale(middle)
    scale_ref[...] = scale
    part = hidden_ref.shape[1] // count
    for i in range(count):
        if i % 2 == 0:
            for copy in copies[2 * i : 2 * i + 4]:
                copy.wait()
        columns = slice(i * part, (i + 1) * part)
        gate = nn(middle, held[2 * i]) * scale
        up = nn(middle, held[2 * i + 1]) * scale
        sigmoid = 1.0 / (1.0 + jnp.exp(-gate))
        silu = gate * sigmoid
        hidden_ref[:, columns] = (silu * up).astype(BF16)
        gate_ref[:, columns] = (up * (sigmoid + silu * (1.0 - sigmoid))).astype(BF16)
        up_ref[:, columns] = silu.astype(BF16)


def activate(feat, m_owns, m_others, gates, ups):
    parts = len(m_owns)
    tokens = m_owns[0].shape[0]
    count, part = len(gates), gates[0].shape[1]
    hidden = jax.ShapeDtypeStruct((parts * tokens, count * part), BF16)
    weights = [w for two in zip(gates, ups) for w in two]
    vmem, anywhere = pl.BlockSpec(memory_space=pltpu.VMEM), pl.BlockSpec(memory_space=pl.ANY)
    return pl.pallas_call(
        functools.partial(activate_kernel, feat, parts, count),
        in_specs=[vmem] * (2 * parts) + [anywhere] * len(weights),
        out_specs=[vmem] * 4,
        out_shape=[hidden] * 3 + [jax.ShapeDtypeStruct((parts * tokens, 1), F32)],
        scratch_shapes=[
            pltpu.VMEM((len(weights),) + weights[0].shape, BF16),
            pltpu.SemaphoreType.DMA((len(weights),)),
        ],
        compiler_params=pltpu.CompilerParams(vmem_limit_bytes=36 * 1024 * 1024),
        cost_estimate=lasts(7.5),
        name="activate",
    )(*m_owns, *m_others, *weights)


def units_back_kernel(feat, parts, count, starts, *refs):
    g_sources, (gate_in, up_in, scale_in) = refs[:2], refs[2:5]
    sources, refs = refs[5 : 5 + 3 * count], refs[5 + 3 * count :]
    gate_ref, up_ref, own_ref, other_ref, held, arrived, g_held, g_arrived = refs
    tokens = own_ref.shape[0] // parts
    copies = [
        pltpu.make_async_copy(source, held.at[at], arrived.at[at]) for at, source in enumerate(sources)
    ]
    g_copies = [
        pltpu.make_async_copy(
            source.at[pl.ds(pl.multiple_of(starts[i] * tokens, tokens), tokens)],
            g_held.at[side, i],
            g_arrived.at[side, i],
        )
        for side, source in enumerate(g_sources)
        for i in range(parts)
    ]
    for copy in g_copies + copies:
        copy.start()
    for copy in g_copies + copies[:count]:
        copy.wait()
    grad = jnp.concatenate([weave(g_held[0, j], g_held[1, j], feat) for j in range(parts)], axis=0)
    scale = scale_in[...]
    part = gate_ref.shape[1] // count
    lefts = [], []
    for i in range(count):
        columns = slice(i * part, (i + 1) * part)
        hidden_grad = nn(grad, held[i])
        for side, (slope, out) in enumerate(((gate_in, gate_ref), (up_in, up_ref))):
            value = hidden_grad * slope[:, columns].astype(F32)
            out[:, columns] = (value * scale).astype(BF16)
            lefts[side].append(value.astype(BF16))
    left = jnp.concatenate(lefts[0] + lefts[1], axis=1)
    for copy in copies[count:]:
        copy.wait()
    for at in range(0, own_ref.shape[1], feat):
        rows = slice(2 * at, 2 * (at + feat))
        right = jnp.concatenate([held[i, rows, :] for i in range(count, 3 * count)], axis=1)
        total = nt(left, right)
        own_ref[:, at : at + feat] = total[:, :feat].astype(BF16)
        other_ref[:, at : at + feat] = total[:, feat:].astype(BF16)


def units_back(feat, starts, g_own, g_other, gate, up, scale, gates, ups, downs):
    tokens, half = gate.shape[0], g_own.shape[1]
    parts = starts.shape[0]
    count = len(gates)
    hidden = jax.ShapeDtypeStruct(gate.shape, BF16)
    share = jax.ShapeDtypeStruct((tokens, half), BF16)
    weights = downs + gates + ups
    vmem, anywhere = pl.BlockSpec(memory_space=pltpu.VMEM), pl.BlockSpec(memory_space=pl.ANY)
    return pl.pallas_call(
        functools.partial(units_back_kernel, feat, parts, count),
        in_specs=[pl.BlockSpec(memory_space=pltpu.SMEM)]
        + [anywhere] * 2
        + [vmem] * 3
        + [anywhere] * len(weights),
        out_specs=[vmem] * 4,
        out_shape=[hidden] * 2 + [share] * 2,
        scratch_shapes=[
            pltpu.VMEM((len(weights),) + weights[0].shape, BF16),
            pltpu.SemaphoreType.DMA((len(weights),)),
            pltpu.VMEM((2, parts, tokens // parts, half), BF16),
            pltpu.SemaphoreType.DMA((2, parts)),
        ],
        compiler_params=pltpu.CompilerParams(vmem_limit_bytes=40 * 1024 * 1024),
        cost_estimate=lasts(9.3),
        name="units_back",
    )(starts, g_own, g_other, gate, up, scale, *weights)


def outer_kernel(groups, count, starts, *refs):
    owns, others, rights = refs[:groups], refs[groups : 2 * groups], refs[2 * groups : len(refs) - count]
    outs = refs[len(refs) - count :]
    if groups == 1:
        tokens = owns[0].shape[0] // starts.shape[0]
        picks = [
            pl.ds(pl.multiple_of(starts[i] * tokens, tokens), tokens) for i in range(starts.shape[0])
        ]
        sides = [(owns[0][pick, :], others[0][pick, :]) for pick in picks]
    else:
        sides = [(own[...], other[...]) for own, other in zip(owns, others)]
    left = jnp.concatenate([jnp.concatenate(pair, axis=1) for pair in sides], axis=0)
    part = outs[0].shape[1]
    for i, out in enumerate(outs):
        columns = slice(i * part, (i + 1) * part)
        right = jnp.concatenate([ref[:, columns] for ref in rights], axis=0)
        out[...] = tn(left, right).astype(BF16)


def outer(feat, name, starts, owns, others, rights, count):
    half, columns = owns[0].shape[1], rights[0].shape[1]
    part = columns // count
    side = pl.BlockSpec((owns[0].shape[0], feat), lambda i: (0, i))
    return pl.pallas_call(
        functools.partial(outer_kernel, len(owns), count),
        grid=(half // feat,),
        in_specs=[pl.BlockSpec(memory_space=pltpu.SMEM)]
        + [side] * (2 * len(owns))
        + [whole_spec(a) for a in rights],
        out_specs=[pl.BlockSpec((2 * feat, part), lambda i: (i, 0))] * count,
        out_shape=[jax.ShapeDtypeStruct((2 * half, part), BF16)] * count,
        compiler_params=pltpu.CompilerParams(vmem_limit_bytes=40 * 1024 * 1024),
        cost_estimate=lasts(6.3),
        name=name,
    )(starts, *owns, *others, *rights)


def heads_outer_kernel(core_ref, x_own, x_other, parts_ref, dq_ref, dk_ref, dv_ref, mixed_ref, scale_ref, weight_ref, out_ref, dot_ref):
    part = mixed_ref.shape[1]
    left = jnp.concatenate([x_own[...], x_other[...]], axis=1)
    dots = None
    for i, ref in enumerate((dq_ref, dk_ref, dv_ref)):
        columns = slice(i * part, (i + 1) * part)
        result = tn(left, (ref[...].astype(F32) * scale_ref[...]).astype(BF16))
        out_ref[:, columns] = result.astype(BF16)
        term = jnp.sum(result * weight_ref[:, columns].astype(F32), axis=1, keepdims=True)
        dots = term if dots is None else dots + term
    dot_ref[...] = dots
    core = core_ref[0]
    left = jnp.concatenate(
        [
            jnp.concatenate([parts_ref[2 * i + core], parts_ref[2 * i + 1 - core]], axis=1)
            for i in range(parts_ref.shape[0] // 2)
        ],
        axis=0,
    )
    out_ref[:, 3 * part :] = tn(left, mixed_ref[...]).astype(BF16)


def heads_outer(feat, core, x_own, x_other, parts, dq, dk, dv, mixed, scale, weight):
    tokens, half = x_own.shape
    part = mixed.shape[1]
    side = pl.BlockSpec((tokens, feat), lambda i: (0, i))
    return pl.pallas_call(
        heads_outer_kernel,
        grid=(half // feat,),
        in_specs=[
            pl.BlockSpec(memory_space=pltpu.SMEM),
            side,
            side,
            pl.BlockSpec(parts.shape[:2] + (feat,), lambda i: (0, 0, i)),
        ]
        + [whole_spec(a) for a in (dq, dk, dv, mixed, scale)]
        + [row_spec(2 * feat, weight)],
        out_specs=[pl.BlockSpec((2 * feat, 4 * part), lambda i: (i, 0)), pl.BlockSpec((2 * feat, 1), lambda i: (i, 0))],
        out_shape=[
            jax.ShapeDtypeStruct((2 * half, 4 * part), BF16),
            jax.ShapeDtypeStruct((2 * half, 1), F32),
        ],
        compiler_params=pltpu.CompilerParams(vmem_limit_bytes=40 * 1024 * 1024),
        cost_estimate=lasts(9.4),
        name="heads_outer",
    )(core, x_own, x_other, parts, dq, dk, dv, mixed, scale, weight)


def finish_kernel(scaled, core_ref, part_ref, gain_ref, *outs):
    feat = gain_ref.shape[0] // 2
    blocks, columns = part_ref.shape[0], part_ref.shape[2] // len(outs)
    for side in range(2):
        rows = slice(side * feat, (side + 1) * feat)
        start = pl.multiple_of(lax.rem(core_ref[0] + side, 2) * feat, feat)
        gain = gain_ref[rows, :]
        for block in range(blocks):
            for i, out in enumerate(outs):
                value = part_ref[block, pl.ds(start, feat), i * columns : (i + 1) * columns].astype(F32)
                at = block * columns
                out[rows, at : at + columns] = value * gain if i < scaled else value


def finish(core, part, gain, scaled, count=1):
    blocks, rows, columns = part.shape
    vmem = pl.BlockSpec(memory_space=pltpu.VMEM)
    result = jax.ShapeDtypeStruct((rows, blocks * columns // count), F32)
    return pl.pallas_call(
        functools.partial(finish_kernel, scaled),
        in_specs=[pl.BlockSpec(memory_space=pltpu.SMEM), vmem, vmem],
        out_specs=[vmem] * count,
        out_shape=[result] * count,
        compiler_params=pltpu.CompilerParams(vmem_limit_bytes=VMEM_BYTES),
        cost_estimate=lasts(2.8),
        name="finish",
    )(core, part, gain)


def fold_kernel(feat, core_ref, parts_ref, weight_ref, out_ref):
    core = core_ref[0]
    values = weave(parts_ref[core], parts_ref[1 - core], feat)
    out_ref[...] = nn(values, weight_ref[...]).astype(BF16)


def fold(feat, core, parts, weight):
    count, tokens, half = parts.shape
    result = jax.ShapeDtypeStruct((count // 2 * tokens, weight.shape[1]), BF16)
    return pl.pallas_call(
        functools.partial(fold_kernel, feat),
        grid=(count // 2,),
        in_specs=[
            pl.BlockSpec(memory_space=pltpu.SMEM),
            pl.BlockSpec((2, tokens, half), lambda i: (i, 0, 0)),
            whole_spec(weight),
        ],
        out_specs=row_spec(tokens, result),
        out_shape=result,
        compiler_params=pltpu.CompilerParams(vmem_limit_bytes=40 * 1024 * 1024),
        cost_estimate=lasts(3.5),
        name="fold",
    )(core, parts, weight)


def allowed_block(start_row, key_base, query_base, keys, queries):
    key_index = key_base + lax.broadcasted_iota(jnp.int32, (keys, queries), 0)
    query_index = query_base + lax.broadcasted_iota(jnp.int32, (keys, queries), 1)
    return (key_index >= start_row) & (key_index <= query_index)


def attend_kernel(q_ref, k_ref, v_ref, start_ref, out_ref, log_ref):
    tokens = q_ref.shape[0]
    block = 256
    keys_all = k_ref[...]
    values_turned = v_ref[...].T
    lane = lax.broadcasted_iota(jnp.int32, (1, LANES), 1)
    sub = lax.broadcasted_iota(jnp.int32, (LANES, 1), 0)
    for place in range(tokens // block):
        rows = slice(place * block, (place + 1) * block)
        reach = (place + 1) * block
        query = q_ref[rows, :]
        start_row = start_ref[:, rows]
        allowed = allowed_block(start_row, 0, place * block, reach, block)
        parts = []
        for head in range(LANES // HEAD_DIM):
            mine = lane // HEAD_DIM == head
            query_head = query * mine.astype(BF16)
            scores = nt(keys_all[:reach], query_head) * (SCORE_SCALE * LOG2E)
            scores = jnp.where(allowed, scores, -1e30)
            peak = jnp.max(scores, axis=0, keepdims=True)
            raised = jnp.exp2(scores - peak)
            total = jnp.sum(raised, axis=0, keepdims=True)
            mixed = nn(values_turned[:, :reach], raised.astype(BF16)) / total
            parts.append(mixed)
            log_ref[0, head : head + 1, rows] = peak + jnp.log2(total)
        joined = jnp.where(sub // HEAD_DIM == 0, parts[0], parts[1])
        out_ref[rows, :] = joined.T.astype(BF16)


def attend(query, key, value, start_row):
    tokens, width = query.shape
    pairs = width // LANES
    column = pl.BlockSpec((tokens, LANES), lambda i: (0, i))
    return pl.pallas_call(
        attend_kernel,
        grid=(pairs,),
        in_specs=[column, column, column, pl.BlockSpec((1, tokens), lambda i: (0, 0))],
        out_specs=[column, pl.BlockSpec((1, 2, tokens), lambda i: (i, 0, 0))],
        out_shape=[
            jax.ShapeDtypeStruct((tokens, width), BF16),
            jax.ShapeDtypeStruct((pairs, 2, tokens), F32),
        ],
        compiler_params=pltpu.CompilerParams(vmem_limit_bytes=VMEM_BYTES),
        cost_estimate=lasts(10),
        name="attend",
    )(query, key, value, start_row)


def attend_back_kernel(
    q_ref, k_ref, v_ref, o_ref, do_ref, start_ref, log_ref, cos_ref, front_ref, back_ref,
    dq_ref, dk_ref, dv_ref, dq_acc,
):
    tokens = q_ref.shape[0]
    block = 256
    lane = lax.broadcasted_iota(jnp.int32, (1, LANES), 1)
    sub = lax.broadcasted_iota(jnp.int32, (LANES, 1), 0)
    query_all = q_ref[...]
    grad_all = do_ref[...]
    product = (o_ref[...].astype(F32) * grad_all.astype(F32)).T
    dots = [
        jnp.sum(product[head * HEAD_DIM : (head + 1) * HEAD_DIM], axis=0, keepdims=True)
        for head in range(LANES // HEAD_DIM)
    ]
    dq_acc[...] = jnp.zeros_like(dq_acc)
    for place in range(tokens // block):
        rows = slice(place * block, (place + 1) * block)
        tail = slice(place * block, tokens)
        keys = k_ref[rows, :]
        values = v_ref[rows, :]
        keys_turned = keys.T
        query = query_all[place * block :]
        grad = grad_all[place * block :]
        start_row = start_ref[:, tail]
        allowed = allowed_block(
            start_row, place * block, place * block, block, tokens - place * block
        )
        key_grad = jnp.zeros((block, LANES), F32)
        value_grad = jnp.zeros((block, LANES), F32)
        for head in range(LANES // HEAD_DIM):
            mine = lane // HEAD_DIM == head
            scores = nt(keys * mine.astype(BF16), query) * (SCORE_SCALE * LOG2E)
            weights = jnp.where(allowed, jnp.exp2(scores - log_ref[0, head : head + 1, tail]), 0.0)
            weight_grad = nt(values * mine.astype(BF16), grad)
            score_grad = (weights * (weight_grad - dots[head][:, place * block :])).astype(BF16)
            value_grad = jnp.where(mine, nn(weights.astype(BF16), grad), value_grad)
            key_grad = jnp.where(mine, nn(score_grad, query), key_grad)
            dq_acc[:, tail] += nn(
                keys_turned * (sub // HEAD_DIM == head).astype(BF16), score_grad
            )
        dv_ref[rows, :] = value_grad.astype(BF16)
        dk_ref[rows, :] = spin(
            key_grad * SCORE_SCALE, cos_ref[rows, :], -front_ref[rows, :], -back_ref[rows, :]
        ).astype(BF16)
    dq_ref[...] = spin(
        dq_acc[...].T * SCORE_SCALE, cos_ref[...], -front_ref[...], -back_ref[...]
    ).astype(BF16)


def attend_back(query, key, value, mixed, mixed_grad, start_row, logs, cosine, front, back):
    tokens, width = query.shape
    pairs = width // LANES
    column = pl.BlockSpec((tokens, LANES), lambda i: (0, i))
    table = pl.BlockSpec((tokens, LANES), lambda i: (0, 0))
    return pl.pallas_call(
        attend_back_kernel,
        grid=(pairs,),
        in_specs=[
            column, column, column, column, column,
            pl.BlockSpec((1, tokens), lambda i: (0, 0)),
            pl.BlockSpec((1, 2, tokens), lambda i: (i, 0, 0)),
            table, table, table,
        ],
        out_specs=[column, column, column],
        out_shape=[jax.ShapeDtypeStruct((tokens, width), BF16)] * 3,
        scratch_shapes=[pltpu.VMEM((LANES, tokens), F32)],
        compiler_params=pltpu.CompilerParams(vmem_limit_bytes=VMEM_BYTES),
        cost_estimate=lasts(11),
        name="attend_back",
    )(query, key, value, mixed, mixed_grad, start_row, logs, cosine, front, back)


def rope_tables(positions, width):
    half = HEAD_DIM // 2
    freqs = jnp.exp(jnp.arange(half, dtype=F32) * (-2.0 * math.log(ROPE_BASE) / HEAD_DIM))
    angles = positions.astype(F32)[:, None] * freqs[None, :]
    cosine, sine = jnp.cos(angles), jnp.sin(angles)
    zero = jnp.zeros_like(sine)
    heads = width // HEAD_DIM
    return (
        jnp.concatenate([cosine] * (2 * heads), axis=1),
        jnp.concatenate([-sine, zero] * heads, axis=1),
        jnp.concatenate([zero, sine] * heads, axis=1),
    )


def local(
    inputs,
    query_weight,
    key_weight,
    value_weight,
    out_weight,
    gate_weight,
    up_weight,
    down_weight,
    first_gain,
    second_gain,
    segment_ids,
    positions,
    out_grad,
):
    rows = lax.axis_size("row")
    cols = lax.axis_size("col")
    places = cols // 2
    row = lax.axis_index("row")
    col = lax.axis_index("col")
    core = col % 2
    place = col // 2
    tokens, feat = inputs.shape
    width = feat * cols
    half = width // 2
    quarter = tokens // places

    def core_swap(a):
        return lax.ppermute(a, "col", [(i, i ^ 1) for i in range(cols)])

    def plane_swap(a, step):
        return lax.ppermute(a, "col", [(i, i ^ (2 * step)) for i in range(cols)])

    def token_part(a, step):
        return lax.dynamic_slice_in_dim(a, (place ^ step) * quarter, quarter, 0)

    def feat_part(a, step):
        return lax.dynamic_slice_in_dim(a, (place ^ step) * feat, feat, 1)

    def own_first(w):
        return jnp.concatenate(
            [jnp.where(core == 0, w[:feat], w[feat:]), jnp.where(core == 0, w[feat:], w[:feat])], axis=0
        )

    def row_swap(a, step):
        return lax.ppermute(a, "row", [(i, i ^ step) for i in range(rows)])

    def gather_row(a):
        got, bit = {0: a}, rows // 2
        while bit:
            for step in list(got):
                got[step ^ bit] = row_swap(got[step], bit)
            bit //= 2
        return [got[step] for step in range(rows)]

    def reduce_row(parts, bit):
        parts = list(parts)
        while bit < rows:
            for at in range(rows - 2 * bit, -1, -2 * bit):
                sent = row_swap(parts[at + bit].astype(BF16), bit)
                parts[at] = parts[at].astype(F32) + sent.astype(F32)
            bit *= 2
        return parts[0]

    def row_part(a, step):
        size = a.shape[0] // rows
        return lax.dynamic_slice_in_dim(a, (row ^ step) * size, size, 0)

    def after(value, *others):
        return lax.optimization_barrier((value,) + others)[0]

    def dep(key, value, *groups):
        chosen = []
        for i in ORDER.get(key, ()):
            group = groups[i]
            chosen += list(group) if isinstance(group, (list, tuple)) else [group]
        return after(value, *chosen) if chosen else value

    def put_rows(pieces):
        whole = jnp.zeros((tokens,) + pieces[0].shape[1:], pieces[0].dtype)
        for step, piece in enumerate(pieces):
            whole = lax.dynamic_update_slice_in_dim(whole, piece, (place ^ step) * quarter, 0)
        return whole

    def put_feats(pieces):
        whole = jnp.zeros((pieces[0].shape[0], half), pieces[0].dtype)
        for step, piece in enumerate(pieces):
            whole = lax.dynamic_update_slice_in_dim(whole, piece, (place ^ step) * feat, 1)
        return whole

    def spread(a):
        return [a] + [plane_swap(a, step) for step in range(1, places)]

    def to_parts(a):
        return put_feats(
            [token_part(a, 0)] + [plane_swap(token_part(a, s), s) for s in range(1, places)]
        )

    def to_home(a):
        return put_rows([feat_part(a, 0)] + [plane_swap(feat_part(a, s), s) for s in range(1, places)])

    def sum_cols(a):
        step = 1
        while step < cols:
            a = a + lax.ppermute(a, "col", [(i, i ^ step) for i in range(cols)])
            step *= 2
        return a

    gain_one = first_gain.astype(F32)[:, None]
    gain_two = second_gain.astype(F32)[:, None]

    def scaled(w, gain):
        return own_first((w.astype(F32) * gain).astype(BF16))

    def cut(w):
        part = w.shape[1] // rows
        return jnp.stack([w[:, s * part : (s + 1) * part] for s in range(rows)])

    def exchange(pieces):
        got = lax.all_to_all(pieces, "row", split_axis=0, concat_axis=0, tiled=True)
        return got.reshape(width, pieces.shape[2])

    def spread_weights(whole):
        if places != 4:
            return spread(whole)
        first, second = plane_swap(whole, 1), plane_swap(whole, 2)
        return [
            whole,
            first,
            second,
            jnp.concatenate([plane_swap(second[:half], 1), plane_swap(first[half:], 2)], axis=0),
        ]

    def plane_first(pieces):
        if places != 4:
            return pieces
        top, bottom = plane_swap(pieces[3][:half], 1), plane_swap(pieces[3][half:], 2)
        to_second = jnp.concatenate(
            [(pieces[2][:half].astype(F32) + top.astype(F32)).astype(BF16), pieces[2][half:]], axis=0
        )
        to_first = jnp.concatenate(
            [pieces[1][:half], (pieces[1][half:].astype(F32) + bottom.astype(F32)).astype(BF16)], axis=0
        )
        return [pieces[0], to_first, to_second]

    def plane_second(pieces, *hold):
        total = pieces[0].astype(F32)
        for s, piece in enumerate(pieces[1:], 1):
            total = total + (after(plane_swap(piece, s), *hold) if hold else plane_swap(piece, s)).astype(F32)
        return total.astype(BF16)

    def give_back(total):
        total = total.reshape(rows, 2 * feat, total.shape[1])
        return lax.all_to_all(total, "row", split_axis=0, concat_axis=0, tiled=True)

    starts = jnp.stack([row ^ s for s in range(rows)])
    cores = core.reshape(1)

    with jax.named_scope("prepare"):
        cosine, front, back = rope_tables(positions, LANES)
        start_row = jnp.sum(
            (segment_ids[None, :] < segment_ids[:, None]).astype(jnp.int32), axis=1
        )[None, :]
        up_cut = cut(scaled(up_weight, gain_two))
        down_cut = cut(own_first(down_weight))
        out_block = own_first(out_weight)
    with jax.named_scope("inputs"):
        x_own = put_feats(spread(inputs))
        x_other = core_swap(x_own)
    with jax.named_scope("qkv_row"):
        qkv_full = lax.all_gather(
            jnp.concatenate(
                [scaled(w, gain_one) for w in (query_weight, key_weight, value_weight)], axis=1
            ),
            "row",
            axis=0,
            tiled=True,
        )
    with jax.named_scope("grad_plane"):
        g_part = to_parts(dep("grad_plane", out_grad, x_own, x_other))
    with jax.named_scope("gate_row"):
        gate_whole = exchange(dep("gate_row", cut(scaled(gate_weight, gain_two)), x_own))
        gate_whole = after(gate_whole, g_part, cosine, front, back, start_row, up_cut, down_cut, out_block)
    with jax.named_scope("up_row"):
        up_whole = exchange(dep("up_row", up_cut, gate_whole, x_other, qkv_full))
    with jax.named_scope("out_row"):
        out_full = lax.all_gather(dep("out_row", out_block, x_own, gate_whole), "row", axis=0, tiled=True)
    with jax.named_scope("down_row"):
        down_whole = exchange(dep("down_row", down_cut, up_whole, qkv_full, out_full, g_part))
    with jax.named_scope("grad_row"):
        g_own = lax.all_gather(dep("grad_row", g_part, gate_whole, qkv_full, up_whole, out_full), "row", axis=0, tiled=True)
    with jax.named_scope("gate_plane"):
        gates = spread_weights(gate_whole)
    with jax.named_scope("up_plane"):
        ups = spread_weights(up_whole)
    query, key, value, scale_one = project(
        feat, dep("project", x_own, gates[1:3], gates[3:], up_whole, g_part, ups[1:3]), x_other, qkv_full, cosine, front, back
    )
    mixed, logs = attend(
        dep("attend", query, gates[1:3], gates[3:], up_whole, g_part, ups[1:3], ups[3:], out_full, down_whole),
        key, value, start_row,
    )
    mixed_in = dep("mix", mixed, gates[1:3], gates[3:], up_whole, ups[1:3], ups[3:], down_whole, g_part)

    def join_cores(own, other):
        return (own.astype(F32) + core_swap(other).astype(F32)).astype(BF16)

    def scatter_parts(low):
        total = token_part(low, 0).astype(F32)
        for s in range(1, places):
            total = total + plane_swap(token_part(low, s), s).astype(F32)
        return total

    with jax.named_scope("mix_plane"):
        own, other = unfold(feat, "mix", [mixed_in], [out_full])
        middle = token_part(x_own, 0).astype(F32) + scatter_parts(join_cores(dep("mix_plane", own, ups[1:3], ups[3:], down_whole, gates[3:], g_part), other))
    middle_low = dep("middle_row", middle.astype(BF16), ups[1:3], ups[3:], down_whole, g_own)
    with jax.named_scope("middle_row"):
        m_list = gather_row(middle_low)
        m_others = [core_swap(m) for m in m_list]
    with jax.named_scope("down_plane"):
        downs = spread_weights(dep("down_plane", down_whole, ups[1:3], ups[3:], middle_low, m_list[1:3], mixed))
    square = jnp.sum(middle * middle, axis=1, keepdims=True)
    square = square + core_swap(square)
    scale_mid = lax.rsqrt(square / width + EPS)

    pairs = [slice(at, at + 2) for at in range(0, rows, 2)]
    found = []
    for pair in pairs:
        key_at = "activate_more" if pair.start else "activate"
        first = dep(key_at, m_list[pair.start], m_list, downs[1:3], downs[3:], g_own, ups)
        found.append(activate(feat, [first, m_list[pair.start + 1]], m_others[pair], gates, ups))
    hiddens = [f[0] for f in found]
    with jax.named_scope("grad_row"):
        g_own = dep("grad_core", g_own, m_others, hiddens[0], hiddens[-1])
        g_other = core_swap(g_own)
    parts, scaled_grads, down_parts = [None] * rows, [None] * len(pairs), None
    down_middle = None
    for at in reversed(range(len(pairs))):
        with jax.named_scope("unit_grad"):
            _, slope_gate, slope_up, scale = found[at]
            if down_parts is None:
                slope_gate = dep("units_back", slope_gate, hiddens, downs)
            else:
                slope_gate = dep("units_back_more", slope_gate, down_parts[:1], sent, low_kept, down_middle[1:])
            gate_grad, up_grad, own, other = units_back(
                feat, starts[pairs[at]], g_own, g_other, slope_gate, slope_up, scale, gates, ups, downs
            )
            scaled_grads[at] = gate_grad, up_grad
            low = own.astype(F32) + core_swap(other).astype(F32)
            sent = low[quarter:].astype(BF16)
            parts[2 * at] = low[:quarter] + row_swap(sent, 1).astype(F32)
        if down_parts is None:
            with jax.named_scope("down_grad"):
                down_parts = outer(
                    feat, "down_outer", starts, [g_own], [g_other], [dep("down_outer", h, sent, hiddens) for h in hiddens], places
                )
                down_middle = plane_first(down_parts)
        low_kept = parts[2 * at].astype(BF16)
    with jax.named_scope("unit_grad"):
        unit_grad = reduce_row(parts, 2)
    with jax.named_scope("down_grad"):
        down_total = plane_second(down_middle)
        down_blocks = give_back(down_total)

    unit_mid = middle * scale_mid
    dot_two = jnp.sum(unit_grad * unit_mid, axis=1, keepdims=True)
    dot_two = dot_two + core_swap(dot_two)
    middle_grad = g_part.astype(F32) + scale_mid * (unit_grad - unit_mid * (dot_two / width))

    d_low = dep("d_low", middle_grad.astype(BF16), down_middle[1:], down_total)
    with jax.named_scope("middle_grad"):
        d_parts = lax.all_gather(d_low, "col")
    with jax.named_scope("feed"):
        kept = [unfold(feat, "feed", [dep("feed", h, low_kept, d_low)], downs) for h in hiddens]
        shares = []
        for own, other in kept:
            low = dep("feed_row", (own.astype(F32) + core_swap(other).astype(F32)).astype(BF16), d_low)
            shares += [low[:quarter], low[quarter:]]
        sent = []
        for at in range(0, rows, 2):
            sent.append(shares[at].astype(F32) + row_swap(shares[at + 1], 1).astype(F32))
            shares[at] = sent[-1]
        feed = reduce_row(shares, 2)
    gate_parts = outer(feat, "gate_outer", starts, m_list, m_others, [dep("gate_outer", a, low_kept, d_low, [own for own, _ in kept]) for a, _ in scaled_grads], places)
    up_parts = outer(feat, "up_outer", starts, m_list, m_others, [dep("up_outer", a, low_kept, d_low, [own for own, _ in kept], gate_parts[:1]) for _, a in scaled_grads], places)
    with jax.named_scope("gate_grad"):
        gate_middle = plane_first([dep("gate_plane_back", a, d_low, d_parts) for a in gate_parts])
    mixed_grad = fold(feat, cores, dep("fold", d_parts, gate_parts[:1], up_parts[:1], sent, gate_middle[1:], down_total), out_full)
    query_grad, key_grad, value_grad = attend_back(
        query, key, value, mixed, dep("attend_back", mixed_grad, gate_middle[1:], down_blocks, feed), start_row, logs, cosine, front, back
    )
    with jax.named_scope("feed"):
        feed_low = (middle + dep("feed_end", feed, query_grad).astype(F32)).astype(BF16)
    with jax.named_scope("gate_grad"):
        gate_total = plane_second(gate_middle, *((query_grad,) if ORDER.get("gate_second") else ()))
        gate_blocks = give_back(gate_total)
    heads_in = dep("heads_outer", query_grad, down_blocks, gate_total, feed_low, gate_middle[1:])
    heads_part, gain_dots = heads_outer(
        feat, cores, x_own, x_other, d_parts, heads_in, key_grad, value_grad, mixed, scale_one, qkv_full
    )
    with jax.named_scope("heads_grad"):
        heads_blocks = lax.psum_scatter(heads_part, "row", scatter_dimension=0, tiled=True)
    with jax.named_scope("first_plane"):
        first_low = join_cores(
            *unfold(feat, "first_grad", [dep("first_grad", query_grad, heads_part, gate_total), key_grad, value_grad], [qkv_full])
        )
        first_unit_grad = scatter_parts(first_low)
    with jax.named_scope("up_grad"):
        up_total = plane_second(plane_first([dep("up_plane_back", a, gate_total, heads_part, first_low, gate_middle[1:]) for a in up_parts]))
        up_blocks = give_back(up_total)
    with jax.named_scope("block_out"):
        block_out = to_home(dep("block_out", feed_low, up_total, gate_total, heads_part, first_low))
    scale_first = token_part(scale_one, 0)
    unit_first = token_part(x_own, 0).astype(F32) * scale_first
    dot_one = jnp.sum(first_unit_grad * unit_first, axis=1, keepdims=True)
    dot_one = dot_one + core_swap(dot_one)
    with jax.named_scope("input_grad"):
        input_grad = to_home(
            (dep("input_grad", middle_grad, up_total, gate_blocks) + scale_first * (first_unit_grad - unit_first * (dot_one / width))).astype(BF16)
        )

    def row_dots(w, d):
        return jnp.sum(w.astype(F32) * d.astype(F32), axis=1)

    with jax.named_scope("gains"):
        dots = jnp.stack(
            [gain_dots[:, 0], row_dots(dep("gain_dots", gates[0], heads_part, up_total), gate_total) + row_dots(ups[0], up_total)]
        ).reshape(2, rows, 2, feat)
        dots = sum_cols(jnp.where(core == 0, dots, dots[:, :, ::-1])).transpose(1, 0, 2, 3)
        dots = dots.reshape(rows, 2, 2 * feat)
        mine = lax.dynamic_index_in_dim(dots, row, 0, False)
        for s in range(1, rows):
            mine = mine + row_swap(lax.dynamic_index_in_dim(dots, row ^ s, 0, False), s)
        first_gain_grad = mine[0] / gain_one[:, 0]
        second_gain_grad = mine[1] / gain_two[:, 0]
    (down_weight_grad,) = finish(cores, down_blocks, gain_two, 0)
    (gate_weight_grad,) = finish(cores, gate_blocks, gain_two, 1)
    (up_weight_grad,) = finish(cores, up_blocks, gain_two, 1)
    heads_blocks = after(
        heads_blocks, down_weight_grad, gate_weight_grad, up_weight_grad, second_gain_grad, input_grad, block_out
    )
    query_weight_grad, key_weight_grad, value_weight_grad, out_weight_grad = finish(
        cores, heads_blocks[None], gain_one, 3, 4
    )
    return (
        block_out,
        input_grad,
        query_weight_grad,
        key_weight_grad,
        value_weight_grad,
        out_weight_grad,
        gate_weight_grad,
        up_weight_grad,
        down_weight_grad,
        first_gain_grad,
        second_gain_grad,
    )


def solution(mesh):
    grid, line = P("row", "col"), P("row")
    return jax.shard_map(
        local,
        mesh=mesh,
        in_specs=(grid,) * 8 + (line,) * 4 + (grid,),
        out_specs=(grid,) * 9 + (line,) * 2,
        check_vma=False,
    )
```

```python
import functools
import math

import jax
import jax.numpy as jnp
from jax import lax
from jax.experimental import pallas as pl
from jax.experimental.pallas import tpu as pltpu
from jax.sharding import PartitionSpec as P

HEAD_DIM = 64
LANES = 128
EPS = 1e-05
ROPE_BASE = 130000.0
LOG2E = math.log2(math.e)
SCORE_SCALE = HEAD_DIM**-0.5
BF16 = jnp.bfloat16
F32 = jnp.float32
VMEM_BYTES = 56 * 1024 * 1024


COST_RATE = 1e10


def lasts(microseconds):
    return pl.CostEstimate(flops=int(microseconds * COST_RATE), bytes_accessed=1, transcendentals=0)


def nn(left, right):
    return lax.dot_general(left, right, (((1,), (0,)), ((), ())), preferred_element_type=F32)


def nt(left, right):
    return lax.dot_general(left, right, (((1,), (1,)), ((), ())), preferred_element_type=F32)


def tn(left, right):
    return lax.dot_general(left, right, (((0,), (0,)), ((), ())), preferred_element_type=F32)


def spin(values, cosine, sine_front, sine_back):
    half = HEAD_DIM // 2
    lanes = values.shape[-1]
    return (
        values * cosine
        + pltpu.roll(values, lanes - half, 1) * sine_front
        + pltpu.roll(values, half, 1) * sine_back
    )


def weave(own, other, feat):
    pieces = []
    for at in range(0, own.shape[1], feat):
        pieces += [own[:, at : at + feat], other[:, at : at + feat]]
    return jnp.concatenate(pieces, axis=1)


def norm_scale(values):
    wide = values.astype(F32)
    return lax.rsqrt(jnp.sum(wide * wide, axis=1, keepdims=True) / values.shape[1] + EPS)


def whole_spec(a):
    return pl.BlockSpec(a.shape, lambda i: (0,) * a.ndim, pipeline_mode=pl.Buffered(1))


def row_spec(block, a):
    return pl.BlockSpec((block, a.shape[1]), lambda i: (i, 0))


def project_kernel(feat, own_ref, other_ref, weight_ref, cos_ref, front_ref, back_ref, *outs):
    values = weave(own_ref[...], other_ref[...], feat)
    scale = norm_scale(values)
    outs[3][...] = scale
    heads = outs[0].shape[1]
    times = heads // cos_ref.shape[1]
    cosine, front, back = (
        jnp.concatenate([ref[...]] * times, axis=1) for ref in (cos_ref, front_ref, back_ref)
    )
    for at, ref in enumerate(outs[:3]):
        result = nn(values, weight_ref[:, at * heads : (at + 1) * heads]) * scale
        if at < 2:
            result = spin(result, cosine, front, back)
        ref[...] = result.astype(BF16)


def project(feat, own, other, weight, cosine, front, back):
    tokens = own.shape[0]
    heads = weight.shape[1] // 3
    block = 256
    result = jax.ShapeDtypeStruct((tokens, heads), BF16)
    scale = jax.ShapeDtypeStruct((tokens, 1), F32)
    return pl.pallas_call(
        functools.partial(project_kernel, feat),
        grid=(tokens // block,),
        in_specs=[row_spec(block, own), row_spec(block, other), whole_spec(weight)]
        + [row_spec(block, cosine)] * 3,
        out_specs=[row_spec(block, result)] * 3 + [row_spec(block, scale)],
        out_shape=[result] * 3 + [scale],
        compiler_params=pltpu.CompilerParams(vmem_limit_bytes=40 * 1024 * 1024),
        cost_estimate=lasts(7),
        name="project",
    )(own, other, weight, cosine, front, back)


def unfold_kernel(feat, joined, *refs):
    own_ref, other_ref = refs[-2:]
    lefts, weights = refs[:joined], refs[joined:-2]
    left = jnp.concatenate([ref[...] for ref in lefts], axis=1)
    part = weights[0].shape[1]
    for at in range(0, own_ref.shape[1], feat):
        rows = slice(2 * at, 2 * (at + feat))
        total = None
        for i, weight in enumerate(weights):
            term = nt(left[:, i * part : (i + 1) * part], weight[rows, :])
            total = term if total is None else total + term
        own_ref[:, at : at + feat] = total[:, :feat].astype(BF16)
        other_ref[:, at : at + feat] = total[:, feat:].astype(BF16)


def unfold(feat, name, lefts, weights):
    tokens, half = lefts[0].shape[0], weights[0].shape[0] // 2
    block = 256
    result = jax.ShapeDtypeStruct((tokens, half), BF16)
    return pl.pallas_call(
        functools.partial(unfold_kernel, feat, len(lefts)),
        grid=(tokens // block,),
        in_specs=[row_spec(block, a) for a in lefts] + [whole_spec(w) for w in weights],
        out_specs=[row_spec(block, result)] * 2,
        out_shape=[result] * 2,
        compiler_params=pltpu.CompilerParams(vmem_limit_bytes=VMEM_BYTES),
        cost_estimate=lasts(6),
        name=name,
    )(*lefts, *weights)


def activate_kernel(feat, parts, count, *refs):
    m_owns, m_others, refs = refs[:parts], refs[parts : 2 * parts], refs[2 * parts :]
    sources, refs = refs[: 2 * count], refs[2 * count :]
    hidden_ref, gate_ref, up_ref, scale_ref, held, arrived = refs
    copies = [
        pltpu.make_async_copy(source, held.at[at], arrived.at[at]) for at, source in enumerate(sources)
    ]
    for copy in copies:
        copy.start()
    middle = jnp.concatenate(
        [weave(a[...], b[...], feat) for a, b in zip(m_owns, m_others)], axis=0
    )
    scale = norm_scale(middle)
    scale_ref[...] = scale
    part = hidden_ref.shape[1] // count
    for i in range(count):
        if i % 2 == 0:
            for copy in copies[2 * i : 2 * i + 4]:
                copy.wait()
        columns = slice(i * part, (i + 1) * part)
        gate = nn(middle, held[2 * i]) * scale
        up = nn(middle, held[2 * i + 1]) * scale
        sigmoid = 1.0 / (1.0 + jnp.exp(-gate))
        silu = gate * sigmoid
        hidden_ref[:, columns] = (silu * up).astype(BF16)
        gate_ref[:, columns] = (up * (sigmoid + silu * (1.0 - sigmoid))).astype(BF16)
        up_ref[:, columns] = silu.astype(BF16)


def activate(feat, m_owns, m_others, gates, ups):
    parts = len(m_owns)
    tokens = m_owns[0].shape[0]
    count, part = len(gates), gates[0].shape[1]
    hidden = jax.ShapeDtypeStruct((parts * tokens, count * part), BF16)
    weights = [w for two in zip(gates, ups) for w in two]
    vmem, anywhere = pl.BlockSpec(memory_space=pltpu.VMEM), pl.BlockSpec(memory_space=pl.ANY)
    return pl.pallas_call(
        functools.partial(activate_kernel, feat, parts, count),
        in_specs=[vmem] * (2 * parts) + [anywhere] * len(weights),
        out_specs=[vmem] * 4,
        out_shape=[hidden] * 3 + [jax.ShapeDtypeStruct((parts * tokens, 1), F32)],
        scratch_shapes=[
            pltpu.VMEM((len(weights),) + weights[0].shape, BF16),
            pltpu.SemaphoreType.DMA((len(weights),)),
        ],
        compiler_params=pltpu.CompilerParams(vmem_limit_bytes=36 * 1024 * 1024),
        cost_estimate=lasts(7.5),
        name="activate",
    )(*m_owns, *m_others, *weights)


def units_back_kernel(feat, parts, count, starts, *refs):
    g_sources, (gate_in, up_in, scale_in) = refs[:2], refs[2:5]
    sources, refs = refs[5 : 5 + 3 * count], refs[5 + 3 * count :]
    gate_ref, up_ref, own_ref, other_ref, held, arrived, g_held, g_arrived = refs
    tokens = own_ref.shape[0] // parts
    copies = [
        pltpu.make_async_copy(source, held.at[at], arrived.at[at]) for at, source in enumerate(sources)
    ]
    g_copies = [
        pltpu.make_async_copy(
            source.at[pl.ds(pl.multiple_of(starts[i] * tokens, tokens), tokens)],
            g_held.at[side, i],
            g_arrived.at[side, i],
        )
        for side, source in enumerate(g_sources)
        for i in range(parts)
    ]
    for copy in g_copies + copies:
        copy.start()
    for copy in g_copies + copies[:count]:
        copy.wait()
    grad = jnp.concatenate([weave(g_held[0, j], g_held[1, j], feat) for j in range(parts)], axis=0)
    scale = scale_in[...]
    part = gate_ref.shape[1] // count
    lefts = [], []
    for i in range(count):
        columns = slice(i * part, (i + 1) * part)
        hidden_grad = nn(grad, held[i])
        for side, (slope, out) in enumerate(((gate_in, gate_ref), (up_in, up_ref))):
            value = hidden_grad * slope[:, columns].astype(F32)
            out[:, columns] = (value * scale).astype(BF16)
            lefts[side].append(value.astype(BF16))
    left = jnp.concatenate(lefts[0] + lefts[1], axis=1)
    for copy in copies[count:]:
        copy.wait()
    for at in range(0, own_ref.shape[1], feat):
        rows = slice(2 * at, 2 * (at + feat))
        right = jnp.concatenate([held[i, rows, :] for i in range(count, 3 * count)], axis=1)
        total = nt(left, right)
        own_ref[:, at : at + feat] = total[:, :feat].astype(BF16)
        other_ref[:, at : at + feat] = total[:, feat:].astype(BF16)


def units_back(feat, starts, g_own, g_other, gate, up, scale, gates, ups, downs):
    tokens, half = gate.shape[0], g_own.shape[1]
    parts = starts.shape[0]
    count = len(gates)
    hidden = jax.ShapeDtypeStruct(gate.shape, BF16)
    share = jax.ShapeDtypeStruct((tokens, half), BF16)
    weights = downs + gates + ups
    vmem, anywhere = pl.BlockSpec(memory_space=pltpu.VMEM), pl.BlockSpec(memory_space=pl.ANY)
    return pl.pallas_call(
        functools.partial(units_back_kernel, feat, parts, count),
        in_specs=[pl.BlockSpec(memory_space=pltpu.SMEM)]
        + [anywhere] * 2
        + [vmem] * 3
        + [anywhere] * len(weights),
        out_specs=[vmem] * 4,
        out_shape=[hidden] * 2 + [share] * 2,
        scratch_shapes=[
            pltpu.VMEM((len(weights),) + weights[0].shape, BF16),
            pltpu.SemaphoreType.DMA((len(weights),)),
            pltpu.VMEM((2, parts, tokens // parts, half), BF16),
            pltpu.SemaphoreType.DMA((2, parts)),
        ],
        compiler_params=pltpu.CompilerParams(vmem_limit_bytes=40 * 1024 * 1024),
        cost_estimate=lasts(9.3),
        name="units_back",
    )(starts, g_own, g_other, gate, up, scale, *weights)


def outer_kernel(groups, count, starts, *refs):
    owns, others, rights = refs[:groups], refs[groups : 2 * groups], refs[2 * groups : len(refs) - count]
    outs = refs[len(refs) - count :]
    if groups == 1:
        tokens = owns[0].shape[0] // starts.shape[0]
        picks = [
            pl.ds(pl.multiple_of(starts[i] * tokens, tokens), tokens) for i in range(starts.shape[0])
        ]
        sides = [(owns[0][pick, :], others[0][pick, :]) for pick in picks]
    else:
        sides = [(own[...], other[...]) for own, other in zip(owns, others)]
    left = jnp.concatenate([jnp.concatenate(pair, axis=1) for pair in sides], axis=0)
    part = outs[0].shape[1]
    for i, out in enumerate(outs):
        columns = slice(i * part, (i + 1) * part)
        right = jnp.concatenate([ref[:, columns] for ref in rights], axis=0)
        out[...] = tn(left, right).astype(BF16)


def outer(feat, name, starts, owns, others, rights, count):
    half, columns = owns[0].shape[1], rights[0].shape[1]
    part = columns // count
    side = pl.BlockSpec((owns[0].shape[0], feat), lambda i: (0, i))
    return pl.pallas_call(
        functools.partial(outer_kernel, len(owns), count),
        grid=(half // feat,),
        in_specs=[pl.BlockSpec(memory_space=pltpu.SMEM)]
        + [side] * (2 * len(owns))
        + [whole_spec(a) for a in rights],
        out_specs=[pl.BlockSpec((2 * feat, part), lambda i: (i, 0))] * count,
        out_shape=[jax.ShapeDtypeStruct((2 * half, part), BF16)] * count,
        compiler_params=pltpu.CompilerParams(vmem_limit_bytes=40 * 1024 * 1024),
        cost_estimate=lasts(6.3),
        name=name,
    )(starts, *owns, *others, *rights)


def heads_outer_kernel(core_ref, x_own, x_other, parts_ref, dq_ref, dk_ref, dv_ref, mixed_ref, scale_ref, weight_ref, out_ref, dot_ref):
    part = mixed_ref.shape[1]
    left = jnp.concatenate([x_own[...], x_other[...]], axis=1)
    dots = None
    for i, ref in enumerate((dq_ref, dk_ref, dv_ref)):
        columns = slice(i * part, (i + 1) * part)
        result = tn(left, (ref[...].astype(F32) * scale_ref[...]).astype(BF16))
        out_ref[:, columns] = result.astype(BF16)
        term = jnp.sum(result * weight_ref[:, columns].astype(F32), axis=1, keepdims=True)
        dots = term if dots is None else dots + term
    dot_ref[...] = dots
    core = core_ref[0]
    left = jnp.concatenate(
        [
            jnp.concatenate([parts_ref[2 * i + core], parts_ref[2 * i + 1 - core]], axis=1)
            for i in range(parts_ref.shape[0] // 2)
        ],
        axis=0,
    )
    out_ref[:, 3 * part :] = tn(left, mixed_ref[...]).astype(BF16)


def heads_outer(feat, core, x_own, x_other, parts, dq, dk, dv, mixed, scale, weight):
    tokens, half = x_own.shape
    part = mixed.shape[1]
    side = pl.BlockSpec((tokens, feat), lambda i: (0, i))
    return pl.pallas_call(
        heads_outer_kernel,
        grid=(half // feat,),
        in_specs=[
            pl.BlockSpec(memory_space=pltpu.SMEM),
            side,
            side,
            pl.BlockSpec(parts.shape[:2] + (feat,), lambda i: (0, 0, i)),
        ]
        + [whole_spec(a) for a in (dq, dk, dv, mixed, scale)]
        + [row_spec(2 * feat, weight)],
        out_specs=[pl.BlockSpec((2 * feat, 4 * part), lambda i: (i, 0)), pl.BlockSpec((2 * feat, 1), lambda i: (i, 0))],
        out_shape=[
            jax.ShapeDtypeStruct((2 * half, 4 * part), BF16),
            jax.ShapeDtypeStruct((2 * half, 1), F32),
        ],
        compiler_params=pltpu.CompilerParams(vmem_limit_bytes=40 * 1024 * 1024),
        cost_estimate=lasts(9.4),
        name="heads_outer",
    )(core, x_own, x_other, parts, dq, dk, dv, mixed, scale, weight)


def finish_kernel(scaled, core_ref, part_ref, gain_ref, *outs):
    feat = gain_ref.shape[0] // 2
    blocks, columns = part_ref.shape[0], part_ref.shape[2] // len(outs)
    for side in range(2):
        rows = slice(side * feat, (side + 1) * feat)
        start = pl.multiple_of(lax.rem(core_ref[0] + side, 2) * feat, feat)
        gain = gain_ref[rows, :]
        for block in range(blocks):
            for i, out in enumerate(outs):
                value = part_ref[block, pl.ds(start, feat), i * columns : (i + 1) * columns].astype(F32)
                at = block * columns
                out[rows, at : at + columns] = value * gain if i < scaled else value


def finish(core, part, gain, scaled, count=1):
    blocks, rows, columns = part.shape
    vmem = pl.BlockSpec(memory_space=pltpu.VMEM)
    result = jax.ShapeDtypeStruct((rows, blocks * columns // count), F32)
    return pl.pallas_call(
        functools.partial(finish_kernel, scaled),
        in_specs=[pl.BlockSpec(memory_space=pltpu.SMEM), vmem, vmem],
        out_specs=[vmem] * count,
        out_shape=[result] * count,
        compiler_params=pltpu.CompilerParams(vmem_limit_bytes=VMEM_BYTES),
        cost_estimate=lasts(2.8),
        name="finish",
    )(core, part, gain)


def fold_kernel(feat, core_ref, parts_ref, weight_ref, out_ref):
    core = core_ref[0]
    values = weave(parts_ref[core], parts_ref[1 - core], feat)
    out_ref[...] = nn(values, weight_ref[...]).astype(BF16)


def fold(feat, core, parts, weight):
    count, tokens, half = parts.shape
    result = jax.ShapeDtypeStruct((count // 2 * tokens, weight.shape[1]), BF16)
    return pl.pallas_call(
        functools.partial(fold_kernel, feat),
        grid=(count // 2,),
        in_specs=[
            pl.BlockSpec(memory_space=pltpu.SMEM),
            pl.BlockSpec((2, tokens, half), lambda i: (i, 0, 0)),
            whole_spec(weight),
        ],
        out_specs=row_spec(tokens, result),
        out_shape=result,
        compiler_params=pltpu.CompilerParams(vmem_limit_bytes=40 * 1024 * 1024),
        cost_estimate=lasts(3.5),
        name="fold",
    )(core, parts, weight)


def allowed_block(start_row, key_base, query_base, keys, queries):
    key_index = key_base + lax.broadcasted_iota(jnp.int32, (keys, queries), 0)
    query_index = query_base + lax.broadcasted_iota(jnp.int32, (keys, queries), 1)
    return (key_index >= start_row) & (key_index <= query_index)


def attend_kernel(q_ref, k_ref, v_ref, start_ref, out_ref, log_ref):
    tokens = q_ref.shape[0]
    block = 256
    keys_all = k_ref[...]
    values_turned = v_ref[...].T
    lane = lax.broadcasted_iota(jnp.int32, (1, LANES), 1)
    sub = lax.broadcasted_iota(jnp.int32, (LANES, 1), 0)
    for place in range(tokens // block):
        rows = slice(place * block, (place + 1) * block)
        reach = (place + 1) * block
        query = q_ref[rows, :]
        start_row = start_ref[:, rows]
        allowed = allowed_block(start_row, 0, place * block, reach, block)
        parts = []
        for head in range(LANES // HEAD_DIM):
            mine = lane // HEAD_DIM == head
            query_head = query * mine.astype(BF16)
            scores = nt(keys_all[:reach], query_head) * (SCORE_SCALE * LOG2E)
            scores = jnp.where(allowed, scores, -1e30)
            peak = jnp.max(scores, axis=0, keepdims=True)
            raised = jnp.exp2(scores - peak)
            total = jnp.sum(raised, axis=0, keepdims=True)
            mixed = nn(values_turned[:, :reach], raised.astype(BF16)) / total
            parts.append(mixed)
            log_ref[0, head : head + 1, rows] = peak + jnp.log2(total)
        joined = jnp.where(sub // HEAD_DIM == 0, parts[0], parts[1])
        out_ref[rows, :] = joined.T.astype(BF16)


def attend(query, key, value, start_row):
    tokens, width = query.shape
    pairs = width // LANES
    column = pl.BlockSpec((tokens, LANES), lambda i: (0, i))
    return pl.pallas_call(
        attend_kernel,
        grid=(pairs,),
        in_specs=[column, column, column, pl.BlockSpec((1, tokens), lambda i: (0, 0))],
        out_specs=[column, pl.BlockSpec((1, 2, tokens), lambda i: (i, 0, 0))],
        out_shape=[
            jax.ShapeDtypeStruct((tokens, width), BF16),
            jax.ShapeDtypeStruct((pairs, 2, tokens), F32),
        ],
        compiler_params=pltpu.CompilerParams(vmem_limit_bytes=VMEM_BYTES),
        cost_estimate=lasts(10),
        name="attend",
    )(query, key, value, start_row)


def attend_back_kernel(
    q_ref, k_ref, v_ref, o_ref, do_ref, start_ref, log_ref, cos_ref, front_ref, back_ref,
    dq_ref, dk_ref, dv_ref, dq_acc,
):
    tokens = q_ref.shape[0]
    block = 256
    lane = lax.broadcasted_iota(jnp.int32, (1, LANES), 1)
    sub = lax.broadcasted_iota(jnp.int32, (LANES, 1), 0)
    query_all = q_ref[...]
    grad_all = do_ref[...]
    product = (o_ref[...].astype(F32) * grad_all.astype(F32)).T
    dots = [
        jnp.sum(product[head * HEAD_DIM : (head + 1) * HEAD_DIM], axis=0, keepdims=True)
        for head in range(LANES // HEAD_DIM)
    ]
    dq_acc[...] = jnp.zeros_like(dq_acc)
    for place in range(tokens // block):
        rows = slice(place * block, (place + 1) * block)
        tail = slice(place * block, tokens)
        keys = k_ref[rows, :]
        values = v_ref[rows, :]
        keys_turned = keys.T
        query = query_all[place * block :]
        grad = grad_all[place * block :]
        start_row = start_ref[:, tail]
        allowed = allowed_block(
            start_row, place * block, place * block, block, tokens - place * block
        )
        key_grad = jnp.zeros((block, LANES), F32)
        value_grad = jnp.zeros((block, LANES), F32)
        for head in range(LANES // HEAD_DIM):
            mine = lane // HEAD_DIM == head
            scores = nt(keys * mine.astype(BF16), query) * (SCORE_SCALE * LOG2E)
            weights = jnp.where(allowed, jnp.exp2(scores - log_ref[0, head : head + 1, tail]), 0.0)
            weight_grad = nt(values * mine.astype(BF16), grad)
            score_grad = (weights * (weight_grad - dots[head][:, place * block :])).astype(BF16)
            value_grad = jnp.where(mine, nn(weights.astype(BF16), grad), value_grad)
            key_grad = jnp.where(mine, nn(score_grad, query), key_grad)
            dq_acc[:, tail] += nn(
                keys_turned * (sub // HEAD_DIM == head).astype(BF16), score_grad
            )
        dv_ref[rows, :] = value_grad.astype(BF16)
        dk_ref[rows, :] = spin(
            key_grad * SCORE_SCALE, cos_ref[rows, :], -front_ref[rows, :], -back_ref[rows, :]
        ).astype(BF16)
    dq_ref[...] = spin(
        dq_acc[...].T * SCORE_SCALE, cos_ref[...], -front_ref[...], -back_ref[...]
    ).astype(BF16)


def attend_back(query, key, value, mixed, mixed_grad, start_row, logs, cosine, front, back):
    tokens, width = query.shape
    pairs = width // LANES
    column = pl.BlockSpec((tokens, LANES), lambda i: (0, i))
    table = pl.BlockSpec((tokens, LANES), lambda i: (0, 0))
    return pl.pallas_call(
        attend_back_kernel,
        grid=(pairs,),
        in_specs=[
            column, column, column, column, column,
            pl.BlockSpec((1, tokens), lambda i: (0, 0)),
            pl.BlockSpec((1, 2, tokens), lambda i: (i, 0, 0)),
            table, table, table,
        ],
        out_specs=[column, column, column],
        out_shape=[jax.ShapeDtypeStruct((tokens, width), BF16)] * 3,
        scratch_shapes=[pltpu.VMEM((LANES, tokens), F32)],
        compiler_params=pltpu.CompilerParams(vmem_limit_bytes=VMEM_BYTES),
        cost_estimate=lasts(11),
        name="attend_back",
    )(query, key, value, mixed, mixed_grad, start_row, logs, cosine, front, back)


def rope_tables(positions, width):
    half = HEAD_DIM // 2
    freqs = jnp.exp(jnp.arange(half, dtype=F32) * (-2.0 * math.log(ROPE_BASE) / HEAD_DIM))
    angles = positions.astype(F32)[:, None] * freqs[None, :]
    cosine, sine = jnp.cos(angles), jnp.sin(angles)
    zero = jnp.zeros_like(sine)
    heads = width // HEAD_DIM
    return (
        jnp.concatenate([cosine] * (2 * heads), axis=1),
        jnp.concatenate([-sine, zero] * heads, axis=1),
        jnp.concatenate([zero, sine] * heads, axis=1),
    )


def local(
    inputs,
    query_weight,
    key_weight,
    value_weight,
    out_weight,
    gate_weight,
    up_weight,
    down_weight,
    first_gain,
    second_gain,
    segment_ids,
    positions,
    out_grad,
):
    rows = lax.axis_size("row")
    cols = lax.axis_size("col")
    places = cols // 2
    row = lax.axis_index("row")
    col = lax.axis_index("col")
    core = col % 2
    place = col // 2
    tokens, feat = inputs.shape
    width = feat * cols
    half = width // 2
    quarter = tokens // places

    def core_swap(a):
        return lax.ppermute(a, "col", [(i, i ^ 1) for i in range(cols)])

    def plane_swap(a, step):
        return lax.ppermute(a, "col", [(i, i ^ (2 * step)) for i in range(cols)])

    def token_part(a, step):
        return lax.dynamic_slice_in_dim(a, (place ^ step) * quarter, quarter, 0)

    def feat_part(a, step):
        return lax.dynamic_slice_in_dim(a, (place ^ step) * feat, feat, 1)

    def own_first(w):
        return jnp.concatenate(
            [jnp.where(core == 0, w[:feat], w[feat:]), jnp.where(core == 0, w[feat:], w[:feat])], axis=0
        )

    def row_swap(a, step):
        return lax.ppermute(a, "row", [(i, i ^ step) for i in range(rows)])

    def gather_row(a):
        got, bit = {0: a}, rows // 2
        while bit:
            for step in list(got):
                got[step ^ bit] = row_swap(got[step], bit)
            bit //= 2
        return [got[step] for step in range(rows)]

    def reduce_row(parts, bit):
        parts = list(parts)
        while bit < rows:
            for at in range(rows - 2 * bit, -1, -2 * bit):
                sent = row_swap(parts[at + bit].astype(BF16), bit)
                parts[at] = parts[at].astype(F32) + sent.astype(F32)
            bit *= 2
        return parts[0]

    def row_part(a, step):
        size = a.shape[0] // rows
        return lax.dynamic_slice_in_dim(a, (row ^ step) * size, size, 0)

    def after(value, *others):
        return lax.optimization_barrier((value,) + others)[0]

    def put_rows(pieces):
        whole = jnp.zeros((tokens,) + pieces[0].shape[1:], pieces[0].dtype)
        for step, piece in enumerate(pieces):
            whole = lax.dynamic_update_slice_in_dim(whole, piece, (place ^ step) * quarter, 0)
        return whole

    def put_feats(pieces):
        whole = jnp.zeros((pieces[0].shape[0], half), pieces[0].dtype)
        for step, piece in enumerate(pieces):
            whole = lax.dynamic_update_slice_in_dim(whole, piece, (place ^ step) * feat, 1)
        return whole

    def spread(a):
        return [a] + [plane_swap(a, step) for step in range(1, places)]

    def to_parts(a):
        return put_feats(
            [token_part(a, 0)] + [plane_swap(token_part(a, s), s) for s in range(1, places)]
        )

    def to_home(a):
        return put_rows([feat_part(a, 0)] + [plane_swap(feat_part(a, s), s) for s in range(1, places)])

    def sum_cols(a):
        step = 1
        while step < cols:
            a = a + lax.ppermute(a, "col", [(i, i ^ step) for i in range(cols)])
            step *= 2
        return a

    gain_one = first_gain.astype(F32)[:, None]
    gain_two = second_gain.astype(F32)[:, None]

    def scaled(w, gain):
        return own_first((w.astype(F32) * gain).astype(BF16))

    def cut(w):
        part = w.shape[1] // rows
        return jnp.stack([w[:, s * part : (s + 1) * part] for s in range(rows)])

    def exchange(pieces):
        got = lax.all_to_all(pieces, "row", split_axis=0, concat_axis=0, tiled=True)
        return got.reshape(width, pieces.shape[2])

    def spread_weights(whole):
        if places != 4:
            return spread(whole)
        first, second = plane_swap(whole, 1), plane_swap(whole, 2)
        return [
            whole,
            first,
            second,
            jnp.concatenate([plane_swap(second[:half], 1), plane_swap(first[half:], 2)], axis=0),
        ]

    def plane_first(pieces):
        if places != 4:
            return pieces
        top, bottom = plane_swap(pieces[3][:half], 1), plane_swap(pieces[3][half:], 2)
        to_second = jnp.concatenate(
            [(pieces[2][:half].astype(F32) + top.astype(F32)).astype(BF16), pieces[2][half:]], axis=0
        )
        to_first = jnp.concatenate(
            [pieces[1][:half], (pieces[1][half:].astype(F32) + bottom.astype(F32)).astype(BF16)], axis=0
        )
        return [pieces[0], to_first, to_second]

    def plane_second(pieces, *hold):
        total = pieces[0].astype(F32)
        for s, piece in enumerate(pieces[1:], 1):
            total = total + (after(plane_swap(piece, s), *hold) if hold else plane_swap(piece, s)).astype(F32)
        return total.astype(BF16)

    def give_back(total):
        total = total.reshape(rows, 2 * feat, total.shape[1])
        return lax.all_to_all(total, "row", split_axis=0, concat_axis=0, tiled=True)

    starts = jnp.stack([row ^ s for s in range(rows)])
    cores = core.reshape(1)

    with jax.named_scope("prepare"):
        cosine, front, back = rope_tables(positions, LANES)
        start_row = jnp.sum(
            (segment_ids[None, :] < segment_ids[:, None]).astype(jnp.int32), axis=1
        )[None, :]
        up_cut = cut(scaled(up_weight, gain_two))
        down_cut = cut(own_first(down_weight))
        out_block = own_first(out_weight)
    with jax.named_scope("inputs"):
        x_own = put_feats(spread(inputs))
        x_other = core_swap(x_own)
    with jax.named_scope("qkv_row"):
        qkv_full = lax.all_gather(
            jnp.concatenate(
                [scaled(w, gain_one) for w in (query_weight, key_weight, value_weight)], axis=1
            ),
            "row",
            axis=0,
            tiled=True,
        )
    with jax.named_scope("grad_plane"):
        g_part = to_parts(after(out_grad, x_own))
    with jax.named_scope("gate_row"):
        gate_whole = exchange(cut(scaled(gate_weight, gain_two)))
        gate_whole = after(gate_whole, g_part, cosine, front, back, start_row, up_cut, down_cut, out_block)
    with jax.named_scope("up_row"):
        up_whole = exchange(after(up_cut, gate_whole))
    with jax.named_scope("out_row"):
        out_full = lax.all_gather(after(out_block, x_own), "row", axis=0, tiled=True)
    with jax.named_scope("down_row"):
        down_whole = exchange(after(down_cut, up_whole))
    with jax.named_scope("grad_row"):
        g_own = lax.all_gather(g_part, "row", axis=0, tiled=True)
    with jax.named_scope("gate_plane"):
        gates = spread_weights(gate_whole)
    with jax.named_scope("up_plane"):
        ups = spread_weights(up_whole)
    query, key, value, scale_one = project(
        feat, x_own, x_other, qkv_full, cosine, front, back
    )
    mixed, logs = attend(
        after(query, gates[1:3], up_whole),
        key, value, start_row,
    )
    mixed_in = after(mixed, gates[3:], ups[1:3], down_whole)

    def join_cores(own, other):
        return (own.astype(F32) + core_swap(other).astype(F32)).astype(BF16)

    def scatter_parts(low):
        total = token_part(low, 0).astype(F32)
        for s in range(1, places):
            total = total + plane_swap(token_part(low, s), s).astype(F32)
        return total

    with jax.named_scope("mix_plane"):
        own, other = unfold(feat, "mix", [mixed_in], [out_full])
        middle = token_part(x_own, 0).astype(F32) + scatter_parts(join_cores(after(own, ups[3:]), other))
    middle_low = after(middle.astype(BF16), g_own)
    with jax.named_scope("middle_row"):
        m_list = gather_row(middle_low)
        m_others = [core_swap(m) for m in m_list]
    with jax.named_scope("down_plane"):
        downs = spread_weights(after(down_whole, middle_low))
    square = jnp.sum(middle * middle, axis=1, keepdims=True)
    square = square + core_swap(square)
    scale_mid = lax.rsqrt(square / width + EPS)

    pairs = [slice(at, at + 2) for at in range(0, rows, 2)]
    found = []
    for pair in pairs:
        first = m_list[pair.start]
        if pair.start:
            first = after(first, downs[1:3])
        found.append(activate(feat, [first, m_list[pair.start + 1]], m_others[pair], gates, ups))
    hiddens = [f[0] for f in found]
    with jax.named_scope("grad_row"):
        g_own = after(g_own, m_others, hiddens[0])
        g_other = core_swap(g_own)
    parts, scaled_grads, down_parts = [None] * rows, [None] * len(pairs), None
    down_middle = None
    for at in reversed(range(len(pairs))):
        with jax.named_scope("unit_grad"):
            _, slope_gate, slope_up, scale = found[at]
            if down_parts is None:
                slope_gate = after(slope_gate, hiddens)
            else:
                slope_gate = after(slope_gate, down_parts[:1], low_kept)
            gate_grad, up_grad, own, other = units_back(
                feat, starts[pairs[at]], g_own, g_other, slope_gate, slope_up, scale, gates, ups, downs
            )
            scaled_grads[at] = gate_grad, up_grad
            low = own.astype(F32) + core_swap(other).astype(F32)
            sent = low[quarter:].astype(BF16)
            parts[2 * at] = low[:quarter] + row_swap(sent, 1).astype(F32)
        if down_parts is None:
            with jax.named_scope("down_grad"):
                down_parts = outer(
                    feat, "down_outer", starts, [g_own], [g_other], [after(h, sent) for h in hiddens], places
                )
                down_middle = plane_first(down_parts)
        low_kept = parts[2 * at].astype(BF16)
    with jax.named_scope("unit_grad"):
        unit_grad = reduce_row(parts, 2)
    with jax.named_scope("down_grad"):
        down_total = plane_second(down_middle)
        down_blocks = give_back(down_total)

    unit_mid = middle * scale_mid
    dot_two = jnp.sum(unit_grad * unit_mid, axis=1, keepdims=True)
    dot_two = dot_two + core_swap(dot_two)
    middle_grad = g_part.astype(F32) + scale_mid * (unit_grad - unit_mid * (dot_two / width))

    d_low = after(middle_grad.astype(BF16), down_total)
    with jax.named_scope("middle_grad"):
        d_parts = lax.all_gather(d_low, "col")
    with jax.named_scope("feed"):
        kept = [unfold(feat, "feed", [after(h, low_kept, d_low)], downs) for h in hiddens]
        shares = []
        for own, other in kept:
            low = after((own.astype(F32) + core_swap(other).astype(F32)).astype(BF16), d_low)
            shares += [low[:quarter], low[quarter:]]
        sent = []
        for at in range(0, rows, 2):
            sent.append(shares[at].astype(F32) + row_swap(shares[at + 1], 1).astype(F32))
            shares[at] = sent[-1]
        feed = reduce_row(shares, 2)
    gate_parts = outer(feat, "gate_outer", starts, m_list, m_others, [after(a, d_low) for a, _ in scaled_grads], places)
    up_parts = outer(feat, "up_outer", starts, m_list, m_others, [a for _, a in scaled_grads], places)
    with jax.named_scope("gate_grad"):
        gate_middle = plane_first([after(a, d_low) for a in gate_parts])
    mixed_grad = fold(feat, cores, after(d_parts, gate_parts[:1], up_parts[:1], sent), out_full)
    query_grad, key_grad, value_grad = attend_back(
        query, key, value, mixed, after(mixed_grad, gate_middle[1:]), start_row, logs, cosine, front, back
    )
    with jax.named_scope("feed"):
        feed_low = (middle + after(feed, query_grad).astype(F32)).astype(BF16)
    with jax.named_scope("gate_grad"):
        gate_total = plane_second(gate_middle, *((query_grad,)))
        gate_blocks = give_back(gate_total)
    heads_in = after(query_grad, down_blocks, gate_total)
    heads_part, gain_dots = heads_outer(
        feat, cores, x_own, x_other, d_parts, heads_in, key_grad, value_grad, mixed, scale_one, qkv_full
    )
    with jax.named_scope("heads_grad"):
        heads_blocks = lax.psum_scatter(heads_part, "row", scatter_dimension=0, tiled=True)
    with jax.named_scope("first_plane"):
        first_low = join_cores(
            *unfold(feat, "first_grad", [after(query_grad, heads_part), key_grad, value_grad], [qkv_full])
        )
        first_unit_grad = scatter_parts(first_low)
    with jax.named_scope("up_grad"):
        up_total = plane_second(plane_first([after(a, gate_middle[1:]) for a in up_parts]))
        up_blocks = give_back(up_total)
    with jax.named_scope("block_out"):
        block_out = to_home(after(feed_low, up_total, first_low))
    scale_first = token_part(scale_one, 0)
    unit_first = token_part(x_own, 0).astype(F32) * scale_first
    dot_one = jnp.sum(first_unit_grad * unit_first, axis=1, keepdims=True)
    dot_one = dot_one + core_swap(dot_one)
    with jax.named_scope("input_grad"):
        input_grad = to_home(
            (after(middle_grad, up_total) + scale_first * (first_unit_grad - unit_first * (dot_one / width))).astype(BF16)
        )

    def row_dots(w, d):
        return jnp.sum(w.astype(F32) * d.astype(F32), axis=1)

    with jax.named_scope("gains"):
        dots = jnp.stack(
            [gain_dots[:, 0], row_dots(gates[0], gate_total) + row_dots(ups[0], up_total)]
        ).reshape(2, rows, 2, feat)
        dots = after(dots, input_grad)
        dots = sum_cols(jnp.where(core == 0, dots, dots[:, :, ::-1])).transpose(1, 0, 2, 3)
        dots = dots.reshape(rows, 2, 2 * feat)
        mine = lax.dynamic_index_in_dim(dots, row, 0, False)
        for s in range(1, rows):
            mine = mine + row_swap(lax.dynamic_index_in_dim(dots, row ^ s, 0, False), s)
        first_gain_grad = mine[0] / gain_one[:, 0]
        second_gain_grad = mine[1] / gain_two[:, 0]
    (down_weight_grad,) = finish(cores, down_blocks, gain_two, 0)
    (gate_weight_grad,) = finish(cores, gate_blocks, gain_two, 1)
    (up_weight_grad,) = finish(cores, up_blocks, gain_two, 1)
    heads_blocks = after(
        heads_blocks, down_weight_grad, gate_weight_grad, up_weight_grad, second_gain_grad, input_grad, block_out
    )
    query_weight_grad, key_weight_grad, value_weight_grad, out_weight_grad = finish(
        cores, heads_blocks[None], gain_one, 3, 4
    )
    return (
        block_out,
        input_grad,
        query_weight_grad,
        key_weight_grad,
        value_weight_grad,
        out_weight_grad,
        gate_weight_grad,
        up_weight_grad,
        down_weight_grad,
        first_gain_grad,
        second_gain_grad,
    )


def solution(mesh):
    grid, line = P("row", "col"), P("row")
    return jax.shard_map(
        local,
        mesh=mesh,
        in_specs=(grid,) * 8 + (line,) * 4 + (grid,),
        out_specs=(grid,) * 9 + (line,) * 2,
        check_vma=False,
    )
```

```python
import functools
import math

import jax
import jax.numpy as jnp
from jax import lax
from jax.experimental import pallas as pl
from jax.experimental.pallas import tpu as pltpu
from jax.sharding import PartitionSpec as P

HEAD_DIM = 64
LANES = 128
EPS = 1e-05
ROPE_BASE = 130000.0
LOG2E = math.log2(math.e)
SCORE_SCALE = HEAD_DIM**-0.5
BF16 = jnp.bfloat16
F32 = jnp.float32
VMEM_BYTES = 56 * 1024 * 1024


COST_RATE = 1e10


def lasts(microseconds):
    return pl.CostEstimate(flops=int(microseconds * COST_RATE), bytes_accessed=1, transcendentals=0)


def nn(left, right):
    return lax.dot_general(left, right, (((1,), (0,)), ((), ())), preferred_element_type=F32)


def nt(left, right):
    return lax.dot_general(left, right, (((1,), (1,)), ((), ())), preferred_element_type=F32)


def tn(left, right):
    return lax.dot_general(left, right, (((0,), (0,)), ((), ())), preferred_element_type=F32)


def spin(values, cosine, sine_front, sine_back):
    half = HEAD_DIM // 2
    lanes = values.shape[-1]
    return (
        values * cosine
        + pltpu.roll(values, lanes - half, 1) * sine_front
        + pltpu.roll(values, half, 1) * sine_back
    )


def weave(own, other, feat):
    pieces = []
    for at in range(0, own.shape[1], feat):
        pieces += [own[:, at : at + feat], other[:, at : at + feat]]
    return jnp.concatenate(pieces, axis=1)


def norm_scale(values):
    wide = values.astype(F32)
    return lax.rsqrt(jnp.sum(wide * wide, axis=1, keepdims=True) / values.shape[1] + EPS)


def whole_spec(a):
    return pl.BlockSpec(a.shape, lambda i: (0,) * a.ndim, pipeline_mode=pl.Buffered(1))


def row_spec(block, a):
    return pl.BlockSpec((block, a.shape[1]), lambda i: (i, 0))


def project_kernel(feat, own_ref, other_ref, weight_ref, cos_ref, front_ref, back_ref, *outs):
    values = weave(own_ref[...], other_ref[...], feat)
    scale = norm_scale(values)
    outs[3][...] = scale
    heads = outs[0].shape[1]
    times = heads // cos_ref.shape[1]
    cosine, front, back = (
        jnp.concatenate([ref[...]] * times, axis=1) for ref in (cos_ref, front_ref, back_ref)
    )
    for at, ref in enumerate(outs[:3]):
        result = nn(values, weight_ref[:, at * heads : (at + 1) * heads]) * scale
        if at < 2:
            result = spin(result, cosine, front, back)
        ref[...] = result.astype(BF16)


def project(feat, own, other, weight, cosine, front, back):
    tokens = own.shape[0]
    heads = weight.shape[1] // 3
    block = 256
    result = jax.ShapeDtypeStruct((tokens, heads), BF16)
    scale = jax.ShapeDtypeStruct((tokens, 1), F32)
    return pl.pallas_call(
        functools.partial(project_kernel, feat),
        grid=(tokens // block,),
        in_specs=[row_spec(block, own), row_spec(block, other), whole_spec(weight)]
        + [row_spec(block, cosine)] * 3,
        out_specs=[row_spec(block, result)] * 3 + [row_spec(block, scale)],
        out_shape=[result] * 3 + [scale],
        compiler_params=pltpu.CompilerParams(vmem_limit_bytes=40 * 1024 * 1024),
        cost_estimate=lasts(7),
        name="project",
    )(own, other, weight, cosine, front, back)


def unfold_kernel(feat, joined, *refs):
    own_ref, other_ref = refs[-2:]
    lefts, weights = refs[:joined], refs[joined:-2]
    left = jnp.concatenate([ref[...] for ref in lefts], axis=1)
    part = weights[0].shape[1]
    for at in range(0, own_ref.shape[1], feat):
        rows = slice(2 * at, 2 * (at + feat))
        total = None
        for i, weight in enumerate(weights):
            term = nt(left[:, i * part : (i + 1) * part], weight[rows, :])
            total = term if total is None else total + term
        own_ref[:, at : at + feat] = total[:, :feat].astype(BF16)
        other_ref[:, at : at + feat] = total[:, feat:].astype(BF16)


def unfold(feat, name, lefts, weights):
    tokens, half = lefts[0].shape[0], weights[0].shape[0] // 2
    block = 256
    result = jax.ShapeDtypeStruct((tokens, half), BF16)
    return pl.pallas_call(
        functools.partial(unfold_kernel, feat, len(lefts)),
        grid=(tokens // block,),
        in_specs=[row_spec(block, a) for a in lefts] + [whole_spec(w) for w in weights],
        out_specs=[row_spec(block, result)] * 2,
        out_shape=[result] * 2,
        compiler_params=pltpu.CompilerParams(vmem_limit_bytes=VMEM_BYTES),
        cost_estimate=lasts(6),
        name=name,
    )(*lefts, *weights)


def activate_kernel(feat, parts, count, *refs):
    m_owns, m_others, refs = refs[:parts], refs[parts : 2 * parts], refs[2 * parts :]
    sources, refs = refs[: 2 * count], refs[2 * count :]
    hidden_ref, gate_ref, up_ref, scale_ref, held, arrived = refs
    copies = [
        pltpu.make_async_copy(source, held.at[at], arrived.at[at]) for at, source in enumerate(sources)
    ]
    for copy in copies:
        copy.start()
    middle = jnp.concatenate(
        [weave(a[...], b[...], feat) for a, b in zip(m_owns, m_others)], axis=0
    )
    scale = norm_scale(middle)
    scale_ref[...] = scale
    part = hidden_ref.shape[1] // count
    for i in range(count):
        if i % 2 == 0:
            for copy in copies[2 * i : 2 * i + 4]:
                copy.wait()
        columns = slice(i * part, (i + 1) * part)
        gate = nn(middle, held[2 * i]) * scale
        up = nn(middle, held[2 * i + 1]) * scale
        sigmoid = 1.0 / (1.0 + jnp.exp(-gate))
        silu = gate * sigmoid
        hidden_ref[:, columns] = (silu * up).astype(BF16)
        gate_ref[:, columns] = (up * (sigmoid + silu * (1.0 - sigmoid))).astype(BF16)
        up_ref[:, columns] = silu.astype(BF16)


def activate(feat, m_owns, m_others, gates, ups):
    parts = len(m_owns)
    tokens = m_owns[0].shape[0]
    count, part = len(gates), gates[0].shape[1]
    hidden = jax.ShapeDtypeStruct((parts * tokens, count * part), BF16)
    weights = [w for two in zip(gates, ups) for w in two]
    vmem, anywhere = pl.BlockSpec(memory_space=pltpu.VMEM), pl.BlockSpec(memory_space=pl.ANY)
    return pl.pallas_call(
        functools.partial(activate_kernel, feat, parts, count),
        in_specs=[vmem] * (2 * parts) + [anywhere] * len(weights),
        out_specs=[vmem] * 4,
        out_shape=[hidden] * 3 + [jax.ShapeDtypeStruct((parts * tokens, 1), F32)],
        scratch_shapes=[
            pltpu.VMEM((len(weights),) + weights[0].shape, BF16),
            pltpu.SemaphoreType.DMA((len(weights),)),
        ],
        compiler_params=pltpu.CompilerParams(vmem_limit_bytes=36 * 1024 * 1024),
        cost_estimate=lasts(7.5),
        name="activate",
    )(*m_owns, *m_others, *weights)


def units_back_kernel(feat, parts, count, starts, *refs):
    g_sources, (gate_in, up_in, scale_in) = refs[:2], refs[2:5]
    sources, refs = refs[5 : 5 + 3 * count], refs[5 + 3 * count :]
    gate_ref, up_ref, own_ref, other_ref, held, arrived, g_held, g_arrived = refs
    tokens = own_ref.shape[0] // parts
    copies = [
        pltpu.make_async_copy(source, held.at[at], arrived.at[at]) for at, source in enumerate(sources)
    ]
    g_copies = [
        pltpu.make_async_copy(
            source.at[pl.ds(pl.multiple_of(starts[i] * tokens, tokens), tokens)],
            g_held.at[side, i],
            g_arrived.at[side, i],
        )
        for side, source in enumerate(g_sources)
        for i in range(parts)
    ]
    for copy in g_copies + copies:
        copy.start()
    for copy in g_copies + copies[:count]:
        copy.wait()
    grad = jnp.concatenate([weave(g_held[0, j], g_held[1, j], feat) for j in range(parts)], axis=0)
    scale = scale_in[...]
    part = gate_ref.shape[1] // count
    lefts = [], []
    for i in range(count):
        columns = slice(i * part, (i + 1) * part)
        hidden_grad = nn(grad, held[i])
        for side, (slope, out) in enumerate(((gate_in, gate_ref), (up_in, up_ref))):
            value = hidden_grad * slope[:, columns].astype(F32)
            out[:, columns] = (value * scale).astype(BF16)
            lefts[side].append(value.astype(BF16))
    left = jnp.concatenate(lefts[0] + lefts[1], axis=1)
    for copy in copies[count:]:
        copy.wait()
    for at in range(0, own_ref.shape[1], feat):
        rows = slice(2 * at, 2 * (at + feat))
        right = jnp.concatenate([held[i, rows, :] for i in range(count, 3 * count)], axis=1)
        total = nt(left, right)
        own_ref[:, at : at + feat] = total[:, :feat].astype(BF16)
        other_ref[:, at : at + feat] = total[:, feat:].astype(BF16)


def units_back(feat, starts, g_own, g_other, gate, up, scale, gates, ups, downs):
    tokens, half = gate.shape[0], g_own.shape[1]
    parts = starts.shape[0]
    count = len(gates)
    hidden = jax.ShapeDtypeStruct(gate.shape, BF16)
    share = jax.ShapeDtypeStruct((tokens, half), BF16)
    weights = downs + gates + ups
    vmem, anywhere = pl.BlockSpec(memory_space=pltpu.VMEM), pl.BlockSpec(memory_space=pl.ANY)
    return pl.pallas_call(
        functools.partial(units_back_kernel, feat, parts, count),
        in_specs=[pl.BlockSpec(memory_space=pltpu.SMEM)]
        + [anywhere] * 2
        + [vmem] * 3
        + [anywhere] * len(weights),
        out_specs=[vmem] * 4,
        out_shape=[hidden] * 2 + [share] * 2,
        scratch_shapes=[
            pltpu.VMEM((len(weights),) + weights[0].shape, BF16),
            pltpu.SemaphoreType.DMA((len(weights),)),
            pltpu.VMEM((2, parts, tokens // parts, half), BF16),
            pltpu.SemaphoreType.DMA((2, parts)),
        ],
        compiler_params=pltpu.CompilerParams(vmem_limit_bytes=40 * 1024 * 1024),
        cost_estimate=lasts(9.3),
        name="units_back",
    )(starts, g_own, g_other, gate, up, scale, *weights)


def outer_kernel(groups, count, starts, *refs):
    owns, others, rights = refs[:groups], refs[groups : 2 * groups], refs[2 * groups : len(refs) - count]
    outs = refs[len(refs) - count :]
    if groups == 1:
        tokens = owns[0].shape[0] // starts.shape[0]
        picks = [
            pl.ds(pl.multiple_of(starts[i] * tokens, tokens), tokens) for i in range(starts.shape[0])
        ]
        sides = [(owns[0][pick, :], others[0][pick, :]) for pick in picks]
    else:
        sides = [(own[...], other[...]) for own, other in zip(owns, others)]
    left = jnp.concatenate([jnp.concatenate(pair, axis=1) for pair in sides], axis=0)
    part = outs[0].shape[1]
    for i, out in enumerate(outs):
        columns = slice(i * part, (i + 1) * part)
        right = jnp.concatenate([ref[:, columns] for ref in rights], axis=0)
        out[...] = tn(left, right).astype(BF16)


def outer(feat, name, starts, owns, others, rights, count):
    half, columns = owns[0].shape[1], rights[0].shape[1]
    part = columns // count
    side = pl.BlockSpec((owns[0].shape[0], feat), lambda i: (0, i))
    return pl.pallas_call(
        functools.partial(outer_kernel, len(owns), count),
        grid=(half // feat,),
        in_specs=[pl.BlockSpec(memory_space=pltpu.SMEM)]
        + [side] * (2 * len(owns))
        + [whole_spec(a) for a in rights],
        out_specs=[pl.BlockSpec((2 * feat, part), lambda i: (i, 0))] * count,
        out_shape=[jax.ShapeDtypeStruct((2 * half, part), BF16)] * count,
        compiler_params=pltpu.CompilerParams(vmem_limit_bytes=40 * 1024 * 1024),
        cost_estimate=lasts(6.3),
        name=name,
    )(starts, *owns, *others, *rights)


def heads_outer_kernel(core_ref, x_own, x_other, parts_ref, dq_ref, dk_ref, dv_ref, mixed_ref, scale_ref, weight_ref, out_ref, dot_ref):
    part = mixed_ref.shape[1]
    left = jnp.concatenate([x_own[...], x_other[...]], axis=1)
    dots = None
    for i, ref in enumerate((dq_ref, dk_ref, dv_ref)):
        columns = slice(i * part, (i + 1) * part)
        result = tn(left, (ref[...].astype(F32) * scale_ref[...]).astype(BF16))
        out_ref[:, columns] = result.astype(BF16)
        term = jnp.sum(result * weight_ref[:, columns].astype(F32), axis=1, keepdims=True)
        dots = term if dots is None else dots + term
    dot_ref[...] = dots
    core = core_ref[0]
    left = jnp.concatenate(
        [
            jnp.concatenate([parts_ref[2 * i + core], parts_ref[2 * i + 1 - core]], axis=1)
            for i in range(parts_ref.shape[0] // 2)
        ],
        axis=0,
    )
    out_ref[:, 3 * part :] = tn(left, mixed_ref[...]).astype(BF16)


def heads_outer(feat, core, x_own, x_other, parts, dq, dk, dv, mixed, scale, weight):
    tokens, half = x_own.shape
    part = mixed.shape[1]
    side = pl.BlockSpec((tokens, feat), lambda i: (0, i))
    return pl.pallas_call(
        heads_outer_kernel,
        grid=(half // feat,),
        in_specs=[
            pl.BlockSpec(memory_space=pltpu.SMEM),
            side,
            side,
            pl.BlockSpec(parts.shape[:2] + (feat,), lambda i: (0, 0, i)),
        ]
        + [whole_spec(a) for a in (dq, dk, dv, mixed, scale)]
        + [row_spec(2 * feat, weight)],
        out_specs=[pl.BlockSpec((2 * feat, 4 * part), lambda i: (i, 0)), pl.BlockSpec((2 * feat, 1), lambda i: (i, 0))],
        out_shape=[
            jax.ShapeDtypeStruct((2 * half, 4 * part), BF16),
            jax.ShapeDtypeStruct((2 * half, 1), F32),
        ],
        compiler_params=pltpu.CompilerParams(vmem_limit_bytes=40 * 1024 * 1024),
        cost_estimate=lasts(9.4),
        name="heads_outer",
    )(core, x_own, x_other, parts, dq, dk, dv, mixed, scale, weight)


def finish_kernel(scaled, core_ref, part_ref, gain_ref, *outs):
    feat = gain_ref.shape[0] // 2
    blocks, columns = part_ref.shape[0], part_ref.shape[2] // len(outs)
    for side in range(2):
        rows = slice(side * feat, (side + 1) * feat)
        start = pl.multiple_of(lax.rem(core_ref[0] + side, 2) * feat, feat)
        gain = gain_ref[rows, :]
        for block in range(blocks):
            for i, out in enumerate(outs):
                value = part_ref[block, pl.ds(start, feat), i * columns : (i + 1) * columns].astype(F32)
                at = block * columns
                out[rows, at : at + columns] = value * gain if i < scaled else value


def finish(core, part, gain, scaled, count=1):
    blocks, rows, columns = part.shape
    vmem = pl.BlockSpec(memory_space=pltpu.VMEM)
    result = jax.ShapeDtypeStruct((rows, blocks * columns // count), F32)
    return pl.pallas_call(
        functools.partial(finish_kernel, scaled),
        in_specs=[pl.BlockSpec(memory_space=pltpu.SMEM), vmem, vmem],
        out_specs=[vmem] * count,
        out_shape=[result] * count,
        compiler_params=pltpu.CompilerParams(vmem_limit_bytes=VMEM_BYTES),
        cost_estimate=lasts(2.8),
        name="finish",
    )(core, part, gain)


def fold_kernel(feat, core_ref, parts_ref, weight_ref, out_ref):
    core = core_ref[0]
    values = weave(parts_ref[core], parts_ref[1 - core], feat)
    out_ref[...] = nn(values, weight_ref[...]).astype(BF16)


def fold(feat, core, parts, weight):
    count, tokens, half = parts.shape
    result = jax.ShapeDtypeStruct((count // 2 * tokens, weight.shape[1]), BF16)
    return pl.pallas_call(
        functools.partial(fold_kernel, feat),
        grid=(count // 2,),
        in_specs=[
            pl.BlockSpec(memory_space=pltpu.SMEM),
            pl.BlockSpec((2, tokens, half), lambda i: (i, 0, 0)),
            whole_spec(weight),
        ],
        out_specs=row_spec(tokens, result),
        out_shape=result,
        compiler_params=pltpu.CompilerParams(vmem_limit_bytes=40 * 1024 * 1024),
        cost_estimate=lasts(3.5),
        name="fold",
    )(core, parts, weight)


def allowed_block(start_row, key_base, query_base, keys, queries):
    key_index = key_base + lax.broadcasted_iota(jnp.int32, (keys, queries), 0)
    query_index = query_base + lax.broadcasted_iota(jnp.int32, (keys, queries), 1)
    return (key_index >= start_row) & (key_index <= query_index)


def attend_kernel(q_ref, k_ref, v_ref, start_ref, out_ref, log_ref):
    tokens = q_ref.shape[0]
    block = 256
    keys_all = k_ref[...]
    values_turned = v_ref[...].T
    lane = lax.broadcasted_iota(jnp.int32, (1, LANES), 1)
    sub = lax.broadcasted_iota(jnp.int32, (LANES, 1), 0)
    for place in range(tokens // block):
        rows = slice(place * block, (place + 1) * block)
        reach = (place + 1) * block
        query = q_ref[rows, :]
        start_row = start_ref[:, rows]
        allowed = allowed_block(start_row, 0, place * block, reach, block)
        parts = []
        for head in range(LANES // HEAD_DIM):
            mine = lane // HEAD_DIM == head
            query_head = query * mine.astype(BF16)
            scores = nt(keys_all[:reach], query_head) * (SCORE_SCALE * LOG2E)
            scores = jnp.where(allowed, scores, -1e30)
            peak = jnp.max(scores, axis=0, keepdims=True)
            raised = jnp.exp2(scores - peak)
            total = jnp.sum(raised, axis=0, keepdims=True)
            mixed = nn(values_turned[:, :reach], raised.astype(BF16)) / total
            parts.append(mixed)
            log_ref[0, head : head + 1, rows] = peak + jnp.log2(total)
        joined = jnp.where(sub // HEAD_DIM == 0, parts[0], parts[1])
        out_ref[rows, :] = joined.T.astype(BF16)


def attend(query, key, value, start_row):
    tokens, width = query.shape
    pairs = width // LANES
    column = pl.BlockSpec((tokens, LANES), lambda i: (0, i))
    return pl.pallas_call(
        attend_kernel,
        grid=(pairs,),
        in_specs=[column, column, column, pl.BlockSpec((1, tokens), lambda i: (0, 0))],
        out_specs=[column, pl.BlockSpec((1, 2, tokens), lambda i: (i, 0, 0))],
        out_shape=[
            jax.ShapeDtypeStruct((tokens, width), BF16),
            jax.ShapeDtypeStruct((pairs, 2, tokens), F32),
        ],
        compiler_params=pltpu.CompilerParams(vmem_limit_bytes=VMEM_BYTES),
        cost_estimate=lasts(10),
        name="attend",
    )(query, key, value, start_row)


def attend_back_kernel(
    q_ref, k_ref, v_ref, o_ref, do_ref, start_ref, log_ref, cos_ref, front_ref, back_ref,
    dq_ref, dk_ref, dv_ref, dq_acc,
):
    tokens = q_ref.shape[0]
    block = 256
    lane = lax.broadcasted_iota(jnp.int32, (1, LANES), 1)
    sub = lax.broadcasted_iota(jnp.int32, (LANES, 1), 0)
    query_all = q_ref[...]
    grad_all = do_ref[...]
    product = (o_ref[...].astype(F32) * grad_all.astype(F32)).T
    dots = [
        jnp.sum(product[head * HEAD_DIM : (head + 1) * HEAD_DIM], axis=0, keepdims=True)
        for head in range(LANES // HEAD_DIM)
    ]
    dq_acc[...] = jnp.zeros_like(dq_acc)
    for place in range(tokens // block):
        rows = slice(place * block, (place + 1) * block)
        tail = slice(place * block, tokens)
        keys = k_ref[rows, :]
        values = v_ref[rows, :]
        keys_turned = keys.T
        query = query_all[place * block :]
        grad = grad_all[place * block :]
        start_row = start_ref[:, tail]
        allowed = allowed_block(
            start_row, place * block, place * block, block, tokens - place * block
        )
        key_grad = jnp.zeros((block, LANES), F32)
        value_grad = jnp.zeros((block, LANES), F32)
        for head in range(LANES // HEAD_DIM):
            mine = lane // HEAD_DIM == head
            scores = nt(keys * mine.astype(BF16), query) * (SCORE_SCALE * LOG2E)
            weights = jnp.where(allowed, jnp.exp2(scores - log_ref[0, head : head + 1, tail]), 0.0)
            weight_grad = nt(values * mine.astype(BF16), grad)
            score_grad = (weights * (weight_grad - dots[head][:, place * block :])).astype(BF16)
            value_grad = jnp.where(mine, nn(weights.astype(BF16), grad), value_grad)
            key_grad = jnp.where(mine, nn(score_grad, query), key_grad)
            dq_acc[:, tail] += nn(
                keys_turned * (sub // HEAD_DIM == head).astype(BF16), score_grad
            )
        dv_ref[rows, :] = value_grad.astype(BF16)
        dk_ref[rows, :] = spin(
            key_grad * SCORE_SCALE, cos_ref[rows, :], -front_ref[rows, :], -back_ref[rows, :]
        ).astype(BF16)
    dq_ref[...] = spin(
        dq_acc[...].T * SCORE_SCALE, cos_ref[...], -front_ref[...], -back_ref[...]
    ).astype(BF16)


def attend_back(query, key, value, mixed, mixed_grad, start_row, logs, cosine, front, back):
    tokens, width = query.shape
    pairs = width // LANES
    column = pl.BlockSpec((tokens, LANES), lambda i: (0, i))
    table = pl.BlockSpec((tokens, LANES), lambda i: (0, 0))
    return pl.pallas_call(
        attend_back_kernel,
        grid=(pairs,),
        in_specs=[
            column, column, column, column, column,
            pl.BlockSpec((1, tokens), lambda i: (0, 0)),
            pl.BlockSpec((1, 2, tokens), lambda i: (i, 0, 0)),
            table, table, table,
        ],
        out_specs=[column, column, column],
        out_shape=[jax.ShapeDtypeStruct((tokens, width), BF16)] * 3,
        scratch_shapes=[pltpu.VMEM((LANES, tokens), F32)],
        compiler_params=pltpu.CompilerParams(vmem_limit_bytes=VMEM_BYTES),
        cost_estimate=lasts(11),
        name="attend_back",
    )(query, key, value, mixed, mixed_grad, start_row, logs, cosine, front, back)


def rope_tables(positions, width):
    half = HEAD_DIM // 2
    freqs = jnp.exp(jnp.arange(half, dtype=F32) * (-2.0 * math.log(ROPE_BASE) / HEAD_DIM))
    angles = positions.astype(F32)[:, None] * freqs[None, :]
    cosine, sine = jnp.cos(angles), jnp.sin(angles)
    zero = jnp.zeros_like(sine)
    heads = width // HEAD_DIM
    return (
        jnp.concatenate([cosine] * (2 * heads), axis=1),
        jnp.concatenate([-sine, zero] * heads, axis=1),
        jnp.concatenate([zero, sine] * heads, axis=1),
    )


def local(
    inputs,
    query_weight,
    key_weight,
    value_weight,
    out_weight,
    gate_weight,
    up_weight,
    down_weight,
    first_gain,
    second_gain,
    segment_ids,
    positions,
    out_grad,
):
    rows = lax.axis_size("row")
    cols = lax.axis_size("col")
    places = cols // 2
    row = lax.axis_index("row")
    col = lax.axis_index("col")
    core = col % 2
    place = col // 2
    tokens, feat = inputs.shape
    width = feat * cols
    half = width // 2
    quarter = tokens // places

    def core_swap(a):
        return lax.ppermute(a, "col", [(i, i ^ 1) for i in range(cols)])

    def plane_swap(a, step):
        return lax.ppermute(a, "col", [(i, i ^ (2 * step)) for i in range(cols)])

    def token_part(a, step):
        return lax.dynamic_slice_in_dim(a, (place ^ step) * quarter, quarter, 0)

    def feat_part(a, step):
        return lax.dynamic_slice_in_dim(a, (place ^ step) * feat, feat, 1)

    def own_first(w):
        return jnp.concatenate(
            [jnp.where(core == 0, w[:feat], w[feat:]), jnp.where(core == 0, w[feat:], w[:feat])], axis=0
        )

    def row_swap(a, step):
        return lax.ppermute(a, "row", [(i, i ^ step) for i in range(rows)])

    def gather_row(a):
        got, bit = {0: a}, rows // 2
        while bit:
            for step in list(got):
                got[step ^ bit] = row_swap(got[step], bit)
            bit //= 2
        return [got[step] for step in range(rows)]

    def reduce_row(parts, bit):
        parts = list(parts)
        while bit < rows:
            for at in range(rows - 2 * bit, -1, -2 * bit):
                sent = row_swap(parts[at + bit].astype(BF16), bit)
                parts[at] = parts[at].astype(F32) + sent.astype(F32)
            bit *= 2
        return parts[0]

    def row_part(a, step):
        size = a.shape[0] // rows
        return lax.dynamic_slice_in_dim(a, (row ^ step) * size, size, 0)

    def after(value, *others):
        return lax.optimization_barrier((value,) + others)[0]

    def put_rows(pieces):
        whole = jnp.zeros((tokens,) + pieces[0].shape[1:], pieces[0].dtype)
        for step, piece in enumerate(pieces):
            whole = lax.dynamic_update_slice_in_dim(whole, piece, (place ^ step) * quarter, 0)
        return whole

    def put_feats(pieces):
        whole = jnp.zeros((pieces[0].shape[0], half), pieces[0].dtype)
        for step, piece in enumerate(pieces):
            whole = lax.dynamic_update_slice_in_dim(whole, piece, (place ^ step) * feat, 1)
        return whole

    def spread(a):
        return [a] + [plane_swap(a, step) for step in range(1, places)]

    def to_parts(a):
        return put_feats(
            [token_part(a, 0)] + [plane_swap(token_part(a, s), s) for s in range(1, places)]
        )

    def to_home(a):
        return put_rows([feat_part(a, 0)] + [plane_swap(feat_part(a, s), s) for s in range(1, places)])

    def sum_cols(a):
        step = 1
        while step < cols:
            a = a + lax.ppermute(a, "col", [(i, i ^ step) for i in range(cols)])
            step *= 2
        return a

    gain_one = first_gain.astype(F32)[:, None]
    gain_two = second_gain.astype(F32)[:, None]

    def scaled(w, gain):
        return own_first((w.astype(F32) * gain).astype(BF16))

    def cut(w):
        part = w.shape[1] // rows
        return jnp.stack([w[:, s * part : (s + 1) * part] for s in range(rows)])

    def exchange(pieces):
        got = lax.all_to_all(pieces, "row", split_axis=0, concat_axis=0, tiled=True)
        return got.reshape(width, pieces.shape[2])

    def spread_weights(whole):
        if places != 4:
            return spread(whole)
        first, second = plane_swap(whole, 1), plane_swap(whole, 2)
        return [
            whole,
            first,
            second,
            jnp.concatenate([plane_swap(second[:half], 1), plane_swap(first[half:], 2)], axis=0),
        ]

    def plane_first(pieces):
        if places != 4:
            return pieces
        top, bottom = plane_swap(pieces[3][:half], 1), plane_swap(pieces[3][half:], 2)
        to_second = jnp.concatenate(
            [(pieces[2][:half].astype(F32) + top.astype(F32)).astype(BF16), pieces[2][half:]], axis=0
        )
        to_first = jnp.concatenate(
            [pieces[1][:half], (pieces[1][half:].astype(F32) + bottom.astype(F32)).astype(BF16)], axis=0
        )
        return [pieces[0], to_first, to_second]

    def plane_second(pieces, *hold):
        total = pieces[0].astype(F32)
        for s, piece in enumerate(pieces[1:], 1):
            total = total + (after(plane_swap(piece, s), *hold) if hold else plane_swap(piece, s)).astype(F32)
        return total.astype(BF16)

    def give_back(total):
        total = total.reshape(rows, 2 * feat, total.shape[1])
        return lax.all_to_all(total, "row", split_axis=0, concat_axis=0, tiled=True)

    starts = jnp.stack([row ^ s for s in range(rows)])
    cores = core.reshape(1)

    with jax.named_scope("prepare"):
        cosine, front, back = rope_tables(positions, LANES)
        start_row = jnp.sum(
            (segment_ids[None, :] < segment_ids[:, None]).astype(jnp.int32), axis=1
        )[None, :]
        up_cut = cut(scaled(up_weight, gain_two))
        down_cut = cut(own_first(down_weight))
        out_block = own_first(out_weight)
    with jax.named_scope("inputs"):
        x_own = put_feats(spread(inputs))
        x_other = core_swap(x_own)
    with jax.named_scope("qkv_row"):
        qkv_full = lax.all_gather(
            jnp.concatenate(
                [scaled(w, gain_one) for w in (query_weight, key_weight, value_weight)], axis=1
            ),
            "row",
            axis=0,
            tiled=True,
        )
    with jax.named_scope("grad_plane"):
        g_part = to_parts(after(out_grad, x_own))
    with jax.named_scope("gate_row"):
        gate_whole = exchange(cut(scaled(gate_weight, gain_two)))
        gate_whole = after(gate_whole, g_part, cosine, front, back, start_row, up_cut, down_cut, out_block)
    with jax.named_scope("up_row"):
        up_whole = exchange(after(up_cut, gate_whole, x_other))
    with jax.named_scope("out_row"):
        out_full = lax.all_gather(after(out_block, x_own), "row", axis=0, tiled=True)
    with jax.named_scope("down_row"):
        down_whole = exchange(after(down_cut, up_whole))
    with jax.named_scope("grad_row"):
        g_own = lax.all_gather(g_part, "row", axis=0, tiled=True)
    with jax.named_scope("gate_plane"):
        gates = spread_weights(gate_whole)
    with jax.named_scope("up_plane"):
        ups = spread_weights(up_whole)
    query, key, value, scale_one = project(
        feat, x_own, x_other, qkv_full, cosine, front, back
    )
    mixed, logs = attend(
        after(query, gates[1:3], up_whole, ups[1:3]),
        key, value, start_row,
    )
    mixed_in = after(mixed, gates[3:], ups[1:3], down_whole)

    def join_cores(own, other):
        return (own.astype(F32) + core_swap(other).astype(F32)).astype(BF16)

    def scatter_parts(low):
        total = token_part(low, 0).astype(F32)
        for s in range(1, places):
            total = total + plane_swap(token_part(low, s), s).astype(F32)
        return total

    with jax.named_scope("mix_plane"):
        own, other = unfold(feat, "mix", [mixed_in], [out_full])
        middle = token_part(x_own, 0).astype(F32) + scatter_parts(join_cores(own, other))
    middle_low = after(middle.astype(BF16), ups[3:], g_own)
    with jax.named_scope("middle_row"):
        m_list = gather_row(middle_low)
        m_others = [core_swap(m) for m in m_list]
    with jax.named_scope("down_plane"):
        downs = spread_weights(after(down_whole, middle_low))
    square = jnp.sum(middle * middle, axis=1, keepdims=True)
    square = square + core_swap(square)
    scale_mid = lax.rsqrt(square / width + EPS)

    pairs = [slice(at, at + 2) for at in range(0, rows, 2)]
    found = []
    for pair in pairs:
        first = m_list[pair.start]
        if pair.start:
            first = after(first, downs[1:3])
        found.append(activate(feat, [first, m_list[pair.start + 1]], m_others[pair], gates, ups))
    hiddens = [f[0] for f in found]
    with jax.named_scope("grad_row"):
        g_own = after(g_own, hiddens[0])
        g_other = core_swap(g_own)
    parts, scaled_grads, down_parts = [None] * rows, [None] * len(pairs), None
    down_middle = None
    for at in reversed(range(len(pairs))):
        with jax.named_scope("unit_grad"):
            _, slope_gate, slope_up, scale = found[at]
            if down_parts is None:
                slope_gate = after(slope_gate, hiddens)
            else:
                slope_gate = slope_gate
            gate_grad, up_grad, own, other = units_back(
                feat, starts[pairs[at]], g_own, g_other, slope_gate, slope_up, scale, gates, ups, downs
            )
            scaled_grads[at] = gate_grad, up_grad
            low = own.astype(F32) + core_swap(other).astype(F32)
            sent = low[quarter:].astype(BF16)
            parts[2 * at] = low[:quarter] + row_swap(sent, 1).astype(F32)
        if down_parts is None:
            with jax.named_scope("down_grad"):
                down_parts = outer(
                    feat, "down_outer", starts, [g_own], [g_other], [after(h, sent) for h in hiddens], places
                )
                down_middle = plane_first(down_parts)
        low_kept = parts[2 * at].astype(BF16)
    with jax.named_scope("unit_grad"):
        unit_grad = reduce_row(parts, 2)
    with jax.named_scope("down_grad"):
        down_total = plane_second(down_middle)
        down_blocks = give_back(down_total)

    unit_mid = middle * scale_mid
    dot_two = jnp.sum(unit_grad * unit_mid, axis=1, keepdims=True)
    dot_two = dot_two + core_swap(dot_two)
    middle_grad = g_part.astype(F32) + scale_mid * (unit_grad - unit_mid * (dot_two / width))

    d_low = after(middle_grad.astype(BF16), down_total)
    with jax.named_scope("middle_grad"):
        d_parts = lax.all_gather(d_low, "col")
    with jax.named_scope("feed"):
        kept = [unfold(feat, "feed", [after(h, low_kept)], downs) for h in hiddens]
        shares = []
        for own, other in kept:
            low = after((own.astype(F32) + core_swap(other).astype(F32)).astype(BF16), d_low)
            shares += [low[:quarter], low[quarter:]]
        sent = []
        for at in range(0, rows, 2):
            sent.append(shares[at].astype(F32) + row_swap(shares[at + 1], 1).astype(F32))
            shares[at] = sent[-1]
        feed = reduce_row(shares, 2)
    gate_parts = outer(feat, "gate_outer", starts, m_list, m_others, [after(a, d_low) for a, _ in scaled_grads], places)
    up_parts = outer(feat, "up_outer", starts, m_list, m_others, [a for _, a in scaled_grads], places)
    with jax.named_scope("gate_grad"):
        gate_middle = plane_first([after(a, d_low) for a in gate_parts])
    mixed_grad = fold(feat, cores, after(d_parts, gate_parts[:1], up_parts[:1], sent), out_full)
    query_grad, key_grad, value_grad = attend_back(
        query, key, value, mixed, after(mixed_grad, gate_middle[1:]), start_row, logs, cosine, front, back
    )
    with jax.named_scope("feed"):
        feed_low = (middle + after(feed, query_grad).astype(F32)).astype(BF16)
    with jax.named_scope("gate_grad"):
        gate_total = plane_second(gate_middle, *((query_grad,)))
        gate_blocks = give_back(gate_total)
    with jax.named_scope("up_grad"):
        up_total = plane_second(plane_first([after(a, gate_middle[1:]) for a in up_parts]))
        up_blocks = give_back(up_total)
    heads_in = after(query_grad, down_blocks)
    heads_part, gain_dots = heads_outer(
        feat, cores, x_own, x_other, d_parts, heads_in, key_grad, value_grad, mixed, scale_one, qkv_full
    )
    with jax.named_scope("heads_grad"):
        heads_blocks = lax.psum_scatter(heads_part, "row", scatter_dimension=0, tiled=True)
    with jax.named_scope("first_plane"):
        first_low = join_cores(
            *unfold(feat, "first_grad", [after(query_grad, heads_part), key_grad, value_grad], [qkv_full])
        )
        first_unit_grad = scatter_parts(first_low)
    with jax.named_scope("block_out"):
        block_out = to_home(after(feed_low, up_total, first_low))
    scale_first = token_part(scale_one, 0)
    unit_first = token_part(x_own, 0).astype(F32) * scale_first
    dot_one = jnp.sum(first_unit_grad * unit_first, axis=1, keepdims=True)
    dot_one = dot_one + core_swap(dot_one)
    with jax.named_scope("input_grad"):
        input_grad = to_home(
            (after(middle_grad, up_total) + scale_first * (first_unit_grad - unit_first * (dot_one / width))).astype(BF16)
        )

    def row_dots(w, d):
        return jnp.sum(w.astype(F32) * d.astype(F32), axis=1)

    with jax.named_scope("gains"):
        dots = jnp.stack(
            [gain_dots[:, 0], row_dots(gates[0], gate_total) + row_dots(ups[0], up_total)]
        ).reshape(2, rows, 2, feat)
        dots = after(dots, input_grad)
        dots = sum_cols(jnp.where(core == 0, dots, dots[:, :, ::-1])).transpose(1, 0, 2, 3)
        dots = dots.reshape(rows, 2, 2 * feat)
        mine = lax.dynamic_index_in_dim(dots, row, 0, False)
        for s in range(1, rows):
            mine = mine + row_swap(lax.dynamic_index_in_dim(dots, row ^ s, 0, False), s)
        first_gain_grad = mine[0] / gain_one[:, 0]
        second_gain_grad = mine[1] / gain_two[:, 0]
    (down_weight_grad,) = finish(cores, down_blocks, gain_two, 0)
    (gate_weight_grad,) = finish(cores, gate_blocks, gain_two, 1)
    (up_weight_grad,) = finish(cores, up_blocks, gain_two, 1)
    heads_blocks = after(
        heads_blocks, down_weight_grad, gate_weight_grad, up_weight_grad, second_gain_grad, input_grad, block_out
    )
    query_weight_grad, key_weight_grad, value_weight_grad, out_weight_grad = finish(
        cores, heads_blocks[None], gain_one, 3, 4
    )
    return (
        block_out,
        input_grad,
        query_weight_grad,
        key_weight_grad,
        value_weight_grad,
        out_weight_grad,
        gate_weight_grad,
        up_weight_grad,
        down_weight_grad,
        first_gain_grad,
        second_gain_grad,
    )


def solution(mesh):
    grid, line = P("row", "col"), P("row")
    return jax.shard_map(
        local,
        mesh=mesh,
        in_specs=(grid,) * 8 + (line,) * 4 + (grid,),
        out_specs=(grid,) * 9 + (line,) * 2,
        check_vma=False,
    )
```

```python
import functools
import math

import jax
import jax.numpy as jnp
from jax import lax
from jax.experimental import pallas as pl
from jax.experimental.pallas import tpu as pltpu
from jax.sharding import PartitionSpec as P

HEAD_DIM = 64
LANES = 128
EPS = 1e-05
ROPE_BASE = 130000.0
LOG2E = math.log2(math.e)
SCORE_SCALE = HEAD_DIM**-0.5
BF16 = jnp.bfloat16
F32 = jnp.float32
VMEM_BYTES = 56 * 1024 * 1024


COST_RATE = 1e10


def lasts(microseconds):
    return pl.CostEstimate(flops=int(microseconds * COST_RATE), bytes_accessed=1, transcendentals=0)


def nn(left, right):
    return lax.dot_general(left, right, (((1,), (0,)), ((), ())), preferred_element_type=F32)


def nt(left, right):
    return lax.dot_general(left, right, (((1,), (1,)), ((), ())), preferred_element_type=F32)


def tn(left, right):
    return lax.dot_general(left, right, (((0,), (0,)), ((), ())), preferred_element_type=F32)


def spin(values, cosine, sine_front, sine_back):
    half = HEAD_DIM // 2
    lanes = values.shape[-1]
    return (
        values * cosine
        + pltpu.roll(values, lanes - half, 1) * sine_front
        + pltpu.roll(values, half, 1) * sine_back
    )


def weave(own, other, feat):
    pieces = []
    for at in range(0, own.shape[1], feat):
        pieces += [own[:, at : at + feat], other[:, at : at + feat]]
    return jnp.concatenate(pieces, axis=1)


def norm_scale(values):
    wide = values.astype(F32)
    return lax.rsqrt(jnp.sum(wide * wide, axis=1, keepdims=True) / values.shape[1] + EPS)


def whole_spec(a):
    return pl.BlockSpec(a.shape, lambda i: (0,) * a.ndim, pipeline_mode=pl.Buffered(1))


def row_spec(block, a):
    return pl.BlockSpec((block, a.shape[1]), lambda i: (i, 0))


def project_kernel(feat, own_ref, other_ref, weight_ref, cos_ref, front_ref, back_ref, *outs):
    values = weave(own_ref[...], other_ref[...], feat)
    scale = norm_scale(values)
    outs[3][...] = scale
    heads = outs[0].shape[1]
    times = heads // cos_ref.shape[1]
    cosine, front, back = (
        jnp.concatenate([ref[...]] * times, axis=1) for ref in (cos_ref, front_ref, back_ref)
    )
    for at, ref in enumerate(outs[:3]):
        result = nn(values, weight_ref[:, at * heads : (at + 1) * heads]) * scale
        if at < 2:
            result = spin(result, cosine, front, back)
        ref[...] = result.astype(BF16)


def project(feat, own, other, weight, cosine, front, back):
    tokens = own.shape[0]
    heads = weight.shape[1] // 3
    block = 256
    result = jax.ShapeDtypeStruct((tokens, heads), BF16)
    scale = jax.ShapeDtypeStruct((tokens, 1), F32)
    return pl.pallas_call(
        functools.partial(project_kernel, feat),
        grid=(tokens // block,),
        in_specs=[row_spec(block, own), row_spec(block, other), whole_spec(weight)]
        + [row_spec(block, cosine)] * 3,
        out_specs=[row_spec(block, result)] * 3 + [row_spec(block, scale)],
        out_shape=[result] * 3 + [scale],
        compiler_params=pltpu.CompilerParams(vmem_limit_bytes=40 * 1024 * 1024),
        cost_estimate=lasts(7),
        name="project",
    )(own, other, weight, cosine, front, back)


def unfold_kernel(feat, joined, *refs):
    own_ref, other_ref = refs[-2:]
    lefts, weights = refs[:joined], refs[joined:-2]
    left = jnp.concatenate([ref[...] for ref in lefts], axis=1)
    part = weights[0].shape[1]
    for at in range(0, own_ref.shape[1], feat):
        rows = slice(2 * at, 2 * (at + feat))
        total = None
        for i, weight in enumerate(weights):
            term = nt(left[:, i * part : (i + 1) * part], weight[rows, :])
            total = term if total is None else total + term
        own_ref[:, at : at + feat] = total[:, :feat].astype(BF16)
        other_ref[:, at : at + feat] = total[:, feat:].astype(BF16)


def unfold(feat, name, lefts, weights):
    tokens, half = lefts[0].shape[0], weights[0].shape[0] // 2
    block = 256
    result = jax.ShapeDtypeStruct((tokens, half), BF16)
    return pl.pallas_call(
        functools.partial(unfold_kernel, feat, len(lefts)),
        grid=(tokens // block,),
        in_specs=[row_spec(block, a) for a in lefts] + [whole_spec(w) for w in weights],
        out_specs=[row_spec(block, result)] * 2,
        out_shape=[result] * 2,
        compiler_params=pltpu.CompilerParams(vmem_limit_bytes=VMEM_BYTES),
        cost_estimate=lasts(6),
        name=name,
    )(*lefts, *weights)


def activate_kernel(feat, parts, count, *refs):
    m_owns, m_others, refs = refs[:parts], refs[parts : 2 * parts], refs[2 * parts :]
    sources, refs = refs[: 2 * count], refs[2 * count :]
    hidden_ref, gate_ref, up_ref, scale_ref, held, arrived = refs
    copies = [
        pltpu.make_async_copy(source, held.at[at], arrived.at[at]) for at, source in enumerate(sources)
    ]
    for copy in copies:
        copy.start()
    middle = jnp.concatenate(
        [weave(a[...], b[...], feat) for a, b in zip(m_owns, m_others)], axis=0
    )
    scale = norm_scale(middle)
    scale_ref[...] = scale
    part = hidden_ref.shape[1] // count
    for i in range(count):
        if i % 2 == 0:
            for copy in copies[2 * i : 2 * i + 4]:
                copy.wait()
        columns = slice(i * part, (i + 1) * part)
        gate = nn(middle, held[2 * i]) * scale
        up = nn(middle, held[2 * i + 1]) * scale
        sigmoid = 1.0 / (1.0 + jnp.exp(-gate))
        silu = gate * sigmoid
        hidden_ref[:, columns] = (silu * up).astype(BF16)
        gate_ref[:, columns] = (up * (sigmoid + silu * (1.0 - sigmoid))).astype(BF16)
        up_ref[:, columns] = silu.astype(BF16)


def activate(feat, m_owns, m_others, gates, ups):
    parts = len(m_owns)
    tokens = m_owns[0].shape[0]
    count, part = len(gates), gates[0].shape[1]
    hidden = jax.ShapeDtypeStruct((parts * tokens, count * part), BF16)
    weights = [w for two in zip(gates, ups) for w in two]
    vmem, anywhere = pl.BlockSpec(memory_space=pltpu.VMEM), pl.BlockSpec(memory_space=pl.ANY)
    return pl.pallas_call(
        functools.partial(activate_kernel, feat, parts, count),
        in_specs=[vmem] * (2 * parts) + [anywhere] * len(weights),
        out_specs=[vmem] * 4,
        out_shape=[hidden] * 3 + [jax.ShapeDtypeStruct((parts * tokens, 1), F32)],
        scratch_shapes=[
            pltpu.VMEM((len(weights),) + weights[0].shape, BF16),
            pltpu.SemaphoreType.DMA((len(weights),)),
        ],
        compiler_params=pltpu.CompilerParams(vmem_limit_bytes=36 * 1024 * 1024),
        cost_estimate=lasts(7.5),
        name="activate",
    )(*m_owns, *m_others, *weights)


def units_back_kernel(feat, parts, count, starts, *refs):
    g_sources, (gate_in, up_in, scale_in) = refs[:2], refs[2:5]
    sources, refs = refs[5 : 5 + 3 * count], refs[5 + 3 * count :]
    gate_ref, up_ref, own_ref, other_ref, held, arrived, g_held, g_arrived = refs
    tokens = own_ref.shape[0] // parts
    copies = [
        pltpu.make_async_copy(source, held.at[at], arrived.at[at]) for at, source in enumerate(sources)
    ]
    g_copies = [
        pltpu.make_async_copy(
            source.at[pl.ds(pl.multiple_of(starts[i] * tokens, tokens), tokens)],
            g_held.at[side, i],
            g_arrived.at[side, i],
        )
        for side, source in enumerate(g_sources)
        for i in range(parts)
    ]
    for copy in g_copies + copies:
        copy.start()
    for copy in g_copies + copies[:count]:
        copy.wait()
    grad = jnp.concatenate([weave(g_held[0, j], g_held[1, j], feat) for j in range(parts)], axis=0)
    scale = scale_in[...]
    part = gate_ref.shape[1] // count
    lefts = [], []
    for i in range(count):
        columns = slice(i * part, (i + 1) * part)
        hidden_grad = nn(grad, held[i])
        for side, (slope, out) in enumerate(((gate_in, gate_ref), (up_in, up_ref))):
            value = hidden_grad * slope[:, columns].astype(F32)
            out[:, columns] = (value * scale).astype(BF16)
            lefts[side].append(value.astype(BF16))
    left = jnp.concatenate(lefts[0] + lefts[1], axis=1)
    for copy in copies[count:]:
        copy.wait()
    for at in range(0, own_ref.shape[1], feat):
        rows = slice(2 * at, 2 * (at + feat))
        right = jnp.concatenate([held[i, rows, :] for i in range(count, 3 * count)], axis=1)
        total = nt(left, right)
        own_ref[:, at : at + feat] = total[:, :feat].astype(BF16)
        other_ref[:, at : at + feat] = total[:, feat:].astype(BF16)


def units_back(feat, starts, g_own, g_other, gate, up, scale, gates, ups, downs):
    tokens, half = gate.shape[0], g_own.shape[1]
    parts = starts.shape[0]
    count = len(gates)
    hidden = jax.ShapeDtypeStruct(gate.shape, BF16)
    share = jax.ShapeDtypeStruct((tokens, half), BF16)
    weights = downs + gates + ups
    vmem, anywhere = pl.BlockSpec(memory_space=pltpu.VMEM), pl.BlockSpec(memory_space=pl.ANY)
    return pl.pallas_call(
        functools.partial(units_back_kernel, feat, parts, count),
        in_specs=[pl.BlockSpec(memory_space=pltpu.SMEM)]
        + [anywhere] * 2
        + [vmem] * 3
        + [anywhere] * len(weights),
        out_specs=[vmem] * 4,
        out_shape=[hidden] * 2 + [share] * 2,
        scratch_shapes=[
            pltpu.VMEM((len(weights),) + weights[0].shape, BF16),
            pltpu.SemaphoreType.DMA((len(weights),)),
            pltpu.VMEM((2, parts, tokens // parts, half), BF16),
            pltpu.SemaphoreType.DMA((2, parts)),
        ],
        compiler_params=pltpu.CompilerParams(vmem_limit_bytes=40 * 1024 * 1024),
        cost_estimate=lasts(9.3),
        name="units_back",
    )(starts, g_own, g_other, gate, up, scale, *weights)


def outer_kernel(groups, count, starts, *refs):
    owns, others, rights = refs[:groups], refs[groups : 2 * groups], refs[2 * groups : len(refs) - count]
    outs = refs[len(refs) - count :]
    if groups == 1:
        tokens = owns[0].shape[0] // starts.shape[0]
        picks = [
            pl.ds(pl.multiple_of(starts[i] * tokens, tokens), tokens) for i in range(starts.shape[0])
        ]
        sides = [(owns[0][pick, :], others[0][pick, :]) for pick in picks]
    else:
        sides = [(own[...], other[...]) for own, other in zip(owns, others)]
    left = jnp.concatenate([jnp.concatenate(pair, axis=1) for pair in sides], axis=0)
    part = outs[0].shape[1]
    for i, out in enumerate(outs):
        columns = slice(i * part, (i + 1) * part)
        right = jnp.concatenate([ref[:, columns] for ref in rights], axis=0)
        out[...] = tn(left, right).astype(BF16)


def outer(feat, name, starts, owns, others, rights, count):
    half, columns = owns[0].shape[1], rights[0].shape[1]
    part = columns // count
    side = pl.BlockSpec((owns[0].shape[0], feat), lambda i: (0, i))
    return pl.pallas_call(
        functools.partial(outer_kernel, len(owns), count),
        grid=(half // feat,),
        in_specs=[pl.BlockSpec(memory_space=pltpu.SMEM)]
        + [side] * (2 * len(owns))
        + [whole_spec(a) for a in rights],
        out_specs=[pl.BlockSpec((2 * feat, part), lambda i: (i, 0))] * count,
        out_shape=[jax.ShapeDtypeStruct((2 * half, part), BF16)] * count,
        compiler_params=pltpu.CompilerParams(vmem_limit_bytes=40 * 1024 * 1024),
        cost_estimate=lasts(6.3),
        name=name,
    )(starts, *owns, *others, *rights)


def heads_outer_kernel(core_ref, x_own, x_other, parts_ref, dq_ref, dk_ref, dv_ref, mixed_ref, scale_ref, weight_ref, out_ref, dot_ref):
    part = mixed_ref.shape[1]
    left = jnp.concatenate([x_own[...], x_other[...]], axis=1)
    dots = None
    for i, ref in enumerate((dq_ref, dk_ref, dv_ref)):
        columns = slice(i * part, (i + 1) * part)
        result = tn(left, (ref[...].astype(F32) * scale_ref[...]).astype(BF16))
        out_ref[:, columns] = result.astype(BF16)
        term = jnp.sum(result * weight_ref[:, columns].astype(F32), axis=1, keepdims=True)
        dots = term if dots is None else dots + term
    dot_ref[...] = dots
    core = core_ref[0]
    left = jnp.concatenate(
        [
            jnp.concatenate([parts_ref[2 * i + core], parts_ref[2 * i + 1 - core]], axis=1)
            for i in range(parts_ref.shape[0] // 2)
        ],
        axis=0,
    )
    out_ref[:, 3 * part :] = tn(left, mixed_ref[...]).astype(BF16)


def heads_outer(feat, core, x_own, x_other, parts, dq, dk, dv, mixed, scale, weight):
    tokens, half = x_own.shape
    part = mixed.shape[1]
    side = pl.BlockSpec((tokens, feat), lambda i: (0, i))
    return pl.pallas_call(
        heads_outer_kernel,
        grid=(half // feat,),
        in_specs=[
            pl.BlockSpec(memory_space=pltpu.SMEM),
            side,
            side,
            pl.BlockSpec(parts.shape[:2] + (feat,), lambda i: (0, 0, i)),
        ]
        + [whole_spec(a) for a in (dq, dk, dv, mixed, scale)]
        + [row_spec(2 * feat, weight)],
        out_specs=[pl.BlockSpec((2 * feat, 4 * part), lambda i: (i, 0)), pl.BlockSpec((2 * feat, 1), lambda i: (i, 0))],
        out_shape=[
            jax.ShapeDtypeStruct((2 * half, 4 * part), BF16),
            jax.ShapeDtypeStruct((2 * half, 1), F32),
        ],
        compiler_params=pltpu.CompilerParams(vmem_limit_bytes=40 * 1024 * 1024),
        cost_estimate=lasts(9.4),
        name="heads_outer",
    )(core, x_own, x_other, parts, dq, dk, dv, mixed, scale, weight)


def finish_kernel(scaled, core_ref, part_ref, gain_ref, *outs):
    feat = gain_ref.shape[0] // 2
    blocks, columns = part_ref.shape[0], part_ref.shape[2] // len(outs)
    for side in range(2):
        rows = slice(side * feat, (side + 1) * feat)
        start = pl.multiple_of(lax.rem(core_ref[0] + side, 2) * feat, feat)
        gain = gain_ref[rows, :]
        for block in range(blocks):
            for i, out in enumerate(outs):
                value = part_ref[block, pl.ds(start, feat), i * columns : (i + 1) * columns].astype(F32)
                at = block * columns
                out[rows, at : at + columns] = value * gain if i < scaled else value


def finish(core, part, gain, scaled, count=1):
    blocks, rows, columns = part.shape
    vmem = pl.BlockSpec(memory_space=pltpu.VMEM)
    result = jax.ShapeDtypeStruct((rows, blocks * columns // count), F32)
    return pl.pallas_call(
        functools.partial(finish_kernel, scaled),
        in_specs=[pl.BlockSpec(memory_space=pltpu.SMEM), vmem, vmem],
        out_specs=[vmem] * count,
        out_shape=[result] * count,
        compiler_params=pltpu.CompilerParams(vmem_limit_bytes=VMEM_BYTES),
        cost_estimate=lasts(2.8),
        name="finish",
    )(core, part, gain)


def fold_kernel(feat, core_ref, parts_ref, weight_ref, out_ref):
    core = core_ref[0]
    values = weave(parts_ref[core], parts_ref[1 - core], feat)
    out_ref[...] = nn(values, weight_ref[...]).astype(BF16)


def fold(feat, core, parts, weight):
    count, tokens, half = parts.shape
    result = jax.ShapeDtypeStruct((count // 2 * tokens, weight.shape[1]), BF16)
    return pl.pallas_call(
        functools.partial(fold_kernel, feat),
        grid=(count // 2,),
        in_specs=[
            pl.BlockSpec(memory_space=pltpu.SMEM),
            pl.BlockSpec((2, tokens, half), lambda i: (i, 0, 0)),
            whole_spec(weight),
        ],
        out_specs=row_spec(tokens, result),
        out_shape=result,
        compiler_params=pltpu.CompilerParams(vmem_limit_bytes=40 * 1024 * 1024),
        cost_estimate=lasts(3.5),
        name="fold",
    )(core, parts, weight)


def allowed_block(start_row, key_base, query_base, keys, queries):
    key_index = key_base + lax.broadcasted_iota(jnp.int32, (keys, queries), 0)
    query_index = query_base + lax.broadcasted_iota(jnp.int32, (keys, queries), 1)
    return (key_index >= start_row) & (key_index <= query_index)


def attend_kernel(q_ref, k_ref, v_ref, start_ref, out_ref, log_ref):
    tokens = q_ref.shape[0]
    block = 256
    keys_all = k_ref[...]
    values_turned = v_ref[...].T
    lane = lax.broadcasted_iota(jnp.int32, (1, LANES), 1)
    sub = lax.broadcasted_iota(jnp.int32, (LANES, 1), 0)
    for place in range(tokens // block):
        rows = slice(place * block, (place + 1) * block)
        reach = (place + 1) * block
        query = q_ref[rows, :]
        start_row = start_ref[:, rows]
        allowed = allowed_block(start_row, 0, place * block, reach, block)
        parts = []
        for head in range(LANES // HEAD_DIM):
            mine = lane // HEAD_DIM == head
            query_head = query * mine.astype(BF16)
            scores = nt(keys_all[:reach], query_head) * (SCORE_SCALE * LOG2E)
            scores = jnp.where(allowed, scores, -1e30)
            peak = jnp.max(scores, axis=0, keepdims=True)
            raised = jnp.exp2(scores - peak)
            total = jnp.sum(raised, axis=0, keepdims=True)
            mixed = nn(values_turned[:, :reach], raised.astype(BF16)) / total
            parts.append(mixed)
            log_ref[0, head : head + 1, rows] = peak + jnp.log2(total)
        joined = jnp.where(sub // HEAD_DIM == 0, parts[0], parts[1])
        out_ref[rows, :] = joined.T.astype(BF16)


def attend(query, key, value, start_row):
    tokens, width = query.shape
    pairs = width // LANES
    column = pl.BlockSpec((tokens, LANES), lambda i: (0, i))
    return pl.pallas_call(
        attend_kernel,
        grid=(pairs,),
        in_specs=[column, column, column, pl.BlockSpec((1, tokens), lambda i: (0, 0))],
        out_specs=[column, pl.BlockSpec((1, 2, tokens), lambda i: (i, 0, 0))],
        out_shape=[
            jax.ShapeDtypeStruct((tokens, width), BF16),
            jax.ShapeDtypeStruct((pairs, 2, tokens), F32),
        ],
        compiler_params=pltpu.CompilerParams(vmem_limit_bytes=VMEM_BYTES),
        cost_estimate=lasts(10),
        name="attend",
    )(query, key, value, start_row)


def attend_back_kernel(
    q_ref, k_ref, v_ref, o_ref, do_ref, start_ref, log_ref, cos_ref, front_ref, back_ref,
    dq_ref, dk_ref, dv_ref, dq_acc,
):
    tokens = q_ref.shape[0]
    block = 256
    lane = lax.broadcasted_iota(jnp.int32, (1, LANES), 1)
    sub = lax.broadcasted_iota(jnp.int32, (LANES, 1), 0)
    query_all = q_ref[...]
    grad_all = do_ref[...]
    product = (o_ref[...].astype(F32) * grad_all.astype(F32)).T
    dots = [
        jnp.sum(product[head * HEAD_DIM : (head + 1) * HEAD_DIM], axis=0, keepdims=True)
        for head in range(LANES // HEAD_DIM)
    ]
    dq_acc[...] = jnp.zeros_like(dq_acc)
    for place in range(tokens // block):
        rows = slice(place * block, (place + 1) * block)
        tail = slice(place * block, tokens)
        keys = k_ref[rows, :]
        values = v_ref[rows, :]
        keys_turned = keys.T
        query = query_all[place * block :]
        grad = grad_all[place * block :]
        start_row = start_ref[:, tail]
        allowed = allowed_block(
            start_row, place * block, place * block, block, tokens - place * block
        )
        key_grad = jnp.zeros((block, LANES), F32)
        value_grad = jnp.zeros((block, LANES), F32)
        for head in range(LANES // HEAD_DIM):
            mine = lane // HEAD_DIM == head
            scores = nt(keys * mine.astype(BF16), query) * (SCORE_SCALE * LOG2E)
            weights = jnp.where(allowed, jnp.exp2(scores - log_ref[0, head : head + 1, tail]), 0.0)
            weight_grad = nt(values * mine.astype(BF16), grad)
            score_grad = (weights * (weight_grad - dots[head][:, place * block :])).astype(BF16)
            value_grad = jnp.where(mine, nn(weights.astype(BF16), grad), value_grad)
            key_grad = jnp.where(mine, nn(score_grad, query), key_grad)
            dq_acc[:, tail] += nn(
                keys_turned * (sub // HEAD_DIM == head).astype(BF16), score_grad
            )
        dv_ref[rows, :] = value_grad.astype(BF16)
        dk_ref[rows, :] = spin(
            key_grad * SCORE_SCALE, cos_ref[rows, :], -front_ref[rows, :], -back_ref[rows, :]
        ).astype(BF16)
    dq_ref[...] = spin(
        dq_acc[...].T * SCORE_SCALE, cos_ref[...], -front_ref[...], -back_ref[...]
    ).astype(BF16)


def attend_back(query, key, value, mixed, mixed_grad, start_row, logs, cosine, front, back):
    tokens, width = query.shape
    pairs = width // LANES
    column = pl.BlockSpec((tokens, LANES), lambda i: (0, i))
    table = pl.BlockSpec((tokens, LANES), lambda i: (0, 0))
    return pl.pallas_call(
        attend_back_kernel,
        grid=(pairs,),
        in_specs=[
            column, column, column, column, column,
            pl.BlockSpec((1, tokens), lambda i: (0, 0)),
            pl.BlockSpec((1, 2, tokens), lambda i: (i, 0, 0)),
            table, table, table,
        ],
        out_specs=[column, column, column],
        out_shape=[jax.ShapeDtypeStruct((tokens, width), BF16)] * 3,
        scratch_shapes=[pltpu.VMEM((LANES, tokens), F32)],
        compiler_params=pltpu.CompilerParams(vmem_limit_bytes=VMEM_BYTES),
        cost_estimate=lasts(11),
        name="attend_back",
    )(query, key, value, mixed, mixed_grad, start_row, logs, cosine, front, back)


def rope_tables(positions, width):
    half = HEAD_DIM // 2
    freqs = jnp.exp(jnp.arange(half, dtype=F32) * (-2.0 * math.log(ROPE_BASE) / HEAD_DIM))
    angles = positions.astype(F32)[:, None] * freqs[None, :]
    cosine, sine = jnp.cos(angles), jnp.sin(angles)
    zero = jnp.zeros_like(sine)
    heads = width // HEAD_DIM
    return (
        jnp.concatenate([cosine] * (2 * heads), axis=1),
        jnp.concatenate([-sine, zero] * heads, axis=1),
        jnp.concatenate([zero, sine] * heads, axis=1),
    )


def local(
    inputs,
    query_weight,
    key_weight,
    value_weight,
    out_weight,
    gate_weight,
    up_weight,
    down_weight,
    first_gain,
    second_gain,
    segment_ids,
    positions,
    out_grad,
):
    rows = lax.axis_size("row")
    cols = lax.axis_size("col")
    places = cols // 2
    row = lax.axis_index("row")
    col = lax.axis_index("col")
    core = col % 2
    place = col // 2
    tokens, feat = inputs.shape
    width = feat * cols
    half = width // 2
    quarter = tokens // places

    def core_swap(a):
        return lax.ppermute(a, "col", [(i, i ^ 1) for i in range(cols)])

    def plane_swap(a, step):
        return lax.ppermute(a, "col", [(i, i ^ (2 * step)) for i in range(cols)])

    def token_part(a, step):
        return lax.dynamic_slice_in_dim(a, (place ^ step) * quarter, quarter, 0)

    def feat_part(a, step):
        return lax.dynamic_slice_in_dim(a, (place ^ step) * feat, feat, 1)

    def own_first(w):
        return jnp.concatenate(
            [jnp.where(core == 0, w[:feat], w[feat:]), jnp.where(core == 0, w[feat:], w[:feat])], axis=0
        )

    def row_swap(a, step):
        return lax.ppermute(a, "row", [(i, i ^ step) for i in range(rows)])

    def gather_row(a):
        got, bit = {0: a}, rows // 2
        while bit:
            for step in list(got):
                got[step ^ bit] = row_swap(got[step], bit)
            bit //= 2
        return [got[step] for step in range(rows)]

    def reduce_row(parts, bit):
        parts = list(parts)
        while bit < rows:
            for at in range(rows - 2 * bit, -1, -2 * bit):
                sent = row_swap(parts[at + bit].astype(BF16), bit)
                parts[at] = parts[at].astype(F32) + sent.astype(F32)
            bit *= 2
        return parts[0]

    def row_part(a, step):
        size = a.shape[0] // rows
        return lax.dynamic_slice_in_dim(a, (row ^ step) * size, size, 0)

    def after(value, *others):
        return lax.optimization_barrier((value,) + others)[0]

    def put_rows(pieces):
        whole = jnp.zeros((tokens,) + pieces[0].shape[1:], pieces[0].dtype)
        for step, piece in enumerate(pieces):
            whole = lax.dynamic_update_slice_in_dim(whole, piece, (place ^ step) * quarter, 0)
        return whole

    def put_feats(pieces):
        whole = jnp.concatenate([pieces[0]] * places, axis=1)
        for step, piece in enumerate(pieces):
            whole = lax.dynamic_update_slice_in_dim(whole, piece, (place ^ step) * feat, 1)
        return whole

    def spread(a):
        return [a] + [plane_swap(a, step) for step in range(1, places)]

    def to_parts(a):
        return put_feats(
            [token_part(a, 0)] + [plane_swap(token_part(a, s), s) for s in range(1, places)]
        )

    def to_home(a):
        return put_rows([feat_part(a, 0)] + [plane_swap(feat_part(a, s), s) for s in range(1, places)])

    def sum_cols(a):
        step = 1
        while step < cols:
            a = a + lax.ppermute(a, "col", [(i, i ^ step) for i in range(cols)])
            step *= 2
        return a

    gain_one = first_gain.astype(F32)[:, None]
    gain_two = second_gain.astype(F32)[:, None]

    def scaled(w, gain):
        return own_first((w.astype(F32) * gain).astype(BF16))

    def cut(w):
        part = w.shape[1] // rows
        return jnp.stack([w[:, s * part : (s + 1) * part] for s in range(rows)])

    def exchange(pieces):
        got = lax.all_to_all(pieces, "row", split_axis=0, concat_axis=0, tiled=True)
        return got.reshape(width, pieces.shape[2])

    def spread_weights(whole):
        if places != 4:
            return spread(whole)
        first, second = plane_swap(whole, 1), plane_swap(whole, 2)
        return [
            whole,
            first,
            second,
            jnp.concatenate([plane_swap(second[:half], 1), plane_swap(first[half:], 2)], axis=0),
        ]

    def plane_first(pieces):
        if places != 4:
            return pieces
        top, bottom = plane_swap(pieces[3][:half], 1), plane_swap(pieces[3][half:], 2)
        to_second = jnp.concatenate(
            [(pieces[2][:half].astype(F32) + top.astype(F32)).astype(BF16), pieces[2][half:]], axis=0
        )
        to_first = jnp.concatenate(
            [pieces[1][:half], (pieces[1][half:].astype(F32) + bottom.astype(F32)).astype(BF16)], axis=0
        )
        return [pieces[0], to_first, to_second]

    def plane_second(pieces, *hold):
        total = pieces[0].astype(F32)
        for s, piece in enumerate(pieces[1:], 1):
            total = total + (after(plane_swap(piece, s), *hold) if hold else plane_swap(piece, s)).astype(F32)
        return total.astype(BF16)

    def give_back(total):
        total = total.reshape(rows, 2 * feat, total.shape[1])
        return lax.all_to_all(total, "row", split_axis=0, concat_axis=0, tiled=True)

    starts = jnp.stack([row ^ s for s in range(rows)])
    cores = core.reshape(1)

    with jax.named_scope("prepare"):
        cosine, front, back = rope_tables(positions, LANES)
        start_row = jnp.sum(
            (segment_ids[None, :] < segment_ids[:, None]).astype(jnp.int32), axis=1
        )[None, :]
        up_cut = cut(scaled(up_weight, gain_two))
        down_cut = cut(own_first(down_weight))
        out_block = own_first(out_weight)
    with jax.named_scope("inputs"):
        x_own = put_feats(spread(inputs))
        x_other = core_swap(x_own)
    with jax.named_scope("qkv_row"):
        qkv_full = lax.all_gather(
            jnp.concatenate(
                [scaled(w, gain_one) for w in (query_weight, key_weight, value_weight)], axis=1
            ),
            "row",
            axis=0,
            tiled=True,
        )
    with jax.named_scope("grad_plane"):
        g_part = to_parts(after(out_grad, x_own))
    with jax.named_scope("gate_row"):
        gate_whole = exchange(cut(scaled(gate_weight, gain_two)))
        gate_whole = after(gate_whole, g_part, cosine, front, back, start_row, up_cut, down_cut, out_block)
    with jax.named_scope("up_row"):
        up_whole = exchange(after(up_cut, gate_whole, x_other))
    with jax.named_scope("out_row"):
        out_full = lax.all_gather(after(out_block, x_own), "row", axis=0, tiled=True)
    with jax.named_scope("down_row"):
        down_whole = exchange(after(down_cut, up_whole))
    with jax.named_scope("grad_row"):
        g_own = lax.all_gather(g_part, "row", axis=0, tiled=True)
    with jax.named_scope("gate_plane"):
        gates = spread_weights(gate_whole)
    with jax.named_scope("up_plane"):
        ups = spread_weights(up_whole)
    query, key, value, scale_one = project(
        feat, x_own, x_other, qkv_full, cosine, front, back
    )
    mixed, logs = attend(
        after(query, gates[1:3], up_whole, ups[1:3]),
        key, value, start_row,
    )
    mixed_in = after(mixed, gates[3:], ups[1:3], down_whole)

    def join_cores(own, other):
        return (own.astype(F32) + core_swap(other).astype(F32)).astype(BF16)

    def scatter_parts(low):
        total = token_part(low, 0).astype(F32)
        for s in range(1, places):
            total = total + plane_swap(token_part(low, s), s).astype(F32)
        return total

    with jax.named_scope("mix_plane"):
        own, other = unfold(feat, "mix", [mixed_in], [out_full])
        middle = token_part(x_own, 0).astype(F32) + scatter_parts(join_cores(own, other))
    middle_low = after(middle.astype(BF16), ups[3:], g_own)
    with jax.named_scope("middle_row"):
        m_list = gather_row(middle_low)
        m_others = [core_swap(m) for m in m_list]
    with jax.named_scope("down_plane"):
        downs = spread_weights(after(down_whole, middle_low))
    square = jnp.sum(middle * middle, axis=1, keepdims=True)
    square = square + core_swap(square)
    scale_mid = lax.rsqrt(square / width + EPS)

    pairs = [slice(at, at + 2) for at in range(0, rows, 2)]
    found = []
    for pair in pairs:
        first = m_list[pair.start]
        if pair.start:
            first = after(first, downs[1:3])
        found.append(activate(feat, [first, m_list[pair.start + 1]], m_others[pair], gates, ups))
    hiddens = [f[0] for f in found]
    with jax.named_scope("grad_row"):
        g_own = after(g_own, hiddens[0])
        g_other = core_swap(g_own)
    parts, scaled_grads, down_parts = [None] * rows, [None] * len(pairs), None
    down_middle = None
    for at in reversed(range(len(pairs))):
        with jax.named_scope("unit_grad"):
            _, slope_gate, slope_up, scale = found[at]
            if down_parts is None:
                slope_gate = after(slope_gate, hiddens)
            else:
                slope_gate = slope_gate
            gate_grad, up_grad, own, other = units_back(
                feat, starts[pairs[at]], g_own, g_other, slope_gate, slope_up, scale, gates, ups, downs
            )
            scaled_grads[at] = gate_grad, up_grad
            low = own.astype(F32) + core_swap(other).astype(F32)
            sent = low[quarter:].astype(BF16)
            parts[2 * at] = low[:quarter] + row_swap(sent, 1).astype(F32)
        if down_parts is None:
            with jax.named_scope("down_grad"):
                down_parts = outer(
                    feat, "down_outer", starts, [g_own], [g_other], [after(h, sent) for h in hiddens], places
                )
                down_middle = plane_first(down_parts)
        low_kept = parts[2 * at].astype(BF16)
    with jax.named_scope("unit_grad"):
        unit_grad = reduce_row(parts, 2)
    with jax.named_scope("down_grad"):
        down_total = plane_second(down_middle)
        down_blocks = give_back(down_total)

    unit_mid = middle * scale_mid
    dot_two = jnp.sum(unit_grad * unit_mid, axis=1, keepdims=True)
    dot_two = dot_two + core_swap(dot_two)
    middle_grad = g_part.astype(F32) + scale_mid * (unit_grad - unit_mid * (dot_two / width))

    d_low = after(middle_grad.astype(BF16), down_total)
    with jax.named_scope("middle_grad"):
        d_parts = lax.all_gather(d_low, "col")
    with jax.named_scope("feed"):
        kept = [unfold(feat, "feed", [after(h, low_kept)], downs) for h in hiddens]
        shares = []
        for own, other in kept:
            low = after((own.astype(F32) + core_swap(other).astype(F32)).astype(BF16), d_low)
            shares += [low[:quarter], low[quarter:]]
        sent = []
        for at in range(0, rows, 2):
            sent.append(shares[at].astype(F32) + row_swap(shares[at + 1], 1).astype(F32))
            shares[at] = sent[-1]
        feed = reduce_row(shares, 2)
    gate_parts = outer(feat, "gate_outer", starts, m_list, m_others, [after(a, d_low) for a, _ in scaled_grads], places)
    up_parts = outer(feat, "up_outer", starts, m_list, m_others, [a for _, a in scaled_grads], places)
    with jax.named_scope("gate_grad"):
        gate_middle = plane_first([after(a, d_low) for a in gate_parts])
    mixed_grad = fold(feat, cores, after(d_parts, gate_parts[:1], up_parts[:1], sent), out_full)
    query_grad, key_grad, value_grad = attend_back(
        query, key, value, mixed, after(mixed_grad, gate_middle[1:]), start_row, logs, cosine, front, back
    )
    with jax.named_scope("feed"):
        feed_low = (middle + after(feed, query_grad).astype(F32)).astype(BF16)
    with jax.named_scope("gate_grad"):
        gate_total = plane_second(gate_middle, *((query_grad,)))
        gate_blocks = give_back(gate_total)
    with jax.named_scope("up_grad"):
        up_total = plane_second(plane_first([after(a, gate_middle[1:]) for a in up_parts]))
        up_blocks = give_back(up_total)
    heads_in = after(query_grad, down_blocks)
    heads_part, gain_dots = heads_outer(
        feat, cores, x_own, x_other, d_parts, heads_in, key_grad, value_grad, mixed, scale_one, qkv_full
    )
    with jax.named_scope("heads_grad"):
        heads_blocks = lax.psum_scatter(heads_part, "row", scatter_dimension=0, tiled=True)
    with jax.named_scope("first_plane"):
        first_low = join_cores(
            *unfold(feat, "first_grad", [after(query_grad, heads_part), key_grad, value_grad], [qkv_full])
        )
        first_unit_grad = scatter_parts(first_low)
    with jax.named_scope("block_out"):
        block_out = to_home(after(feed_low, up_total, first_low))
    scale_first = token_part(scale_one, 0)
    unit_first = token_part(x_own, 0).astype(F32) * scale_first
    dot_one = jnp.sum(first_unit_grad * unit_first, axis=1, keepdims=True)
    dot_one = dot_one + core_swap(dot_one)
    with jax.named_scope("input_grad"):
        input_grad = to_home(
            (after(middle_grad, up_total) + scale_first * (first_unit_grad - unit_first * (dot_one / width))).astype(BF16)
        )

    def row_dots(w, d):
        return jnp.sum(w.astype(F32) * d.astype(F32), axis=1)

    with jax.named_scope("gains"):
        dots = jnp.stack(
            [gain_dots[:, 0], row_dots(gates[0], gate_total) + row_dots(ups[0], up_total)]
        ).reshape(2, rows, 2, feat)
        dots = after(dots, input_grad)
        dots = sum_cols(jnp.where(core == 0, dots, dots[:, :, ::-1])).transpose(1, 0, 2, 3)
        dots = dots.reshape(rows, 2, 2 * feat)
        mine = lax.dynamic_index_in_dim(dots, row, 0, False)
        for s in range(1, rows):
            mine = mine + row_swap(lax.dynamic_index_in_dim(dots, row ^ s, 0, False), s)
        first_gain_grad = mine[0] / gain_one[:, 0]
        second_gain_grad = mine[1] / gain_two[:, 0]
    (down_weight_grad,) = finish(cores, down_blocks, gain_two, 0)
    (gate_weight_grad,) = finish(cores, gate_blocks, gain_two, 1)
    (up_weight_grad,) = finish(cores, up_blocks, gain_two, 1)
    heads_blocks = after(
        heads_blocks, down_weight_grad, gate_weight_grad, up_weight_grad, second_gain_grad, input_grad, block_out
    )
    query_weight_grad, key_weight_grad, value_weight_grad, out_weight_grad = finish(
        cores, heads_blocks[None], gain_one, 3, 4
    )
    return (
        block_out,
        input_grad,
        query_weight_grad,
        key_weight_grad,
        value_weight_grad,
        out_weight_grad,
        gate_weight_grad,
        up_weight_grad,
        down_weight_grad,
        first_gain_grad,
        second_gain_grad,
    )


def solution(mesh):
    grid, line = P("row", "col"), P("row")
    return jax.shard_map(
        local,
        mesh=mesh,
        in_specs=(grid,) * 8 + (line,) * 4 + (grid,),
        out_specs=(grid,) * 9 + (line,) * 2,
        check_vma=False,
    )
```
